32 devices in a mesh: ctx: 8 (over z, y), fsdp: 4 (over x, core).
Axes of the slice: x: 2, y: 2, z: 4, core: 2. Of those that a mesh axis runs over, the one named last changes fastest.
Arguments:
- tokens: bfloat16 [8, 1024, 1536], P('fsdp', 'ctx'), may hold values from -6 to 6
- segments: int32 [8, 1024], P('fsdp'), may hold values from 0 to 6, as said below
- valid: int32 [8, 1024], P('fsdp'), may hold values from 0 to 1, as said below
- expert_ids: int32 [8, 1024, 8], P('fsdp', 'ctx'), may hold values from 0 to 15, all different within a row
- slot_order: int32 [8, 1024], P('fsdp', 'ctx'), may hold values from 0 to 127, as said below
- cotangent: bfloat16 [8, 1024, 1536], P('fsdp', 'ctx'), may hold values from -6 to 6
- norm1_gain: bfloat16 [1536], P('fsdp'), may hold values from 0.5 to 1.5
- w_query: bfloat16 [1536, 1536], P('fsdp'), may hold values from -0.15625 to 0.15625
- key_weight: bfloat16 [1536, 512], P('fsdp'), may hold values from -0.15625 to 0.15625
- value_weight: bfloat16 [1536, 512], P('fsdp'), may hold values from -0.15625 to 0.15625
- w_output: bfloat16 [1536, 1536], P('fsdp'), may hold values from -2.5 to 2.5
- norm2_gain: bfloat16 [1536], P('fsdp'), may hold values from 0.5 to 1.5
- w_router: bfloat16 [1536, 16], P('fsdp'), may hold values from -0.078125 to 0.078125
- w_gate: bfloat16 [1536, 16, 512], P('fsdp'), may hold values from -0.15625 to 0.15625
- w_up: bfloat16 [1536, 16, 512], P('fsdp'), may hold values from -0.15625 to 0.15625
- w_down: bfloat16 [1536, 16, 512], P('fsdp'), may hold values from -0.75 to 0.75
Outputs:
- layer_out: bfloat16 [8, 1024, 1536], P('fsdp', 'ctx')
- input_grad: bfloat16 [8, 1024, 1536], P('fsdp', 'ctx')
- grad_norm1_gain: float32 [1536], P(('ctx', 'fsdp'))
- grad_query: float32 [1536, 1536], P(('ctx', 'fsdp'))
- grad_key: float32 [1536, 512], P(('ctx', 'fsdp'))
- grad_value: float32 [1536, 512], P(('ctx', 'fsdp'))
- grad_output: float32 [1536, 1536], P(('ctx', 'fsdp'))
- grad_norm2_gain: float32 [1536], P(('ctx', 'fsdp'))
- grad_router: float32 [1536, 16], P(('ctx', 'fsdp'))
- grad_gate: float32 [1536, 16, 512], P(('ctx', 'fsdp'))
- grad_up: float32 [1536, 16, 512], P(('ctx', 'fsdp'))
- grad_down: float32 [1536, 16, 512], P(('ctx', 'fsdp'))
The draws below stay inside these ranges and needn't reach their ends.
Inputs may be any that keep to these rules, and one draw needn't show every extreme that they name: `segments`: segment numbers of a sequence start at 0 and never fall; documents hold 200 to 2000 tokens, the last one before padding possibly fewer; padding tokens carry 7 - 1; in each aligned run of 2 sequences one, drawn from the seed, is a single document. `valid`: each sequence is 1 on a leading run and 0 after it; the single-document sequences have no 0, every other one ends in at least one 0. `expert_ids`: the 8 experts of a token are different. `slot_order`: each aligned block of 128 tokens of a sequence holds a permutation of 0 to 127.
All inputs are finite; a program needn't handle non-finite values.
Results may differ from the reference program's by a relative error of at most 0.018.
Values may be sent and summed in bfloat16 or wider, within the bound.
A program may use at most 640 MiB of HBM per device.

```python
import jax
import jax.numpy as jnp
from jax import lax

D = 1536
QUERY_HEADS = 24
KEY_VALUE_HEADS = 8
HEAD_SIZE = 64
FF = 512
TOPK = 8
EXPERTS = 16
DOC_MIN = 200
DOC_MAX = 2000
SEQ_DEV = 128
SEQS = 2
BATCH = 8
LENGTH = 1024
QW = 1536
KVW = 512
CAP = 80
NDOC = 7


def doc_layout(key):
    lengths = jax.random.randint(key, (BATCH, NDOC), DOC_MIN, DOC_MAX + 1)
    ends = jnp.cumsum(lengths, axis=1)
    positions = jnp.arange(LENGTH, dtype=jnp.int32)
    segment_ids = jnp.sum((ends[:, None, :] <= positions[None, :, None]).astype(jnp.int32), axis=2)
    fitted = jnp.max(jnp.where(ends <= LENGTH, ends, 0), axis=1)
    filled = jnp.maximum(fitted, jnp.minimum(ends[:, 0], LENGTH))
    filled = jnp.minimum(filled, LENGTH - 1)
    live = (positions[None, :] < filled[:, None]).astype(jnp.int32)
    segment_ids = jnp.where(live > 0, segment_ids, NDOC - 1)
    whole_pick = jax.random.randint(jax.random.fold_in(key, 1), (BATCH // SEQS,), 0, SEQS)
    is_whole = jnp.repeat(whole_pick, SEQS) == jnp.arange(BATCH, dtype=jnp.int32) % SEQS
    segment_ids = jnp.where(is_whole[:, None], 0, segment_ids)
    live = jnp.where(is_whole[:, None], 1, live)
    return (segment_ids.astype(jnp.int32), live.astype(jnp.int32))


def draw_segments(key, part):
    shared = doc_layout(key)
    return shared[0]


def draw_valid(key, part):
    shared = doc_layout(key)
    return shared[1]


def draw_slot_order(key, part):
    key = jax.random.fold_in(key, 3)
    blocks = BATCH * (LENGTH // SEQ_DEV)
    block_keys = jax.random.split(key, blocks)
    orders = jax.vmap(lambda item_key: jax.random.permutation(item_key, SEQ_DEV))(block_keys)
    return orders.reshape(BATCH, LENGTH).astype(jnp.int32)


def levels(key, extent, shards, low, largest):
    level, own = 1.0, jax.random.fold_in(key, 6)
    for axis_at, shards_of in shards:
        heights = jnp.exp(jax.random.uniform(jax.random.fold_in(own, axis_at), (shards_of,), jnp.float32, low / len(shards), largest / len(shards)))
        level = level * jnp.repeat(heights, extent[axis_at] // shards_of).reshape([-1 if axis == axis_at else 1 for axis in range(len(extent))])
    return level


def choose_distinct(rng, rows, amount, top, lift):
    order = jax.random.permutation(jax.random.fold_in(rng, 1), amount)
    favour = order
    for power in range(3):
        favour = favour * favour // amount
    favour = favour * lift // amount
    chance = jax.random.randint(jax.random.fold_in(rng, 2), (rows, amount), 0, 4096) + favour
    fixed_rows = jax.random.permutation(jax.random.fold_in(rng, 3), rows)[jnp.arange(amount) % rows]
    chance = jnp.where(jnp.arange(rows)[:, None] == fixed_rows[None, :], 1 << 14, chance)
    priority = chance * amount + jnp.arange(amount)
    return lax.top_k(priority.astype(jnp.int32), top)[1].astype(jnp.int32)


def bell_draw(rng, extent, width, reach, cuts=(), held_as=jnp.bfloat16):
    result = width * jax.random.normal(rng, extent, jnp.float32)
    if cuts:
        result = result * levels(rng, extent, cuts, -0.22, 0.18)
    return jnp.clip(result, -reach, reach).astype(held_as)


def setup_inputs(seed: int = 0) -> dict:
    splits = jax.random.split(jax.random.key(seed), 17)
    return {
        "tokens": bell_draw(splits[0], (BATCH, LENGTH, D), 1.0, 6.0, ((0, 4), (1, 8))),
        "segments": draw_segments(jax.random.fold_in(splits[16], 71), 0),
        "valid": draw_valid(jax.random.fold_in(splits[16], 71), 0),
        "expert_ids": choose_distinct(splits[3], BATCH * LENGTH, EXPERTS, TOPK, 4096).reshape((BATCH, LENGTH, TOPK)),
        "slot_order": draw_slot_order(jax.random.fold_in(splits[16], 71), 0),
        "cotangent": bell_draw(splits[5], (BATCH, LENGTH, D), 1.0, 6.0, ((0, 4), (1, 8))),
        "norm1_gain": jnp.clip(1.0 + 0.1 * jax.random.normal(splits[6], (D,), jnp.float32), 0.5, 1.5).astype(jnp.bfloat16),
        "w_query": bell_draw(splits[7], (D, QW), D ** -0.5, 0.15625, ((0, 4),)),
        "key_weight": bell_draw(splits[8], (D, KVW), D ** -0.5, 0.15625, ((0, 4),)),
        "value_weight": bell_draw(splits[9], (D, KVW), D ** -0.5, 0.15625, ((0, 4),)),
        "w_output": bell_draw(splits[10], (D, QW), (max(QW // 256, 1)) ** -0.5, 2.5, ((0, 4),)),
        "norm2_gain": jnp.clip(1.0 + 0.1 * jax.random.normal(splits[11], (D,), jnp.float32), 0.5, 1.5).astype(jnp.bfloat16),
        "w_router": bell_draw(splits[12], (D, EXPERTS), (4 * D) ** -0.5, 0.078125, ((0, 4),)),
        "w_gate": bell_draw(splits[13], (D, EXPERTS, FF), D ** -0.5, 0.15625, ((0, 4),)),
        "w_up": bell_draw(splits[14], (D, EXPERTS, FF), D ** -0.5, 0.15625, ((0, 4),)),
        "w_down": bell_draw(splits[15], (D, EXPERTS, FF), (FF // 8) ** -0.5, 0.75, ((0, 4),)),
    }


HIGH_PRECISION = lax.Precision.HIGHEST
EPS = 1e-05
ROPE_BASE = 10000.0
MASKED = -1e+30

@jax.custom_vjp
def reduced_precision(v):
    return lax.optimization_barrier(v.astype(jnp.bfloat16)).astype(jnp.float32)

@jax.custom_vjp
def reduced_backward(v):
    return v

def low_keep(v):
    return (reduced_precision(v), None)

def low_pass(kept, grad):
    return (grad,)

def back_keep(v):
    return (v, None)

def back_low(kept, grad):
    return (reduced_precision(grad),)
reduced_precision.defvjp(low_keep, low_pass)
reduced_backward.defvjp(back_keep, back_low)

def rope_tables(count):
    half_dim = HEAD_SIZE // 2
    frequency = ROPE_BASE ** (-jnp.arange(half_dim, dtype=jnp.float32) * 2.0 / HEAD_SIZE)
    angle = jnp.arange(count, dtype=jnp.float32)[:, None] * frequency[None, :]
    angle = jnp.concatenate([angle, angle], axis=1)
    return (jnp.cos(angle), jnp.sin(angle))

def apply_rotation(field, cosine, sine_table):
    half_dim = field.shape[-1] // 2
    turned = jnp.concatenate([-field[..., half_dim:], field[..., :half_dim]], axis=-1)
    return field * cosine + turned * sine_table

def normed(field, gain_vec):
    return field * lax.rsqrt(lax.optimization_barrier(jnp.mean(field * field, axis=-1, keepdims=True)) + EPS) * gain_vec

def routes(choice_ids, order_rows):
    onehot = (choice_ids[..., None] == jnp.arange(EXPERTS, dtype=jnp.int32)).astype(jnp.int32)
    picked = lax.optimization_barrier(jnp.sum(onehot, axis=2))
    before = (order_rows[:, None, :] < order_rows[:, :, None]).astype(jnp.int32)
    counts = jnp.matmul(before, picked)
    place_in = lax.optimization_barrier(jnp.sum(onehot * counts[:, :, None, :], axis=-1))
    is_kept = place_in < CAP
    target = choice_ids * CAP + place_in
    slot_table = (target[..., None] == jnp.arange(EXPERTS * CAP, dtype=jnp.int32)) & is_kept[..., None]
    return (onehot.astype(jnp.float32), slot_table.astype(jnp.float32))

def attend_heads(layer_block, allowed_mask):
    query_head, key_head, value_head = layer_block
    raw_scores = jnp.einsum('rqd,kd->rqk', query_head, key_head, precision=HIGH_PRECISION) * HEAD_SIZE ** (-0.5)
    scores = jnp.where(allowed_mask[None], reduced_backward(raw_scores), MASKED)
    weights_soft = reduced_precision(jax.nn.softmax(scores, axis=-1))
    return jnp.einsum('rqk,kd->rqd', weights_soft, value_head, precision=HIGH_PRECISION)

def sequence_layer(params, inputs, seg_row, valid_row, choice_ids, order_row):
    gain_first, w_query, key_weight, value_weight, w_output, gain_second, w_router, w_gate, w_up, w_down = params
    token_length = inputs.shape[0]
    queries_per_group = QUERY_HEADS // KEY_VALUE_HEADS
    cosine, sine_table = rope_tables(token_length)
    cosine_heads = cosine[:, None, :]
    sine_heads = sine_table[:, None, :]
    normalized_input = reduced_precision(normed(inputs, gain_first))
    query_rows = reduced_backward(jnp.dot(normalized_input, w_query, precision=HIGH_PRECISION)).reshape(token_length, QUERY_HEADS, HEAD_SIZE)
    query_rows = reduced_precision(apply_rotation(query_rows, cosine_heads, sine_heads))
    key_row_block = reduced_backward(jnp.dot(normalized_input, key_weight, precision=HIGH_PRECISION)).reshape(token_length, KEY_VALUE_HEADS, HEAD_SIZE)
    key_row_block = reduced_precision(apply_rotation(key_row_block, cosine_heads, sine_heads))
    value_rows = reduced_precision(reduced_backward(jnp.dot(normalized_input, value_weight, precision=HIGH_PRECISION))).reshape(token_length, KEY_VALUE_HEADS, HEAD_SIZE)
    positions = jnp.arange(token_length, dtype=jnp.int32)
    allowed_mask = (seg_row[:, None] == seg_row[None, :]) & (positions[None, :] <= positions[:, None])
    allowed_mask = allowed_mask & ((valid_row[None, :] > 0) | (positions[None, :] == positions[:, None]))
    head_output = lax.map(jax.checkpoint(lambda layer_block: attend_heads(layer_block, allowed_mask)), (query_rows.reshape(token_length, KEY_VALUE_HEADS, queries_per_group, HEAD_SIZE).transpose(1, 2, 0, 3), key_row_block.transpose(1, 0, 2), value_rows.transpose(1, 0, 2)))
    mixed = reduced_precision(reduced_backward(head_output.transpose(2, 0, 1, 3).reshape(token_length, QUERY_HEADS * HEAD_SIZE)))
    residual = inputs + reduced_backward(jnp.einsum('lq,dq->ld', mixed, w_output, precision=HIGH_PRECISION))
    normed_mid = reduced_precision(normed(residual, gain_second))
    groups = token_length // SEQ_DEV
    mid_groups = normed_mid.reshape(groups, SEQ_DEV, D)
    onehot, slot_table = routes(choice_ids.reshape(groups, SEQ_DEV, TOPK), order_row.reshape(groups, SEQ_DEV))
    logits = reduced_backward(jnp.einsum('ngd,de->nge', mid_groups, w_router, precision=HIGH_PRECISION))
    chosen = lax.optimization_barrier(jnp.sum(onehot * logits[:, :, None, :], axis=-1))
    gate_weights = jax.nn.softmax(chosen, axis=-1)
    dispatch = lax.optimization_barrier(jnp.sum(slot_table, axis=2))
    expert_in = reduced_backward(jnp.einsum('ngx,ngd->nxd', dispatch, mid_groups, precision=HIGH_PRECISION))
    expert_in = expert_in.reshape(groups, EXPERTS, CAP, D)
    gate_pre = reduced_backward(jnp.einsum('necd,def->necf', expert_in, w_gate, precision=HIGH_PRECISION))
    up_pre = reduced_backward(jnp.einsum('necd,def->necf', expert_in, w_up, precision=HIGH_PRECISION))
    hidden = reduced_precision(jax.nn.silu(gate_pre) * up_pre)
    expert_out = reduced_precision(reduced_backward(jnp.einsum('necf,def->necd', hidden, w_down, precision=HIGH_PRECISION)))
    expert_out = expert_out.reshape(groups, EXPERTS * CAP, D)
    combine = reduced_precision(jnp.einsum('ngk,ngkx->ngx', gate_weights, slot_table, precision=HIGH_PRECISION))
    expert_mix = reduced_backward(jnp.einsum('ngx,nxd->ngd', combine, expert_out, precision=HIGH_PRECISION))
    return residual + expert_mix.reshape(token_length, D)

def reference(tokens, segments, valid, expert_ids, slot_order, cotangent, norm1_gain, w_query, key_weight, value_weight, w_output, norm2_gain, w_router, w_gate, w_up, w_down):
    params = tuple((weight.astype(jnp.float32) for weight in (norm1_gain, w_query, key_weight, value_weight, w_output, norm2_gain, w_router, w_gate, w_up, w_down)))
    per_seq = jax.checkpoint(sequence_layer)

    def forward(inputs, weights):
        return lax.map(lambda item_rows: per_seq(weights, *item_rows), (inputs, segments, valid, expert_ids, slot_order))
    layer_out, pullback = jax.vjp(forward, tokens.astype(jnp.float32), params)
    input_grad, gradients = pullback(cotangent.astype(jnp.float32))
    return (layer_out.astype(jnp.bfloat16), input_grad.astype(jnp.bfloat16), gradients[0], gradients[1], gradients[2], gradients[3], gradients[4], gradients[5], gradients[6], gradients[7], gradients[8], gradients[9])
```

```python
import functools

import jax
import jax.numpy as jnp
from jax import lax
from jax.experimental import pallas as pl
from jax.experimental.pallas import tpu as pltpu
from jax.sharding import PartitionSpec as P

D = 1536
QUERY_HEADS = 24
KEY_VALUE_HEADS = 8
REP = QUERY_HEADS // KEY_VALUE_HEADS
HEAD_SIZE = 64
FF = 512
EXPERTS = 16
CAP = 80
RANKS = 8
OWN = EXPERTS // RANKS
SEQS = 2
BLOCK = 128
KEYS = 256

EPS = 1e-05
ROPE_BASE = 10000.0
MASKED = -1e30
SCALE = HEAD_SIZE ** (-0.5)
MESH = pl.DeviceIdType.MESH
BF16 = jnp.bfloat16
F32 = jnp.float32


def flip(index, constant):
    result, bit = index, 1
    while bit <= constant:
        if constant & bit:
            result = result + bit - 2 * bit * lax.rem(lax.div(index, bit), 2)
        bit *= 2
    return result


def lasting(microseconds):
    return pl.CostEstimate(flops=0, bytes_accessed=int(microseconds * 3.3e6), transcendentals=0)


def exchange(cid, name, routes, operands, outs, microseconds=30):
    remote = [r for r in routes if r[0] or r[1]]
    local = [r for r in routes if not (r[0] or r[1])]
    amount = sum(len(r[2]) for r in remote)
    local_amount = sum(len(r[2]) for r in local)

    def kernel(*refs):
        ins = refs[: len(operands)]
        out = refs[len(operands) : len(operands) + len(outs)]
        send, recv, own = refs[len(operands) + len(outs) :]
        c, f = lax.axis_index("ctx"), lax.axis_index("fsdp")
        barrier = pltpu.get_barrier_semaphore()
        for dc, df, _ in remote:
            pl.semaphore_signal(
                barrier, inc=1, device_id=(flip(c, dc), flip(f, df)), device_id_type=MESH
            )
        copies = []
        for dc, df, moves in local:
            for a, src, b, dst in moves:
                copy = pltpu.make_async_copy(
                    ins[a].at[src(c, f)], out[b].at[dst(c, f)], own.at[len(copies)]
                )
                copy.start()
                copies.append(copy)
        pl.semaphore_wait(barrier, len(remote))
        number = 0
        for dc, df, moves in remote:
            for a, src, b, dst in moves:
                copy = pltpu.make_async_remote_copy(
                    ins[a].at[src(c, f)],
                    out[b].at[dst(c, f)],
                    send.at[number],
                    recv.at[number],
                    device_id=(flip(c, dc), flip(f, df)),
                    device_id_type=MESH,
                )
                copy.start()
                copies.append(copy)
                number += 1
        for copy in copies:
            copy.wait()

    anywhere = pl.BlockSpec(memory_space=pl.ANY)
    return pl.pallas_call(
        kernel,
        name=name,
        out_shape=[jax.ShapeDtypeStruct(shape, dtype) for shape, dtype in outs],
        in_specs=[anywhere] * len(operands),
        out_specs=[anywhere] * len(outs),
        scratch_shapes=[
            pltpu.SemaphoreType.DMA((amount,)),
            pltpu.SemaphoreType.DMA((amount,)),
            pltpu.SemaphoreType.DMA((max(local_amount, 1),)),
        ],
        compiler_params=pltpu.CompilerParams(collective_id=cid, has_side_effects=True),
        cost_estimate=lasting(microseconds),
    )(*operands)


PAY = D + 128
GROUPS = 4
ROWS = GROUPS * CAP


def other_chip(c, f, k):
    pair, x = lax.div(k, 2), lax.rem(k, 2)
    return (
        c + pair * (1 - 2 * lax.rem(c, 2)),
        f + 2 * x * (1 - 2 * lax.rem(lax.div(f, 2), 2)),
    )


def plane_order(replicas):
    order = [0]
    while len(order) < replicas:
        order = [2 * i for i in order] + [2 * i + 1 for i in order]
    return order


def experts_kernel(
    replicas, pay, cot, gate_own, up_own, down_own, after,
    back, mix, grads, pay_in, cot_in,
    weights, total, pay_now, cot_now, xs, gs, eo, gi, hid, dgate, dup, disp, comb,
    own, out, sib, ret, mix_now,
    send_first, recv_first, send_fwd, recv_fwd, send_sib, recv_sib, send_chip, recv_chip,
    load_w, load, store, piece_sem,
):
    c, f = lax.axis_index("ctx"), lax.axis_index("fsdp")
    rank = lax.rem(c, 2) * 4 + f
    sibling = (c, flip(f, 1))
    barrier = pltpu.get_barrier_semaphore()
    pl.semaphore_signal(barrier, inc=1, device_id=sibling, device_id_type=MESH)
    for k in range(1, 4):
        pl.semaphore_signal(barrier, inc=1, device_id=other_chip(c, f, k), device_id_type=MESH)
    bring = []
    for m, own_weight in enumerate((gate_own, up_own, down_own)):
        bring.append(pltpu.make_async_copy(own_weight, weights.at[m], load_w.at[m]))
        bring[-1].start()
    pl.semaphore_wait(barrier, 4)
    sources, landed = (pay, cot), (pay_in, cot_in)

    def push(k, a):
        slot = 1 if k == 0 else 2 * k
        return pltpu.make_async_remote_copy(
            sources[a], landed[a].at[slot - 1], send_first.at[k, a], recv_first.at[k, a],
            device_id=sibling if k == 0 else other_chip(c, f, k), device_id_type=MESH,
        )

    def forward(k, a):
        return pltpu.make_async_remote_copy(
            landed[a].at[2 * k - 1], landed[a].at[2 * k], send_fwd.at[k - 1, a], recv_fwd.at[k - 1, a],
            device_id=sibling, device_id_type=MESH,
        )

    def to_sibling(k):
        return pltpu.make_async_remote_copy(
            out.at[lax.rem(k, 2)], sib.at[k], send_sib.at[k], recv_sib.at[k],
            device_id=sibling, device_id_type=MESH,
        )

    def to_chip(k):
        return pltpu.make_async_remote_copy(
            sib.at[k], ret.at[k - 1], send_chip.at[k - 1], recv_chip.at[k - 1],
            device_id=other_chip(c, f, k), device_id_type=MESH,
        )

    def store_mix(k, s):
        return pltpu.make_async_copy(mix_now.at[s], mix.at[2 * k + s], store.at[s])

    for k, a in ((0, 0), (0, 1), (1, 0), (2, 0), (1, 1), (2, 1), (3, 0), (3, 1)):
        push(k, a).start()

    def clear(i, carry):
        total[lax.div(i, OWN), lax.rem(i, OWN)] = jnp.zeros((FF, D), F32)
        return carry

    lax.fori_loop(0, 3 * OWN, clear, 0)
    lane = lax.broadcasted_iota(jnp.int32, (BLOCK, 128), 1)
    wide = lax.broadcasted_iota(jnp.int32, (BLOCK, 2 * BLOCK), 1).astype(F32)
    both = lax.broadcasted_iota(jnp.int32, (BLOCK, OWN * CAP), 1)

    def chunk(k, carry):
        now = (pay_now, cot_now)

        def fetch(a, s, source):
            copy = pltpu.make_async_copy(source, now[a].at[s], load.at[a, s])
            copy.start()
            return copy

        @pl.when(k == 0)
        def _():
            copies = [fetch(a, 0, sources[a]) for a in range(2)]
            for a in range(2):
                push(0, a).wait_recv()
            copies += [fetch(a, 1, landed[a].at[0]) for a in range(2)]
            for copy in copies:
                copy.wait()
            for copy in bring:
                copy.wait()

        @pl.when(k > 0)
        def _():
            for a in range(2):
                pltpu.make_async_remote_copy(
                    sources[a], landed[a].at[2 * k - 1], send_first.at[k, a], recv_first.at[k, a],
                    device_id=other_chip(c, f, k), device_id_type=MESH,
                ).wait_recv()
                forward(k, a).start()
            copies = [fetch(a, 0, landed[a].at[2 * k - 1]) for a in range(2)]
            for a in range(2):
                forward(k, a).wait_recv()
            copies += [fetch(a, 1, landed[a].at[2 * k]) for a in range(2)]
            for copy in copies:
                copy.wait()

        for g in range(GROUPS):
            s, at = g // 2, (g % 2) * BLOCK
            tail = pay_now[s, at : at + BLOCK, D:].astype(F32)

            def column(index):
                return jnp.sum(jnp.where(lane == index, tail, 0.0), axis=1, keepdims=True)

            table = jnp.zeros((BLOCK, 2 * BLOCK), F32)
            gated = jnp.zeros((BLOCK, 2 * BLOCK), F32)
            for e in range(OWN):
                place = column(rank * OWN + e)
                place = jnp.where(place < 0.0, -1000.0, place + e * CAP)
                here = wide == place
                table = jnp.where(here, 1.0, table)
                gated = jnp.where(here, column(EXPERTS + rank * OWN + e), gated)
            table, gated = table.astype(BF16), gated.astype(BF16)
            disp[g] = table
            comb[g] = gated
            for weight, source, keep in (
                (table, pay_now[s, at : at + BLOCK, :D], xs),
                (gated, cot_now[s, at : at + BLOCK], gs),
            ):
                moved = lax.dot_general(
                    weight, source, (((0,), (0,)), ((), ())), preferred_element_type=F32
                ).astype(BF16)
                for e in range(OWN):
                    keep[e, g * CAP : (g + 1) * CAP] = moved[e * CAP : (e + 1) * CAP]

        def expert(e, carry):
            at = pl.multiple_of(e * CAP, 16)
            gate_pre = jnp.dot(xs[e], weights[0, e], preferred_element_type=F32)
            up_pre = jnp.dot(xs[e], weights[1, e], preferred_element_type=F32)
            sigmoid = 1.0 / (1.0 + jnp.exp(-gate_pre))
            activated = gate_pre * sigmoid
            hidden = (activated * up_pre).astype(BF16)
            hid[e] = hidden
            made = lax.dot_general(
                hidden, weights[2, e], (((1,), (1,)), ((), ())), preferred_element_type=F32
            ).astype(BF16)
            for g in range(GROUPS):
                eo[pl.ds(pl.multiple_of(g * OWN * CAP + at, 16), CAP)] = made[g * CAP : (g + 1) * CAP]
            grad_hidden = jnp.dot(gs[e], weights[2, e], preferred_element_type=F32)
            slope = sigmoid * (1.0 + gate_pre * (1.0 - sigmoid))
            grad_gate = (grad_hidden * up_pre * slope).astype(BF16)
            grad_up = (grad_hidden * activated).astype(BF16)
            dgate[e] = grad_gate
            dup[e] = grad_up
            made = lax.dot_general(
                grad_gate, weights[0, e], (((1,), (1,)), ((), ())), preferred_element_type=F32
            )
            made = made + lax.dot_general(
                grad_up, weights[1, e], (((1,), (1,)), ((), ())), preferred_element_type=F32
            )
            made = made.astype(BF16)
            for g in range(GROUPS):
                gi[pl.ds(pl.multiple_of(g * OWN * CAP + at, 16), CAP)] = made[g * CAP : (g + 1) * CAP]
            return carry

        lax.fori_loop(0, OWN, expert, 0)

        @pl.when(k > 0)
        def _():
            for s in range(2):
                store_mix(k - 1, s).wait()

        @pl.when(k > 1)
        def _():
            to_sibling(k - 2).wait_send()

        parity = lax.rem(k, 2)
        for g in range(GROUPS):
            s, at = g // 2, (g % 2) * BLOCK
            slots = pl.ds(g * OWN * CAP, OWN * CAP)
            made = eo[slots]
            mix_now[s, at : at + BLOCK] = jnp.dot(
                comb[g][:, : OWN * CAP], made, preferred_element_type=F32
            ).astype(BF16)
            table = disp[g][:, : OWN * CAP]
            grad_mid = jnp.dot(table, gi[slots], preferred_element_type=F32).astype(BF16)
            met = lax.dot_general(
                cot_now[s, at : at + BLOCK], made, (((1,), (1,)), ((), ())), preferred_element_type=F32
            ) * table.astype(F32)
            values = jnp.zeros((BLOCK, 128), F32)
            for e in range(OWN):
                inside = (both >= e * CAP) & (both < (e + 1) * CAP)
                value = jnp.sum(jnp.where(inside, met, 0.0), axis=1, keepdims=True)
                values = jnp.where(lane == rank * OWN + e, value, values)
            target = own if s == 0 else out
            target[parity, at : at + BLOCK, :D] = grad_mid
            target[parity, at : at + BLOCK, D:] = values.astype(BF16)
        to_sibling(k).start()
        for s in range(2):
            store_mix(k, s).start()

        def weight_grads(e, carry):
            for m, (left, right) in enumerate(((dgate, xs), (dup, xs), (hid, gs))):
                total[m, e] += lax.dot_general(
                    left[e], right[e], (((0,), (0,)), ((), ())), preferred_element_type=F32
                )
            return carry

        lax.fori_loop(0, OWN, weight_grads, 0)
        to_sibling(k).wait_recv()
        sib[k] = (sib[k].astype(F32) + own[parity].astype(F32)).astype(BF16)

        @pl.when(k > 0)
        def _():
            to_chip(k).start()

        return carry

    lax.fori_loop(0, 4, chunk, 0)
    for s in range(2):
        store_mix(3, s).wait()
    stages = (eo, gi)
    pending = []
    for i in range(3 * OWN):
        m, e = i // OWN, i % OWN
        if i >= 2:
            for copy in pending[i - 2]:
                copy.wait()
        stages[i % 2][:FF] = total[m, e].astype(BF16)
        pending.append([])
        if len(grads.shape) == 4:
            pending[i].append(
                pltpu.make_async_copy(stages[i % 2].at[:FF], grads.at[m, e], piece_sem.at[i % 2, 0])
            )
        else:
            width = D // replicas
            for at, plane in enumerate(plane_order(replicas)):
                pending[i].append(
                    pltpu.make_async_copy(
                        stages[i % 2].at[:FF, plane * width : (plane + 1) * width],
                        grads.at[m, at, e],
                        piece_sem.at[i % 2, at],
                    )
                )
        for copy in pending[i]:
            copy.start()
    for copy in pending[-2] + pending[-1]:
        copy.wait()
    for k in (2, 3):
        to_sibling(k).wait_send()
    for k in range(4):
        for a in range(2):
            push(k, a).wait_send()
            if k:
                forward(k, a).wait_send()
    for k in range(1, 4):
        to_chip(k).wait_recv()
    back[...] = (sib[0].astype(F32) + ret[0].astype(F32)) + (ret[1].astype(F32) + ret[2].astype(F32))
    for k in range(1, 4):
        to_chip(k).wait_send()


def run_experts(cid, replicas, pay, cot, owns, after):
    width = D // replicas
    apart = width % 128 == 0
    tokens = SEQS * BLOCK
    anywhere = pl.BlockSpec(memory_space=pl.ANY)
    inside = pl.BlockSpec(memory_space=pltpu.VMEM)
    dma = pltpu.SemaphoreType.DMA
    back, mix, grads, _, _ = pl.pallas_call(
        functools.partial(experts_kernel, replicas),
        name="experts",
        out_shape=[
            jax.ShapeDtypeStruct((tokens, PAY), F32),
            jax.ShapeDtypeStruct((RANKS, tokens, D), BF16),
            jax.ShapeDtypeStruct((3, replicas, OWN, FF, width) if apart else (3, OWN, FF, D), BF16),
            jax.ShapeDtypeStruct((RANKS - 1, tokens, PAY), BF16),
            jax.ShapeDtypeStruct((RANKS - 1, tokens, D), BF16),
        ],
        in_specs=[anywhere] * 6,
        out_specs=[inside] + [anywhere] * 4,
        scratch_shapes=[
            pltpu.VMEM((3, OWN, D, FF), BF16),
            pltpu.VMEM((3, OWN, FF, D), F32),
            pltpu.VMEM((2, tokens, PAY), BF16),
            pltpu.VMEM((2, tokens, D), BF16),
            pltpu.VMEM((OWN, ROWS, D), BF16),
            pltpu.VMEM((OWN, ROWS, D), BF16),
            pltpu.VMEM((OWN * ROWS, D), BF16),
            pltpu.VMEM((OWN * ROWS, D), BF16),
            pltpu.VMEM((OWN, ROWS, FF), BF16),
            pltpu.VMEM((OWN, ROWS, FF), BF16),
            pltpu.VMEM((OWN, ROWS, FF), BF16),
            pltpu.VMEM((GROUPS, BLOCK, 2 * BLOCK), BF16),
            pltpu.VMEM((GROUPS, BLOCK, 2 * BLOCK), BF16),
            pltpu.VMEM((2, tokens, PAY), BF16),
            pltpu.VMEM((2, tokens, PAY), BF16),
            pltpu.VMEM((4, tokens, PAY), BF16),
            pltpu.VMEM((3, tokens, PAY), BF16),
            pltpu.VMEM((2, tokens, D), BF16),
            dma((4, 2)), dma((4, 2)), dma((3, 2)), dma((3, 2)),
            dma((4,)), dma((4,)), dma((3,)), dma((3,)),
            dma((4,)), dma((2, 2)), dma((2,)), dma((2, replicas)),
        ],
        compiler_params=pltpu.CompilerParams(
            collective_id=cid, has_side_effects=True, vmem_limit_bytes=63 << 20
        ),
        cost_estimate=lasting(110),
    )(pay, cot, *owns, after)
    if not apart:
        grads = grads.reshape(3, OWN, FF, replicas, width).transpose(0, 3, 1, 2, 4)
        grads = grads[:, jnp.array(plane_order(replicas))]
    return back, mix, grads


def half_masks(dtype):
    lane = lax.broadcasted_iota(jnp.int32, (1, 2 * HEAD_SIZE), 1)
    low = (lane < HEAD_SIZE).astype(F32)
    return low.astype(dtype), (1.0 - low).astype(dtype)


def allowed_at(block, step, segq, keycode):
    token = block * BLOCK + lax.broadcasted_iota(jnp.int32, (BLOCK, KEYS), 0)
    key = step * KEYS + lax.broadcasted_iota(jnp.int32, (BLOCK, KEYS), 1)
    return ((segq == keycode) & (key < token)) | (key == token)


SMALL = 32


def turn(field, cosine, sine):
    half = HEAD_SIZE // 2
    lane = lax.broadcasted_iota(jnp.int32, field.shape, field.ndim - 1)
    up = pltpu.roll(field, 2 * HEAD_SIZE - half, field.ndim - 1)
    down = pltpu.roll(field, half, field.ndim - 1)
    return field * cosine + jnp.where(lax.rem(lane, HEAD_SIZE) < half, -up, down) * sine


def attention_forward_kernel(
    parts, n_ctx, tok, small, w_q, w_k, w_v, w_o, pack0, pack1, pack2, cos_ref, sin_ref, seg_ref, code_ref,
    normed, small_all, q_full, k_full, v_full, q_ref, kv_ref, full_ref, log_ref, o_back, o_full,
    gate_own, up_own, down_own,
    acc, q_pack, kv_pack, o_buf,
    send_w, recv_w, send_s, recv_s, send_e, recv_e, send_q, recv_q, send_kv, recv_kv, send_o, recv_o, here,
):
    c, f = lax.axis_index("ctx"), lax.axis_index("fsdp")
    head, part, pair = lax.div(c, parts), lax.rem(c, parts), lax.rem(c, 2)
    rows = D // 4
    half = rows // 2
    wide = 2 * HEAD_SIZE
    barrier = pltpu.get_barrier_semaphore()
    peers = [(i, 0) for i in range(1, n_ctx)] + [(0, k) for k in range(1, 4)]
    for dc, df in peers:
        pl.semaphore_signal(
            barrier, inc=1, device_id=(flip(c, dc), flip(f, df)), device_id_type=MESH
        )
    shards = (w_q, w_k, w_v, w_o)
    fulls = (q_full, k_full, v_full, o_full)
    packs, owns = (pack0, pack1, pack2), (gate_own, up_own, down_own)
    my_rows = pl.ds(pl.multiple_of(f * rows, rows), rows)
    local = [pltpu.make_async_copy(shards[a], fulls[a].at[f], here.at[a]) for a in range(4)]
    local += [pltpu.make_async_copy(small, small_all.at[f], here.at[4])]
    local += [pltpu.make_async_copy(packs[m].at[f], owns[m].at[:, my_rows], here.at[5 + m]) for m in range(3)]
    for copy in local:
        copy.start()
    pl.semaphore_wait(barrier, len(peers))
    near = pl.ds(pl.multiple_of(pair * half, half), half)
    far = pl.ds(pl.multiple_of((1 - pair) * half, half), half)
    sibling, over_x, over_pair = (c, flip(f, 1)), (c, flip(f, 2)), (flip(c, 1), f)

    def weight(a, kind):
        beyond = flip(f, 2)
        source, target, device = (
            (shards[a], fulls[a].at[f], sibling),
            (shards[a].at[near], fulls[a].at[f, near], over_x),
            (fulls[a].at[beyond, near], fulls[a].at[beyond, near], sibling),
            (fulls[a].at[beyond, near], fulls[a].at[beyond, near], over_pair),
            (fulls[a].at[beyond, far], fulls[a].at[beyond, far], sibling),
        )[kind]
        return pltpu.make_async_remote_copy(
            source, target, send_w.at[a, kind], recv_w.at[a, kind], device_id=device, device_id_type=MESH
        )

    smalls = [
        pltpu.make_async_remote_copy(
            small, small_all.at[f], send_s.at[i - 1], recv_s.at[i - 1],
            device_id=(c, flip(f, i)), device_id_type=MESH,
        )
        for i in range(1, 4)
    ]
    for copy in smalls:
        copy.start()
    for a in range(4):
        weight(a, 1).start()
        weight(a, 0).start()
    experts = [
        pltpu.make_async_remote_copy(
            packs[m].at[flip(f, i)], owns[m].at[:, my_rows], send_e.at[i - 1, m], recv_e.at[i - 1, m],
            device_id=(c, flip(f, i)), device_id_type=MESH,
        )
        for m in range(3)
        for i in range(1, 4)
    ]
    for copy in experts:
        copy.start()

    x = tok[...].astype(F32)
    scale = lax.rsqrt(jnp.mean(x * x, axis=1, keepdims=True) + EPS)
    for copy in smalls:
        copy.wait_recv()
    local[4].wait()
    for b in range(4):
        columns = slice(b * rows, (b + 1) * rows)
        normed[:, columns] = (x[:, columns] * scale * small_all[b, :1].astype(F32)).astype(BF16)

    def project(b, first):
        block = normed[:, pl.ds(pl.multiple_of(b * rows, rows), rows)]
        at = 0
        for a in range(3):
            width = fulls[a].shape[2]
            made = jnp.dot(block, fulls[a][b], preferred_element_type=F32)
            acc[:, at : at + width] = made if first else acc[:, at : at + width] + made
            at += width

    for a in range(3):
        local[a].wait()
    project(f, True)
    for a in range(3):
        weight(a, 0).wait_recv()
    project(flip(f, 1), False)
    for a in range(3):
        weight(a, 1).wait_recv()
        weight(a, 2).start()
        weight(a, 3).start()
    for a in range(3):
        weight(a, 3).wait_recv()
        weight(a, 4).start()
    project(flip(f, 2), False)
    for a in range(3):
        weight(a, 2).wait_recv()
        weight(a, 4).wait_recv()
    project(flip(f, 3), False)

    lane = lax.broadcasted_iota(jnp.int32, (BLOCK, wide), 1)
    low = lane < HEAD_SIZE
    cosine, sine = cos_ref[...], sin_ref[...]
    for m in range((QUERY_HEADS + 2 * KEY_VALUE_HEADS) // 2):
        pieces = []
        for s in range(SEQS):
            piece = acc[s * BLOCK : (s + 1) * BLOCK, m * wide : (m + 1) * wide]
            pieces.append(turn(piece, cosine, sine) if m < (QUERY_HEADS + KEY_VALUE_HEADS) // 2 else piece)
        even = jnp.where(low, pieces[0], pltpu.roll(pieces[1], HEAD_SIZE, 1)).astype(BF16)
        odd = jnp.where(low, pltpu.roll(pieces[0], HEAD_SIZE, 1), pieces[1]).astype(BF16)
        for h, value in ((2 * m, even), (2 * m + 1, odd)):
            if h < QUERY_HEADS:
                q_pack[h // REP, h % REP] = value
            else:
                h -= QUERY_HEADS
                kv_pack[h % KEY_VALUE_HEADS, h // KEY_VALUE_HEADS] = value

    q_stays = pltpu.make_async_copy(q_pack.at[head], q_ref.at[head], here.at[8])
    kv_stays = pltpu.make_async_copy(kv_pack.at[head], kv_ref.at[c], here.at[9])
    q_stays.start()
    kv_stays.start()
    to_heads = []
    for i in range(1, n_ctx):
        peer = flip(c, i)
        moves = [(kv_pack.at[lax.div(peer, parts)], kv_ref.at[c], send_kv.at[i - 1], recv_kv.at[i - 1])]
        if i % parts == 0:
            number = i // parts - 1
            moves.append(
                (q_pack.at[lax.div(peer, parts)], q_ref.at[head], send_q.at[number], recv_q.at[number])
            )
        for source, target, sent, came in moves:
            copy = pltpu.make_async_remote_copy(
                source, target, sent, came, device_id=(peer, f), device_id_type=MESH
            )
            copy.start()
            to_heads.append(copy)
    weight(3, 1).wait_recv()
    weight(3, 2).start()
    weight(3, 3).start()
    q_stays.wait()
    kv_stays.wait()
    for copy in to_heads:
        copy.wait_recv()

    count = REP * BLOCK
    halves = half_masks(BF16)
    across = lax.broadcasted_iota(jnp.int32, (count, wide), 1)

    def out_back(j):
        return pltpu.make_async_remote_copy(
            o_buf.at[j], o_back.at[head], send_o.at[j], recv_o.at[head],
            device_id=(j * parts + part, f), device_id_type=MESH,
        )

    def out_stays(j):
        return pltpu.make_async_copy(o_buf.at[j], o_back.at[head], here.at[10])

    def one_block(j, nothing):
        block = j * parts + part
        q = q_ref[j].reshape(count, wide)
        queries = [q * half for half in halves]

        def step(number, carry):
            k = kv_ref[pl.ds(2 * number, 2), 0].reshape(KEYS, wide)
            v = kv_ref[pl.ds(2 * number, 2), 1].reshape(KEYS, wide)
            codes = code_ref[number]
            after = []
            for s in range(SEQS):
                largest, total, out = carry[s]
                mask = allowed_at(block, number, seg_ref[j, s], codes[s : s + 1])
                scores = lax.dot_general(
                    queries[s], k, (((1,), (1,)), ((), ())), preferred_element_type=F32
                )
                scores = jnp.where(mask[None], scores.reshape(REP, BLOCK, KEYS) * SCALE, MASKED)
                scores = scores.reshape(count, KEYS)
                new = jnp.maximum(largest, jnp.max(scores, axis=1, keepdims=True))
                probs = jnp.exp(scores - new)
                shrink = jnp.exp(largest - new)
                total = total * shrink + jnp.sum(probs, axis=1, keepdims=True)
                out = out * shrink + jnp.dot(probs.astype(BF16), v, preferred_element_type=F32)
                after.append((new, total, out))
            return tuple(after)

        start = (
            jnp.full((count, 1), MASKED, F32),
            jnp.zeros((count, 1), F32),
            jnp.zeros((count, wide), F32),
        )
        done = lax.fori_loop(0, lax.div(block, 2) + 1, step, (start,) * SEQS)
        outs, logs = [], []
        for largest, total, out in done:
            outs.append(out / total)
            logs.append(jnp.broadcast_to(largest + jnp.log(total), (count, wide)))
        out = jnp.where(across < HEAD_SIZE, outs[0], outs[1])
        full_ref[j] = out.reshape(REP, BLOCK, wide)
        log_ref[j] = jnp.where(across < HEAD_SIZE, logs[0], logs[1]).reshape(REP, BLOCK, wide)
        o_buf[j] = out.astype(BF16).reshape(REP, BLOCK, wide)

        @pl.when(j != head)
        def _():
            out_back(j).start()

        @pl.when(j == head)
        def _():
            out_stays(j).start()

        return nothing

    lax.fori_loop(0, KEY_VALUE_HEADS, one_block, 0)
    weight(3, 3).wait_recv()
    weight(3, 4).start()

    def came_out(h, nothing):
        @pl.when(h != head)
        def _():
            pltpu.make_async_remote_copy(
                o_buf.at[h], o_back.at[h], send_o.at[h], recv_o.at[h],
                device_id=(h * parts + part, f), device_id_type=MESH,
            ).wait()

        @pl.when(h == head)
        def _():
            out_stays(h).wait()

        return nothing

    lax.fori_loop(0, KEY_VALUE_HEADS, came_out, 0)
    for kind in (0, 2, 4):
        weight(3, kind).wait_recv()
    local[3].wait()
    for copy in local[5:]:
        copy.wait()
    for copy in experts:
        copy.wait()
    for copy in smalls + to_heads:
        copy.wait_send()
    for a in range(4):
        for kind in range(5):
            weight(a, kind).wait_send()


def attention_forward(
    cid, parts, n_ctx, tok, small, w_q, w_k, w_v, w_o, packs, cosine, sine, segq, codes
):
    wide = 2 * HEAD_SIZE
    anywhere = pl.BlockSpec(memory_space=pl.ANY)
    inside = pl.BlockSpec(memory_space=pltpu.VMEM)
    dma = pltpu.SemaphoreType.DMA
    heads = (KEY_VALUE_HEADS, REP, BLOCK, wide)
    keys = (n_ctx, 2, BLOCK, wide)
    others = max(n_ctx // parts - 1, 1)
    columns = w_q.shape[1] + w_k.shape[1] + w_v.shape[1]
    own = jax.ShapeDtypeStruct((OWN, D, FF), BF16)

    def full(x):
        return jax.ShapeDtypeStruct((4,) + x.shape, BF16)

    return pl.pallas_call(
        functools.partial(attention_forward_kernel, parts, n_ctx),
        name="attention_forward",
        out_shape=[
            jax.ShapeDtypeStruct(tok.shape, BF16),
            full(small), full(w_q), full(w_k), full(w_v),
            jax.ShapeDtypeStruct(heads, BF16),
            jax.ShapeDtypeStruct(keys, BF16),
            jax.ShapeDtypeStruct(heads, F32),
            jax.ShapeDtypeStruct(heads, F32),
            jax.ShapeDtypeStruct(heads, BF16),
            full(w_o), own, own, own,
        ],
        in_specs=[inside] + [anywhere] * 8 + [inside] * 4,
        out_specs=[inside] * 9 + [anywhere] * 5,
        scratch_shapes=[
            pltpu.VMEM((SEQS * BLOCK, columns), F32),
            pltpu.VMEM(heads, BF16),
            pltpu.VMEM((KEY_VALUE_HEADS, 2, BLOCK, wide), BF16),
            pltpu.VMEM(heads, BF16),
            dma((4, 5)), dma((4, 5)), dma((3,)), dma((3,)), dma((3, 3)), dma((3, 3)),
            dma((others,)), dma((others,)), dma((n_ctx - 1,)), dma((n_ctx - 1,)),
            dma((KEY_VALUE_HEADS,)), dma((KEY_VALUE_HEADS,)), dma((11,)),
        ],
        compiler_params=pltpu.CompilerParams(
            collective_id=cid, has_side_effects=True, vmem_limit_bytes=56 << 20
        ),
        cost_estimate=lasting(130),
    )(tok, small, w_q, w_k, w_v, w_o, *packs, cosine, sine, segq, codes)


def turn_back(field, cosine, sine):
    half = HEAD_SIZE // 2
    lane = lax.broadcasted_iota(jnp.int32, field.shape, field.ndim - 1)
    up = pltpu.roll(field, 2 * HEAD_SIZE - half, field.ndim - 1)
    down = pltpu.roll(field, half, field.ndim - 1)
    turned = jnp.where(lax.rem(lane, HEAD_SIZE) < half, -up, down)
    return field * cosine - turned * sine


def attention_backward_kernel(
    parts, n_ctx, g_own, q_ref, kv_ref, seg_ref, code_ref, full_ref, log_ref, cos_ref, sin_ref,
    grads, mix, dq_ref, dkv_ref, dq_back, dkv_back, gate_came, down_keep, down_came, mix_in,
    g_ref, total, kept, came,
    send_g, recv_g, send_q, recv_q, send_kv, recv_kv, send_mix, recv_mix, send_half, recv_half, here,
):
    c, f = lax.axis_index("ctx"), lax.axis_index("fsdp")
    head, part = lax.div(c, parts), lax.rem(c, parts)
    rows = REP * BLOCK
    wide = 2 * HEAD_SIZE
    barrier = pltpu.get_barrier_semaphore()
    peers = [(i, 0) for i in range(1, n_ctx)]
    peers += [(i // 4, i % 4) for i in range(1, RANKS) if i % 4]
    for dc, df in peers:
        pl.semaphore_signal(
            barrier, inc=1, device_id=(flip(c, dc), flip(f, df)), device_id_type=MESH
        )
    first = pltpu.make_async_copy(g_own.at[head], g_ref.at[head], here.at[0])
    first.start()
    pl.semaphore_wait(barrier, len(peers))
    to_heads = []
    for number, i in enumerate(range(parts, n_ctx, parts)):
        to_heads.append(
            pltpu.make_async_remote_copy(
                g_own.at[lax.div(flip(c, i), parts)], g_ref.at[head],
                send_g.at[number], recv_g.at[number],
                device_id=(flip(c, i), f), device_id_type=MESH,
            )
        )
        to_heads[-1].start()
    half = grads.shape[1] // 2
    quarter = half // 2
    mine = lax.rem(lax.div(c, 2), 2)
    second = lax.rem(lax.div(c, 4), 2)

    def halving(matrix, target, number):
        return pltpu.make_async_remote_copy(
            grads.at[matrix, pl.ds((1 - mine) * half, half)], target,
            send_half.at[number], recv_half.at[number],
            device_id=(flip(c, 2), f), device_id_type=MESH,
        )

    down_halving, gate_halving = halving(2, came, 0), halving(0, gate_came, 1)
    down_halving.start()
    keeping = pltpu.make_async_copy(grads.at[2, pl.ds(mine * half, half)], kept, here.at[3])
    keeping.start()
    returns = []
    for i in range(1, RANKS):
        returns.append(
            pltpu.make_async_remote_copy(
                mix.at[i], mix_in.at[i - 1], send_mix.at[i - 1], recv_mix.at[i - 1],
                device_id=(flip(c, i // 4), flip(f, i % 4)), device_id_type=MESH,
            )
        )
        returns[-1].start()
    total[...] = jnp.zeros_like(total)
    first.wait()
    for copy in to_heads:
        copy.wait_recv()
    halves = half_masks(BF16)
    lane = lax.broadcasted_iota(jnp.int32, (rows, wide), 1)

    def query_back(j):
        return pltpu.make_async_remote_copy(
            dq_ref.at[j], dq_back.at[head], send_q.at[j], recv_q.at[head],
            device_id=(j * parts + part, f), device_id_type=MESH,
        )

    def key_back(b):
        return pltpu.make_async_remote_copy(
            dkv_ref.at[b], dkv_back.at[c], send_kv.at[b], recv_kv.at[c],
            device_id=(b, f), device_id_type=MESH,
        )

    def query_stays(j):
        return pltpu.make_async_copy(dq_ref.at[j], dq_back.at[head], here.at[1])

    def key_stays(b):
        return pltpu.make_async_copy(dkv_ref.at[b], dkv_back.at[c], here.at[2])

    def one_block(j, nothing):
        block = j * parts + part
        q = q_ref[j].reshape(rows, wide)
        g = g_ref[j].reshape(rows, wide)
        queries = [q * half for half in halves]
        partial = [g * half for half in halves]
        product = g.astype(F32) * full_ref[j].reshape(rows, wide)
        logs = log_ref[j].reshape(rows, wide)
        log_total = [logs[:, :1], logs[:, HEAD_SIZE : HEAD_SIZE + 1]]
        inner = [jnp.sum(product * half, axis=1, keepdims=True) for half in half_masks(F32)]

        def step(number, carry):
            k = kv_ref[pl.ds(2 * number, 2), 0].reshape(KEYS, wide)
            v = kv_ref[pl.ds(2 * number, 2), 1].reshape(KEYS, wide)
            codes = code_ref[number]
            after = []
            dk = jnp.zeros((KEYS, wide), F32)
            dv = jnp.zeros((KEYS, wide), F32)
            for s in range(SEQS):
                mask = allowed_at(block, number, seg_ref[j, s], codes[s : s + 1])
                scores = lax.dot_general(
                    queries[s], k, (((1,), (1,)), ((), ())), preferred_element_type=F32
                )
                scores = jnp.where(mask[None], scores.reshape(REP, BLOCK, KEYS) * SCALE, MASKED)
                probs = jnp.exp(scores.reshape(rows, KEYS) - log_total[s])
                grad_probs = lax.dot_general(
                    partial[s], v, (((1,), (1,)), ((), ())), preferred_element_type=F32
                )
                grad_scores = (probs * (grad_probs - inner[s])).astype(BF16)
                dv = dv + lax.dot_general(
                    probs.astype(BF16), partial[s], (((0,), (0,)), ((), ())), preferred_element_type=F32
                )
                dk = dk + lax.dot_general(
                    grad_scores, queries[s], (((0,), (0,)), ((), ())), preferred_element_type=F32
                )
                after.append(carry[s] + jnp.dot(grad_scores, k, preferred_element_type=F32))
            total[pl.ds(2 * number, 2), 0] += dk.reshape(2, BLOCK, wide)
            total[pl.ds(2 * number, 2), 1] += dv.reshape(2, BLOCK, wide)
            return tuple(after)

        start = jnp.zeros((rows, wide), F32)
        done = lax.fori_loop(0, lax.div(block, 2) + 1, step, (start,) * SEQS)
        dq = (jnp.where(lane < HEAD_SIZE, done[0], done[1]) * SCALE).reshape(REP, BLOCK, wide)
        dq_ref[j] = turn_back(dq, cos_ref[block][None], sin_ref[block][None]).astype(BF16)

        @pl.when(j != head)
        def _():
            query_back(j).start()

        @pl.when(j == head)
        def _():
            query_stays(j).start()

        return nothing

    lax.fori_loop(0, KEY_VALUE_HEADS, one_block, 0)

    def finish(b, nothing):
        dkv_ref[b, 0] = turn_back(total[b, 0] * SCALE, cos_ref[b], sin_ref[b]).astype(BF16)
        dkv_ref[b, 1] = total[b, 1].astype(BF16)

        @pl.when(b != c)
        def _():
            key_back(b).start()

        @pl.when(b == c)
        def _():
            key_stays(b).start()

        return nothing

    lax.fori_loop(0, n_ctx, finish, 0)
    gate_halving.start()
    keeping.wait()
    down_halving.wait_recv()

    def add(i, nothing):
        at, e = lax.div(i, OWN), lax.rem(i, OWN)
        kept[at, e] = (kept[at, e].astype(F32) + came[at, e].astype(F32)).astype(BF16)
        return nothing

    lax.fori_loop(0, half * OWN, add, 0)
    down_second = pltpu.make_async_remote_copy(
        kept.at[pl.ds((1 - second) * quarter, quarter)], down_came, send_half.at[2], recv_half.at[2],
        device_id=(flip(c, 4), f), device_id_type=MESH,
    )
    down_second.start()
    leaving = pltpu.make_async_copy(kept.at[pl.ds(second * quarter, quarter)], down_keep, here.at[4])
    leaving.start()

    def came_query(h, nothing):
        @pl.when(h != head)
        def _():
            pltpu.make_async_remote_copy(
                dq_ref.at[h], dq_back.at[h], send_q.at[h], recv_q.at[h],
                device_id=(h * parts + part, f), device_id_type=MESH,
            ).wait()

        @pl.when(h == head)
        def _():
            query_stays(h).wait()

        return nothing

    def came_key(b, nothing):
        @pl.when(b != c)
        def _():
            pltpu.make_async_remote_copy(
                dkv_ref.at[b], dkv_back.at[b], send_kv.at[b], recv_kv.at[b],
                device_id=(b, f), device_id_type=MESH,
            ).wait()

        @pl.when(b == c)
        def _():
            key_stays(b).wait()

        return nothing

    lax.fori_loop(0, KEY_VALUE_HEADS, came_query, 0)
    lax.fori_loop(0, n_ctx, came_key, 0)
    for copy in to_heads:
        copy.wait_send()
    for copy in returns + [gate_halving, down_second, leaving]:
        copy.wait()
    down_halving.wait_send()


def attention_backward(
    cid, parts, n_ctx, g_own, q, kv, segq, codes, full, logs, cosine, sine, grads, mix
):
    wide = 2 * HEAD_SIZE
    anywhere = pl.BlockSpec(memory_space=pl.ANY)
    inside = pl.BlockSpec(memory_space=pltpu.VMEM)
    dma = pltpu.SemaphoreType.DMA
    others = max(n_ctx // parts - 1, 1)
    return pl.pallas_call(
        functools.partial(attention_backward_kernel, parts, n_ctx),
        name="attention_backward",
        out_shape=[
            jax.ShapeDtypeStruct(q.shape, BF16),
            jax.ShapeDtypeStruct(kv.shape, BF16),
            jax.ShapeDtypeStruct(q.shape, BF16),
            jax.ShapeDtypeStruct(kv.shape, BF16),
            jax.ShapeDtypeStruct((grads.shape[1] // 2,) + grads.shape[2:], BF16),
            jax.ShapeDtypeStruct((grads.shape[1] // 4,) + grads.shape[2:], BF16),
            jax.ShapeDtypeStruct((grads.shape[1] // 4,) + grads.shape[2:], BF16),
            jax.ShapeDtypeStruct((RANKS - 1,) + mix.shape[1:], BF16),
        ],
        in_specs=[anywhere] + [inside] * 8 + [anywhere] * 2,
        out_specs=[inside] * 2 + [anywhere] * 6,
        scratch_shapes=[
            pltpu.VMEM(q.shape, BF16),
            pltpu.VMEM((n_ctx, 2, BLOCK, wide), F32),
            pltpu.VMEM((grads.shape[1] // 2,) + grads.shape[2:], BF16),
            pltpu.VMEM((grads.shape[1] // 2,) + grads.shape[2:], BF16),
            dma((others,)), dma((others,)), dma((KEY_VALUE_HEADS,)), dma((KEY_VALUE_HEADS,)),
            dma((n_ctx,)), dma((n_ctx,)), dma((RANKS - 1,)), dma((RANKS - 1,)), dma((3,)), dma((3,)), dma((5,)),
        ],
        compiler_params=pltpu.CompilerParams(
            collective_id=cid, has_side_effects=True, vmem_limit_bytes=48 << 20
        ),
        cost_estimate=lasting(90),
    )(g_own, q, kv, segq, codes, full, logs, cosine, sine, grads, mix)


def rope_tables(positions):
    half_dim = HEAD_SIZE // 2
    frequency = ROPE_BASE ** (-jnp.arange(half_dim, dtype=F32) * 2.0 / HEAD_SIZE)
    angle = positions.astype(F32)[:, None] * frequency[None, :]
    angle = jnp.concatenate([angle, angle], axis=1)
    return (jnp.cos(angle), jnp.sin(angle))


def heads_out(field, per):
    field = field.reshape(SEQS, BLOCK, KEY_VALUE_HEADS, per, HEAD_SIZE)
    return field.transpose(2, 3, 1, 0, 4).reshape(KEY_VALUE_HEADS, per, BLOCK, SEQS * HEAD_SIZE)


def heads_in(field):
    per = field.shape[1]
    field = field.reshape(KEY_VALUE_HEADS, per, BLOCK, SEQS, HEAD_SIZE)
    return field.transpose(3, 2, 0, 1, 4).reshape(SEQS, BLOCK, KEY_VALUE_HEADS * per * HEAD_SIZE)


def on_device(
    n_ctx,
    n_fsdp,
    tokens,
    segments,
    valid,
    expert_ids,
    slot_order,
    cotangent,
    norm1_gain,
    w_query,
    key_weight,
    value_weight,
    w_output,
    norm2_gain,
    w_router,
    w_gate,
    w_up,
    w_down,
):
    parts = n_ctx // KEY_VALUE_HEADS
    replicas = n_ctx // 2
    full_len = segments.shape[1]
    c_index, f_index = lax.axis_index("ctx"), lax.axis_index("fsdp")
    pair = lax.rem(c_index, 2)
    rank = pair * n_fsdp + f_index
    part = lax.rem(c_index, parts)
    head = lax.div(c_index, parts)
    positions = c_index * BLOCK + jnp.arange(BLOCK, dtype=jnp.int32)

    def tie(x, after):
        return lax.optimization_barrier((x, after))[0]

    tokens_all = lax.all_gather(tokens, "ctx", axis=0, tiled=False)
    small = jnp.concatenate(
        [
            norm1_gain[None],
            norm2_gain[None],
            w_router.T,
            jnp.zeros((SMALL - EXPERTS - 2, D // n_fsdp), BF16),
        ],
        axis=0,
    )
    packs = [
        lax.dynamic_slice_in_dim(w, pair * (EXPERTS // 2), EXPERTS // 2, 1)
        .reshape(D // n_fsdp, n_fsdp, OWN, FF)
        .transpose(1, 2, 0, 3)
        for w in (w_gate, w_up, w_down)
    ]
    inputs_f = tokens.astype(F32)
    scale_one = lax.rsqrt(jnp.mean(inputs_f * inputs_f, axis=-1, keepdims=True) + EPS)
    segq = segments.reshape(SEQS, KEY_VALUE_HEADS, parts, BLOCK)
    segq = lax.dynamic_index_in_dim(segq, part, 2, keepdims=False).transpose(1, 0, 2)[..., None]
    codes = jnp.where(valid > 0, segments, -1)
    codes = codes.reshape(SEQS, full_len // KEYS, KEYS).transpose(1, 0, 2)
    all_cosine, all_sine = rope_tables(jnp.arange(full_len, dtype=jnp.int32))
    all_cosine = jnp.tile(all_cosine, (1, 2)).reshape(n_ctx, BLOCK, 2 * HEAD_SIZE)
    all_sine = jnp.tile(all_sine, (1, 2)).reshape(n_ctx, BLOCK, 2 * HEAD_SIZE)
    (
        normed_in, small_all, full_query, full_key, full_value, q_all, kv_all, head_full, head_logs,
        attn_heads, full_output, own_gate, own_up, own_down,
    ) = attention_forward(
        0, parts, n_ctx, tokens.reshape(SEQS * BLOCK, D), small, w_query, key_weight, value_weight,
        w_output, packs,
        lax.dynamic_index_in_dim(all_cosine, c_index, 0, keepdims=False),
        lax.dynamic_index_in_dim(all_sine, c_index, 0, keepdims=False),
        segq, codes,
    )
    gain_first = small_all[:, 0].reshape(D).astype(F32)
    gain_second = small_all[:, 1].reshape(D).astype(F32)
    full_router = small_all[:, 2 : 2 + EXPERTS].transpose(1, 0, 2).reshape(EXPERTS, D)
    full_output = full_output.reshape(D, D)
    attn_out = heads_in(attn_heads)
    attn_proj = jnp.einsum("sgq,dq->sgd", attn_out, full_output, preferred_element_type=F32)
    residual = inputs_f + attn_proj
    scale_two = lax.rsqrt(jnp.mean(residual * residual, axis=-1, keepdims=True) + EPS)
    normed_mid = (residual * scale_two * gain_second).astype(BF16)

    logits = jnp.einsum("sgd,ed->sge", normed_mid, full_router, preferred_element_type=F32)
    picked = jnp.any(expert_ids[..., None] == jnp.arange(EXPERTS, dtype=jnp.int32), axis=2)
    before = (slot_order[:, None, :] < slot_order[:, :, None]).astype(BF16)
    place = jnp.matmul(before, picked.astype(BF16), preferred_element_type=F32)
    is_kept = picked & (place < CAP)
    chosen = jnp.where(picked, logits, MASKED)
    raised = jnp.where(picked, jnp.exp(chosen - jnp.max(chosen, axis=-1, keepdims=True)), 0.0)
    gates = raised / jnp.sum(raised, axis=-1, keepdims=True)
    payload = jnp.concatenate(
        [
            normed_mid,
            jnp.where(is_kept, place, -1.0).astype(BF16),
            gates.astype(BF16),
            jnp.zeros((SEQS, BLOCK, 128 - 2 * EXPERTS), BF16),
        ],
        axis=2,
    )
    back, mix_part, own_grads = run_experts(
        2, replicas, payload.reshape(SEQS * BLOCK, PAY), cotangent.reshape(SEQS * BLOCK, D),
        (own_gate, own_up, own_down), tokens_all
    )

    replica = lax.div(c_index, 2)

    def halve(grad, bit):
        grad = grad.reshape((2, -1) + grad.shape[1:])
        mine = lax.rem(lax.div(replica, bit), 2)
        send = lax.dynamic_index_in_dim(grad, 1 - mine, 0, keepdims=False)
        keep = lax.dynamic_index_in_dim(grad, mine, 0, keepdims=False)
        return keep, lax.ppermute(send, "ctx", [(a, a ^ (2 * bit)) for a in range(n_ctx)])

    def joined(halves, after):
        keep, came = halves
        return (keep.astype(F32) + tie(came, after).astype(F32)).astype(BF16)

    back = back.reshape(SEQS, BLOCK, D + 128)
    grad_gates = jnp.where(is_kept, back[..., D : D + EXPERTS], 0.0)
    grad_chosen = gates * (grad_gates - jnp.sum(gates * grad_gates, axis=-1, keepdims=True))
    grad_logits = grad_chosen.astype(BF16)
    grad_mid = back[..., :D] + jnp.einsum(
        "sge,ed->sgd", grad_logits, full_router, preferred_element_type=F32
    )
    grad_router = jnp.einsum("sgd,sge->de", normed_mid, grad_logits, preferred_element_type=F32)

    grad_f = cotangent.astype(F32)
    weighted_two = gain_second * grad_mid
    grad_gain_second = jnp.sum(grad_mid * residual * scale_two, axis=(0, 1))
    cube_two = scale_two * scale_two * scale_two
    grad_resid = (
        grad_f
        + scale_two * weighted_two
        - residual * cube_two * jnp.mean(weighted_two * residual, axis=-1, keepdims=True)
    )
    grad_resid_low = grad_resid.astype(BF16)
    grad_attn = jnp.einsum("sgd,dq->sgq", grad_resid_low, full_output, preferred_element_type=F32)
    grad_attn = grad_attn.astype(BF16)
    grad_output_w = jnp.einsum("sgd,sgq->dq", grad_resid_low, attn_out, preferred_element_type=F32)
    rows = D // (n_ctx * n_fsdp)
    x_bit, core_bit = lax.div(f_index, 2), lax.rem(f_index, 2)

    def two(field, axis, bit):
        return (
            lax.dynamic_index_in_dim(field, 1 - bit, axis, keepdims=False),
            lax.dynamic_index_in_dim(field, bit, axis, keepdims=False),
        )

    def summed(mine, came):
        return (mine.astype(F32) + came.astype(F32)).astype(BF16)

    output_part = grad_output_w.astype(BF16).reshape(replicas, 2, 2, 2, rows, D)
    send, output_mine = two(output_part, 3, core_bit)
    output_came = lax.ppermute(send, "fsdp", [(a, a ^ 1) for a in range(n_fsdp)])

    dq_heads, dkv_heads, dq_back, dkv_back, gate_came, down_keep, down_came, mix_in = attention_backward(
        6, parts, n_ctx, heads_out(grad_attn, REP), q_all, kv_all, segq, codes, head_full, head_logs,
        all_cosine, all_sine, own_grads, mix_part,
    )
    layer_out = (
        residual.reshape(SEQS * BLOCK, D) + mix_part[0].astype(F32) + jnp.sum(mix_in.astype(F32), axis=0)
    ).astype(BF16).reshape(SEQS, BLOCK, D)
    gate_keep = own_grads[0].reshape((2, replicas // 2, OWN, FF, D // replicas))
    gate_half = (lax.dynamic_index_in_dim(gate_keep, lax.rem(replica, 2), 0, keepdims=False), gate_came)
    up_half = halve(tie(own_grads[1], dq_back), 1)
    gate_half = halve(joined(gate_half, dq_back), 2)
    send, output_mine = two(summed(output_mine, output_came), 2, x_bit)
    output_came = lax.ppermute(send, "fsdp", [(a, a ^ 2) for a in range(n_fsdp)])
    send, output_mine = two(summed(output_mine, output_came), 1, pair)
    output_came = lax.ppermute(send, "ctx", [(a, a ^ 1) for a in range(n_ctx)])
    down_half, bit = (down_keep, down_came), 4
    while bit < replicas:
        down_half = halve(joined(down_half, dq_back), bit)
        gate_half = halve(joined(gate_half, dq_back), bit)
        bit *= 2

    tokens_f = tokens_all.astype(F32)
    scale_all = lax.rsqrt(jnp.mean(tokens_f * tokens_f, axis=-1) + EPS)

    def head_weights(field, inputs, scales):
        blocks, per = field.shape[:2]
        field = field.reshape(blocks, per, BLOCK, SEQS, HEAD_SIZE).transpose(0, 3, 2, 1, 4)
        field = (field.astype(F32) * scales[..., None, None]).astype(BF16)
        made = jnp.dot(
            inputs.reshape(blocks * SEQS * BLOCK, D).T,
            field.reshape(blocks * SEQS * BLOCK, per * HEAD_SIZE),
            preferred_element_type=F32,
        )
        return made * gain_first[:, None]

    if parts == 1:
        head_grad = head_weights(jnp.concatenate([dq_heads, dkv_heads], axis=1), tokens_all, scale_all)
    else:
        tokens_part, scale_part = (
            lax.dynamic_index_in_dim(
                x.reshape((KEY_VALUE_HEADS, parts) + x.shape[1:]), part, 1, keepdims=False
            )
            for x in (tokens_all, scale_all)
        )
        head_grad = jnp.concatenate(
            [
                head_weights(dq_heads, tokens_part, scale_part),
                head_weights(dkv_heads, tokens_all, scale_all),
            ],
            axis=1,
        )
    head_width = (REP + 2) * HEAD_SIZE
    head_grad = head_grad.astype(BF16).reshape(n_ctx * n_fsdp, rows, head_width)
    dkv_back = dkv_back.reshape(KEY_VALUE_HEADS, parts, 2, BLOCK, SEQS * HEAD_SIZE)
    if parts == 1:
        dkv_back = dkv_back[:, 0]
    else:
        dkv_back = jnp.sum(dkv_back.astype(F32), axis=1).astype(BF16)
    grad_in = sum(
        jnp.einsum("sgq,dq->sgd", heads_in(grad), weight.reshape(D, -1), preferred_element_type=F32)
        for grad, weight in (
            (dq_back, full_query), (dkv_back[:, :1], full_key), (dkv_back[:, 1:], full_value)
        )
    )
    weighted_one = gain_first * grad_in
    grad_gain_first = jnp.sum(grad_in * inputs_f * scale_one, axis=(0, 1))
    cube_one = scale_one * scale_one * scale_one
    input_grad = (
        grad_resid
        + scale_one * weighted_one
        - inputs_f * cube_one * jnp.mean(weighted_one * inputs_f, axis=-1, keepdims=True)
    ).astype(BF16)
    small_grads = jnp.concatenate(
        [
            grad_router,
            grad_gain_first[:, None],
            grad_gain_second[:, None],
            jnp.zeros((D, 128 - EXPERTS - 2), F32),
        ],
        axis=1,
    ).reshape(n_ctx * n_fsdp, rows, 128)

    def device(c, f):
        return c * n_fsdp + f

    def ranked(c, f):
        return lax.rem(c, 2) * n_fsdp + f

    def by_rank(sums):
        field = jnp.stack(sums).reshape(len(sums), OWN, FF, RANKS, rows)
        return field.transpose(3, 0, 1, 4, 2)

    output_sum = summed(output_mine, output_came)
    gate_down = by_rank([joined(gate_half, head_grad), joined(down_half, head_grad)])
    up_other, up_mine = two(
        joined(up_half, head_grad).reshape(2, replicas // 4, OWN, FF, D // replicas),
        0,
        lax.rem(lax.div(replica, 2), 2),
    )
    routes = []
    for i in range(n_ctx):
        for k in range(n_fsdp):
            moves = [
                (a, lambda c, f, i=i, k=k: device(flip(c, i), flip(f, k)), a, device)
                for a in range(2)
            ]
            if k == 0 and i % 2 == 0:
                moves.append(
                    (2, lambda c, f, i=i: lax.div(flip(c, i), 2), 2, lambda c, f: lax.div(c, 2))
                )
            if i < 2:
                moves.append((4, lambda c, f, j=4 * i + k: flip(ranked(c, f), j), 4, ranked))
            if k == 0 and i == 4:
                moves.append((3, lambda c, f: slice(None), 3, lambda c, f: slice(None)))
            routes.append((i, k, moves))
    operands = [head_grad, small_grads, output_sum, up_other, gate_down]
    head_grads, small_all, output_all, up_came, gate_down = exchange(
        9, "sum_grads", routes, operands, [(x.shape, x.dtype) for x in operands], 60
    )
    output_grad = jnp.sum(output_all.astype(F32), axis=0)
    up_half, bit = (up_mine, up_came), 4
    while bit < replicas:
        up_half = halve(joined(up_half, up_came), bit)
        bit *= 2
    head_grads = head_grads.reshape(KEY_VALUE_HEADS, parts * n_fsdp, rows, head_width)
    head_grads = jnp.sum(head_grads.astype(F32), axis=1).transpose(1, 0, 2)
    query_grad = head_grads[..., : REP * HEAD_SIZE].reshape(rows, D)
    key_grad = head_grads[..., REP * HEAD_SIZE : (REP + 1) * HEAD_SIZE].reshape(rows, -1)
    value_grad = head_grads[..., (REP + 1) * HEAD_SIZE :].reshape(rows, -1)
    small_sum = jnp.sum(small_all, axis=0)

    up_sum = by_rank([joined(up_half, up_came)])
    (up_sum,) = exchange(
        8,
        "swap_up",
        [
            (i // 4, i % 4, [(0, lambda c, f, i=i: flip(ranked(c, f), i), 0, ranked)])
            for i in range(RANKS)
        ],
        [up_sum],
        [(up_sum.shape, BF16)],
    )

    def by_row(swapped, matrix):
        return swapped[:, matrix].transpose(2, 0, 1, 3).reshape(rows, EXPERTS, FF).astype(F32)

    return (
        layer_out,
        input_grad,
        small_sum[:, EXPERTS],
        query_grad,
        key_grad,
        value_grad,
        output_grad,
        small_sum[:, EXPERTS + 1],
        small_sum[:, :EXPERTS],
        by_row(gate_down, 0),
        by_row(up_sum, 0),
        by_row(gate_down, 1),
    )


def solution(mesh):
    placed = (
        P("fsdp", "ctx", None),
        P("fsdp", None),
        P("fsdp", None),
        P("fsdp", "ctx", None),
        P("fsdp", "ctx"),
        P("fsdp", "ctx", None),
        P("fsdp"),
        P("fsdp", None),
        P("fsdp", None),
        P("fsdp", None),
        P("fsdp", None),
        P("fsdp"),
        P("fsdp", None),
        P("fsdp", None, None),
        P("fsdp", None, None),
        P("fsdp", None, None),
    )
    return jax.shard_map(
        functools.partial(on_device, mesh.shape["ctx"], mesh.shape["fsdp"]),
        mesh=mesh,
        in_specs=placed,
        out_specs=(
            P("fsdp", "ctx", None),
            P("fsdp", "ctx", None),
            P(("ctx", "fsdp")),
            P(("ctx", "fsdp"), None),
            P(("ctx", "fsdp"), None),
            P(("ctx", "fsdp"), None),
            P(("ctx", "fsdp"), None),
            P(("ctx", "fsdp")),
            P(("ctx", "fsdp"), None),
            P(("ctx", "fsdp"), None, None),
            P(("ctx", "fsdp"), None, None),
            P(("ctx", "fsdp"), None, None),
        ),
        check_vma=False,
    )
```

```python
import functools

import jax
import jax.numpy as jnp
from jax import lax
from jax.experimental import pallas as pl
from jax.experimental.pallas import tpu as pltpu
from jax.sharding import PartitionSpec as P

D = 1536
QUERY_HEADS = 24
KEY_VALUE_HEADS = 8
REP = QUERY_HEADS // KEY_VALUE_HEADS
HEAD_SIZE = 64
FF = 512
EXPERTS = 16
CAP = 80
RANKS = 8
OWN = EXPERTS // RANKS
SEQS = 2
BLOCK = 128
KEYS = 256

EPS = 1e-05
ROPE_BASE = 10000.0
MASKED = -1e30
SCALE = HEAD_SIZE ** (-0.5)
MESH = pl.DeviceIdType.MESH
BF16 = jnp.bfloat16
F32 = jnp.float32


def flip(index, constant):
    result, bit = index, 1
    while bit <= constant:
        if constant & bit:
            result = result + bit - 2 * bit * lax.rem(lax.div(index, bit), 2)
        bit *= 2
    return result


def lasting(microseconds):
    return pl.CostEstimate(flops=0, bytes_accessed=int(microseconds * 3.3e6), transcendentals=0)


def exchange(cid, name, routes, operands, outs, microseconds=30):
    remote = [r for r in routes if r[0] or r[1]]
    local = [r for r in routes if not (r[0] or r[1])]
    amount = sum(len(r[2]) for r in remote)
    local_amount = sum(len(r[2]) for r in local)

    def kernel(*refs):
        ins = refs[: len(operands)]
        out = refs[len(operands) : len(operands) + len(outs)]
        send, recv, own = refs[len(operands) + len(outs) :]
        c, f = lax.axis_index("ctx"), lax.axis_index("fsdp")
        barrier = pltpu.get_barrier_semaphore()
        for dc, df, _ in remote:
            pl.semaphore_signal(
                barrier, inc=1, device_id=(flip(c, dc), flip(f, df)), device_id_type=MESH
            )
        copies = []
        for dc, df, moves in local:
            for a, src, b, dst in moves:
                copy = pltpu.make_async_copy(
                    ins[a].at[src(c, f)], out[b].at[dst(c, f)], own.at[len(copies)]
                )
                copy.start()
                copies.append(copy)
        pl.semaphore_wait(barrier, len(remote))
        number = 0
        for dc, df, moves in remote:
            for a, src, b, dst in moves:
                copy = pltpu.make_async_remote_copy(
                    ins[a].at[src(c, f)],
                    out[b].at[dst(c, f)],
                    send.at[number],
                    recv.at[number],
                    device_id=(flip(c, dc), flip(f, df)),
                    device_id_type=MESH,
                )
                copy.start()
                copies.append(copy)
                number += 1
        for copy in copies:
            copy.wait()

    anywhere = pl.BlockSpec(memory_space=pl.ANY)
    return pl.pallas_call(
        kernel,
        name=name,
        out_shape=[jax.ShapeDtypeStruct(shape, dtype) for shape, dtype in outs],
        in_specs=[anywhere] * len(operands),
        out_specs=[anywhere] * len(outs),
        scratch_shapes=[
            pltpu.SemaphoreType.DMA((amount,)),
            pltpu.SemaphoreType.DMA((amount,)),
            pltpu.SemaphoreType.DMA((max(local_amount, 1),)),
        ],
        compiler_params=pltpu.CompilerParams(collective_id=cid, has_side_effects=True),
        cost_estimate=lasting(microseconds),
    )(*operands)


PAY = D + 128
GROUPS = 4
ROWS = GROUPS * CAP


def other_chip(c, f, k):
    pair, x = lax.div(k, 2), lax.rem(k, 2)
    return (
        c + pair * (1 - 2 * lax.rem(c, 2)),
        f + 2 * x * (1 - 2 * lax.rem(lax.div(f, 2), 2)),
    )


def plane_order(replicas):
    order = [0]
    while len(order) < replicas:
        order = [2 * i for i in order] + [2 * i + 1 for i in order]
    return order


def experts_kernel(
    replicas, pay, cot, gate_own, up_own, down_own, after,
    back, mix, grads, pay_in, cot_in,
    weights, total, pay_now, cot_now, xs, gs, eo, gi, hid, dgate, dup, disp, comb,
    own, out, sib, ret, mix_now,
    send_first, recv_first, send_fwd, recv_fwd, send_sib, recv_sib, send_chip, recv_chip,
    load_w, load, store, piece_sem,
):
    c, f = lax.axis_index("ctx"), lax.axis_index("fsdp")
    rank = lax.rem(c, 2) * 4 + f
    sibling = (c, flip(f, 1))
    barrier = pltpu.get_barrier_semaphore()
    pl.semaphore_signal(barrier, inc=1, device_id=sibling, device_id_type=MESH)
    for k in range(1, 4):
        pl.semaphore_signal(barrier, inc=1, device_id=other_chip(c, f, k), device_id_type=MESH)
    bring = []
    for m, own_weight in enumerate((gate_own, up_own, down_own)):
        bring.append(pltpu.make_async_copy(own_weight, weights.at[m], load_w.at[m]))
        bring[-1].start()
    pl.semaphore_wait(barrier, 4)
    sources, landed = (pay, cot), (pay_in, cot_in)

    def push(k, a):
        slot = 1 if k == 0 else 2 * k
        return pltpu.make_async_remote_copy(
            sources[a], landed[a].at[slot - 1], send_first.at[k, a], recv_first.at[k, a],
            device_id=sibling if k == 0 else other_chip(c, f, k), device_id_type=MESH,
        )

    def forward(k, a):
        return pltpu.make_async_remote_copy(
            landed[a].at[2 * k - 1], landed[a].at[2 * k], send_fwd.at[k - 1, a], recv_fwd.at[k - 1, a],
            device_id=sibling, device_id_type=MESH,
        )

    def to_sibling(k):
        return pltpu.make_async_remote_copy(
            out.at[lax.rem(k, 2)], sib.at[k], send_sib.at[k], recv_sib.at[k],
            device_id=sibling, device_id_type=MESH,
        )

    def to_chip(k):
        return pltpu.make_async_remote_copy(
            sib.at[k], ret.at[k - 1], send_chip.at[k - 1], recv_chip.at[k - 1],
            device_id=other_chip(c, f, k), device_id_type=MESH,
        )

    def store_mix(k, s):
        return pltpu.make_async_copy(mix_now.at[s], mix.at[2 * k + s], store.at[s])

    for k, a in ((0, 0), (0, 1), (1, 0), (2, 0), (1, 1), (2, 1), (3, 0), (3, 1)):
        push(k, a).start()

    def clear(i, carry):
        total[lax.div(i, OWN), lax.rem(i, OWN)] = jnp.zeros((FF, D), F32)
        return carry

    lax.fori_loop(0, 3 * OWN, clear, 0)
    lane = lax.broadcasted_iota(jnp.int32, (BLOCK, 128), 1)
    wide = lax.broadcasted_iota(jnp.int32, (BLOCK, 2 * BLOCK), 1).astype(F32)
    both = lax.broadcasted_iota(jnp.int32, (BLOCK, OWN * CAP), 1)

    def chunk(k, carry):
        now = (pay_now, cot_now)

        def fetch(a, s, source):
            copy = pltpu.make_async_copy(source, now[a].at[s], load.at[a, s])
            copy.start()
            return copy

        @pl.when(k == 0)
        def _():
            copies = [fetch(a, 0, sources[a]) for a in range(2)]
            for a in range(2):
                push(0, a).wait_recv()
            copies += [fetch(a, 1, landed[a].at[0]) for a in range(2)]
            for copy in copies:
                copy.wait()
            for copy in bring:
                copy.wait()

        @pl.when(k > 0)
        def _():
            for a in range(2):
                pltpu.make_async_remote_copy(
                    sources[a], landed[a].at[2 * k - 1], send_first.at[k, a], recv_first.at[k, a],
                    device_id=other_chip(c, f, k), device_id_type=MESH,
                ).wait_recv()
                forward(k, a).start()
            copies = [fetch(a, 0, landed[a].at[2 * k - 1]) for a in range(2)]
            for a in range(2):
                forward(k, a).wait_recv()
            copies += [fetch(a, 1, landed[a].at[2 * k]) for a in range(2)]
            for copy in copies:
                copy.wait()

        for g in range(GROUPS):
            s, at = g // 2, (g % 2) * BLOCK
            tail = pay_now[s, at : at + BLOCK, D:].astype(F32)

            def column(index):
                return jnp.sum(jnp.where(lane == index, tail, 0.0), axis=1, keepdims=True)

            table = jnp.zeros((BLOCK, 2 * BLOCK), F32)
            gated = jnp.zeros((BLOCK, 2 * BLOCK), F32)
            for e in range(OWN):
                place = column(rank * OWN + e)
                place = jnp.where(place < 0.0, -1000.0, place + e * CAP)
                here = wide == place
                table = jnp.where(here, 1.0, table)
                gated = jnp.where(here, column(EXPERTS + rank * OWN + e), gated)
            table, gated = table.astype(BF16), gated.astype(BF16)
            disp[g] = table
            comb[g] = gated
            for weight, source, keep in (
                (table, pay_now[s, at : at + BLOCK, :D], xs),
                (gated, cot_now[s, at : at + BLOCK], gs),
            ):
                moved = lax.dot_general(
                    weight, source, (((0,), (0,)), ((), ())), preferred_element_type=F32
                ).astype(BF16)
                for e in range(OWN):
                    keep[e, g * CAP : (g + 1) * CAP] = moved[e * CAP : (e + 1) * CAP]

        def expert(e, carry):
            at = pl.multiple_of(e * CAP, 16)
            gate_pre = jnp.dot(xs[e], weights[0, e], preferred_element_type=F32)
            up_pre = jnp.dot(xs[e], weights[1, e], preferred_element_type=F32)
            sigmoid = 1.0 / (1.0 + jnp.exp(-gate_pre))
            activated = gate_pre * sigmoid
            hidden = (activated * up_pre).astype(BF16)
            hid[e] = hidden
            made = lax.dot_general(
                hidden, weights[2, e], (((1,), (1,)), ((), ())), preferred_element_type=F32
            ).astype(BF16)
            for g in range(GROUPS):
                eo[pl.ds(pl.multiple_of(g * OWN * CAP + at, 16), CAP)] = made[g * CAP : (g + 1) * CAP]
            grad_hidden = jnp.dot(gs[e], weights[2, e], preferred_element_type=F32)
            slope = sigmoid * (1.0 + gate_pre * (1.0 - sigmoid))
            grad_gate = (grad_hidden * up_pre * slope).astype(BF16)
            grad_up = (grad_hidden * activated).astype(BF16)
            dgate[e] = grad_gate
            dup[e] = grad_up
            made = lax.dot_general(
                grad_gate, weights[0, e], (((1,), (1,)), ((), ())), preferred_element_type=F32
            )
            made = made + lax.dot_general(
                grad_up, weights[1, e], (((1,), (1,)), ((), ())), preferred_element_type=F32
            )
            made = made.astype(BF16)
            for g in range(GROUPS):
                gi[pl.ds(pl.multiple_of(g * OWN * CAP + at, 16), CAP)] = made[g * CAP : (g + 1) * CAP]
            return carry

        lax.fori_loop(0, OWN, expert, 0)

        @pl.when(k > 0)
        def _():
            for s in range(2):
                store_mix(k - 1, s).wait()

        @pl.when(k > 1)
        def _():
            to_sibling(k - 2).wait_send()

        parity = lax.rem(k, 2)
        for g in range(GROUPS):
            s, at = g // 2, (g % 2) * BLOCK
            slots = pl.ds(g * OWN * CAP, OWN * CAP)
            made = eo[slots]
            mix_now[s, at : at + BLOCK] = jnp.dot(
                comb[g][:, : OWN * CAP], made, preferred_element_type=F32
            ).astype(BF16)
            table = disp[g][:, : OWN * CAP]
            grad_mid = jnp.dot(table, gi[slots], preferred_element_type=F32).astype(BF16)
            met = lax.dot_general(
                cot_now[s, at : at + BLOCK], made, (((1,), (1,)), ((), ())), preferred_element_type=F32
            ) * table.astype(F32)
            values = jnp.zeros((BLOCK, 128), F32)
            for e in range(OWN):
                inside = (both >= e * CAP) & (both < (e + 1) * CAP)
                value = jnp.sum(jnp.where(inside, met, 0.0), axis=1, keepdims=True)
                values = jnp.where(lane == rank * OWN + e, value, values)
            target = own if s == 0 else out
            target[parity, at : at + BLOCK, :D] = grad_mid
            target[parity, at : at + BLOCK, D:] = values.astype(BF16)
        to_sibling(k).start()
        for s in range(2):
            store_mix(k, s).start()

        def weight_grads(e, carry):
            for m, (left, right) in enumerate(((dgate, xs), (dup, xs), (hid, gs))):
                total[m, e] += lax.dot_general(
                    left[e], right[e], (((0,), (0,)), ((), ())), preferred_element_type=F32
                )
            return carry

        lax.fori_loop(0, OWN, weight_grads, 0)
        to_sibling(k).wait_recv()
        sib[k] = (sib[k].astype(F32) + own[parity].astype(F32)).astype(BF16)

        @pl.when(k > 0)
        def _():
            to_chip(k).start()

        return carry

    lax.fori_loop(0, 4, chunk, 0)
    for s in range(2):
        store_mix(3, s).wait()
    stages = (eo, gi)
    pending = []
    for i in range(3 * OWN):
        m, e = i // OWN, i % OWN
        if i >= 2:
            for copy in pending[i - 2]:
                copy.wait()
        stages[i % 2][:FF] = total[m, e].astype(BF16)
        pending.append([])
        if len(grads.shape) == 4:
            pending[i].append(
                pltpu.make_async_copy(stages[i % 2].at[:FF], grads.at[m, e], piece_sem.at[i % 2, 0])
            )
        else:
            width = D // replicas
            for at, plane in enumerate(plane_order(replicas)):
                pending[i].append(
                    pltpu.make_async_copy(
                        stages[i % 2].at[:FF, plane * width : (plane + 1) * width],
                        grads.at[m, at, e],
                        piece_sem.at[i % 2, at],
                    )
                )
        for copy in pending[i]:
            copy.start()
    for copy in pending[-2] + pending[-1]:
        copy.wait()
    for k in (2, 3):
        to_sibling(k).wait_send()
    for k in range(4):
        for a in range(2):
            push(k, a).wait_send()
            if k:
                forward(k, a).wait_send()
    for k in range(1, 4):
        to_chip(k).wait_recv()
    back[...] = (sib[0].astype(F32) + ret[0].astype(F32)) + (ret[1].astype(F32) + ret[2].astype(F32))
    for k in range(1, 4):
        to_chip(k).wait_send()


def run_experts(cid, replicas, pay, cot, owns, after):
    width = D // replicas
    apart = width % 128 == 0
    tokens = SEQS * BLOCK
    anywhere = pl.BlockSpec(memory_space=pl.ANY)
    inside = pl.BlockSpec(memory_space=pltpu.VMEM)
    dma = pltpu.SemaphoreType.DMA
    back, mix, grads, _, _ = pl.pallas_call(
        functools.partial(experts_kernel, replicas),
        name="experts",
        out_shape=[
            jax.ShapeDtypeStruct((tokens, PAY), F32),
            jax.ShapeDtypeStruct((RANKS, tokens, D), BF16),
            jax.ShapeDtypeStruct((3, replicas, OWN, FF, width) if apart else (3, OWN, FF, D), BF16),
            jax.ShapeDtypeStruct((RANKS - 1, tokens, PAY), BF16),
            jax.ShapeDtypeStruct((RANKS - 1, tokens, D), BF16),
        ],
        in_specs=[anywhere] * 6,
        out_specs=[inside] + [anywhere] * 4,
        scratch_shapes=[
            pltpu.VMEM((3, OWN, D, FF), BF16),
            pltpu.VMEM((3, OWN, FF, D), F32),
            pltpu.VMEM((2, tokens, PAY), BF16),
            pltpu.VMEM((2, tokens, D), BF16),
            pltpu.VMEM((OWN, ROWS, D), BF16),
            pltpu.VMEM((OWN, ROWS, D), BF16),
            pltpu.VMEM((OWN * ROWS, D), BF16),
            pltpu.VMEM((OWN * ROWS, D), BF16),
            pltpu.VMEM((OWN, ROWS, FF), BF16),
            pltpu.VMEM((OWN, ROWS, FF), BF16),
            pltpu.VMEM((OWN, ROWS, FF), BF16),
            pltpu.VMEM((GROUPS, BLOCK, 2 * BLOCK), BF16),
            pltpu.VMEM((GROUPS, BLOCK, 2 * BLOCK), BF16),
            pltpu.VMEM((2, tokens, PAY), BF16),
            pltpu.VMEM((2, tokens, PAY), BF16),
            pltpu.VMEM((4, tokens, PAY), BF16),
            pltpu.VMEM((3, tokens, PAY), BF16),
            pltpu.VMEM((2, tokens, D), BF16),
            dma((4, 2)), dma((4, 2)), dma((3, 2)), dma((3, 2)),
            dma((4,)), dma((4,)), dma((3,)), dma((3,)),
            dma((4,)), dma((2, 2)), dma((2,)), dma((2, replicas)),
        ],
        compiler_params=pltpu.CompilerParams(
            collective_id=cid, has_side_effects=True, vmem_limit_bytes=63 << 20
        ),
        cost_estimate=lasting(110),
    )(pay, cot, *owns, after)
    if not apart:
        grads = grads.reshape(3, OWN, FF, replicas, width).transpose(0, 3, 1, 2, 4)
        grads = grads[:, jnp.array(plane_order(replicas))]
    return back, mix, grads


def half_masks(dtype):
    lane = lax.broadcasted_iota(jnp.int32, (1, 2 * HEAD_SIZE), 1)
    low = (lane < HEAD_SIZE).astype(F32)
    return low.astype(dtype), (1.0 - low).astype(dtype)


def allowed_at(block, step, segq, keycode):
    token = block * BLOCK + lax.broadcasted_iota(jnp.int32, (BLOCK, KEYS), 0)
    key = step * KEYS + lax.broadcasted_iota(jnp.int32, (BLOCK, KEYS), 1)
    return ((segq == keycode) & (key < token)) | (key == token)


SMALL = 32


def turn(field, cosine, sine):
    half = HEAD_SIZE // 2
    lane = lax.broadcasted_iota(jnp.int32, field.shape, field.ndim - 1)
    up = pltpu.roll(field, 2 * HEAD_SIZE - half, field.ndim - 1)
    down = pltpu.roll(field, half, field.ndim - 1)
    return field * cosine + jnp.where(lax.rem(lane, HEAD_SIZE) < half, -up, down) * sine


def attention_forward_kernel(
    parts, n_ctx, tok, small, w_q, w_k, w_v, w_o, pack0, pack1, pack2, cos_ref, sin_ref, seg_ref, code_ref,
    normed, small_all, q_full, k_full, v_full, q_ref, kv_ref, full_ref, log_ref, o_back, o_full,
    gate_own, up_own, down_own,
    acc, q_pack, kv_pack, o_buf,
    send_w, recv_w, send_s, recv_s, send_e, recv_e, send_q, recv_q, send_kv, recv_kv, send_o, recv_o, here,
):
    c, f = lax.axis_index("ctx"), lax.axis_index("fsdp")
    head, part, pair = lax.div(c, parts), lax.rem(c, parts), lax.rem(c, 2)
    rows = D // 4
    half = rows // 2
    wide = 2 * HEAD_SIZE
    barrier = pltpu.get_barrier_semaphore()
    peers = [(i, 0) for i in range(1, n_ctx)] + [(0, k) for k in range(1, 4)]
    for dc, df in peers:
        pl.semaphore_signal(
            barrier, inc=1, device_id=(flip(c, dc), flip(f, df)), device_id_type=MESH
        )
    shards = (w_q, w_k, w_v, w_o)
    fulls = (q_full, k_full, v_full, o_full)
    packs, owns = (pack0, pack1, pack2), (gate_own, up_own, down_own)
    my_rows = pl.ds(pl.multiple_of(f * rows, rows), rows)
    local = [pltpu.make_async_copy(shards[a], fulls[a].at[f], here.at[a]) for a in range(4)]
    local += [pltpu.make_async_copy(small, small_all.at[f], here.at[4])]
    local += [pltpu.make_async_copy(packs[m].at[f], owns[m].at[:, my_rows], here.at[5 + m]) for m in range(3)]
    for copy in local:
        copy.start()
    pl.semaphore_wait(barrier, len(peers))
    near = pl.ds(pl.multiple_of(pair * half, half), half)
    far = pl.ds(pl.multiple_of((1 - pair) * half, half), half)
    sibling, over_x, over_pair = (c, flip(f, 1)), (c, flip(f, 2)), (flip(c, 1), f)

    def weight(a, kind):
        beyond = flip(f, 2)
        source, target, device = (
            (shards[a], fulls[a].at[f], sibling),
            (shards[a].at[near], fulls[a].at[f, near], over_x),
            (fulls[a].at[beyond, near], fulls[a].at[beyond, near], sibling),
            (fulls[a].at[beyond, near], fulls[a].at[beyond, near], over_pair),
            (fulls[a].at[beyond, far], fulls[a].at[beyond, far], sibling),
        )[kind]
        return pltpu.make_async_remote_copy(
            source, target, send_w.at[a, kind], recv_w.at[a, kind], device_id=device, device_id_type=MESH
        )

    smalls = [
        pltpu.make_async_remote_copy(
            small, small_all.at[f], send_s.at[i - 1], recv_s.at[i - 1],
            device_id=(c, flip(f, i)), device_id_type=MESH,
        )
        for i in range(1, 4)
    ]
    for copy in smalls:
        copy.start()
    for a in range(4):
        weight(a, 1).start()
        weight(a, 0).start()
    experts = [
        pltpu.make_async_remote_copy(
            packs[m].at[flip(f, i)], owns[m].at[:, my_rows], send_e.at[i - 1, m], recv_e.at[i - 1, m],
            device_id=(c, flip(f, i)), device_id_type=MESH,
        )
        for m in range(3)
        for i in range(1, 4)
    ]
    for copy in experts:
        copy.start()

    x = tok[...].astype(F32)
    scale = lax.rsqrt(jnp.mean(x * x, axis=1, keepdims=True) + EPS)
    for copy in smalls:
        copy.wait_recv()
    local[4].wait()
    for b in range(4):
        columns = slice(b * rows, (b + 1) * rows)
        normed[:, columns] = (x[:, columns] * scale * small_all[b, :1].astype(F32)).astype(BF16)

    def project(b, first):
        block = normed[:, pl.ds(pl.multiple_of(b * rows, rows), rows)]
        at = 0
        for a in range(3):
            width = fulls[a].shape[2]
            made = jnp.dot(block, fulls[a][b], preferred_element_type=F32)
            acc[:, at : at + width] = made if first else acc[:, at : at + width] + made
            at += width

    for a in range(3):
        local[a].wait()
    project(f, True)
    for a in range(3):
        weight(a, 0).wait_recv()
    project(flip(f, 1), False)
    for a in range(3):
        weight(a, 1).wait_recv()
        weight(a, 2).start()
        weight(a, 3).start()
    for a in range(3):
        weight(a, 3).wait_recv()
        weight(a, 4).start()
    project(flip(f, 2), False)
    for a in range(3):
        weight(a, 2).wait_recv()
        weight(a, 4).wait_recv()
    project(flip(f, 3), False)

    lane = lax.broadcasted_iota(jnp.int32, (BLOCK, wide), 1)
    low = lane < HEAD_SIZE
    cosine, sine = cos_ref[...], sin_ref[...]
    for m in range((QUERY_HEADS + 2 * KEY_VALUE_HEADS) // 2):
        pieces = []
        for s in range(SEQS):
            piece = acc[s * BLOCK : (s + 1) * BLOCK, m * wide : (m + 1) * wide]
            pieces.append(turn(piece, cosine, sine) if m < (QUERY_HEADS + KEY_VALUE_HEADS) // 2 else piece)
        even = jnp.where(low, pieces[0], pltpu.roll(pieces[1], HEAD_SIZE, 1)).astype(BF16)
        odd = jnp.where(low, pltpu.roll(pieces[0], HEAD_SIZE, 1), pieces[1]).astype(BF16)
        for h, value in ((2 * m, even), (2 * m + 1, odd)):
            if h < QUERY_HEADS:
                q_pack[h // REP, h % REP] = value
            else:
                h -= QUERY_HEADS
                kv_pack[h % KEY_VALUE_HEADS, h // KEY_VALUE_HEADS] = value

    q_stays = pltpu.make_async_copy(q_pack.at[head], q_ref.at[head], here.at[8])
    kv_stays = pltpu.make_async_copy(kv_pack.at[head], kv_ref.at[c], here.at[9])
    q_stays.start()
    kv_stays.start()
    to_heads = []
    for i in range(1, n_ctx):
        peer = flip(c, i)
        moves = [(kv_pack.at[lax.div(peer, parts)], kv_ref.at[c], send_kv.at[i - 1], recv_kv.at[i - 1])]
        if i % parts == 0:
            number = i // parts - 1
            moves.append(
                (q_pack.at[lax.div(peer, parts)], q_ref.at[head], send_q.at[number], recv_q.at[number])
            )
        for source, target, sent, came in moves:
            copy = pltpu.make_async_remote_copy(
                source, target, sent, came, device_id=(peer, f), device_id_type=MESH
            )
            copy.start()
            to_heads.append(copy)
    weight(3, 1).wait_recv()
    weight(3, 2).start()
    weight(3, 3).start()
    q_stays.wait()
    kv_stays.wait()
    for copy in to_heads:
        copy.wait_recv()

    count = REP * BLOCK
    halves = half_masks(BF16)
    across = lax.broadcasted_iota(jnp.int32, (count, wide), 1)

    def out_back(j):
        return pltpu.make_async_remote_copy(
            o_buf.at[j], o_back.at[head], send_o.at[j], recv_o.at[head],
            device_id=(j * parts + part, f), device_id_type=MESH,
        )

    def out_stays(j):
        return pltpu.make_async_copy(o_buf.at[j], o_back.at[head], here.at[10])

    def one_block(j, nothing):
        block = j * parts + part
        q = q_ref[j].reshape(count, wide)
        queries = [q * half for half in halves]

        def step(number, carry):
            k = kv_ref[pl.ds(2 * number, 2), 0].reshape(KEYS, wide)
            v = kv_ref[pl.ds(2 * number, 2), 1].reshape(KEYS, wide)
            codes = code_ref[number]
            after = []
            for s in range(SEQS):
                largest, total, out = carry[s]
                mask = allowed_at(block, number, seg_ref[j, s], codes[s : s + 1])
                scores = lax.dot_general(
                    queries[s], k, (((1,), (1,)), ((), ())), preferred_element_type=F32
                )
                scores = jnp.where(mask[None], scores.reshape(REP, BLOCK, KEYS) * SCALE, MASKED)
                scores = scores.reshape(count, KEYS)
                new = jnp.maximum(largest, jnp.max(scores, axis=1, keepdims=True))
                probs = jnp.exp(scores - new)
                shrink = jnp.exp(largest - new)
                total = total * shrink + jnp.sum(probs, axis=1, keepdims=True)
                out = out * shrink + jnp.dot(probs.astype(BF16), v, preferred_element_type=F32)
                after.append((new, total, out))
            return tuple(after)

        start = (
            jnp.full((count, 1), MASKED, F32),
            jnp.zeros((count, 1), F32),
            jnp.zeros((count, wide), F32),
        )
        done = lax.fori_loop(0, lax.div(block, 2) + 1, step, (start,) * SEQS)
        outs, logs = [], []
        for largest, total, out in done:
            outs.append(out / total)
            logs.append(jnp.broadcast_to(largest + jnp.log(total), (count, wide)))
        out = jnp.where(across < HEAD_SIZE, outs[0], outs[1])
        full_ref[j] = out.reshape(REP, BLOCK, wide)
        log_ref[j] = jnp.where(across < HEAD_SIZE, logs[0], logs[1]).reshape(REP, BLOCK, wide)
        o_buf[j] = out.astype(BF16).reshape(REP, BLOCK, wide)

        @pl.when(j != head)
        def _():
            out_back(j).start()

        @pl.when(j == head)
        def _():
            out_stays(j).start()

        return nothing

    lax.fori_loop(0, KEY_VALUE_HEADS, one_block, 0)
    weight(3, 3).wait_recv()
    weight(3, 4).start()

    def came_out(h, nothing):
        @pl.when(h != head)
        def _():
            pltpu.make_async_remote_copy(
                o_buf.at[h], o_back.at[h], send_o.at[h], recv_o.at[h],
                device_id=(h * parts + part, f), device_id_type=MESH,
            ).wait()

        @pl.when(h == head)
        def _():
            out_stays(h).wait()

        return nothing

    lax.fori_loop(0, KEY_VALUE_HEADS, came_out, 0)
    for kind in (0, 2, 4):
        weight(3, kind).wait_recv()
    local[3].wait()
    for copy in local[5:]:
        copy.wait()
    for copy in experts:
        copy.wait()
    for copy in smalls + to_heads:
        copy.wait_send()
    for a in range(4):
        for kind in range(5):
            weight(a, kind).wait_send()


def attention_forward(
    cid, parts, n_ctx, tok, small, w_q, w_k, w_v, w_o, packs, cosine, sine, segq, codes
):
    wide = 2 * HEAD_SIZE
    anywhere = pl.BlockSpec(memory_space=pl.ANY)
    inside = pl.BlockSpec(memory_space=pltpu.VMEM)
    dma = pltpu.SemaphoreType.DMA
    heads = (KEY_VALUE_HEADS, REP, BLOCK, wide)
    keys = (n_ctx, 2, BLOCK, wide)
    others = max(n_ctx // parts - 1, 1)
    columns = w_q.shape[1] + w_k.shape[1] + w_v.shape[1]
    own = jax.ShapeDtypeStruct((OWN, D, FF), BF16)

    def full(x):
        return jax.ShapeDtypeStruct((4,) + x.shape, BF16)

    return pl.pallas_call(
        functools.partial(attention_forward_kernel, parts, n_ctx),
        name="attention_forward",
        out_shape=[
            jax.ShapeDtypeStruct(tok.shape, BF16),
            full(small), full(w_q), full(w_k), full(w_v),
            jax.ShapeDtypeStruct(heads, BF16),
            jax.ShapeDtypeStruct(keys, BF16),
            jax.ShapeDtypeStruct(heads, F32),
            jax.ShapeDtypeStruct(heads, F32),
            jax.ShapeDtypeStruct(heads, BF16),
            full(w_o), own, own, own,
        ],
        in_specs=[inside] + [anywhere] * 8 + [inside] * 4,
        out_specs=[inside] * 9 + [anywhere] * 5,
        scratch_shapes=[
            pltpu.VMEM((SEQS * BLOCK, columns), F32),
            pltpu.VMEM(heads, BF16),
            pltpu.VMEM((KEY_VALUE_HEADS, 2, BLOCK, wide), BF16),
            pltpu.VMEM(heads, BF16),
            dma((4, 5)), dma((4, 5)), dma((3,)), dma((3,)), dma((3, 3)), dma((3, 3)),
            dma((others,)), dma((others,)), dma((n_ctx - 1,)), dma((n_ctx - 1,)),
            dma((KEY_VALUE_HEADS,)), dma((KEY_VALUE_HEADS,)), dma((11,)),
        ],
        compiler_params=pltpu.CompilerParams(
            collective_id=cid, has_side_effects=True, vmem_limit_bytes=56 << 20
        ),
        cost_estimate=lasting(130),
    )(tok, small, w_q, w_k, w_v, w_o, *packs, cosine, sine, segq, codes)


def turn_back(field, cosine, sine):
    half = HEAD_SIZE // 2
    lane = lax.broadcasted_iota(jnp.int32, field.shape, field.ndim - 1)
    up = pltpu.roll(field, 2 * HEAD_SIZE - half, field.ndim - 1)
    down = pltpu.roll(field, half, field.ndim - 1)
    turned = jnp.where(lax.rem(lane, HEAD_SIZE) < half, -up, down)
    return field * cosine - turned * sine


def attention_backward_kernel(
    parts, n_ctx, g_own, q_ref, kv_ref, seg_ref, code_ref, full_ref, log_ref, cos_ref, sin_ref,
    tok, gain, resid_grad, grads, mix, output_part, tokens_all, q_full, k_full, v_full,
    input_grad, gain_grad, output_sum, gate_came, down_keep, down_came, mix_in, head_in,
    g_ref, total, kept, came, dq_ref, dkv_ref, dq_back, dkv_back, w_q, w_k, w_v, grad_qkv, grad_in,
    token_buf, field, head_acc, head_out, output_keep, output_came, output_x, output_pair,
    send_g, recv_g, send_q, recv_q, send_kv, recv_kv, send_mix, recv_mix, send_half, recv_half, here,
    send_out, recv_out, send_head, recv_head, load_t,
):
    c, f = lax.axis_index("ctx"), lax.axis_index("fsdp")
    head, part = lax.div(c, parts), lax.rem(c, parts)
    rows = REP * BLOCK
    wide = 2 * HEAD_SIZE
    barrier = pltpu.get_barrier_semaphore()
    peers = [(i, k) for i in range(n_ctx) for k in range(4) if i or k]
    for dc, df in peers:
        pl.semaphore_signal(
            barrier, inc=1, device_id=(flip(c, dc), flip(f, df)), device_id_type=MESH
        )
    pair, x_bit, core_bit = lax.rem(c, 2), lax.div(f, 2), lax.rem(f, 2)
    loads = [
        pltpu.make_async_copy(source, target, here.at[5 + i])
        for i, (source, target) in enumerate(
            (
                (q_full, w_q), (k_full, w_k), (v_full, w_v),
                (output_part.at[:, :, :, core_bit], output_keep),
            )
        )
    ]

    def bring(b):
        return pltpu.make_async_copy(
            tokens_all.at[b], token_buf.at[lax.rem(b, 2)], load_t.at[lax.rem(b, 2)]
        )

    for copy in loads + [bring(0), bring(1)]:
        copy.start()
    first = pltpu.make_async_copy(g_own.at[head], g_ref.at[head], here.at[0])
    first.start()
    pl.semaphore_wait(barrier, len(peers))
    to_heads = []
    for number, i in enumerate(range(parts, n_ctx, parts)):
        to_heads.append(
            pltpu.make_async_remote_copy(
                g_own.at[lax.div(flip(c, i), parts)], g_ref.at[head],
                send_g.at[number], recv_g.at[number],
                device_id=(flip(c, i), f), device_id_type=MESH,
            )
        )
        to_heads[-1].start()
    half = grads.shape[1] // 2
    quarter = half // 2
    mine = lax.rem(lax.div(c, 2), 2)
    second = lax.rem(lax.div(c, 4), 2)

    def halving(matrix, target, number):
        return pltpu.make_async_remote_copy(
            grads.at[matrix, pl.ds((1 - mine) * half, half)], target,
            send_half.at[number], recv_half.at[number],
            device_id=(flip(c, 2), f), device_id_type=MESH,
        )

    down_halving, gate_halving = halving(2, came, 0), halving(0, gate_came, 1)
    down_halving.start()
    keeping = pltpu.make_async_copy(grads.at[2, pl.ds(mine * half, half)], kept, here.at[3])
    keeping.start()
    output_stages = [
        pltpu.make_async_remote_copy(
            source, target, send_out.at[i], recv_out.at[i], device_id=device, device_id_type=MESH
        )
        for i, (source, target, device) in enumerate(
            (
                (output_part.at[:, :, :, 1 - core_bit], output_came, (c, flip(f, 1))),
                (output_keep.at[:, :, 1 - x_bit], output_x, (c, flip(f, 2))),
                (output_x.at[:, 1 - pair], output_pair, (flip(c, 1), f)),
            )
        )
    ]
    output_stages[0].start()
    returns = []
    for i in range(1, RANKS):
        returns.append(
            pltpu.make_async_remote_copy(
                mix.at[i], mix_in.at[i - 1], send_mix.at[i - 1], recv_mix.at[i - 1],
                device_id=(flip(c, i // 4), flip(f, i % 4)), device_id_type=MESH,
            )
        )
        returns[-1].start()
    total[...] = jnp.zeros_like(total)
    first.wait()
    for copy in to_heads:
        copy.wait_recv()
    halves = half_masks(BF16)
    lane = lax.broadcasted_iota(jnp.int32, (rows, wide), 1)

    def query_back(j):
        return pltpu.make_async_remote_copy(
            dq_ref.at[j], dq_back.at[head], send_q.at[j], recv_q.at[head],
            device_id=(j * parts + part, f), device_id_type=MESH,
        )

    def key_back(b):
        return pltpu.make_async_remote_copy(
            dkv_ref.at[b], dkv_back.at[c], send_kv.at[b], recv_kv.at[c],
            device_id=(b, f), device_id_type=MESH,
        )

    def query_stays(j):
        return pltpu.make_async_copy(dq_ref.at[j], dq_back.at[head], here.at[1])

    def key_stays(b):
        return pltpu.make_async_copy(dkv_ref.at[b], dkv_back.at[c], here.at[2])

    def one_block(j, nothing):
        block = j * parts + part
        q = q_ref[j].reshape(rows, wide)
        g = g_ref[j].reshape(rows, wide)
        queries = [q * half for half in halves]
        partial = [g * half for half in halves]
        product = g.astype(F32) * full_ref[j].reshape(rows, wide)
        logs = log_ref[j].reshape(rows, wide)
        log_total = [logs[:, :1], logs[:, HEAD_SIZE : HEAD_SIZE + 1]]
        inner = [jnp.sum(product * half, axis=1, keepdims=True) for half in half_masks(F32)]

        def step(number, carry):
            k = kv_ref[pl.ds(2 * number, 2), 0].reshape(KEYS, wide)
            v = kv_ref[pl.ds(2 * number, 2), 1].reshape(KEYS, wide)
            codes = code_ref[number]
            after = []
            dk = jnp.zeros((KEYS, wide), F32)
            dv = jnp.zeros((KEYS, wide), F32)
            for s in range(SEQS):
                mask = allowed_at(block, number, seg_ref[j, s], codes[s : s + 1])
                scores = lax.dot_general(
                    queries[s], k, (((1,), (1,)), ((), ())), preferred_element_type=F32
                )
                scores = jnp.where(mask[None], scores.reshape(REP, BLOCK, KEYS) * SCALE, MASKED)
                probs = jnp.exp(scores.reshape(rows, KEYS) - log_total[s])
                grad_probs = lax.dot_general(
                    partial[s], v, (((1,), (1,)), ((), ())), preferred_element_type=F32
                )
                grad_scores = (probs * (grad_probs - inner[s])).astype(BF16)
                dv = dv + lax.dot_general(
                    probs.astype(BF16), partial[s], (((0,), (0,)), ((), ())), preferred_element_type=F32
                )
                dk = dk + lax.dot_general(
                    grad_scores, queries[s], (((0,), (0,)), ((), ())), preferred_element_type=F32
                )
                after.append(carry[s] + jnp.dot(grad_scores, k, preferred_element_type=F32))
            total[pl.ds(2 * number, 2), 0] += dk.reshape(2, BLOCK, wide)
            total[pl.ds(2 * number, 2), 1] += dv.reshape(2, BLOCK, wide)
            return tuple(after)

        start = jnp.zeros((rows, wide), F32)
        done = lax.fori_loop(0, lax.div(block, 2) + 1, step, (start,) * SEQS)
        dq = (jnp.where(lane < HEAD_SIZE, done[0], done[1]) * SCALE).reshape(REP, BLOCK, wide)
        dq_ref[j] = turn_back(dq, cos_ref[block][None], sin_ref[block][None]).astype(BF16)

        @pl.when(j != head)
        def _():
            query_back(j).start()

        @pl.when(j == head)
        def _():
            query_stays(j).start()

        return nothing

    lax.fori_loop(0, KEY_VALUE_HEADS, one_block, 0)

    def finish(b, nothing):
        dkv_ref[b, 0] = turn_back(total[b, 0] * SCALE, cos_ref[b], sin_ref[b]).astype(BF16)
        dkv_ref[b, 1] = total[b, 1].astype(BF16)

        @pl.when(b != c)
        def _():
            key_back(b).start()

        @pl.when(b == c)
        def _():
            key_stays(b).start()

        return nothing

    lax.fori_loop(0, n_ctx, finish, 0)
    gate_halving.start()
    keeping.wait()
    down_halving.wait_recv()

    def add(i, nothing):
        at, e = lax.div(i, OWN), lax.rem(i, OWN)
        kept[at, e] = (kept[at, e].astype(F32) + came[at, e].astype(F32)).astype(BF16)
        return nothing

    lax.fori_loop(0, half * OWN, add, 0)
    down_second = pltpu.make_async_remote_copy(
        kept.at[pl.ds((1 - second) * quarter, quarter)], down_came, send_half.at[2], recv_half.at[2],
        device_id=(flip(c, 4), f), device_id_type=MESH,
    )
    down_second.start()
    leaving = pltpu.make_async_copy(kept.at[pl.ds(second * quarter, quarter)], down_keep, here.at[4])
    leaving.start()

    planes = output_keep.shape[0]

    def plus(mine, came):
        return (mine.astype(F32) + came.astype(F32)).astype(BF16)

    loads[3].wait()
    output_stages[0].wait_recv()

    def cores(i, nothing):
        r, p, x = lax.div(i, 4), lax.rem(lax.div(i, 2), 2), lax.rem(i, 2)
        output_keep[r, p, x] = plus(output_keep[r, p, x], output_came[r, p, x])
        return nothing

    lax.fori_loop(0, planes * 4, cores, 0)
    output_stages[1].start()

    low = lax.broadcasted_iota(jnp.int32, (BLOCK, wide), 1) < HEAD_SIZE

    def side_by_side(even, odd):
        even, odd = even.astype(F32), odd.astype(F32)
        return (
            jnp.where(low, even, pltpu.roll(odd, HEAD_SIZE, 1)),
            jnp.where(low, pltpu.roll(even, HEAD_SIZE, 1), odd),
        )

    head_acc[...] = jnp.zeros_like(head_acc)

    def head_weights(b, nothing):
        bring(b).wait()
        block = token_buf[lax.rem(b, 2)].reshape(SEQS * BLOCK, D)
        wide_block = block.astype(F32)
        scales = lax.rsqrt(jnp.mean(wide_block * wide_block, axis=1, keepdims=True) + EPS)
        j = lax.div(b, parts)
        have = jnp.where(lax.rem(b, parts) == part, 1.0, 0.0)
        heads = [dq_ref[j, r].astype(F32) * have for r in range(REP)] + [dkv_ref[b, 0], dkv_ref[b, 1]]
        heads.append(jnp.zeros((BLOCK, wide), F32))
        for m in range((REP + 3) // 2):
            for s, value in enumerate(side_by_side(heads[2 * m], heads[2 * m + 1])):
                at = slice(s * BLOCK, (s + 1) * BLOCK)
                field[at, m * wide : (m + 1) * wide] = (value * scales[at]).astype(BF16)
        head_acc[...] += lax.dot_general(
            block, field[...], (((0,), (0,)), ((), ())), preferred_element_type=F32
        )

        @pl.when(b + 2 < n_ctx)
        def _():
            bring(b + 2).start()

        return nothing

    lax.fori_loop(0, n_ctx, head_weights, 0)
    slab = D // (n_ctx * 4)
    for d in range(n_ctx * 4):
        head_out[d] = head_acc[d * slab : (d + 1) * slab, : head_out.shape[2]].astype(BF16)
    me = c * 4 + f
    head_stays = pltpu.make_async_copy(head_out.at[me], head_in.at[me], here.at[9])
    head_stays.start()
    to_all = []
    for number, (i, k) in enumerate(peers):
        peer_c, peer_f = flip(c, i), flip(f, k)
        to_all.append(
            pltpu.make_async_remote_copy(
                head_out.at[peer_c * 4 + peer_f], head_in.at[me],
                send_head.at[number], recv_head.at[number],
                device_id=(peer_c, peer_f), device_id_type=MESH,
            )
        )
        to_all[-1].start()

    def came_query(h, nothing):
        @pl.when(h != head)
        def _():
            pltpu.make_async_remote_copy(
                dq_ref.at[h], dq_back.at[h], send_q.at[h], recv_q.at[h],
                device_id=(h * parts + part, f), device_id_type=MESH,
            ).wait()

        @pl.when(h == head)
        def _():
            query_stays(h).wait()

        return nothing

    def came_key(b, nothing):
        @pl.when(b != c)
        def _():
            pltpu.make_async_remote_copy(
                dkv_ref.at[b], dkv_back.at[b], send_kv.at[b], recv_kv.at[b],
                device_id=(b, f), device_id_type=MESH,
            ).wait()

        @pl.when(b == c)
        def _():
            key_stays(b).wait()

        return nothing

    lax.fori_loop(0, KEY_VALUE_HEADS, came_query, 0)
    lax.fori_loop(0, n_ctx, came_key, 0)

    def head_of(h):
        if h < QUERY_HEADS:
            return dq_back[h // REP, h % REP]
        kind, h = (h - QUERY_HEADS) // KEY_VALUE_HEADS, (h - QUERY_HEADS) % KEY_VALUE_HEADS
        value = dkv_back[h * parts, kind]
        if parts > 1:
            value = value.astype(F32)
            for p in range(1, parts):
                value = value + dkv_back[h * parts + p, kind].astype(F32)
        return value

    for m in range((QUERY_HEADS + 2 * KEY_VALUE_HEADS) // 2):
        for s, value in enumerate(side_by_side(head_of(2 * m), head_of(2 * m + 1))):
            grad_qkv[s * BLOCK : (s + 1) * BLOCK, m * wide : (m + 1) * wide] = value.astype(BF16)
    for copy in loads[:3]:
        copy.wait()
    depth = D // 4
    for b in range(4):
        made, at = 0.0, 0
        for weight in (w_q, w_k, w_v):
            width = weight.shape[2]
            made = made + lax.dot_general(
                grad_qkv[:, at : at + width], weight[b], (((1,), (1,)), ((), ())),
                preferred_element_type=F32,
            )
            at += width
        grad_in[:, b * depth : (b + 1) * depth] = made
    x = tok[...].astype(F32)
    scale = lax.rsqrt(jnp.mean(x * x, axis=1, keepdims=True) + EPS)
    gain_grad[...] = jnp.sum(grad_in[...] * x * scale, axis=0, keepdims=True)
    weighted = grad_in[...] * gain[...]
    input_grad[...] = (
        resid_grad[...]
        + scale * weighted
        - x * (scale * scale * scale) * jnp.mean(weighted * x, axis=1, keepdims=True)
    ).astype(BF16)

    output_stages[1].wait_recv()

    def over_x(i, nothing):
        r, p = lax.div(i, 2), lax.rem(i, 2)
        output_x[r, p] = plus(output_keep[r, p, x_bit], output_x[r, p])
        return nothing

    lax.fori_loop(0, planes * 2, over_x, 0)
    output_stages[2].start()
    output_stages[2].wait_recv()

    def over_pair(r, nothing):
        output_sum[r] = plus(output_x[r, pair], output_pair[r])
        return nothing

    lax.fori_loop(0, planes, over_pair, 0)
    for copy in to_heads:
        copy.wait_send()
    for copy in returns + to_all + [gate_halving, down_second, leaving, head_stays]:
        copy.wait()
    for copy in output_stages:
        copy.wait_send()
    down_halving.wait_send()


def attention_backward(
    cid, parts, n_ctx, g_own, q, kv, segq, codes, full, logs, cosine, sine,
    tok, gain, resid_grad, grads, mix, output_part, tokens_all, q_full, k_full, v_full,
):
    wide = 2 * HEAD_SIZE
    anywhere = pl.BlockSpec(memory_space=pl.ANY)
    inside = pl.BlockSpec(memory_space=pltpu.VMEM)
    dma = pltpu.SemaphoreType.DMA
    others = max(n_ctx // parts - 1, 1)
    devices, planes = n_ctx * 4, n_ctx // 2
    slab, head_width = D // devices, (REP + 2) * HEAD_SIZE
    half = (grads.shape[1] // 2,) + grads.shape[2:]
    quarter = (grads.shape[1] // 4,) + grads.shape[2:]
    columns = q_full.shape[2] + k_full.shape[2] + v_full.shape[2]
    return pl.pallas_call(
        functools.partial(attention_backward_kernel, parts, n_ctx),
        name="attention_backward",
        out_shape=[
            jax.ShapeDtypeStruct(tok.shape, BF16),
            jax.ShapeDtypeStruct((1, D), F32),
            jax.ShapeDtypeStruct((planes, slab, D), BF16),
            jax.ShapeDtypeStruct(half, BF16),
            jax.ShapeDtypeStruct(quarter, BF16),
            jax.ShapeDtypeStruct(quarter, BF16),
            jax.ShapeDtypeStruct((RANKS - 1,) + mix.shape[1:], BF16),
            jax.ShapeDtypeStruct((devices, slab, head_width), BF16),
        ],
        in_specs=[anywhere] + [inside] * 11 + [anywhere] * 7,
        out_specs=[inside] * 3 + [anywhere] * 5,
        scratch_shapes=[
            pltpu.VMEM(q.shape, BF16),
            pltpu.VMEM((n_ctx, 2, BLOCK, wide), F32),
            pltpu.VMEM(half, BF16),
            pltpu.VMEM(half, BF16),
            pltpu.VMEM(q.shape, BF16),
            pltpu.VMEM(kv.shape, BF16),
            pltpu.VMEM(q.shape, BF16),
            pltpu.VMEM(kv.shape, BF16),
            pltpu.VMEM(q_full.shape, BF16),
            pltpu.VMEM(k_full.shape, BF16),
            pltpu.VMEM(v_full.shape, BF16),
            pltpu.VMEM((SEQS * BLOCK, columns), BF16),
            pltpu.VMEM((SEQS * BLOCK, D), F32),
            pltpu.VMEM((2, SEQS, BLOCK, D), BF16),
            pltpu.VMEM((SEQS * BLOCK, 3 * wide), BF16),
            pltpu.VMEM((D, 3 * wide), F32),
            pltpu.VMEM((devices, slab, head_width), BF16),
            pltpu.VMEM((planes, 2, 2, slab, D), BF16),
            pltpu.VMEM((planes, 2, 2, slab, D), BF16),
            pltpu.VMEM((planes, 2, slab, D), BF16),
            pltpu.VMEM((planes, slab, D), BF16),
            dma((others,)), dma((others,)), dma((KEY_VALUE_HEADS,)), dma((KEY_VALUE_HEADS,)),
            dma((n_ctx,)), dma((n_ctx,)), dma((RANKS - 1,)), dma((RANKS - 1,)), dma((3,)), dma((3,)),
            dma((10,)), dma((3,)), dma((3,)), dma((devices - 1,)), dma((devices - 1,)), dma((2,)),
        ],
        compiler_params=pltpu.CompilerParams(
            collective_id=cid, has_side_effects=True, vmem_limit_bytes=60 << 20
        ),
        cost_estimate=lasting(125),
    )(
        g_own, q, kv, segq, codes, full, logs, cosine, sine, tok, gain, resid_grad,
        grads, mix, output_part, tokens_all, q_full, k_full, v_full,
    )


def rope_tables(positions):
    half_dim = HEAD_SIZE // 2
    frequency = ROPE_BASE ** (-jnp.arange(half_dim, dtype=F32) * 2.0 / HEAD_SIZE)
    angle = positions.astype(F32)[:, None] * frequency[None, :]
    angle = jnp.concatenate([angle, angle], axis=1)
    return (jnp.cos(angle), jnp.sin(angle))


def heads_out(field, per):
    field = field.reshape(SEQS, BLOCK, KEY_VALUE_HEADS, per, HEAD_SIZE)
    return field.transpose(2, 3, 1, 0, 4).reshape(KEY_VALUE_HEADS, per, BLOCK, SEQS * HEAD_SIZE)


def heads_in(field):
    per = field.shape[1]
    field = field.reshape(KEY_VALUE_HEADS, per, BLOCK, SEQS, HEAD_SIZE)
    return field.transpose(3, 2, 0, 1, 4).reshape(SEQS, BLOCK, KEY_VALUE_HEADS * per * HEAD_SIZE)


def on_device(
    n_ctx,
    n_fsdp,
    tokens,
    segments,
    valid,
    expert_ids,
    slot_order,
    cotangent,
    norm1_gain,
    w_query,
    key_weight,
    value_weight,
    w_output,
    norm2_gain,
    w_router,
    w_gate,
    w_up,
    w_down,
):
    parts = n_ctx // KEY_VALUE_HEADS
    replicas = n_ctx // 2
    full_len = segments.shape[1]
    c_index, f_index = lax.axis_index("ctx"), lax.axis_index("fsdp")
    pair = lax.rem(c_index, 2)
    rank = pair * n_fsdp + f_index
    part = lax.rem(c_index, parts)
    head = lax.div(c_index, parts)
    positions = c_index * BLOCK + jnp.arange(BLOCK, dtype=jnp.int32)

    def tie(x, after):
        return lax.optimization_barrier((x, after))[0]

    tokens_all = lax.all_gather(tokens, "ctx", axis=0, tiled=False)
    small = jnp.concatenate(
        [
            norm1_gain[None],
            norm2_gain[None],
            w_router.T,
            jnp.zeros((SMALL - EXPERTS - 2, D // n_fsdp), BF16),
        ],
        axis=0,
    )
    packs = [
        lax.dynamic_slice_in_dim(w, pair * (EXPERTS // 2), EXPERTS // 2, 1)
        .reshape(D // n_fsdp, n_fsdp, OWN, FF)
        .transpose(1, 2, 0, 3)
        for w in (w_gate, w_up, w_down)
    ]
    inputs_f = tokens.astype(F32)
    scale_one = lax.rsqrt(jnp.mean(inputs_f * inputs_f, axis=-1, keepdims=True) + EPS)
    segq = segments.reshape(SEQS, KEY_VALUE_HEADS, parts, BLOCK)
    segq = lax.dynamic_index_in_dim(segq, part, 2, keepdims=False).transpose(1, 0, 2)[..., None]
    codes = jnp.where(valid > 0, segments, -1)
    codes = codes.reshape(SEQS, full_len // KEYS, KEYS).transpose(1, 0, 2)
    all_cosine, all_sine = rope_tables(jnp.arange(full_len, dtype=jnp.int32))
    all_cosine = jnp.tile(all_cosine, (1, 2)).reshape(n_ctx, BLOCK, 2 * HEAD_SIZE)
    all_sine = jnp.tile(all_sine, (1, 2)).reshape(n_ctx, BLOCK, 2 * HEAD_SIZE)
    (
        normed_in, small_all, full_query, full_key, full_value, q_all, kv_all, head_full, head_logs,
        attn_heads, full_output, own_gate, own_up, own_down,
    ) = attention_forward(
        0, parts, n_ctx, tokens.reshape(SEQS * BLOCK, D), small, w_query, key_weight, value_weight,
        w_output, packs,
        lax.dynamic_index_in_dim(all_cosine, c_index, 0, keepdims=False),
        lax.dynamic_index_in_dim(all_sine, c_index, 0, keepdims=False),
        segq, codes,
    )
    gain_first = small_all[:, 0].reshape(D).astype(F32)
    gain_second = small_all[:, 1].reshape(D).astype(F32)
    full_router = small_all[:, 2 : 2 + EXPERTS].transpose(1, 0, 2).reshape(EXPERTS, D)
    full_output = full_output.reshape(D, D)
    attn_out = heads_in(attn_heads)
    attn_proj = jnp.einsum("sgq,dq->sgd", attn_out, full_output, preferred_element_type=F32)
    residual = inputs_f + attn_proj
    scale_two = lax.rsqrt(jnp.mean(residual * residual, axis=-1, keepdims=True) + EPS)
    normed_mid = (residual * scale_two * gain_second).astype(BF16)

    logits = jnp.einsum("sgd,ed->sge", normed_mid, full_router, preferred_element_type=F32)
    picked = jnp.any(expert_ids[..., None] == jnp.arange(EXPERTS, dtype=jnp.int32), axis=2)
    before = (slot_order[:, None, :] < slot_order[:, :, None]).astype(BF16)
    place = jnp.matmul(before, picked.astype(BF16), preferred_element_type=F32)
    is_kept = picked & (place < CAP)
    chosen = jnp.where(picked, logits, MASKED)
    raised = jnp.where(picked, jnp.exp(chosen - jnp.max(chosen, axis=-1, keepdims=True)), 0.0)
    gates = raised / jnp.sum(raised, axis=-1, keepdims=True)
    payload = jnp.concatenate(
        [
            normed_mid,
            jnp.where(is_kept, place, -1.0).astype(BF16),
            gates.astype(BF16),
            jnp.zeros((SEQS, BLOCK, 128 - 2 * EXPERTS), BF16),
        ],
        axis=2,
    )
    back, mix_part, own_grads = run_experts(
        2, replicas, payload.reshape(SEQS * BLOCK, PAY), cotangent.reshape(SEQS * BLOCK, D),
        (own_gate, own_up, own_down), tokens_all
    )

    replica = lax.div(c_index, 2)

    def halve(grad, bit):
        grad = grad.reshape((2, -1) + grad.shape[1:])
        mine = lax.rem(lax.div(replica, bit), 2)
        send = lax.dynamic_index_in_dim(grad, 1 - mine, 0, keepdims=False)
        keep = lax.dynamic_index_in_dim(grad, mine, 0, keepdims=False)
        return keep, lax.ppermute(send, "ctx", [(a, a ^ (2 * bit)) for a in range(n_ctx)])

    def joined(halves, after):
        keep, came = halves
        return (keep.astype(F32) + tie(came, after).astype(F32)).astype(BF16)

    back = back.reshape(SEQS, BLOCK, D + 128)
    grad_gates = jnp.where(is_kept, back[..., D : D + EXPERTS], 0.0)
    grad_chosen = gates * (grad_gates - jnp.sum(gates * grad_gates, axis=-1, keepdims=True))
    grad_logits = grad_chosen.astype(BF16)
    grad_mid = back[..., :D] + jnp.einsum(
        "sge,ed->sgd", grad_logits, full_router, preferred_element_type=F32
    )
    grad_router = jnp.einsum("sgd,sge->de", normed_mid, grad_logits, preferred_element_type=F32)

    grad_f = cotangent.astype(F32)
    weighted_two = gain_second * grad_mid
    grad_gain_second = jnp.sum(grad_mid * residual * scale_two, axis=(0, 1))
    cube_two = scale_two * scale_two * scale_two
    grad_resid = (
        grad_f
        + scale_two * weighted_two
        - residual * cube_two * jnp.mean(weighted_two * residual, axis=-1, keepdims=True)
    )
    grad_resid_low = grad_resid.astype(BF16)
    grad_attn = jnp.einsum("sgd,dq->sgq", grad_resid_low, full_output, preferred_element_type=F32)
    grad_attn = grad_attn.astype(BF16)
    grad_output_w = jnp.einsum("sgd,sgq->dq", grad_resid_low, attn_out, preferred_element_type=F32)
    rows = D // (n_ctx * n_fsdp)
    def two(field, axis, bit):
        return (
            lax.dynamic_index_in_dim(field, 1 - bit, axis, keepdims=False),
            lax.dynamic_index_in_dim(field, bit, axis, keepdims=False),
        )

    def summed(mine, came):
        return (mine.astype(F32) + came.astype(F32)).astype(BF16)

    output_part = grad_output_w.astype(BF16).reshape(replicas, 2, 2, 2, rows, D)

    input_grad, gain_grad, output_sum, gate_came, down_keep, down_came, mix_in, head_grads = attention_backward(
        6, parts, n_ctx, heads_out(grad_attn, REP), q_all, kv_all, segq, codes, head_full, head_logs,
        all_cosine, all_sine, tokens.reshape(SEQS * BLOCK, D), gain_first[None],
        grad_resid.reshape(SEQS * BLOCK, D), own_grads, mix_part, output_part, tokens_all,
        full_query, full_key, full_value,
    )
    input_grad = input_grad.reshape(SEQS, BLOCK, D)
    layer_out = (
        residual.reshape(SEQS * BLOCK, D) + mix_part[0].astype(F32) + jnp.sum(mix_in.astype(F32), axis=0)
    ).astype(BF16).reshape(SEQS, BLOCK, D)
    gate_keep = own_grads[0].reshape((2, replicas // 2, OWN, FF, D // replicas))
    gate_half = (lax.dynamic_index_in_dim(gate_keep, lax.rem(replica, 2), 0, keepdims=False), gate_came)
    small_grads = jnp.concatenate(
        [grad_router, gain_grad.T, grad_gain_second[:, None], jnp.zeros((D, 128 - EXPERTS - 2), F32)],
        axis=1,
    ).reshape(n_ctx * n_fsdp, rows, 128)

    def device(c, f):
        return c * n_fsdp + f

    def ranked(c, f):
        return lax.rem(c, 2) * n_fsdp + f

    def by_rank(sums):
        field = jnp.stack(sums).reshape(len(sums), OWN, FF, RANKS, rows)
        return field.transpose(3, 0, 1, 4, 2)

    def quarters(halves):
        return two(
            summed(*halves).reshape(2, replicas // 4, OWN, FF, D // replicas),
            0,
            lax.rem(lax.div(replica, 2), 2),
        )

    def whole(keep, came):
        bit = 4
        while bit < replicas:
            keep, came = halve(summed(keep, came), bit)
            bit *= 2
        return summed(keep, came)

    everything = lambda c, f: slice(None)

    def kept_half(grad):
        grad = grad.reshape((2, replicas // 2) + grad.shape[1:])
        return lax.dynamic_index_in_dim(grad, lax.rem(replica, 2), 0, keepdims=False)

    gate_other, gate_mine = quarters((kept_half(own_grads[0]), gate_came))
    routes = []
    for i in range(n_ctx):
        for k in range(n_fsdp):
            moves = []
            if k == 0 and i == 4:
                moves.append((2, everything, 2, everything))
            if k == 0 and i == 2:
                moves.append(
                    (
                        3,
                        lambda c, f: (
                            1,
                            pl.ds((1 - lax.rem(lax.div(c, 2), 2)) * (replicas // 2), replicas // 2),
                        ),
                        3,
                        everything,
                    )
                )
            moves.append(
                (0, lambda c, f, i=i, k=k: device(flip(c, i), flip(f, k)), 0, device)
            )
            if k == 0 and i % 2 == 0:
                moves.append(
                    (1, lambda c, f, i=i: lax.div(flip(c, i), 2), 1, lambda c, f: lax.div(c, 2))
                )
            routes.append((i, k, moves))
    routes.sort(key=lambda r: not (r[1] == 0 and r[0] in (2, 4)))
    operands = [small_grads, output_sum, gate_other, own_grads]
    outs = [(x.shape, x.dtype) for x in operands[:3]] + [(gate_came.shape, BF16)]
    small_all, output_all, gate_came, up_came = exchange(9, "sum_grads", routes, operands, outs, 60)
    output_grad = jnp.sum(output_all.astype(F32), axis=0)
    up_other, up_mine = quarters((kept_half(own_grads[1]), up_came))
    gate_down = by_rank([whole(gate_mine, gate_came), whole(down_keep, down_came)])
    routes = [
        (i // 4, i % 4, [(0, lambda c, f, i=i: flip(ranked(c, f), i), 0, ranked)]) for i in range(RANKS)
    ]
    gate_down, up_came = exchange(
        10,
        "swap_gate_down",
        [(4, 0, [(1, everything, 1, everything)])] + routes,
        [gate_down, up_other],
        [(gate_down.shape, BF16), (up_other.shape, BF16)],
        40,
    )
    head_grads = head_grads.reshape(KEY_VALUE_HEADS, parts * n_fsdp, rows, (REP + 2) * HEAD_SIZE)
    own_gain = lax.dynamic_slice_in_dim(gain_first, device(c_index, f_index) * rows, rows, 0)
    head_grads = jnp.sum(head_grads.astype(F32), axis=1).transpose(1, 0, 2) * own_gain[:, None, None]
    query_grad = head_grads[..., : REP * HEAD_SIZE].reshape(rows, D)
    key_grad = head_grads[..., REP * HEAD_SIZE : (REP + 1) * HEAD_SIZE].reshape(rows, -1)
    value_grad = head_grads[..., (REP + 1) * HEAD_SIZE :].reshape(rows, -1)
    small_sum = jnp.sum(small_all, axis=0)

    up_sum = by_rank([whole(up_mine, up_came)])
    (up_sum,) = exchange(
        8,
        "swap_up",
        routes,
        [up_sum],
        [(up_sum.shape, BF16)],
    )

    def by_row(swapped, matrix):
        return swapped[:, matrix].transpose(2, 0, 1, 3).reshape(rows, EXPERTS, FF).astype(F32)

    return (
        layer_out,
        input_grad,
        small_sum[:, EXPERTS],
        query_grad,
        key_grad,
        value_grad,
        output_grad,
        small_sum[:, EXPERTS + 1],
        small_sum[:, :EXPERTS],
        by_row(gate_down, 0),
        by_row(up_sum, 0),
        by_row(gate_down, 1),
    )


def solution(mesh):
    placed = (
        P("fsdp", "ctx", None),
        P("fsdp", None),
        P("fsdp", None),
        P("fsdp", "ctx", None),
        P("fsdp", "ctx"),
        P("fsdp", "ctx", None),
        P("fsdp"),
        P("fsdp", None),
        P("fsdp", None),
        P("fsdp", None),
        P("fsdp", None),
        P("fsdp"),
        P("fsdp", None),
        P("fsdp", None, None),
        P("fsdp", None, None),
        P("fsdp", None, None),
    )
    return jax.shard_map(
        functools.partial(on_device, mesh.shape["ctx"], mesh.shape["fsdp"]),
        mesh=mesh,
        in_specs=placed,
        out_specs=(
            P("fsdp", "ctx", None),
            P("fsdp", "ctx", None),
            P(("ctx", "fsdp")),
            P(("ctx", "fsdp"), None),
            P(("ctx", "fsdp"), None),
            P(("ctx", "fsdp"), None),
            P(("ctx", "fsdp"), None),
            P(("ctx", "fsdp")),
            P(("ctx", "fsdp"), None),
            P(("ctx", "fsdp"), None, None),
            P(("ctx", "fsdp"), None, None),
            P(("ctx", "fsdp"), None, None),
        ),
        check_vma=False,
    )
```

```python
import functools

import jax
import jax.numpy as jnp
from jax import lax
from jax.experimental import pallas as pl
from jax.experimental.pallas import tpu as pltpu
from jax.sharding import PartitionSpec as P

D = 1536
QUERY_HEADS = 24
KEY_VALUE_HEADS = 8
REP = QUERY_HEADS // KEY_VALUE_HEADS
HEAD_SIZE = 64
FF = 512
EXPERTS = 16
CAP = 80
RANKS = 8
OWN = EXPERTS // RANKS
SEQS = 2
BLOCK = 128
KEYS = 256

EPS = 1e-05
ROPE_BASE = 10000.0
MASKED = -1e30
SCALE = HEAD_SIZE ** (-0.5)
MESH = pl.DeviceIdType.MESH
BF16 = jnp.bfloat16
F32 = jnp.float32


def flip(index, constant):
    result, bit = index, 1
    while bit <= constant:
        if constant & bit:
            result = result + bit - 2 * bit * lax.rem(lax.div(index, bit), 2)
        bit *= 2
    return result


def lasting(microseconds):
    return pl.CostEstimate(flops=0, bytes_accessed=int(microseconds * 3.3e6), transcendentals=0)


PAY = D + 128
GROUPS = 4
ROWS = GROUPS * CAP


def other_chip(c, f, k):
    pair, x = lax.div(k, 2), lax.rem(k, 2)
    return (
        c + pair * (1 - 2 * lax.rem(c, 2)),
        f + 2 * x * (1 - 2 * lax.rem(lax.div(f, 2), 2)),
    )


def plane_order(replicas):
    order = [0]
    while len(order) < replicas:
        order = [2 * i for i in order] + [2 * i + 1 for i in order]
    return order


def experts_kernel(
    replicas, pay, cot, gate_own, up_own, down_own, after,
    back, mix, grads, pay_in, cot_in,
    weights, total, pay_now, cot_now, xs, gs, eo, gi, hid, dgate, dup, disp, comb,
    own, out, sib, ret, mix_now,
    send_first, recv_first, send_fwd, recv_fwd, send_sib, recv_sib, send_chip, recv_chip,
    load_w, load, store, piece_sem,
):
    c, f = lax.axis_index("ctx"), lax.axis_index("fsdp")
    rank = lax.rem(c, 2) * 4 + f
    sibling = (c, flip(f, 1))
    barrier = pltpu.get_barrier_semaphore()
    pl.semaphore_signal(barrier, inc=1, device_id=sibling, device_id_type=MESH)
    for k in range(1, 4):
        pl.semaphore_signal(barrier, inc=1, device_id=other_chip(c, f, k), device_id_type=MESH)
    bring = []
    for m, own_weight in enumerate((gate_own, up_own, down_own)):
        bring.append(pltpu.make_async_copy(own_weight, weights.at[m], load_w.at[m]))
        bring[-1].start()
    pl.semaphore_wait(barrier, 4)
    sources, landed = (pay, cot), (pay_in, cot_in)

    def push(k, a):
        slot = 1 if k == 0 else 2 * k
        return pltpu.make_async_remote_copy(
            sources[a], landed[a].at[slot - 1], send_first.at[k, a], recv_first.at[k, a],
            device_id=sibling if k == 0 else other_chip(c, f, k), device_id_type=MESH,
        )

    def forward(k, a):
        return pltpu.make_async_remote_copy(
            landed[a].at[2 * k - 1], landed[a].at[2 * k], send_fwd.at[k - 1, a], recv_fwd.at[k - 1, a],
            device_id=sibling, device_id_type=MESH,
        )

    def to_sibling(k):
        return pltpu.make_async_remote_copy(
            out.at[lax.rem(k, 2)], sib.at[k], send_sib.at[k], recv_sib.at[k],
            device_id=sibling, device_id_type=MESH,
        )

    def to_chip(k):
        return pltpu.make_async_remote_copy(
            sib.at[k], ret.at[k - 1], send_chip.at[k - 1], recv_chip.at[k - 1],
            device_id=other_chip(c, f, k), device_id_type=MESH,
        )

    def store_mix(k, s):
        return pltpu.make_async_copy(mix_now.at[s], mix.at[2 * k + s], store.at[s])

    for k, a in ((0, 0), (0, 1), (1, 0), (2, 0), (1, 1), (2, 1), (3, 0), (3, 1)):
        push(k, a).start()

    def clear(i, carry):
        total[lax.div(i, OWN), lax.rem(i, OWN)] = jnp.zeros((FF, D), F32)
        return carry

    lax.fori_loop(0, 3 * OWN, clear, 0)
    lane = lax.broadcasted_iota(jnp.int32, (BLOCK, 128), 1)
    wide = lax.broadcasted_iota(jnp.int32, (BLOCK, 2 * BLOCK), 1).astype(F32)
    both = lax.broadcasted_iota(jnp.int32, (BLOCK, OWN * CAP), 1)

    def chunk(k, carry):
        now = (pay_now, cot_now)

        def fetch(a, s, source):
            copy = pltpu.make_async_copy(source, now[a].at[s], load.at[a, s])
            copy.start()
            return copy

        @pl.when(k == 0)
        def _():
            copies = [fetch(a, 0, sources[a]) for a in range(2)]
            for a in range(2):
                push(0, a).wait_recv()
            copies += [fetch(a, 1, landed[a].at[0]) for a in range(2)]
            for copy in copies:
                copy.wait()
            for copy in bring:
                copy.wait()

        @pl.when(k > 0)
        def _():
            for a in range(2):
                pltpu.make_async_remote_copy(
                    sources[a], landed[a].at[2 * k - 1], send_first.at[k, a], recv_first.at[k, a],
                    device_id=other_chip(c, f, k), device_id_type=MESH,
                ).wait_recv()
                forward(k, a).start()
            copies = [fetch(a, 0, landed[a].at[2 * k - 1]) for a in range(2)]
            for a in range(2):
                forward(k, a).wait_recv()
            copies += [fetch(a, 1, landed[a].at[2 * k]) for a in range(2)]
            for copy in copies:
                copy.wait()

        for g in range(GROUPS):
            s, at = g // 2, (g % 2) * BLOCK
            tail = pay_now[s, at : at + BLOCK, D:].astype(F32)

            def column(index):
                return jnp.sum(jnp.where(lane == index, tail, 0.0), axis=1, keepdims=True)

            table = jnp.zeros((BLOCK, 2 * BLOCK), F32)
            gated = jnp.zeros((BLOCK, 2 * BLOCK), F32)
            for e in range(OWN):
                place = column(rank * OWN + e)
                place = jnp.where(place < 0.0, -1000.0, place + e * CAP)
                here = wide == place
                table = jnp.where(here, 1.0, table)
                gated = jnp.where(here, column(EXPERTS + rank * OWN + e), gated)
            table, gated = table.astype(BF16), gated.astype(BF16)
            disp[g] = table
            comb[g] = gated
            for weight, source, keep in (
                (table, pay_now[s, at : at + BLOCK, :D], xs),
                (gated, cot_now[s, at : at + BLOCK], gs),
            ):
                moved = lax.dot_general(
                    weight, source, (((0,), (0,)), ((), ())), preferred_element_type=F32
                ).astype(BF16)
                for e in range(OWN):
                    keep[e, g * CAP : (g + 1) * CAP] = moved[e * CAP : (e + 1) * CAP]

        def expert(e, carry):
            at = pl.multiple_of(e * CAP, 16)
            gate_pre = jnp.dot(xs[e], weights[0, e], preferred_element_type=F32)
            up_pre = jnp.dot(xs[e], weights[1, e], preferred_element_type=F32)
            sigmoid = 1.0 / (1.0 + jnp.exp(-gate_pre))
            activated = gate_pre * sigmoid
            hidden = (activated * up_pre).astype(BF16)
            hid[e] = hidden
            made = lax.dot_general(
                hidden, weights[2, e], (((1,), (1,)), ((), ())), preferred_element_type=F32
            ).astype(BF16)
            for g in range(GROUPS):
                eo[pl.ds(pl.multiple_of(g * OWN * CAP + at, 16), CAP)] = made[g * CAP : (g + 1) * CAP]
            grad_hidden = jnp.dot(gs[e], weights[2, e], preferred_element_type=F32)
            slope = sigmoid * (1.0 + gate_pre * (1.0 - sigmoid))
            grad_gate = (grad_hidden * up_pre * slope).astype(BF16)
            grad_up = (grad_hidden * activated).astype(BF16)
            dgate[e] = grad_gate
            dup[e] = grad_up
            made = lax.dot_general(
                grad_gate, weights[0, e], (((1,), (1,)), ((), ())), preferred_element_type=F32
            )
            made = made + lax.dot_general(
                grad_up, weights[1, e], (((1,), (1,)), ((), ())), preferred_element_type=F32
            )
            made = made.astype(BF16)
            for g in range(GROUPS):
                gi[pl.ds(pl.multiple_of(g * OWN * CAP + at, 16), CAP)] = made[g * CAP : (g + 1) * CAP]
            return carry

        lax.fori_loop(0, OWN, expert, 0)

        @pl.when(k > 0)
        def _():
            for s in range(2):
                store_mix(k - 1, s).wait()

        @pl.when(k > 1)
        def _():
            to_sibling(k - 2).wait_send()

        parity = lax.rem(k, 2)
        for g in range(GROUPS):
            s, at = g // 2, (g % 2) * BLOCK
            slots = pl.ds(g * OWN * CAP, OWN * CAP)
            made = eo[slots]
            mix_now[s, at : at + BLOCK] = jnp.dot(
                comb[g][:, : OWN * CAP], made, preferred_element_type=F32
            ).astype(BF16)
            table = disp[g][:, : OWN * CAP]
            grad_mid = jnp.dot(table, gi[slots], preferred_element_type=F32).astype(BF16)
            met = lax.dot_general(
                cot_now[s, at : at + BLOCK], made, (((1,), (1,)), ((), ())), preferred_element_type=F32
            ) * table.astype(F32)
            values = jnp.zeros((BLOCK, 128), F32)
            for e in range(OWN):
                inside = (both >= e * CAP) & (both < (e + 1) * CAP)
                value = jnp.sum(jnp.where(inside, met, 0.0), axis=1, keepdims=True)
                values = jnp.where(lane == rank * OWN + e, value, values)
            target = own if s == 0 else out
            target[parity, at : at + BLOCK, :D] = grad_mid
            target[parity, at : at + BLOCK, D:] = values.astype(BF16)
        to_sibling(k).start()
        for s in range(2):
            store_mix(k, s).start()

        def weight_grads(e, carry):
            for m, (left, right) in enumerate(((dgate, xs), (dup, xs), (hid, gs))):
                total[m, e] += lax.dot_general(
                    left[e], right[e], (((0,), (0,)), ((), ())), preferred_element_type=F32
                )
            return carry

        lax.fori_loop(0, OWN, weight_grads, 0)
        to_sibling(k).wait_recv()
        sib[k] = (sib[k].astype(F32) + own[parity].astype(F32)).astype(BF16)

        @pl.when(k > 0)
        def _():
            to_chip(k).start()

        return carry

    lax.fori_loop(0, 4, chunk, 0)
    for s in range(2):
        store_mix(3, s).wait()
    stages = (eo, gi)
    pending = []
    for i in range(3 * OWN):
        m, e = i // OWN, i % OWN
        if i >= 2:
            for copy in pending[i - 2]:
                copy.wait()
        stages[i % 2][:FF] = total[m, e].astype(BF16)
        pending.append([])
        if len(grads.shape) == 4:
            pending[i].append(
                pltpu.make_async_copy(stages[i % 2].at[:FF], grads.at[m, e], piece_sem.at[i % 2, 0])
            )
        else:
            width = D // replicas
            for at, plane in enumerate(plane_order(replicas)):
                pending[i].append(
                    pltpu.make_async_copy(
                        stages[i % 2].at[:FF, plane * width : (plane + 1) * width],
                        grads.at[m, at, e],
                        piece_sem.at[i % 2, at],
                    )
                )
        for copy in pending[i]:
            copy.start()
    for copy in pending[-2] + pending[-1]:
        copy.wait()
    for k in (2, 3):
        to_sibling(k).wait_send()
    for k in range(4):
        for a in range(2):
            push(k, a).wait_send()
            if k:
                forward(k, a).wait_send()
    for k in range(1, 4):
        to_chip(k).wait_recv()
    back[...] = (sib[0].astype(F32) + ret[0].astype(F32)) + (ret[1].astype(F32) + ret[2].astype(F32))
    for k in range(1, 4):
        to_chip(k).wait_send()


def run_experts(cid, replicas, pay, cot, owns, after):
    width = D // replicas
    apart = width % 128 == 0
    tokens = SEQS * BLOCK
    anywhere = pl.BlockSpec(memory_space=pl.ANY)
    inside = pl.BlockSpec(memory_space=pltpu.VMEM)
    dma = pltpu.SemaphoreType.DMA
    back, mix, grads, _, _ = pl.pallas_call(
        functools.partial(experts_kernel, replicas),
        name="experts",
        out_shape=[
            jax.ShapeDtypeStruct((tokens, PAY), F32),
            jax.ShapeDtypeStruct((RANKS, tokens, D), BF16),
            jax.ShapeDtypeStruct((3, replicas, OWN, FF, width) if apart else (3, OWN, FF, D), BF16),
            jax.ShapeDtypeStruct((RANKS - 1, tokens, PAY), BF16),
            jax.ShapeDtypeStruct((RANKS - 1, tokens, D), BF16),
        ],
        in_specs=[anywhere] * 6,
        out_specs=[inside] + [anywhere] * 4,
        scratch_shapes=[
            pltpu.VMEM((3, OWN, D, FF), BF16),
            pltpu.VMEM((3, OWN, FF, D), F32),
            pltpu.VMEM((2, tokens, PAY), BF16),
            pltpu.VMEM((2, tokens, D), BF16),
            pltpu.VMEM((OWN, ROWS, D), BF16),
            pltpu.VMEM((OWN, ROWS, D), BF16),
            pltpu.VMEM((OWN * ROWS, D), BF16),
            pltpu.VMEM((OWN * ROWS, D), BF16),
            pltpu.VMEM((OWN, ROWS, FF), BF16),
            pltpu.VMEM((OWN, ROWS, FF), BF16),
            pltpu.VMEM((OWN, ROWS, FF), BF16),
            pltpu.VMEM((GROUPS, BLOCK, 2 * BLOCK), BF16),
            pltpu.VMEM((GROUPS, BLOCK, 2 * BLOCK), BF16),
            pltpu.VMEM((2, tokens, PAY), BF16),
            pltpu.VMEM((2, tokens, PAY), BF16),
            pltpu.VMEM((4, tokens, PAY), BF16),
            pltpu.VMEM((3, tokens, PAY), BF16),
            pltpu.VMEM((2, tokens, D), BF16),
            dma((4, 2)), dma((4, 2)), dma((3, 2)), dma((3, 2)),
            dma((4,)), dma((4,)), dma((3,)), dma((3,)),
            dma((4,)), dma((2, 2)), dma((2,)), dma((2, replicas)),
        ],
        compiler_params=pltpu.CompilerParams(
            collective_id=cid, has_side_effects=True, vmem_limit_bytes=63 << 20
        ),
        cost_estimate=lasting(110),
    )(pay, cot, *owns, after)
    if not apart:
        grads = grads.reshape(3, OWN, FF, replicas, width).transpose(0, 3, 1, 2, 4)
        grads = grads[:, jnp.array(plane_order(replicas))]
    return back, mix, grads


def half_masks(dtype):
    lane = lax.broadcasted_iota(jnp.int32, (1, 2 * HEAD_SIZE), 1)
    low = (lane < HEAD_SIZE).astype(F32)
    return low.astype(dtype), (1.0 - low).astype(dtype)


def allowed_at(block, step, segq, keycode):
    token = block * BLOCK + lax.broadcasted_iota(jnp.int32, (BLOCK, KEYS), 0)
    key = step * KEYS + lax.broadcasted_iota(jnp.int32, (BLOCK, KEYS), 1)
    return ((segq == keycode) & (key < token)) | (key == token)


SMALL = 32


def turn(field, cosine, sine):
    half = HEAD_SIZE // 2
    lane = lax.broadcasted_iota(jnp.int32, field.shape, field.ndim - 1)
    up = pltpu.roll(field, 2 * HEAD_SIZE - half, field.ndim - 1)
    down = pltpu.roll(field, half, field.ndim - 1)
    return field * cosine + jnp.where(lax.rem(lane, HEAD_SIZE) < half, -up, down) * sine


def attention_forward_kernel(
    parts, n_ctx, tok, small, w_q, w_k, w_v, w_o, pack0, pack1, pack2, cos_ref, sin_ref, seg_ref, code_ref,
    normed, small_all, q_full, k_full, v_full, q_ref, kv_ref, full_ref, log_ref, o_back, o_full,
    gate_own, up_own, down_own,
    acc, q_pack, kv_pack, o_buf,
    send_w, recv_w, send_s, recv_s, send_e, recv_e, send_q, recv_q, send_kv, recv_kv, send_o, recv_o, here,
):
    c, f = lax.axis_index("ctx"), lax.axis_index("fsdp")
    head, part, pair = lax.div(c, parts), lax.rem(c, parts), lax.rem(c, 2)
    rows = D // 4
    half = rows // 2
    wide = 2 * HEAD_SIZE
    barrier = pltpu.get_barrier_semaphore()
    peers = [(i, 0) for i in range(1, n_ctx)] + [(0, k) for k in range(1, 4)]
    for dc, df in peers:
        pl.semaphore_signal(
            barrier, inc=1, device_id=(flip(c, dc), flip(f, df)), device_id_type=MESH
        )
    shards = (w_q, w_k, w_v, w_o)
    fulls = (q_full, k_full, v_full, o_full)
    packs, owns = (pack0, pack1, pack2), (gate_own, up_own, down_own)
    my_rows = pl.ds(pl.multiple_of(f * rows, rows), rows)
    local = [pltpu.make_async_copy(shards[a], fulls[a].at[f], here.at[a]) for a in range(4)]
    local += [pltpu.make_async_copy(small, small_all.at[f], here.at[4])]
    local += [pltpu.make_async_copy(packs[m].at[f], owns[m].at[:, my_rows], here.at[5 + m]) for m in range(3)]
    for copy in local:
        copy.start()
    pl.semaphore_wait(barrier, len(peers))
    near = pl.ds(pl.multiple_of(pair * half, half), half)
    far = pl.ds(pl.multiple_of((1 - pair) * half, half), half)
    sibling, over_x, over_pair = (c, flip(f, 1)), (c, flip(f, 2)), (flip(c, 1), f)

    def weight(a, kind):
        beyond = flip(f, 2)
        source, target, device = (
            (shards[a], fulls[a].at[f], sibling),
            (shards[a].at[near], fulls[a].at[f, near], over_x),
            (fulls[a].at[beyond, near], fulls[a].at[beyond, near], sibling),
            (fulls[a].at[beyond, near], fulls[a].at[beyond, near], over_pair),
            (fulls[a].at[beyond, far], fulls[a].at[beyond, far], sibling),
        )[kind]
        return pltpu.make_async_remote_copy(
            source, target, send_w.at[a, kind], recv_w.at[a, kind], device_id=device, device_id_type=MESH
        )

    smalls = [
        pltpu.make_async_remote_copy(
            small, small_all.at[f], send_s.at[i - 1], recv_s.at[i - 1],
            device_id=(c, flip(f, i)), device_id_type=MESH,
        )
        for i in range(1, 4)
    ]
    for copy in smalls:
        copy.start()
    for a in range(4):
        weight(a, 1).start()
        weight(a, 0).start()
    experts = [
        pltpu.make_async_remote_copy(
            packs[m].at[flip(f, i)], owns[m].at[:, my_rows], send_e.at[i - 1, m], recv_e.at[i - 1, m],
            device_id=(c, flip(f, i)), device_id_type=MESH,
        )
        for m in range(3)
        for i in range(1, 4)
    ]
    for copy in experts:
        copy.start()

    x = tok[...].astype(F32)
    scale = lax.rsqrt(jnp.mean(x * x, axis=1, keepdims=True) + EPS)
    for copy in smalls:
        copy.wait_recv()
    local[4].wait()
    for b in range(4):
        columns = slice(b * rows, (b + 1) * rows)
        normed[:, columns] = (x[:, columns] * scale * small_all[b, :1].astype(F32)).astype(BF16)

    def project(b, first):
        block = normed[:, pl.ds(pl.multiple_of(b * rows, rows), rows)]
        at = 0
        for a in range(3):
            width = fulls[a].shape[2]
            made = jnp.dot(block, fulls[a][b], preferred_element_type=F32)
            acc[:, at : at + width] = made if first else acc[:, at : at + width] + made
            at += width

    for a in range(3):
        local[a].wait()
    project(f, True)
    for a in range(3):
        weight(a, 0).wait_recv()
    project(flip(f, 1), False)
    for a in range(3):
        weight(a, 1).wait_recv()
        weight(a, 2).start()
        weight(a, 3).start()
    for a in range(3):
        weight(a, 3).wait_recv()
        weight(a, 4).start()
    project(flip(f, 2), False)
    for a in range(3):
        weight(a, 2).wait_recv()
        weight(a, 4).wait_recv()
    project(flip(f, 3), False)

    lane = lax.broadcasted_iota(jnp.int32, (BLOCK, wide), 1)
    low = lane < HEAD_SIZE
    cosine, sine = cos_ref[...], sin_ref[...]
    for m in range((QUERY_HEADS + 2 * KEY_VALUE_HEADS) // 2):
        pieces = []
        for s in range(SEQS):
            piece = acc[s * BLOCK : (s + 1) * BLOCK, m * wide : (m + 1) * wide]
            pieces.append(turn(piece, cosine, sine) if m < (QUERY_HEADS + KEY_VALUE_HEADS) // 2 else piece)
        even = jnp.where(low, pieces[0], pltpu.roll(pieces[1], HEAD_SIZE, 1)).astype(BF16)
        odd = jnp.where(low, pltpu.roll(pieces[0], HEAD_SIZE, 1), pieces[1]).astype(BF16)
        for h, value in ((2 * m, even), (2 * m + 1, odd)):
            if h < QUERY_HEADS:
                q_pack[h // REP, h % REP] = value
            else:
                h -= QUERY_HEADS
                kv_pack[h % KEY_VALUE_HEADS, h // KEY_VALUE_HEADS] = value

    q_stays = pltpu.make_async_copy(q_pack.at[head], q_ref.at[head], here.at[8])
    kv_stays = pltpu.make_async_copy(kv_pack.at[head], kv_ref.at[c], here.at[9])
    q_stays.start()
    kv_stays.start()
    to_heads = []
    for i in range(1, n_ctx):
        peer = flip(c, i)
        moves = [(kv_pack.at[lax.div(peer, parts)], kv_ref.at[c], send_kv.at[i - 1], recv_kv.at[i - 1])]
        if i % parts == 0:
            number = i // parts - 1
            moves.append(
                (q_pack.at[lax.div(peer, parts)], q_ref.at[head], send_q.at[number], recv_q.at[number])
            )
        for source, target, sent, came in moves:
            copy = pltpu.make_async_remote_copy(
                source, target, sent, came, device_id=(peer, f), device_id_type=MESH
            )
            copy.start()
            to_heads.append(copy)
    weight(3, 1).wait_recv()
    weight(3, 2).start()
    weight(3, 3).start()
    q_stays.wait()
    kv_stays.wait()
    for copy in to_heads:
        copy.wait_recv()

    count = REP * BLOCK
    halves = half_masks(BF16)
    across = lax.broadcasted_iota(jnp.int32, (count, wide), 1)

    def out_back(j):
        return pltpu.make_async_remote_copy(
            o_buf.at[j], o_back.at[head], send_o.at[j], recv_o.at[head],
            device_id=(j * parts + part, f), device_id_type=MESH,
        )

    def out_stays(j):
        return pltpu.make_async_copy(o_buf.at[j], o_back.at[head], here.at[10])

    def one_block(j, nothing):
        block = j * parts + part
        q = q_ref[j].reshape(count, wide)
        queries = [q * half for half in halves]

        def step(number, carry):
            k = kv_ref[pl.ds(2 * number, 2), 0].reshape(KEYS, wide)
            v = kv_ref[pl.ds(2 * number, 2), 1].reshape(KEYS, wide)
            codes = code_ref[number]
            after = []
            for s in range(SEQS):
                largest, total, out = carry[s]
                mask = allowed_at(block, number, seg_ref[j, s], codes[s : s + 1])
                scores = lax.dot_general(
                    queries[s], k, (((1,), (1,)), ((), ())), preferred_element_type=F32
                )
                scores = jnp.where(mask[None], scores.reshape(REP, BLOCK, KEYS) * SCALE, MASKED)
                scores = scores.reshape(count, KEYS)
                new = jnp.maximum(largest, jnp.max(scores, axis=1, keepdims=True))
                probs = jnp.exp(scores - new)
                shrink = jnp.exp(largest - new)
                total = total * shrink + jnp.sum(probs, axis=1, keepdims=True)
                out = out * shrink + jnp.dot(probs.astype(BF16), v, preferred_element_type=F32)
                after.append((new, total, out))
            return tuple(after)

        start = (
            jnp.full((count, 1), MASKED, F32),
            jnp.zeros((count, 1), F32),
            jnp.zeros((count, wide), F32),
        )
        done = lax.fori_loop(0, lax.div(block, 2) + 1, step, (start,) * SEQS)
        outs, logs = [], []
        for largest, total, out in done:
            outs.append(out / total)
            logs.append(jnp.broadcast_to(largest + jnp.log(total), (count, wide)))
        out = jnp.where(across < HEAD_SIZE, outs[0], outs[1])
        full_ref[j] = out.reshape(REP, BLOCK, wide)
        log_ref[j] = jnp.where(across < HEAD_SIZE, logs[0], logs[1]).reshape(REP, BLOCK, wide)
        o_buf[j] = out.astype(BF16).reshape(REP, BLOCK, wide)

        @pl.when(j != head)
        def _():
            out_back(j).start()

        @pl.when(j == head)
        def _():
            out_stays(j).start()

        return nothing

    lax.fori_loop(0, KEY_VALUE_HEADS, one_block, 0)
    weight(3, 3).wait_recv()
    weight(3, 4).start()

    def came_out(h, nothing):
        @pl.when(h != head)
        def _():
            pltpu.make_async_remote_copy(
                o_buf.at[h], o_back.at[h], send_o.at[h], recv_o.at[h],
                device_id=(h * parts + part, f), device_id_type=MESH,
            ).wait()

        @pl.when(h == head)
        def _():
            out_stays(h).wait()

        return nothing

    lax.fori_loop(0, KEY_VALUE_HEADS, came_out, 0)
    for kind in (0, 2, 4):
        weight(3, kind).wait_recv()
    local[3].wait()
    for copy in local[5:]:
        copy.wait()
    for copy in experts:
        copy.wait()
    for copy in smalls + to_heads:
        copy.wait_send()
    for a in range(4):
        for kind in range(5):
            weight(a, kind).wait_send()


def attention_forward(
    cid, parts, n_ctx, tok, small, w_q, w_k, w_v, w_o, packs, cosine, sine, segq, codes
):
    wide = 2 * HEAD_SIZE
    anywhere = pl.BlockSpec(memory_space=pl.ANY)
    inside = pl.BlockSpec(memory_space=pltpu.VMEM)
    dma = pltpu.SemaphoreType.DMA
    heads = (KEY_VALUE_HEADS, REP, BLOCK, wide)
    keys = (n_ctx, 2, BLOCK, wide)
    others = max(n_ctx // parts - 1, 1)
    columns = w_q.shape[1] + w_k.shape[1] + w_v.shape[1]
    own = jax.ShapeDtypeStruct((OWN, D, FF), BF16)

    def full(x):
        return jax.ShapeDtypeStruct((4,) + x.shape, BF16)

    return pl.pallas_call(
        functools.partial(attention_forward_kernel, parts, n_ctx),
        name="attention_forward",
        out_shape=[
            jax.ShapeDtypeStruct(tok.shape, BF16),
            full(small), full(w_q), full(w_k), full(w_v),
            jax.ShapeDtypeStruct(heads, BF16),
            jax.ShapeDtypeStruct(keys, BF16),
            jax.ShapeDtypeStruct(heads, F32),
            jax.ShapeDtypeStruct(heads, F32),
            jax.ShapeDtypeStruct(heads, BF16),
            full(w_o), own, own, own,
        ],
        in_specs=[inside] + [anywhere] * 8 + [inside] * 4,
        out_specs=[inside] * 9 + [anywhere] * 5,
        scratch_shapes=[
            pltpu.VMEM((SEQS * BLOCK, columns), F32),
            pltpu.VMEM(heads, BF16),
            pltpu.VMEM((KEY_VALUE_HEADS, 2, BLOCK, wide), BF16),
            pltpu.VMEM(heads, BF16),
            dma((4, 5)), dma((4, 5)), dma((3,)), dma((3,)), dma((3, 3)), dma((3, 3)),
            dma((others,)), dma((others,)), dma((n_ctx - 1,)), dma((n_ctx - 1,)),
            dma((KEY_VALUE_HEADS,)), dma((KEY_VALUE_HEADS,)), dma((11,)),
        ],
        compiler_params=pltpu.CompilerParams(
            collective_id=cid, has_side_effects=True, vmem_limit_bytes=56 << 20
        ),
        cost_estimate=lasting(130),
    )(tok, small, w_q, w_k, w_v, w_o, *packs, cosine, sine, segq, codes)


def turn_back(field, cosine, sine):
    half = HEAD_SIZE // 2
    lane = lax.broadcasted_iota(jnp.int32, field.shape, field.ndim - 1)
    up = pltpu.roll(field, 2 * HEAD_SIZE - half, field.ndim - 1)
    down = pltpu.roll(field, half, field.ndim - 1)
    turned = jnp.where(lax.rem(lane, HEAD_SIZE) < half, -up, down)
    return field * cosine - turned * sine


def attention_backward_kernel(
    parts, n_ctx, g_own, q_ref, kv_ref, seg_ref, code_ref, full_ref, log_ref, cos_ref, sin_ref,
    tok, gain, resid_grad, residual, grads, mix, output_part, tokens_all, q_full, k_full, v_full,
    input_grad, layer_out, gain_grad, output_sum, gate_came, down_keep, down_came, mix_in, head_in,
    g_ref, total, kept, came, dq_ref, dkv_ref, dq_back, dkv_back, w_q, w_k, w_v, grad_qkv, grad_in,
    token_buf, field, head_acc, head_out, output_keep, output_came, output_x, output_pair,
    send_g, recv_g, send_q, recv_q, send_kv, recv_kv, send_mix, recv_mix, send_half, recv_half, here,
    send_out, recv_out, send_head, recv_head, load_t,
):
    c, f = lax.axis_index("ctx"), lax.axis_index("fsdp")
    head, part = lax.div(c, parts), lax.rem(c, parts)
    rows = REP * BLOCK
    wide = 2 * HEAD_SIZE
    barrier = pltpu.get_barrier_semaphore()
    peers = [(i, k) for i in range(n_ctx) for k in range(4) if i or k]
    for dc, df in peers:
        pl.semaphore_signal(
            barrier, inc=1, device_id=(flip(c, dc), flip(f, df)), device_id_type=MESH
        )
    pair, x_bit, core_bit = lax.rem(c, 2), lax.div(f, 2), lax.rem(f, 2)
    loads = [
        pltpu.make_async_copy(source, target, here.at[5 + i])
        for i, (source, target) in enumerate(
            (
                (q_full, w_q), (k_full, w_k), (v_full, w_v),
                (output_part.at[:, :, :, core_bit], output_keep),
            )
        )
    ]

    def bring(b):
        return pltpu.make_async_copy(
            tokens_all.at[b], token_buf.at[lax.rem(b, 2)], load_t.at[lax.rem(b, 2)]
        )

    for copy in loads + [bring(0), bring(1)]:
        copy.start()
    first = pltpu.make_async_copy(g_own.at[head], g_ref.at[head], here.at[0])
    first.start()
    pl.semaphore_wait(barrier, len(peers))
    to_heads = []
    for number, i in enumerate(range(parts, n_ctx, parts)):
        to_heads.append(
            pltpu.make_async_remote_copy(
                g_own.at[lax.div(flip(c, i), parts)], g_ref.at[head],
                send_g.at[number], recv_g.at[number],
                device_id=(flip(c, i), f), device_id_type=MESH,
            )
        )
        to_heads[-1].start()
    half = grads.shape[1] // 2
    quarter = half // 2
    mine = lax.rem(lax.div(c, 2), 2)
    second = lax.rem(lax.div(c, 4), 2)

    def halving(matrix, target, number):
        return pltpu.make_async_remote_copy(
            grads.at[matrix, pl.ds((1 - mine) * half, half)], target,
            send_half.at[number], recv_half.at[number],
            device_id=(flip(c, 2), f), device_id_type=MESH,
        )

    down_halving, gate_halving = halving(2, came, 0), halving(0, gate_came, 1)
    down_halving.start()
    keeping = pltpu.make_async_copy(grads.at[2, pl.ds(mine * half, half)], kept, here.at[3])
    keeping.start()
    output_stages = [
        pltpu.make_async_remote_copy(
            source, target, send_out.at[i], recv_out.at[i], device_id=device, device_id_type=MESH
        )
        for i, (source, target, device) in enumerate(
            (
                (output_part.at[:, :, :, 1 - core_bit], output_came, (c, flip(f, 1))),
                (output_keep.at[:, :, 1 - x_bit], output_x, (c, flip(f, 2))),
                (output_x.at[:, 1 - pair], output_pair, (flip(c, 1), f)),
            )
        )
    ]
    output_stages[0].start()
    returns = []
    for i in range(1, RANKS):
        returns.append(
            pltpu.make_async_remote_copy(
                mix.at[i], mix_in.at[i - 1], send_mix.at[i - 1], recv_mix.at[i - 1],
                device_id=(flip(c, i // 4), flip(f, i % 4)), device_id_type=MESH,
            )
        )
        returns[-1].start()
    total[...] = jnp.zeros_like(total)
    first.wait()
    for copy in to_heads:
        copy.wait_recv()
    halves = half_masks(BF16)
    lane = lax.broadcasted_iota(jnp.int32, (rows, wide), 1)

    def query_back(j):
        return pltpu.make_async_remote_copy(
            dq_ref.at[j], dq_back.at[head], send_q.at[j], recv_q.at[head],
            device_id=(j * parts + part, f), device_id_type=MESH,
        )

    def key_back(b):
        return pltpu.make_async_remote_copy(
            dkv_ref.at[b], dkv_back.at[c], send_kv.at[b], recv_kv.at[c],
            device_id=(b, f), device_id_type=MESH,
        )

    def query_stays(j):
        return pltpu.make_async_copy(dq_ref.at[j], dq_back.at[head], here.at[1])

    def key_stays(b):
        return pltpu.make_async_copy(dkv_ref.at[b], dkv_back.at[c], here.at[2])

    def one_block(j, nothing):
        block = j * parts + part
        q = q_ref[j].reshape(rows, wide)
        g = g_ref[j].reshape(rows, wide)
        queries = [q * half for half in halves]
        partial = [g * half for half in halves]
        product = g.astype(F32) * full_ref[j].reshape(rows, wide)
        logs = log_ref[j].reshape(rows, wide)
        log_total = [logs[:, :1], logs[:, HEAD_SIZE : HEAD_SIZE + 1]]
        inner = [jnp.sum(product * half, axis=1, keepdims=True) for half in half_masks(F32)]

        def step(number, carry):
            k = kv_ref[pl.ds(2 * number, 2), 0].reshape(KEYS, wide)
            v = kv_ref[pl.ds(2 * number, 2), 1].reshape(KEYS, wide)
            codes = code_ref[number]
            after = []
            dk = jnp.zeros((KEYS, wide), F32)
            dv = jnp.zeros((KEYS, wide), F32)
            for s in range(SEQS):
                mask = allowed_at(block, number, seg_ref[j, s], codes[s : s + 1])
                scores = lax.dot_general(
                    queries[s], k, (((1,), (1,)), ((), ())), preferred_element_type=F32
                )
                scores = jnp.where(mask[None], scores.reshape(REP, BLOCK, KEYS) * SCALE, MASKED)
                probs = jnp.exp(scores.reshape(rows, KEYS) - log_total[s])
                grad_probs = lax.dot_general(
                    partial[s], v, (((1,), (1,)), ((), ())), preferred_element_type=F32
                )
                grad_scores = (probs * (grad_probs - inner[s])).astype(BF16)
                dv = dv + lax.dot_general(
                    probs.astype(BF16), partial[s], (((0,), (0,)), ((), ())), preferred_element_type=F32
                )
                dk = dk + lax.dot_general(
                    grad_scores, queries[s], (((0,), (0,)), ((), ())), preferred_element_type=F32
                )
                after.append(carry[s] + jnp.dot(grad_scores, k, preferred_element_type=F32))
            total[pl.ds(2 * number, 2), 0] += dk.reshape(2, BLOCK, wide)
            total[pl.ds(2 * number, 2), 1] += dv.reshape(2, BLOCK, wide)
            return tuple(after)

        start = jnp.zeros((rows, wide), F32)
        done = lax.fori_loop(0, lax.div(block, 2) + 1, step, (start,) * SEQS)
        dq = (jnp.where(lane < HEAD_SIZE, done[0], done[1]) * SCALE).reshape(REP, BLOCK, wide)
        dq_ref[j] = turn_back(dq, cos_ref[block][None], sin_ref[block][None]).astype(BF16)

        @pl.when(j != head)
        def _():
            query_back(j).start()

        @pl.when(j == head)
        def _():
            query_stays(j).start()

        return nothing

    lax.fori_loop(0, KEY_VALUE_HEADS, one_block, 0)

    def finish(b, nothing):
        dkv_ref[b, 0] = turn_back(total[b, 0] * SCALE, cos_ref[b], sin_ref[b]).astype(BF16)
        dkv_ref[b, 1] = total[b, 1].astype(BF16)

        @pl.when(b != c)
        def _():
            key_back(b).start()

        @pl.when(b == c)
        def _():
            key_stays(b).start()

        return nothing

    lax.fori_loop(0, n_ctx, finish, 0)
    gate_halving.start()
    keeping.wait()
    down_halving.wait_recv()

    def add(i, nothing):
        at, e = lax.div(i, OWN), lax.rem(i, OWN)
        kept[at, e] = (kept[at, e].astype(F32) + came[at, e].astype(F32)).astype(BF16)
        return nothing

    lax.fori_loop(0, half * OWN, add, 0)
    down_second = pltpu.make_async_remote_copy(
        kept.at[pl.ds((1 - second) * quarter, quarter)], down_came, send_half.at[2], recv_half.at[2],
        device_id=(flip(c, 4), f), device_id_type=MESH,
    )
    down_second.start()
    leaving = pltpu.make_async_copy(kept.at[pl.ds(second * quarter, quarter)], down_keep, here.at[4])
    leaving.start()

    planes = output_keep.shape[0]

    def plus(mine, came):
        return (mine.astype(F32) + came.astype(F32)).astype(BF16)

    loads[3].wait()
    output_stages[0].wait_recv()

    def cores(i, nothing):
        r, p, x = lax.div(i, 4), lax.rem(lax.div(i, 2), 2), lax.rem(i, 2)
        output_keep[r, p, x] = plus(output_keep[r, p, x], output_came[r, p, x])
        return nothing

    lax.fori_loop(0, planes * 4, cores, 0)
    output_stages[1].start()

    low = lax.broadcasted_iota(jnp.int32, (BLOCK, wide), 1) < HEAD_SIZE

    def side_by_side(even, odd):
        even, odd = even.astype(F32), odd.astype(F32)
        return (
            jnp.where(low, even, pltpu.roll(odd, HEAD_SIZE, 1)),
            jnp.where(low, pltpu.roll(even, HEAD_SIZE, 1), odd),
        )

    head_acc[...] = jnp.zeros_like(head_acc)

    def head_weights(b, nothing):
        bring(b).wait()
        block = token_buf[lax.rem(b, 2)]
        wide_block = block.astype(F32)
        scales = lax.rsqrt(jnp.mean(wide_block * wide_block, axis=1, keepdims=True) + EPS)
        j = lax.div(b, parts)
        have = jnp.where(lax.rem(b, parts) == part, 1.0, 0.0)
        heads = [dq_ref[j, r].astype(F32) * have for r in range(REP)] + [dkv_ref[b, 0], dkv_ref[b, 1]]
        heads.append(jnp.zeros((BLOCK, wide), F32))
        for m in range((REP + 3) // 2):
            for s, value in enumerate(side_by_side(heads[2 * m], heads[2 * m + 1])):
                at = slice(s * BLOCK, (s + 1) * BLOCK)
                field[at, m * wide : (m + 1) * wide] = (value * scales[at]).astype(BF16)
        head_acc[...] += lax.dot_general(
            block, field[...], (((0,), (0,)), ((), ())), preferred_element_type=F32
        )

        @pl.when(b + 2 < n_ctx)
        def _():
            bring(b + 2).start()

        return nothing

    lax.fori_loop(0, n_ctx, head_weights, 0)
    slab = D // (n_ctx * 4)
    for d in range(n_ctx * 4):
        head_out[d] = head_acc[d * slab : (d + 1) * slab, : head_out.shape[2]].astype(BF16)
    me = c * 4 + f
    head_stays = pltpu.make_async_copy(head_out.at[me], head_in.at[me], here.at[9])
    head_stays.start()
    to_all = []
    for number, (i, k) in enumerate(peers):
        peer_c, peer_f = flip(c, i), flip(f, k)
        to_all.append(
            pltpu.make_async_remote_copy(
                head_out.at[peer_c * 4 + peer_f], head_in.at[me],
                send_head.at[number], recv_head.at[number],
                device_id=(peer_c, peer_f), device_id_type=MESH,
            )
        )
        to_all[-1].start()

    def came_query(h, nothing):
        @pl.when(h != head)
        def _():
            pltpu.make_async_remote_copy(
                dq_ref.at[h], dq_back.at[h], send_q.at[h], recv_q.at[h],
                device_id=(h * parts + part, f), device_id_type=MESH,
            ).wait()

        @pl.when(h == head)
        def _():
            query_stays(h).wait()

        return nothing

    def came_key(b, nothing):
        @pl.when(b != c)
        def _():
            pltpu.make_async_remote_copy(
                dkv_ref.at[b], dkv_back.at[b], send_kv.at[b], recv_kv.at[b],
                device_id=(b, f), device_id_type=MESH,
            ).wait()

        @pl.when(b == c)
        def _():
            key_stays(b).wait()

        return nothing

    lax.fori_loop(0, KEY_VALUE_HEADS, came_query, 0)
    lax.fori_loop(0, n_ctx, came_key, 0)

    def head_of(h):
        if h < QUERY_HEADS:
            return dq_back[h // REP, h % REP]
        kind, h = (h - QUERY_HEADS) // KEY_VALUE_HEADS, (h - QUERY_HEADS) % KEY_VALUE_HEADS
        value = dkv_back[h * parts, kind]
        if parts > 1:
            value = value.astype(F32)
            for p in range(1, parts):
                value = value + dkv_back[h * parts + p, kind].astype(F32)
        return value

    for m in range((QUERY_HEADS + 2 * KEY_VALUE_HEADS) // 2):
        for s, value in enumerate(side_by_side(head_of(2 * m), head_of(2 * m + 1))):
            grad_qkv[s * BLOCK : (s + 1) * BLOCK, m * wide : (m + 1) * wide] = value.astype(BF16)
    for copy in loads[:3]:
        copy.wait()
    depth = D // 4
    for b in range(4):
        made, at = 0.0, 0
        for weight in (w_q, w_k, w_v):
            width = weight.shape[2]
            made = made + lax.dot_general(
                grad_qkv[:, at : at + width], weight[b], (((1,), (1,)), ((), ())),
                preferred_element_type=F32,
            )
            at += width
        grad_in[:, b * depth : (b + 1) * depth] = made
    x = tok[...].astype(F32)
    scale = lax.rsqrt(jnp.mean(x * x, axis=1, keepdims=True) + EPS)
    gain_grad[...] = jnp.sum(grad_in[...] * x * scale, axis=0, keepdims=True)
    weighted = grad_in[...] * gain[...]
    input_grad[...] = (
        resid_grad[...]
        + scale * weighted
        - x * (scale * scale * scale) * jnp.mean(weighted * x, axis=1, keepdims=True)
    ).astype(BF16)

    staying = pltpu.make_async_copy(residual, grad_in, here.at[8])
    staying.start()
    staying.wait()

    def share(i):
        return pltpu.make_async_copy(
            mix_in.at[i - 1] if i else mix.at[0], token_buf.at[i % 2], load_t.at[i % 2]
        )

    share(0).start()
    for i in range(RANKS):
        if i + 1 < RANKS:
            returns[i].wait_recv()
            share(i + 1).start()
        share(i).wait()
        grad_in[...] += token_buf[i % 2].astype(F32)
    layer_out[...] = grad_in[...].astype(BF16)

    output_stages[1].wait_recv()

    def over_x(i, nothing):
        r, p = lax.div(i, 2), lax.rem(i, 2)
        output_x[r, p] = plus(output_keep[r, p, x_bit], output_x[r, p])
        return nothing

    lax.fori_loop(0, planes * 2, over_x, 0)
    output_stages[2].start()
    output_stages[2].wait_recv()

    def over_pair(r, nothing):
        output_sum[r] = plus(output_x[r, pair], output_pair[r])
        return nothing

    lax.fori_loop(0, planes, over_pair, 0)
    for copy in to_heads:
        copy.wait_send()
    for copy in to_all + [gate_halving, down_second, leaving, head_stays]:
        copy.wait()
    for copy in returns + output_stages:
        copy.wait_send()
    down_halving.wait_send()


def attention_backward(
    cid, parts, n_ctx, g_own, q, kv, segq, codes, full, logs, cosine, sine,
    tok, gain, resid_grad, residual, grads, mix, output_part, tokens_all, q_full, k_full, v_full,
):
    wide = 2 * HEAD_SIZE
    anywhere = pl.BlockSpec(memory_space=pl.ANY)
    inside = pl.BlockSpec(memory_space=pltpu.VMEM)
    dma = pltpu.SemaphoreType.DMA
    others = max(n_ctx // parts - 1, 1)
    devices, planes = n_ctx * 4, n_ctx // 2
    slab, head_width = D // devices, (REP + 2) * HEAD_SIZE
    half = (grads.shape[1] // 2,) + grads.shape[2:]
    quarter = (grads.shape[1] // 4,) + grads.shape[2:]
    columns = q_full.shape[2] + k_full.shape[2] + v_full.shape[2]
    return pl.pallas_call(
        functools.partial(attention_backward_kernel, parts, n_ctx),
        name="attention_backward",
        out_shape=[
            jax.ShapeDtypeStruct(tok.shape, BF16),
            jax.ShapeDtypeStruct(tok.shape, BF16),
            jax.ShapeDtypeStruct((1, D), F32),
            jax.ShapeDtypeStruct((planes, slab, D), BF16),
            jax.ShapeDtypeStruct(half, BF16),
            jax.ShapeDtypeStruct(quarter, BF16),
            jax.ShapeDtypeStruct(quarter, BF16),
            jax.ShapeDtypeStruct((RANKS - 1,) + mix.shape[1:], BF16),
            jax.ShapeDtypeStruct((devices, slab, head_width), BF16),
        ],
        in_specs=[anywhere] + [inside] * 11 + [anywhere] * 8,
        out_specs=[inside] * 4 + [anywhere] * 5,
        scratch_shapes=[
            pltpu.VMEM(q.shape, BF16),
            pltpu.VMEM((n_ctx, 2, BLOCK, wide), F32),
            pltpu.VMEM(half, BF16),
            pltpu.VMEM(half, BF16),
            pltpu.VMEM(q.shape, BF16),
            pltpu.VMEM(kv.shape, BF16),
            pltpu.VMEM(q.shape, BF16),
            pltpu.VMEM(kv.shape, BF16),
            pltpu.VMEM(q_full.shape, BF16),
            pltpu.VMEM(k_full.shape, BF16),
            pltpu.VMEM(v_full.shape, BF16),
            pltpu.VMEM((SEQS * BLOCK, columns), BF16),
            pltpu.VMEM((SEQS * BLOCK, D), F32),
            pltpu.VMEM((2, SEQS * BLOCK, D), BF16),
            pltpu.VMEM((SEQS * BLOCK, 3 * wide), BF16),
            pltpu.VMEM((D, 3 * wide), F32),
            pltpu.VMEM((devices, slab, head_width), BF16),
            pltpu.VMEM((planes, 2, 2, slab, D), BF16),
            pltpu.VMEM((planes, 2, 2, slab, D), BF16),
            pltpu.VMEM((planes, 2, slab, D), BF16),
            pltpu.VMEM((planes, slab, D), BF16),
            dma((others,)), dma((others,)), dma((KEY_VALUE_HEADS,)), dma((KEY_VALUE_HEADS,)),
            dma((n_ctx,)), dma((n_ctx,)), dma((RANKS - 1,)), dma((RANKS - 1,)), dma((3,)), dma((3,)),
            dma((10,)), dma((3,)), dma((3,)), dma((devices - 1,)), dma((devices - 1,)), dma((2,)),
        ],
        compiler_params=pltpu.CompilerParams(
            collective_id=cid, has_side_effects=True, vmem_limit_bytes=60 << 20
        ),
        cost_estimate=lasting(125),
    )(
        g_own, q, kv, segq, codes, full, logs, cosine, sine, tok, gain, resid_grad, residual,
        grads, mix, output_part, tokens_all, q_full, k_full, v_full,
    )


def final_kernel(
    n_ctx, small, output_part, grads, gate_came, down_keep, down_came,
    swapped, output_grad, small_sum,
    halves, landed, rest, rest_landed, last, last_landed, turned, output_in, small_in,
    send_half, recv_half, send_out, recv_out, send_small, recv_small, send_swap, recv_swap, load,
):
    c, f = lax.axis_index("ctx"), lax.axis_index("fsdp")
    me, plane, rank = c * 4 + f, lax.div(c, 2), lax.rem(c, 2) * 4 + f
    planes = n_ctx // 2
    half, quarter = planes // 2, planes // 4
    barrier = pltpu.get_barrier_semaphore()
    peers = [(i, k) for i in range(n_ctx) for k in range(4) if i or k]
    for dc, df in peers:
        pl.semaphore_signal(
            barrier, inc=1, device_id=(flip(c, dc), flip(f, df)), device_id_type=MESH
        )
    first, second = lax.rem(plane, 2), lax.rem(lax.div(plane, 2), 2)
    loads = [
        pltpu.make_async_copy(source, target, load.at[i])
        for i, (source, target) in enumerate(
            (
                (grads.at[0, pl.ds(first * half, half)], halves.at[0]),
                (gate_came, landed.at[0]),
                (grads.at[1, pl.ds(first * half, half)], halves.at[1]),
                (down_keep, rest.at[2]),
                (down_came, rest_landed.at[2]),
                (output_part.at[plane], output_in.at[plane]),
                (small.at[me], small_in.at[me]),
            )
        )
    ]
    for copy in loads:
        copy.start()
    pl.semaphore_wait(barrier, len(peers))

    def over(source, target, number, bit):
        return pltpu.make_async_remote_copy(
            source, target, send_half.at[number], recv_half.at[number],
            device_id=(flip(c, 2 * bit), f), device_id_type=MESH,
        )

    up_first = over(grads.at[1, pl.ds((1 - first) * half, half)], landed.at[1], 0, 1)
    up_first.start()

    def plus(mine, came):
        return (mine.astype(F32) + came.astype(F32)).astype(BF16)

    def join(mine, came, amount):
        def one(i, nothing):
            at, e = lax.div(i, OWN), lax.rem(i, OWN)
            mine[at, e] = plus(mine[at, e], came[at, e])
            return nothing

        lax.fori_loop(0, amount * OWN, one, 0)

    def second_halving(m):
        copy = over(halves.at[m, pl.ds((1 - second) * quarter, quarter)], rest_landed.at[m], 1 + m, 2)
        copy.start()
        return copy

    loads[0].wait()
    loads[1].wait()
    join(halves.at[0], landed.at[0], half)
    gate_second = second_halving(0)
    smalls = []
    for number, (i, k) in enumerate(peers):
        peer_c, peer_f = flip(c, i), flip(f, k)
        smalls.append(
            pltpu.make_async_remote_copy(
                small.at[peer_c * 4 + peer_f], small_in.at[me], send_small.at[number], recv_small.at[number],
                device_id=(peer_c, peer_f), device_id_type=MESH,
            )
        )
    outputs = []
    for i in range(1, planes):
        outputs.append(
            pltpu.make_async_remote_copy(
                output_part.at[flip(plane, i)], output_in.at[plane], send_out.at[i - 1], recv_out.at[i - 1],
                device_id=(flip(c, 2 * i), f), device_id_type=MESH,
            )
        )
    for copy in smalls + outputs:
        copy.start()

    def more_halvings(m):
        count, bit, number = quarter, 4, 0
        mine, sent = rest.at[m], []
        join(mine, rest_landed.at[m], quarter)
        while count > 1:
            count //= 2
            chosen = lax.rem(lax.div(plane, bit), 2)
            came = last_landed.at[m, number, pl.ds(0, count)]
            copy = over(mine.at[pl.ds((1 - chosen) * count, count)], came, 4 + 2 * m + number, bit)
            copy.start()
            copy.wait_recv()
            sent.append(copy)
            kept = last.at[m, number, pl.ds(0, count)]
            for at in range(count):
                for e in range(OWN):
                    kept[at, e] = plus(mine[chosen * count + at, e], came[at, e])
            mine, bit, number = kept, bit * 2, number + 1
        rows = turned.shape[3]
        for e in range(OWN):
            across = mine[0, e].astype(F32).T
            for r in range(RANKS):
                turned[m, r, e] = across[r * rows : (r + 1) * rows].astype(BF16)
        for i in range(RANKS):
            source, target = turned.at[m, flip(rank, i)], swapped.at[rank, m]
            if i:
                copy = pltpu.make_async_remote_copy(
                    source, target, send_swap.at[m, i], recv_swap.at[m, i],
                    device_id=(flip(c, i // 4), flip(f, i % 4)), device_id_type=MESH,
                )
            else:
                copy = pltpu.make_async_copy(source, target, load.at[7 + m])
            copy.start()
            swaps.append(copy)
        return sent

    swaps = []
    loads[3].wait()
    loads[4].wait()
    sent = more_halvings(2)
    loads[2].wait()
    up_first.wait_recv()
    join(halves.at[1], landed.at[1], half)
    up_second = second_halving(1)

    def quarter_sum(m, copy):
        for at in range(quarter):
            for e in range(OWN):
                rest[m, at, e] = halves[m, second * quarter + at, e]
        copy.wait_recv()

    quarter_sum(0, gate_second)
    sent += more_halvings(0)
    loads[5].wait()
    loads[6].wait()
    for copy in outputs + smalls:
        copy.wait_recv()
    made = output_in[0].astype(F32)
    for i in range(1, planes):
        made = made + output_in[i].astype(F32)
    output_grad[...] = made
    small_sum[...] = jnp.sum(small_in[...], axis=0)
    quarter_sum(1, up_second)
    sent += more_halvings(1)
    for copy in swaps:
        copy.wait()
    for copy in smalls + outputs + sent + [up_first, gate_second, up_second]:
        copy.wait_send()


def final_sums(cid, n_ctx, small, output_part, grads, gate_came, down_keep, down_came):
    anywhere = pl.BlockSpec(memory_space=pl.ANY)
    inside = pl.BlockSpec(memory_space=pltpu.VMEM)
    dma = pltpu.SemaphoreType.DMA
    devices, planes = n_ctx * 4, n_ctx // 2
    slab, piece = D // devices, grads.shape[2:]
    half, quarter = (planes // 2,) + piece, (planes // 4,) + piece
    deep = (3, 2, max(planes // 8, 1)) + piece
    return pl.pallas_call(
        functools.partial(final_kernel, n_ctx),
        name="final_sums",
        out_shape=[
            jax.ShapeDtypeStruct((RANKS, 3, OWN, slab, FF), BF16),
            jax.ShapeDtypeStruct((slab, D), F32),
            jax.ShapeDtypeStruct(small.shape[1:], F32),
        ],
        in_specs=[anywhere] * 6,
        out_specs=[anywhere] + [inside] * 2,
        scratch_shapes=[
            pltpu.VMEM((2,) + half, BF16),
            pltpu.VMEM((2,) + half, BF16),
            pltpu.VMEM((3,) + quarter, BF16),
            pltpu.VMEM((3,) + quarter, BF16),
            pltpu.VMEM(deep if planes > 4 else (1, 1, 1, 1, 8, 128), BF16),
            pltpu.VMEM(deep if planes > 4 else (1, 1, 1, 1, 8, 128), BF16),
            pltpu.VMEM((3, RANKS, OWN, slab, FF), BF16),
            pltpu.VMEM((planes, slab, D), BF16),
            pltpu.VMEM(small.shape, F32),
            dma((10,)), dma((10,)), dma((planes - 1,)), dma((planes - 1,)),
            dma((devices - 1,)), dma((devices - 1,)), dma((3, RANKS)), dma((3, RANKS)), dma((10,)),
        ],
        compiler_params=pltpu.CompilerParams(
            collective_id=cid, has_side_effects=True, vmem_limit_bytes=56 << 20
        ),
        cost_estimate=lasting(100),
    )(small, output_part, grads, gate_came, down_keep, down_came)


def rope_tables(positions):
    half_dim = HEAD_SIZE // 2
    frequency = ROPE_BASE ** (-jnp.arange(half_dim, dtype=F32) * 2.0 / HEAD_SIZE)
    angle = positions.astype(F32)[:, None] * frequency[None, :]
    angle = jnp.concatenate([angle, angle], axis=1)
    return (jnp.cos(angle), jnp.sin(angle))


def heads_out(field, per):
    field = field.reshape(SEQS, BLOCK, KEY_VALUE_HEADS, per, HEAD_SIZE)
    return field.transpose(2, 3, 1, 0, 4).reshape(KEY_VALUE_HEADS, per, BLOCK, SEQS * HEAD_SIZE)


def heads_in(field):
    per = field.shape[1]
    field = field.reshape(KEY_VALUE_HEADS, per, BLOCK, SEQS, HEAD_SIZE)
    return field.transpose(3, 2, 0, 1, 4).reshape(SEQS, BLOCK, KEY_VALUE_HEADS * per * HEAD_SIZE)


def on_device(
    n_ctx,
    n_fsdp,
    tokens,
    segments,
    valid,
    expert_ids,
    slot_order,
    cotangent,
    norm1_gain,
    w_query,
    key_weight,
    value_weight,
    w_output,
    norm2_gain,
    w_router,
    w_gate,
    w_up,
    w_down,
):
    parts = n_ctx // KEY_VALUE_HEADS
    replicas = n_ctx // 2
    full_len = segments.shape[1]
    c_index, f_index = lax.axis_index("ctx"), lax.axis_index("fsdp")
    pair = lax.rem(c_index, 2)
    rank = pair * n_fsdp + f_index
    part = lax.rem(c_index, parts)
    head = lax.div(c_index, parts)
    positions = c_index * BLOCK + jnp.arange(BLOCK, dtype=jnp.int32)

    tokens_all = lax.all_gather(tokens, "ctx", axis=0, tiled=False)
    small = jnp.concatenate(
        [
            norm1_gain[None],
            norm2_gain[None],
            w_router.T,
            jnp.zeros((SMALL - EXPERTS - 2, D // n_fsdp), BF16),
        ],
        axis=0,
    )
    packs = [
        lax.dynamic_slice_in_dim(w, pair * (EXPERTS // 2), EXPERTS // 2, 1)
        .reshape(D // n_fsdp, n_fsdp, OWN, FF)
        .transpose(1, 2, 0, 3)
        for w in (w_gate, w_up, w_down)
    ]
    inputs_f = tokens.astype(F32)
    scale_one = lax.rsqrt(jnp.mean(inputs_f * inputs_f, axis=-1, keepdims=True) + EPS)
    segq = segments.reshape(SEQS, KEY_VALUE_HEADS, parts, BLOCK)
    segq = lax.dynamic_index_in_dim(segq, part, 2, keepdims=False).transpose(1, 0, 2)[..., None]
    codes = jnp.where(valid > 0, segments, -1)
    codes = codes.reshape(SEQS, full_len // KEYS, KEYS).transpose(1, 0, 2)
    all_cosine, all_sine = rope_tables(jnp.arange(full_len, dtype=jnp.int32))
    all_cosine = jnp.tile(all_cosine, (1, 2)).reshape(n_ctx, BLOCK, 2 * HEAD_SIZE)
    all_sine = jnp.tile(all_sine, (1, 2)).reshape(n_ctx, BLOCK, 2 * HEAD_SIZE)
    (
        normed_in, small_all, full_query, full_key, full_value, q_all, kv_all, head_full, head_logs,
        attn_heads, full_output, own_gate, own_up, own_down,
    ) = attention_forward(
        0, parts, n_ctx, tokens.reshape(SEQS * BLOCK, D), small, w_query, key_weight, value_weight,
        w_output, packs,
        lax.dynamic_index_in_dim(all_cosine, c_index, 0, keepdims=False),
        lax.dynamic_index_in_dim(all_sine, c_index, 0, keepdims=False),
        segq, codes,
    )
    gain_first = small_all[:, 0].reshape(D).astype(F32)
    gain_second = small_all[:, 1].reshape(D).astype(F32)
    full_router = small_all[:, 2 : 2 + EXPERTS].transpose(1, 0, 2).reshape(EXPERTS, D)
    full_output = full_output.reshape(D, D)
    attn_out = heads_in(attn_heads)
    attn_proj = jnp.einsum("sgq,dq->sgd", attn_out, full_output, preferred_element_type=F32)
    residual = inputs_f + attn_proj
    scale_two = lax.rsqrt(jnp.mean(residual * residual, axis=-1, keepdims=True) + EPS)
    normed_mid = (residual * scale_two * gain_second).astype(BF16)

    logits = jnp.einsum("sgd,ed->sge", normed_mid, full_router, preferred_element_type=F32)
    picked = jnp.any(expert_ids[..., None] == jnp.arange(EXPERTS, dtype=jnp.int32), axis=2)
    before = (slot_order[:, None, :] < slot_order[:, :, None]).astype(BF16)
    place = jnp.matmul(before, picked.astype(BF16), preferred_element_type=F32)
    is_kept = picked & (place < CAP)
    chosen = jnp.where(picked, logits, MASKED)
    raised = jnp.where(picked, jnp.exp(chosen - jnp.max(chosen, axis=-1, keepdims=True)), 0.0)
    gates = raised / jnp.sum(raised, axis=-1, keepdims=True)
    payload = jnp.concatenate(
        [
            normed_mid,
            jnp.where(is_kept, place, -1.0).astype(BF16),
            gates.astype(BF16),
            jnp.zeros((SEQS, BLOCK, 128 - 2 * EXPERTS), BF16),
        ],
        axis=2,
    )
    back, mix_part, own_grads = run_experts(
        2, replicas, payload.reshape(SEQS * BLOCK, PAY), cotangent.reshape(SEQS * BLOCK, D),
        (own_gate, own_up, own_down), tokens_all
    )

    back = back.reshape(SEQS, BLOCK, D + 128)
    grad_gates = jnp.where(is_kept, back[..., D : D + EXPERTS], 0.0)
    grad_chosen = gates * (grad_gates - jnp.sum(gates * grad_gates, axis=-1, keepdims=True))
    grad_logits = grad_chosen.astype(BF16)
    grad_mid = back[..., :D] + jnp.einsum(
        "sge,ed->sgd", grad_logits, full_router, preferred_element_type=F32
    )
    grad_router = jnp.einsum("sgd,sge->de", normed_mid, grad_logits, preferred_element_type=F32)

    grad_f = cotangent.astype(F32)
    weighted_two = gain_second * grad_mid
    grad_gain_second = jnp.sum(grad_mid * residual * scale_two, axis=(0, 1))
    cube_two = scale_two * scale_two * scale_two
    grad_resid = (
        grad_f
        + scale_two * weighted_two
        - residual * cube_two * jnp.mean(weighted_two * residual, axis=-1, keepdims=True)
    )
    grad_resid_low = grad_resid.astype(BF16)
    grad_attn = jnp.einsum("sgd,dq->sgq", grad_resid_low, full_output, preferred_element_type=F32)
    grad_attn = grad_attn.astype(BF16)
    grad_output_w = jnp.einsum("sgd,sgq->dq", grad_resid_low, attn_out, preferred_element_type=F32)
    rows = D // (n_ctx * n_fsdp)
    output_part = grad_output_w.astype(BF16).reshape(replicas, 2, 2, 2, rows, D)

    input_grad, layer_out, gain_grad, output_sum, gate_came, down_keep, down_came, _, head_grads = attention_backward(
        6, parts, n_ctx, heads_out(grad_attn, REP), q_all, kv_all, segq, codes, head_full, head_logs,
        all_cosine, all_sine, tokens.reshape(SEQS * BLOCK, D), gain_first[None],
        grad_resid.reshape(SEQS * BLOCK, D), residual.reshape(SEQS * BLOCK, D), own_grads, mix_part, output_part,
        tokens_all.reshape(n_ctx, SEQS * BLOCK, D), full_query, full_key, full_value,
    )
    input_grad = input_grad.reshape(SEQS, BLOCK, D)
    layer_out = layer_out.reshape(SEQS, BLOCK, D)
    amount = rows * (EXPERTS + 2)
    tiles = -(-amount // 1024) * 8
    small_grads = jnp.concatenate([grad_router, gain_grad.T, grad_gain_second[:, None]], axis=1)
    small_grads = jnp.pad(
        small_grads.reshape(n_ctx * n_fsdp, amount), ((0, 0), (0, tiles * 128 - amount))
    ).reshape(n_ctx * n_fsdp, tiles, 128)
    swapped, output_grad, small_sum = final_sums(
        9, n_ctx, small_grads, output_sum, own_grads, gate_came, down_keep, down_came
    )
    small_sum = small_sum.reshape(tiles * 128)[:amount].reshape(rows, EXPERTS + 2)
    head_grads = head_grads.reshape(KEY_VALUE_HEADS, parts * n_fsdp, rows, (REP + 2) * HEAD_SIZE)
    own_gain = lax.dynamic_slice_in_dim(gain_first, (c_index * n_fsdp + f_index) * rows, rows, 0)
    head_grads = jnp.sum(head_grads.astype(F32), axis=1).transpose(1, 0, 2) * own_gain[:, None, None]
    query_grad = head_grads[..., : REP * HEAD_SIZE].reshape(rows, D)
    key_grad = head_grads[..., REP * HEAD_SIZE : (REP + 1) * HEAD_SIZE].reshape(rows, -1)
    value_grad = head_grads[..., (REP + 1) * HEAD_SIZE :].reshape(rows, -1)

    def by_row(matrix):
        return swapped[:, matrix].transpose(2, 0, 1, 3).reshape(rows, EXPERTS, FF).astype(F32)

    return (
        layer_out,
        input_grad,
        small_sum[:, EXPERTS],
        query_grad,
        key_grad,
        value_grad,
        output_grad,
        small_sum[:, EXPERTS + 1],
        small_sum[:, :EXPERTS],
        by_row(0),
        by_row(1),
        by_row(2),
    )


def solution(mesh):
    placed = (
        P("fsdp", "ctx", None),
        P("fsdp", None),
        P("fsdp", None),
        P("fsdp", "ctx", None),
        P("fsdp", "ctx"),
        P("fsdp", "ctx", None),
        P("fsdp"),
        P("fsdp", None),
        P("fsdp", None),
        P("fsdp", None),
        P("fsdp", None),
        P("fsdp"),
        P("fsdp", None),
        P("fsdp", None, None),
        P("fsdp", None, None),
        P("fsdp", None, None),
    )
    return jax.shard_map(
        functools.partial(on_device, mesh.shape["ctx"], mesh.shape["fsdp"]),
        mesh=mesh,
        in_specs=placed,
        out_specs=(
            P("fsdp", "ctx", None),
            P("fsdp", "ctx", None),
            P(("ctx", "fsdp")),
            P(("ctx", "fsdp"), None),
            P(("ctx", "fsdp"), None),
            P(("ctx", "fsdp"), None),
            P(("ctx", "fsdp"), None),
            P(("ctx", "fsdp")),
            P(("ctx", "fsdp"), None),
            P(("ctx", "fsdp"), None, None),
            P(("ctx", "fsdp"), None, None),
            P(("ctx", "fsdp"), None, None),
        ),
        check_vma=False,
    )
```

```python
import functools

import jax
import jax.numpy as jnp
from jax import lax
from jax.experimental import pallas as pl
from jax.experimental.pallas import tpu as pltpu
from jax.sharding import PartitionSpec as P

D = 1536
QUERY_HEADS = 24
KEY_VALUE_HEADS = 8
REP = QUERY_HEADS // KEY_VALUE_HEADS
HEAD_SIZE = 64
FF = 512
EXPERTS = 16
CAP = 80
RANKS = 8
OWN = EXPERTS // RANKS
SEQS = 2
BLOCK = 128
KEYS = 256

EPS = 1e-05
ROPE_BASE = 10000.0
MASKED = -1e30
SCALE = HEAD_SIZE ** (-0.5)
MESH = pl.DeviceIdType.MESH
BF16 = jnp.bfloat16
F32 = jnp.float32


def flip(index, constant):
    result, bit = index, 1
    while bit <= constant:
        if constant & bit:
            result = result + bit - 2 * bit * lax.rem(lax.div(index, bit), 2)
        bit *= 2
    return result


def lasting(microseconds):
    return pl.CostEstimate(flops=0, bytes_accessed=int(microseconds * 3.3e6), transcendentals=0)


PAY = D + 128
GROUPS = 4
ROWS = GROUPS * CAP


def other_chip(c, f, k):
    pair, x = lax.div(k, 2), lax.rem(k, 2)
    return (
        c + pair * (1 - 2 * lax.rem(c, 2)),
        f + 2 * x * (1 - 2 * lax.rem(lax.div(f, 2), 2)),
    )


def plane_order(replicas):
    order = [0]
    while len(order) < replicas:
        order = [2 * i for i in order] + [2 * i + 1 for i in order]
    return order


def experts_kernel(
    replicas, pay, cot, gate_own, up_own, down_own, after,
    back, mix, grads, down_came, pay_in, cot_in,
    weights, total, pay_now, cot_now, xs, gs, eo, gi, hid, dgate, dup, disp, comb,
    own, out, sib, ret, mix_now,
    send_first, recv_first, send_fwd, recv_fwd, send_sib, recv_sib, send_chip, recv_chip,
    load_w, load, store, piece_sem, send_down, recv_down,
):
    c, f = lax.axis_index("ctx"), lax.axis_index("fsdp")
    rank = lax.rem(c, 2) * 4 + f
    sibling = (c, flip(f, 1))
    barrier = pltpu.get_barrier_semaphore()
    pl.semaphore_signal(barrier, inc=1, device_id=sibling, device_id_type=MESH)
    for k in range(1, 4):
        pl.semaphore_signal(barrier, inc=1, device_id=other_chip(c, f, k), device_id_type=MESH)
    apart = len(grads.shape) == 5
    if apart:
        pl.semaphore_signal(barrier, inc=1, device_id=(flip(c, 2), f), device_id_type=MESH)
    bring = []
    for m, own_weight in enumerate((gate_own, up_own, down_own)):
        bring.append(pltpu.make_async_copy(own_weight, weights.at[m], load_w.at[m]))
        bring[-1].start()
    pl.semaphore_wait(barrier, 5 if apart else 4)
    sources, landed = (pay, cot), (pay_in, cot_in)

    def push(k, a):
        slot = 1 if k == 0 else 2 * k
        return pltpu.make_async_remote_copy(
            sources[a], landed[a].at[slot - 1], send_first.at[k, a], recv_first.at[k, a],
            device_id=sibling if k == 0 else other_chip(c, f, k), device_id_type=MESH,
        )

    def forward(k, a):
        return pltpu.make_async_remote_copy(
            landed[a].at[2 * k - 1], landed[a].at[2 * k], send_fwd.at[k - 1, a], recv_fwd.at[k - 1, a],
            device_id=sibling, device_id_type=MESH,
        )

    def to_sibling(k):
        return pltpu.make_async_remote_copy(
            out.at[lax.rem(k, 2)], sib.at[k], send_sib.at[k], recv_sib.at[k],
            device_id=sibling, device_id_type=MESH,
        )

    def to_chip(k):
        return pltpu.make_async_remote_copy(
            sib.at[k], ret.at[k - 1], send_chip.at[k - 1], recv_chip.at[k - 1],
            device_id=other_chip(c, f, k), device_id_type=MESH,
        )

    def store_mix(k, s):
        return pltpu.make_async_copy(mix_now.at[s], mix.at[2 * k + s], store.at[s])

    for k, a in ((0, 0), (0, 1), (1, 0), (2, 0), (1, 1), (2, 1), (3, 0), (3, 1)):
        push(k, a).start()

    def clear(i, carry):
        total[lax.div(i, OWN), lax.rem(i, OWN)] = jnp.zeros((FF, D), F32)
        return carry

    lax.fori_loop(0, 3 * OWN, clear, 0)
    lane = lax.broadcasted_iota(jnp.int32, (BLOCK, 128), 1)
    wide = lax.broadcasted_iota(jnp.int32, (BLOCK, 2 * BLOCK), 1).astype(F32)
    both = lax.broadcasted_iota(jnp.int32, (BLOCK, OWN * CAP), 1)

    def chunk(k, carry):
        now = (pay_now, cot_now)

        def fetch(a, s, source):
            copy = pltpu.make_async_copy(source, now[a].at[s], load.at[a, s])
            copy.start()
            return copy

        @pl.when(k == 0)
        def _():
            copies = [fetch(a, 0, sources[a]) for a in range(2)]
            for a in range(2):
                push(0, a).wait_recv()
            copies += [fetch(a, 1, landed[a].at[0]) for a in range(2)]
            for copy in copies:
                copy.wait()
            for copy in bring:
                copy.wait()

        @pl.when(k > 0)
        def _():
            for a in range(2):
                pltpu.make_async_remote_copy(
                    sources[a], landed[a].at[2 * k - 1], send_first.at[k, a], recv_first.at[k, a],
                    device_id=other_chip(c, f, k), device_id_type=MESH,
                ).wait_recv()
                forward(k, a).start()
            copies = [fetch(a, 0, landed[a].at[2 * k - 1]) for a in range(2)]
            for a in range(2):
                forward(k, a).wait_recv()
            copies += [fetch(a, 1, landed[a].at[2 * k]) for a in range(2)]
            for copy in copies:
                copy.wait()

        for g in range(GROUPS):
            s, at = g // 2, (g % 2) * BLOCK
            tail = pay_now[s, at : at + BLOCK, D:].astype(F32)

            def column(index):
                return jnp.sum(jnp.where(lane == index, tail, 0.0), axis=1, keepdims=True)

            table = jnp.zeros((BLOCK, 2 * BLOCK), F32)
            gated = jnp.zeros((BLOCK, 2 * BLOCK), F32)
            for e in range(OWN):
                place = column(rank * OWN + e)
                place = jnp.where(place < 0.0, -1000.0, place + e * CAP)
                here = wide == place
                table = jnp.where(here, 1.0, table)
                gated = jnp.where(here, column(EXPERTS + rank * OWN + e), gated)
            table, gated = table.astype(BF16), gated.astype(BF16)
            disp[g] = table
            comb[g] = gated
            for weight, source, keep in (
                (table, pay_now[s, at : at + BLOCK, :D], xs),
                (gated, cot_now[s, at : at + BLOCK], gs),
            ):
                moved = lax.dot_general(
                    weight, source, (((0,), (0,)), ((), ())), preferred_element_type=F32
                ).astype(BF16)
                for e in range(OWN):
                    keep[e, g * CAP : (g + 1) * CAP] = moved[e * CAP : (e + 1) * CAP]

        def expert(e, carry):
            at = pl.multiple_of(e * CAP, 16)
            gate_pre = jnp.dot(xs[e], weights[0, e], preferred_element_type=F32)
            up_pre = jnp.dot(xs[e], weights[1, e], preferred_element_type=F32)
            sigmoid = 1.0 / (1.0 + jnp.exp(-gate_pre))
            activated = gate_pre * sigmoid
            hidden = (activated * up_pre).astype(BF16)
            hid[e] = hidden
            made = lax.dot_general(
                hidden, weights[2, e], (((1,), (1,)), ((), ())), preferred_element_type=F32
            ).astype(BF16)
            for g in range(GROUPS):
                eo[pl.ds(pl.multiple_of(g * OWN * CAP + at, 16), CAP)] = made[g * CAP : (g + 1) * CAP]
            grad_hidden = jnp.dot(gs[e], weights[2, e], preferred_element_type=F32)
            slope = sigmoid * (1.0 + gate_pre * (1.0 - sigmoid))
            grad_gate = (grad_hidden * up_pre * slope).astype(BF16)
            grad_up = (grad_hidden * activated).astype(BF16)
            dgate[e] = grad_gate
            dup[e] = grad_up
            made = lax.dot_general(
                grad_gate, weights[0, e], (((1,), (1,)), ((), ())), preferred_element_type=F32
            )
            made = made + lax.dot_general(
                grad_up, weights[1, e], (((1,), (1,)), ((), ())), preferred_element_type=F32
            )
            made = made.astype(BF16)
            for g in range(GROUPS):
                gi[pl.ds(pl.multiple_of(g * OWN * CAP + at, 16), CAP)] = made[g * CAP : (g + 1) * CAP]
            return carry

        lax.fori_loop(0, OWN, expert, 0)

        @pl.when(k > 0)
        def _():
            for s in range(2):
                store_mix(k - 1, s).wait()

        @pl.when(k > 1)
        def _():
            to_sibling(k - 2).wait_send()

        parity = lax.rem(k, 2)
        for g in range(GROUPS):
            s, at = g // 2, (g % 2) * BLOCK
            slots = pl.ds(g * OWN * CAP, OWN * CAP)
            made = eo[slots]
            mix_now[s, at : at + BLOCK] = jnp.dot(
                comb[g][:, : OWN * CAP], made, preferred_element_type=F32
            ).astype(BF16)
            table = disp[g][:, : OWN * CAP]
            grad_mid = jnp.dot(table, gi[slots], preferred_element_type=F32).astype(BF16)
            met = lax.dot_general(
                cot_now[s, at : at + BLOCK], made, (((1,), (1,)), ((), ())), preferred_element_type=F32
            ) * table.astype(F32)
            values = jnp.zeros((BLOCK, 128), F32)
            for e in range(OWN):
                inside = (both >= e * CAP) & (both < (e + 1) * CAP)
                value = jnp.sum(jnp.where(inside, met, 0.0), axis=1, keepdims=True)
                values = jnp.where(lane == rank * OWN + e, value, values)
            target = own if s == 0 else out
            target[parity, at : at + BLOCK, :D] = grad_mid
            target[parity, at : at + BLOCK, D:] = values.astype(BF16)
        to_sibling(k).start()
        for s in range(2):
            store_mix(k, s).start()

        def weight_grads(e, carry):
            for m, (left, right) in enumerate(((dgate, xs), (dup, xs), (hid, gs))):
                total[m, e] += lax.dot_general(
                    left[e], right[e], (((0,), (0,)), ((), ())), preferred_element_type=F32
                )
            return carry

        lax.fori_loop(0, OWN, weight_grads, 0)
        to_sibling(k).wait_recv()
        sib[k] = (sib[k].astype(F32) + own[parity].astype(F32)).astype(BF16)

        @pl.when(k > 0)
        def _():
            to_chip(k).start()

        return carry

    lax.fori_loop(0, 4, chunk, 0)
    for s in range(2):
        store_mix(3, s).wait()
    stages = (eo, gi)
    pending = []
    if apart:
        half = replicas // 2
        down_first = pltpu.make_async_remote_copy(
            grads.at[2, pl.ds((1 - lax.rem(lax.div(c, 2), 2)) * half, half)], down_came,
            send_down, recv_down, device_id=(flip(c, 2), f), device_id_type=MESH,
        )
    for i in range(3 * OWN):
        m, e = (2, 0, 1)[i // OWN], i % OWN
        if i >= 2:
            for copy in pending[i - 2]:
                copy.wait()
        if i == OWN + 1 and apart:
            down_first.start()
        stages[i % 2][:FF] = total[m, e].astype(BF16)
        pending.append([])
        if not apart:
            pending[i].append(
                pltpu.make_async_copy(stages[i % 2].at[:FF], grads.at[m, e], piece_sem.at[i % 2, 0])
            )
        else:
            width = D // replicas
            for at, plane in enumerate(plane_order(replicas)):
                pending[i].append(
                    pltpu.make_async_copy(
                        stages[i % 2].at[:FF, plane * width : (plane + 1) * width],
                        grads.at[m, at, e],
                        piece_sem.at[i % 2, at],
                    )
                )
        for copy in pending[i]:
            copy.start()
    for copy in pending[-2] + pending[-1]:
        copy.wait()
    for k in (2, 3):
        to_sibling(k).wait_send()
    for k in range(4):
        for a in range(2):
            push(k, a).wait_send()
            if k:
                forward(k, a).wait_send()
    for k in range(1, 4):
        to_chip(k).wait_recv()
    back[...] = (sib[0].astype(F32) + ret[0].astype(F32)) + (ret[1].astype(F32) + ret[2].astype(F32))
    for k in range(1, 4):
        to_chip(k).wait_send()
    if apart:
        down_first.wait()


def run_experts(cid, replicas, pay, cot, owns, after):
    width = D // replicas
    apart = width % 128 == 0
    tokens = SEQS * BLOCK
    anywhere = pl.BlockSpec(memory_space=pl.ANY)
    inside = pl.BlockSpec(memory_space=pltpu.VMEM)
    dma = pltpu.SemaphoreType.DMA
    back, mix, grads, down_came, _, _ = pl.pallas_call(
        functools.partial(experts_kernel, replicas),
        name="experts",
        out_shape=[
            jax.ShapeDtypeStruct((tokens, PAY), F32),
            jax.ShapeDtypeStruct((RANKS, tokens, D), BF16),
            jax.ShapeDtypeStruct((3, replicas, OWN, FF, width) if apart else (3, OWN, FF, D), BF16),
            jax.ShapeDtypeStruct((replicas // 2, OWN, FF, width) if apart else (8, 128), BF16),
            jax.ShapeDtypeStruct((RANKS - 1, tokens, PAY), BF16),
            jax.ShapeDtypeStruct((RANKS - 1, tokens, D), BF16),
        ],
        in_specs=[anywhere] * 6,
        out_specs=[inside] + [anywhere] * 5,
        scratch_shapes=[
            pltpu.VMEM((3, OWN, D, FF), BF16),
            pltpu.VMEM((3, OWN, FF, D), F32),
            pltpu.VMEM((2, tokens, PAY), BF16),
            pltpu.VMEM((2, tokens, D), BF16),
            pltpu.VMEM((OWN, ROWS, D), BF16),
            pltpu.VMEM((OWN, ROWS, D), BF16),
            pltpu.VMEM((OWN * ROWS, D), BF16),
            pltpu.VMEM((OWN * ROWS, D), BF16),
            pltpu.VMEM((OWN, ROWS, FF), BF16),
            pltpu.VMEM((OWN, ROWS, FF), BF16),
            pltpu.VMEM((OWN, ROWS, FF), BF16),
            pltpu.VMEM((GROUPS, BLOCK, 2 * BLOCK), BF16),
            pltpu.VMEM((GROUPS, BLOCK, 2 * BLOCK), BF16),
            pltpu.VMEM((2, tokens, PAY), BF16),
            pltpu.VMEM((2, tokens, PAY), BF16),
            pltpu.VMEM((4, tokens, PAY), BF16),
            pltpu.VMEM((3, tokens, PAY), BF16),
            pltpu.VMEM((2, tokens, D), BF16),
            dma((4, 2)), dma((4, 2)), dma((3, 2)), dma((3, 2)),
            dma((4,)), dma((4,)), dma((3,)), dma((3,)),
            dma((4,)), dma((2, 2)), dma((2,)), dma((2, replicas)), dma, dma,
        ],
        compiler_params=pltpu.CompilerParams(
            collective_id=cid, has_side_effects=True, vmem_limit_bytes=63 << 20
        ),
        cost_estimate=lasting(110),
    )(pay, cot, *owns, after)
    if not apart:
        grads = grads.reshape(3, OWN, FF, replicas, width).transpose(0, 3, 1, 2, 4)
        grads = grads[:, jnp.array(plane_order(replicas))]
    return back, mix, grads, down_came, apart


def half_masks(dtype):
    lane = lax.broadcasted_iota(jnp.int32, (1, 2 * HEAD_SIZE), 1)
    low = (lane < HEAD_SIZE).astype(F32)
    return low.astype(dtype), (1.0 - low).astype(dtype)


def allowed_at(block, step, segq, keycode):
    token = block * BLOCK + lax.broadcasted_iota(jnp.int32, (BLOCK, KEYS), 0)
    key = step * KEYS + lax.broadcasted_iota(jnp.int32, (BLOCK, KEYS), 1)
    return ((segq == keycode) & (key < token)) | (key == token)


SMALL = 32


def turn(field, cosine, sine):
    half = HEAD_SIZE // 2
    lane = lax.broadcasted_iota(jnp.int32, field.shape, field.ndim - 1)
    up = pltpu.roll(field, 2 * HEAD_SIZE - half, field.ndim - 1)
    down = pltpu.roll(field, half, field.ndim - 1)
    return field * cosine + jnp.where(lax.rem(lane, HEAD_SIZE) < half, -up, down) * sine


def attention_forward_kernel(
    parts, n_ctx, tok, small, w_q, w_k, w_v, w_o, pack0, pack1, pack2, cos_ref, sin_ref, seg_ref, code_ref,
    normed, small_all, q_full, k_full, v_full, q_ref, kv_ref, full_ref, log_ref, o_back, o_full,
    gate_own, up_own, down_own,
    acc, q_pack, kv_pack, o_buf,
    send_w, recv_w, send_s, recv_s, send_e, recv_e, send_q, recv_q, send_kv, recv_kv, send_o, recv_o, here,
):
    c, f = lax.axis_index("ctx"), lax.axis_index("fsdp")
    head, part, pair = lax.div(c, parts), lax.rem(c, parts), lax.rem(c, 2)
    rows = D // 4
    half = rows // 2
    wide = 2 * HEAD_SIZE
    barrier = pltpu.get_barrier_semaphore()
    peers = [(i, 0) for i in range(1, n_ctx)] + [(0, k) for k in range(1, 4)]
    for dc, df in peers:
        pl.semaphore_signal(
            barrier, inc=1, device_id=(flip(c, dc), flip(f, df)), device_id_type=MESH
        )
    shards = (w_q, w_k, w_v, w_o)
    fulls = (q_full, k_full, v_full, o_full)
    packs, owns = (pack0, pack1, pack2), (gate_own, up_own, down_own)
    my_rows = pl.ds(pl.multiple_of(f * rows, rows), rows)
    local = [pltpu.make_async_copy(shards[a], fulls[a].at[f], here.at[a]) for a in range(4)]
    local += [pltpu.make_async_copy(small, small_all.at[f], here.at[4])]
    local += [pltpu.make_async_copy(packs[m].at[f], owns[m].at[:, my_rows], here.at[5 + m]) for m in range(3)]
    for copy in local:
        copy.start()
    pl.semaphore_wait(barrier, len(peers))
    near = pl.ds(pl.multiple_of(pair * half, half), half)
    far = pl.ds(pl.multiple_of((1 - pair) * half, half), half)
    sibling, over_x, over_pair = (c, flip(f, 1)), (c, flip(f, 2)), (flip(c, 1), f)

    def weight(a, kind):
        beyond = flip(f, 2)
        source, target, device = (
            (shards[a], fulls[a].at[f], sibling),
            (shards[a].at[near], fulls[a].at[f, near], over_x),
            (fulls[a].at[beyond, near], fulls[a].at[beyond, near], sibling),
            (fulls[a].at[beyond, near], fulls[a].at[beyond, near], over_pair),
            (fulls[a].at[beyond, far], fulls[a].at[beyond, far], sibling),
        )[kind]
        return pltpu.make_async_remote_copy(
            source, target, send_w.at[a, kind], recv_w.at[a, kind], device_id=device, device_id_type=MESH
        )

    smalls = [
        pltpu.make_async_remote_copy(
            small, small_all.at[f], send_s.at[i - 1], recv_s.at[i - 1],
            device_id=(c, flip(f, i)), device_id_type=MESH,
        )
        for i in range(1, 4)
    ]
    for copy in smalls:
        copy.start()
    for a in range(4):
        weight(a, 1).start()
        weight(a, 0).start()
    experts = [
        pltpu.make_async_remote_copy(
            packs[m].at[flip(f, i)], owns[m].at[:, my_rows], send_e.at[i - 1, m], recv_e.at[i - 1, m],
            device_id=(c, flip(f, i)), device_id_type=MESH,
        )
        for m in range(3)
        for i in range(1, 4)
    ]
    for copy in experts:
        copy.start()

    x = tok[...].astype(F32)
    scale = lax.rsqrt(jnp.mean(x * x, axis=1, keepdims=True) + EPS)
    for copy in smalls:
        copy.wait_recv()
    local[4].wait()
    for b in range(4):
        columns = slice(b * rows, (b + 1) * rows)
        normed[:, columns] = (x[:, columns] * scale * small_all[b, :1].astype(F32)).astype(BF16)

    def project(b, first):
        block = normed[:, pl.ds(pl.multiple_of(b * rows, rows), rows)]
        at = 0
        for a in range(3):
            width = fulls[a].shape[2]
            made = jnp.dot(block, fulls[a][b], preferred_element_type=F32)
            acc[:, at : at + width] = made if first else acc[:, at : at + width] + made
            at += width

    for a in range(3):
        local[a].wait()
    project(f, True)
    for a in range(3):
        weight(a, 0).wait_recv()
    project(flip(f, 1), False)
    for a in range(3):
        weight(a, 1).wait_recv()
        weight(a, 2).start()
        weight(a, 3).start()
    for a in range(3):
        weight(a, 3).wait_recv()
        weight(a, 4).start()
    project(flip(f, 2), False)
    for a in range(3):
        weight(a, 2).wait_recv()
        weight(a, 4).wait_recv()
    project(flip(f, 3), False)

    lane = lax.broadcasted_iota(jnp.int32, (BLOCK, wide), 1)
    low = lane < HEAD_SIZE
    cosine, sine = cos_ref[...], sin_ref[...]
    for m in range((QUERY_HEADS + 2 * KEY_VALUE_HEADS) // 2):
        pieces = []
        for s in range(SEQS):
            piece = acc[s * BLOCK : (s + 1) * BLOCK, m * wide : (m + 1) * wide]
            pieces.append(turn(piece, cosine, sine) if m < (QUERY_HEADS + KEY_VALUE_HEADS) // 2 else piece)
        even = jnp.where(low, pieces[0], pltpu.roll(pieces[1], HEAD_SIZE, 1)).astype(BF16)
        odd = jnp.where(low, pltpu.roll(pieces[0], HEAD_SIZE, 1), pieces[1]).astype(BF16)
        for h, value in ((2 * m, even), (2 * m + 1, odd)):
            if h < QUERY_HEADS:
                q_pack[h // REP, h % REP] = value
            else:
                h -= QUERY_HEADS
                kv_pack[h % KEY_VALUE_HEADS, h // KEY_VALUE_HEADS] = value

    q_stays = pltpu.make_async_copy(q_pack.at[head], q_ref.at[head], here.at[8])
    kv_stays = pltpu.make_async_copy(kv_pack.at[head], kv_ref.at[c], here.at[9])
    q_stays.start()
    kv_stays.start()
    to_heads = []
    for i in range(1, n_ctx):
        peer = flip(c, i)
        moves = [(kv_pack.at[lax.div(peer, parts)], kv_ref.at[c], send_kv.at[i - 1], recv_kv.at[i - 1])]
        if i % parts == 0:
            number = i // parts - 1
            moves.append(
                (q_pack.at[lax.div(peer, parts)], q_ref.at[head], send_q.at[number], recv_q.at[number])
            )
        for source, target, sent, came in moves:
            copy = pltpu.make_async_remote_copy(
                source, target, sent, came, device_id=(peer, f), device_id_type=MESH
            )
            copy.start()
            to_heads.append(copy)
    weight(3, 1).wait_recv()
    weight(3, 2).start()
    weight(3, 3).start()
    q_stays.wait()
    kv_stays.wait()
    for copy in to_heads:
        copy.wait_recv()

    count = REP * BLOCK
    halves = half_masks(BF16)
    across = lax.broadcasted_iota(jnp.int32, (count, wide), 1)

    def out_back(j):
        return pltpu.make_async_remote_copy(
            o_buf.at[j], o_back.at[head], send_o.at[j], recv_o.at[head],
            device_id=(j * parts + part, f), device_id_type=MESH,
        )

    def out_stays(j):
        return pltpu.make_async_copy(o_buf.at[j], o_back.at[head], here.at[10])

    def one_block(j, nothing):
        block = j * parts + part
        q = q_ref[j].reshape(count, wide)
        queries = [q * half for half in halves]

        def step(number, carry):
            k = kv_ref[pl.ds(2 * number, 2), 0].reshape(KEYS, wide)
            v = kv_ref[pl.ds(2 * number, 2), 1].reshape(KEYS, wide)
            codes = code_ref[number]
            after = []
            for s in range(SEQS):
                largest, total, out = carry[s]
                mask = allowed_at(block, number, seg_ref[j, s], codes[s : s + 1])
                scores = lax.dot_general(
                    queries[s], k, (((1,), (1,)), ((), ())), preferred_element_type=F32
                )
                scores = jnp.where(mask[None], scores.reshape(REP, BLOCK, KEYS) * SCALE, MASKED)
                scores = scores.reshape(count, KEYS)
                new = jnp.maximum(largest, jnp.max(scores, axis=1, keepdims=True))
                probs = jnp.exp(scores - new)
                shrink = jnp.exp(largest - new)
                total = total * shrink + jnp.sum(probs, axis=1, keepdims=True)
                out = out * shrink + jnp.dot(probs.astype(BF16), v, preferred_element_type=F32)
                after.append((new, total, out))
            return tuple(after)

        start = (
            jnp.full((count, 1), MASKED, F32),
            jnp.zeros((count, 1), F32),
            jnp.zeros((count, wide), F32),
        )
        done = lax.fori_loop(0, lax.div(block, 2) + 1, step, (start,) * SEQS)
        outs, logs = [], []
        for largest, total, out in done:
            outs.append(out / total)
            logs.append(jnp.broadcast_to(largest + jnp.log(total), (count, wide)))
        out = jnp.where(across < HEAD_SIZE, outs[0], outs[1])
        full_ref[j] = out.reshape(REP, BLOCK, wide)
        log_ref[j] = jnp.where(across < HEAD_SIZE, logs[0], logs[1]).reshape(REP, BLOCK, wide)
        o_buf[j] = out.astype(BF16).reshape(REP, BLOCK, wide)

        @pl.when(j != head)
        def _():
            out_back(j).start()

        @pl.when(j == head)
        def _():
            out_stays(j).start()

        return nothing

    lax.fori_loop(0, KEY_VALUE_HEADS, one_block, 0)
    weight(3, 3).wait_recv()
    weight(3, 4).start()

    def came_out(h, nothing):
        @pl.when(h != head)
        def _():
            pltpu.make_async_remote_copy(
                o_buf.at[h], o_back.at[h], send_o.at[h], recv_o.at[h],
                device_id=(h * parts + part, f), device_id_type=MESH,
            ).wait()

        @pl.when(h == head)
        def _():
            out_stays(h).wait()

        return nothing

    lax.fori_loop(0, KEY_VALUE_HEADS, came_out, 0)
    for kind in (0, 2, 4):
        weight(3, kind).wait_recv()
    local[3].wait()
    for copy in local[5:]:
        copy.wait()
    for copy in experts:
        copy.wait()
    for copy in smalls + to_heads:
        copy.wait_send()
    for a in range(4):
        for kind in range(5):
            weight(a, kind).wait_send()


def attention_forward(
    cid, parts, n_ctx, tok, small, w_q, w_k, w_v, w_o, packs, cosine, sine, segq, codes
):
    wide = 2 * HEAD_SIZE
    anywhere = pl.BlockSpec(memory_space=pl.ANY)
    inside = pl.BlockSpec(memory_space=pltpu.VMEM)
    dma = pltpu.SemaphoreType.DMA
    heads = (KEY_VALUE_HEADS, REP, BLOCK, wide)
    keys = (n_ctx, 2, BLOCK, wide)
    others = max(n_ctx // parts - 1, 1)
    columns = w_q.shape[1] + w_k.shape[1] + w_v.shape[1]
    own = jax.ShapeDtypeStruct((OWN, D, FF), BF16)

    def full(x):
        return jax.ShapeDtypeStruct((4,) + x.shape, BF16)

    return pl.pallas_call(
        functools.partial(attention_forward_kernel, parts, n_ctx),
        name="attention_forward",
        out_shape=[
            jax.ShapeDtypeStruct(tok.shape, BF16),
            full(small), full(w_q), full(w_k), full(w_v),
            jax.ShapeDtypeStruct(heads, BF16),
            jax.ShapeDtypeStruct(keys, BF16),
            jax.ShapeDtypeStruct(heads, F32),
            jax.ShapeDtypeStruct(heads, F32),
            jax.ShapeDtypeStruct(heads, BF16),
            full(w_o), own, own, own,
        ],
        in_specs=[inside] + [anywhere] * 8 + [inside] * 4,
        out_specs=[inside] * 9 + [anywhere] * 5,
        scratch_shapes=[
            pltpu.VMEM((SEQS * BLOCK, columns), F32),
            pltpu.VMEM(heads, BF16),
            pltpu.VMEM((KEY_VALUE_HEADS, 2, BLOCK, wide), BF16),
            pltpu.VMEM(heads, BF16),
            dma((4, 5)), dma((4, 5)), dma((3,)), dma((3,)), dma((3, 3)), dma((3, 3)),
            dma((others,)), dma((others,)), dma((n_ctx - 1,)), dma((n_ctx - 1,)),
            dma((KEY_VALUE_HEADS,)), dma((KEY_VALUE_HEADS,)), dma((11,)),
        ],
        compiler_params=pltpu.CompilerParams(
            collective_id=cid, has_side_effects=True, vmem_limit_bytes=56 << 20
        ),
        cost_estimate=lasting(130),
    )(tok, small, w_q, w_k, w_v, w_o, *packs, cosine, sine, segq, codes)


def turn_back(field, cosine, sine):
    half = HEAD_SIZE // 2
    lane = lax.broadcasted_iota(jnp.int32, field.shape, field.ndim - 1)
    up = pltpu.roll(field, 2 * HEAD_SIZE - half, field.ndim - 1)
    down = pltpu.roll(field, half, field.ndim - 1)
    turned = jnp.where(lax.rem(lane, HEAD_SIZE) < half, -up, down)
    return field * cosine - turned * sine


def attention_backward_kernel(
    parts, n_ctx, early, g_own, q_ref, kv_ref, seg_ref, code_ref, full_ref, log_ref, cos_ref, sin_ref,
    tok, gain, resid_grad, residual, grads, down_in, mix, output_part, tokens_all, q_full, k_full, v_full,
    input_grad, layer_out, gain_grad, output_sum, gate_first, gate_keep, gate_came, down_keep, down_came, mix_in,
    head_in, g_ref, total, kept, came, dq_ref, dkv_ref, dq_back, dkv_back, w_q, w_k, w_v, grad_qkv, grad_in,
    token_buf, field, head_acc, head_out, output_keep, output_came, output_x, output_pair,
    send_g, recv_g, send_q, recv_q, send_kv, recv_kv, send_mix, recv_mix, send_half, recv_half, here,
    send_out, recv_out, send_head, recv_head, load_t,
):
    c, f = lax.axis_index("ctx"), lax.axis_index("fsdp")
    head, part = lax.div(c, parts), lax.rem(c, parts)
    rows = REP * BLOCK
    wide = 2 * HEAD_SIZE
    barrier = pltpu.get_barrier_semaphore()
    peers = [(i, k) for i in range(n_ctx) for k in range(4) if i or k]
    for dc, df in peers:
        pl.semaphore_signal(
            barrier, inc=1, device_id=(flip(c, dc), flip(f, df)), device_id_type=MESH
        )
    pair, x_bit, core_bit = lax.rem(c, 2), lax.div(f, 2), lax.rem(f, 2)
    loads = [
        pltpu.make_async_copy(source, target, here.at[5 + i])
        for i, (source, target) in enumerate(
            (
                (q_full, w_q), (k_full, w_k), (v_full, w_v),
                (output_part.at[:, :, :, core_bit], output_keep),
            )
        )
    ]

    def bring(b):
        return pltpu.make_async_copy(
            tokens_all.at[b], token_buf.at[lax.rem(b, 2)], load_t.at[lax.rem(b, 2)]
        )

    for copy in loads + [bring(0), bring(1)]:
        copy.start()
    first = pltpu.make_async_copy(g_own.at[head], g_ref.at[head], here.at[0])
    first.start()
    pl.semaphore_wait(barrier, len(peers))
    to_heads = []
    for number, i in enumerate(range(parts, n_ctx, parts)):
        to_heads.append(
            pltpu.make_async_remote_copy(
                g_own.at[lax.div(flip(c, i), parts)], g_ref.at[head],
                send_g.at[number], recv_g.at[number],
                device_id=(flip(c, i), f), device_id_type=MESH,
            )
        )
        to_heads[-1].start()
    half = grads.shape[1] // 2
    quarter = half // 2
    mine = lax.rem(lax.div(c, 2), 2)
    second = lax.rem(lax.div(c, 4), 2)

    def halving(matrix, target, number):
        return pltpu.make_async_remote_copy(
            grads.at[matrix, pl.ds((1 - mine) * half, half)], target,
            send_half.at[number], recv_half.at[number],
            device_id=(flip(c, 2), f), device_id_type=MESH,
        )

    down_halving, gate_halving = halving(2, came, 0), halving(0, gate_first, 1)
    arriving = pltpu.make_async_copy(down_in, came, here.at[10]) if early else down_halving
    arriving.start()
    keeping = pltpu.make_async_copy(grads.at[2, pl.ds(mine * half, half)], kept, here.at[3])
    keeping.start()
    output_stages = [
        pltpu.make_async_remote_copy(
            source, target, send_out.at[i], recv_out.at[i], device_id=device, device_id_type=MESH
        )
        for i, (source, target, device) in enumerate(
            (
                (output_part.at[:, :, :, 1 - core_bit], output_came, (c, flip(f, 1))),
                (output_keep.at[:, :, 1 - x_bit], output_x, (c, flip(f, 2))),
                (output_x.at[:, 1 - pair], output_pair, (flip(c, 1), f)),
            )
        )
    ]
    output_stages[0].start()
    returns = []
    for i in range(1, RANKS):
        returns.append(
            pltpu.make_async_remote_copy(
                mix.at[i], mix_in.at[i - 1], send_mix.at[i - 1], recv_mix.at[i - 1],
                device_id=(flip(c, i // 4), flip(f, i % 4)), device_id_type=MESH,
            )
        )
        returns[-1].start()
    def plus(mine, came):
        return (mine.astype(F32) + came.astype(F32)).astype(BF16)

    def second_halving(keep, target, number):
        def add(i, nothing):
            at, e = lax.div(i, OWN), lax.rem(i, OWN)
            kept[at, e] = plus(kept[at, e], came[at, e])
            return nothing

        lax.fori_loop(0, half * OWN, add, 0)
        going = pltpu.make_async_remote_copy(
            kept.at[pl.ds((1 - second) * quarter, quarter)], target, send_half.at[number], recv_half.at[number],
            device_id=(flip(c, 4), f), device_id_type=MESH,
        )
        going.start()
        staying = pltpu.make_async_copy(kept.at[pl.ds(second * quarter, quarter)], keep, here.at[4])
        staying.start()
        return going, staying

    if early:
        keeping.wait()
        arriving.wait()
        down_second, leaving = second_halving(down_keep, down_came, 2)
    gate_halving.start()
    total[...] = jnp.zeros_like(total)
    first.wait()
    for copy in to_heads:
        copy.wait_recv()
    halves = half_masks(BF16)
    lane = lax.broadcasted_iota(jnp.int32, (rows, wide), 1)

    def query_back(j):
        return pltpu.make_async_remote_copy(
            dq_ref.at[j], dq_back.at[head], send_q.at[j], recv_q.at[head],
            device_id=(j * parts + part, f), device_id_type=MESH,
        )

    def key_back(b):
        return pltpu.make_async_remote_copy(
            dkv_ref.at[b], dkv_back.at[c], send_kv.at[b], recv_kv.at[c],
            device_id=(b, f), device_id_type=MESH,
        )

    def query_stays(j):
        return pltpu.make_async_copy(dq_ref.at[j], dq_back.at[head], here.at[1])

    def key_stays(b):
        return pltpu.make_async_copy(dkv_ref.at[b], dkv_back.at[c], here.at[2])

    def one_block(j, nothing):
        block = j * parts + part
        q = q_ref[j].reshape(rows, wide)
        g = g_ref[j].reshape(rows, wide)
        queries = [q * half for half in halves]
        partial = [g * half for half in halves]
        product = g.astype(F32) * full_ref[j].reshape(rows, wide)
        logs = log_ref[j].reshape(rows, wide)
        log_total = [logs[:, :1], logs[:, HEAD_SIZE : HEAD_SIZE + 1]]
        inner = [jnp.sum(product * half, axis=1, keepdims=True) for half in half_masks(F32)]

        def step(number, carry):
            k = kv_ref[pl.ds(2 * number, 2), 0].reshape(KEYS, wide)
            v = kv_ref[pl.ds(2 * number, 2), 1].reshape(KEYS, wide)
            codes = code_ref[number]
            after = []
            dk = jnp.zeros((KEYS, wide), F32)
            dv = jnp.zeros((KEYS, wide), F32)
            for s in range(SEQS):
                mask = allowed_at(block, number, seg_ref[j, s], codes[s : s + 1])
                scores = lax.dot_general(
                    queries[s], k, (((1,), (1,)), ((), ())), preferred_element_type=F32
                )
                scores = jnp.where(mask[None], scores.reshape(REP, BLOCK, KEYS) * SCALE, MASKED)
                probs = jnp.exp(scores.reshape(rows, KEYS) - log_total[s])
                grad_probs = lax.dot_general(
                    partial[s], v, (((1,), (1,)), ((), ())), preferred_element_type=F32
                )
                grad_scores = (probs * (grad_probs - inner[s])).astype(BF16)
                dv = dv + lax.dot_general(
                    probs.astype(BF16), partial[s], (((0,), (0,)), ((), ())), preferred_element_type=F32
                )
                dk = dk + lax.dot_general(
                    grad_scores, queries[s], (((0,), (0,)), ((), ())), preferred_element_type=F32
                )
                after.append(carry[s] + jnp.dot(grad_scores, k, preferred_element_type=F32))
            total[pl.ds(2 * number, 2), 0] += dk.reshape(2, BLOCK, wide)
            total[pl.ds(2 * number, 2), 1] += dv.reshape(2, BLOCK, wide)
            return tuple(after)

        start = jnp.zeros((rows, wide), F32)
        done = lax.fori_loop(0, lax.div(block, 2) + 1, step, (start,) * SEQS)
        dq = (jnp.where(lane < HEAD_SIZE, done[0], done[1]) * SCALE).reshape(REP, BLOCK, wide)
        dq_ref[j] = turn_back(dq, cos_ref[block][None], sin_ref[block][None]).astype(BF16)

        @pl.when(j != head)
        def _():
            query_back(j).start()

        @pl.when(j == head)
        def _():
            query_stays(j).start()

        return nothing

    lax.fori_loop(0, KEY_VALUE_HEADS, one_block, 0)

    def finish(b, nothing):
        dkv_ref[b, 0] = turn_back(total[b, 0] * SCALE, cos_ref[b], sin_ref[b]).astype(BF16)
        dkv_ref[b, 1] = total[b, 1].astype(BF16)

        @pl.when(b != c)
        def _():
            key_back(b).start()

        @pl.when(b == c)
        def _():
            key_stays(b).start()

        return nothing

    lax.fori_loop(0, n_ctx, finish, 0)
    if not early:
        keeping.wait()
        down_halving.wait_recv()
        down_second, leaving = second_halving(down_keep, down_came, 2)

    planes = output_keep.shape[0]

    loads[3].wait()
    output_stages[0].wait_recv()

    def cores(i, nothing):
        r, p, x = lax.div(i, 4), lax.rem(lax.div(i, 2), 2), lax.rem(i, 2)
        output_keep[r, p, x] = plus(output_keep[r, p, x], output_came[r, p, x])
        return nothing

    lax.fori_loop(0, planes * 4, cores, 0)
    output_stages[1].start()

    low = lax.broadcasted_iota(jnp.int32, (BLOCK, wide), 1) < HEAD_SIZE

    def side_by_side(even, odd):
        even, odd = even.astype(F32), odd.astype(F32)
        return (
            jnp.where(low, even, pltpu.roll(odd, HEAD_SIZE, 1)),
            jnp.where(low, pltpu.roll(even, HEAD_SIZE, 1), odd),
        )

    head_acc[...] = jnp.zeros_like(head_acc)

    def head_weights(b, nothing):
        bring(b).wait()
        block = token_buf[lax.rem(b, 2)]
        wide_block = block.astype(F32)
        scales = lax.rsqrt(jnp.mean(wide_block * wide_block, axis=1, keepdims=True) + EPS)
        j = lax.div(b, parts)
        have = jnp.where(lax.rem(b, parts) == part, 1.0, 0.0)
        heads = [dq_ref[j, r].astype(F32) * have for r in range(REP)] + [dkv_ref[b, 0], dkv_ref[b, 1]]
        heads.append(jnp.zeros((BLOCK, wide), F32))
        for m in range((REP + 3) // 2):
            for s, value in enumerate(side_by_side(heads[2 * m], heads[2 * m + 1])):
                at = slice(s * BLOCK, (s + 1) * BLOCK)
                field[at, m * wide : (m + 1) * wide] = (value * scales[at]).astype(BF16)
        head_acc[...] += lax.dot_general(
            block, field[...], (((0,), (0,)), ((), ())), preferred_element_type=F32
        )

        @pl.when(b + 2 < n_ctx)
        def _():
            bring(b + 2).start()

        return nothing

    lax.fori_loop(0, n_ctx, head_weights, 0)
    slab = D // (n_ctx * 4)
    for d in range(n_ctx * 4):
        head_out[d] = head_acc[d * slab : (d + 1) * slab, : head_out.shape[2]].astype(BF16)
    me = c * 4 + f
    head_stays = pltpu.make_async_copy(head_out.at[me], head_in.at[me], here.at[9])
    head_stays.start()
    to_all = []
    for number, (i, k) in enumerate(peers):
        peer_c, peer_f = flip(c, i), flip(f, k)
        to_all.append(
            pltpu.make_async_remote_copy(
                head_out.at[peer_c * 4 + peer_f], head_in.at[me],
                send_head.at[number], recv_head.at[number],
                device_id=(peer_c, peer_f), device_id_type=MESH,
            )
        )
        to_all[-1].start()

    down_second.wait_send()
    leaving.wait()
    gate_halving.wait_recv()
    refill = [
        pltpu.make_async_copy(grads.at[0, pl.ds(mine * half, half)], kept, here.at[3]),
        pltpu.make_async_copy(gate_first, came, here.at[10]),
    ]
    for copy in refill:
        copy.start()
    for copy in refill:
        copy.wait()
    gate_second, leaving = second_halving(gate_keep, gate_came, 3)

    def came_query(h, nothing):
        @pl.when(h != head)
        def _():
            pltpu.make_async_remote_copy(
                dq_ref.at[h], dq_back.at[h], send_q.at[h], recv_q.at[h],
                device_id=(h * parts + part, f), device_id_type=MESH,
            ).wait()

        @pl.when(h == head)
        def _():
            query_stays(h).wait()

        return nothing

    def came_key(b, nothing):
        @pl.when(b != c)
        def _():
            pltpu.make_async_remote_copy(
                dkv_ref.at[b], dkv_back.at[b], send_kv.at[b], recv_kv.at[b],
                device_id=(b, f), device_id_type=MESH,
            ).wait()

        @pl.when(b == c)
        def _():
            key_stays(b).wait()

        return nothing

    lax.fori_loop(0, KEY_VALUE_HEADS, came_query, 0)
    lax.fori_loop(0, n_ctx, came_key, 0)

    def head_of(h):
        if h < QUERY_HEADS:
            return dq_back[h // REP, h % REP]
        kind, h = (h - QUERY_HEADS) // KEY_VALUE_HEADS, (h - QUERY_HEADS) % KEY_VALUE_HEADS
        value = dkv_back[h * parts, kind]
        if parts > 1:
            value = value.astype(F32)
            for p in range(1, parts):
                value = value + dkv_back[h * parts + p, kind].astype(F32)
        return value

    for m in range((QUERY_HEADS + 2 * KEY_VALUE_HEADS) // 2):
        for s, value in enumerate(side_by_side(head_of(2 * m), head_of(2 * m + 1))):
            grad_qkv[s * BLOCK : (s + 1) * BLOCK, m * wide : (m + 1) * wide] = value.astype(BF16)
    for copy in loads[:3]:
        copy.wait()
    depth = D // 4
    for b in range(4):
        made, at = 0.0, 0
        for weight in (w_q, w_k, w_v):
            width = weight.shape[2]
            made = made + lax.dot_general(
                grad_qkv[:, at : at + width], weight[b], (((1,), (1,)), ((), ())),
                preferred_element_type=F32,
            )
            at += width
        grad_in[:, b * depth : (b + 1) * depth] = made
    x = tok[...].astype(F32)
    scale = lax.rsqrt(jnp.mean(x * x, axis=1, keepdims=True) + EPS)
    gain_grad[...] = jnp.sum(grad_in[...] * x * scale, axis=0, keepdims=True)
    weighted = grad_in[...] * gain[...]
    input_grad[...] = (
        resid_grad[...]
        + scale * weighted
        - x * (scale * scale * scale) * jnp.mean(weighted * x, axis=1, keepdims=True)
    ).astype(BF16)

    staying = pltpu.make_async_copy(residual, grad_in, here.at[8])
    staying.start()
    staying.wait()

    def share(i):
        return pltpu.make_async_copy(
            mix_in.at[i - 1] if i else mix.at[0], token_buf.at[i % 2], load_t.at[i % 2]
        )

    share(0).start()
    for i in range(RANKS):
        if i + 1 < RANKS:
            returns[i].wait_recv()
            share(i + 1).start()
        share(i).wait()
        grad_in[...] += token_buf[i % 2].astype(F32)
    layer_out[...] = grad_in[...].astype(BF16)

    output_stages[1].wait_recv()

    def over_x(i, nothing):
        r, p = lax.div(i, 2), lax.rem(i, 2)
        output_x[r, p] = plus(output_keep[r, p, x_bit], output_x[r, p])
        return nothing

    lax.fori_loop(0, planes * 2, over_x, 0)
    output_stages[2].start()
    output_stages[2].wait_recv()

    def over_pair(r, nothing):
        output_sum[r] = plus(output_x[r, pair], output_pair[r])
        return nothing

    lax.fori_loop(0, planes, over_pair, 0)
    for copy in to_heads:
        copy.wait_send()
    for copy in to_all + [gate_second, leaving, head_stays]:
        copy.wait()
    down_second.wait_recv()
    for copy in returns + output_stages + [gate_halving] + ([] if early else [down_halving]):
        copy.wait_send()


def attention_backward(
    cid, parts, n_ctx, early, g_own, q, kv, segq, codes, full, logs, cosine, sine,
    tok, gain, resid_grad, residual, grads, down_in, mix, output_part, tokens_all, q_full, k_full, v_full,
):
    wide = 2 * HEAD_SIZE
    anywhere = pl.BlockSpec(memory_space=pl.ANY)
    inside = pl.BlockSpec(memory_space=pltpu.VMEM)
    dma = pltpu.SemaphoreType.DMA
    others = max(n_ctx // parts - 1, 1)
    devices, planes = n_ctx * 4, n_ctx // 2
    slab, head_width = D // devices, (REP + 2) * HEAD_SIZE
    half = (grads.shape[1] // 2,) + grads.shape[2:]
    quarter = (grads.shape[1] // 4,) + grads.shape[2:]
    columns = q_full.shape[2] + k_full.shape[2] + v_full.shape[2]
    return pl.pallas_call(
        functools.partial(attention_backward_kernel, parts, n_ctx, early),
        name="attention_backward",
        out_shape=[
            jax.ShapeDtypeStruct(tok.shape, BF16),
            jax.ShapeDtypeStruct(tok.shape, BF16),
            jax.ShapeDtypeStruct((1, D), F32),
            jax.ShapeDtypeStruct((planes, slab, D), BF16),
            jax.ShapeDtypeStruct(half, BF16),
            jax.ShapeDtypeStruct(quarter, BF16),
            jax.ShapeDtypeStruct(quarter, BF16),
            jax.ShapeDtypeStruct(quarter, BF16),
            jax.ShapeDtypeStruct(quarter, BF16),
            jax.ShapeDtypeStruct((RANKS - 1,) + mix.shape[1:], BF16),
            jax.ShapeDtypeStruct((devices, slab, head_width), BF16),
        ],
        in_specs=[anywhere] + [inside] * 11 + [anywhere] * 9,
        out_specs=[inside] * 4 + [anywhere] * 7,
        scratch_shapes=[
            pltpu.VMEM(q.shape, BF16),
            pltpu.VMEM((n_ctx, 2, BLOCK, wide), F32),
            pltpu.VMEM(half, BF16),
            pltpu.VMEM(half, BF16),
            pltpu.VMEM(q.shape, BF16),
            pltpu.VMEM(kv.shape, BF16),
            pltpu.VMEM(q.shape, BF16),
            pltpu.VMEM(kv.shape, BF16),
            pltpu.VMEM(q_full.shape, BF16),
            pltpu.VMEM(k_full.shape, BF16),
            pltpu.VMEM(v_full.shape, BF16),
            pltpu.VMEM((SEQS * BLOCK, columns), BF16),
            pltpu.VMEM((SEQS * BLOCK, D), F32),
            pltpu.VMEM((2, SEQS * BLOCK, D), BF16),
            pltpu.VMEM((SEQS * BLOCK, 3 * wide), BF16),
            pltpu.VMEM((D, 3 * wide), F32),
            pltpu.VMEM((devices, slab, head_width), BF16),
            pltpu.VMEM((planes, 2, 2, slab, D), BF16),
            pltpu.VMEM((planes, 2, 2, slab, D), BF16),
            pltpu.VMEM((planes, 2, slab, D), BF16),
            pltpu.VMEM((planes, slab, D), BF16),
            dma((others,)), dma((others,)), dma((KEY_VALUE_HEADS,)), dma((KEY_VALUE_HEADS,)),
            dma((n_ctx,)), dma((n_ctx,)), dma((RANKS - 1,)), dma((RANKS - 1,)), dma((4,)), dma((4,)),
            dma((11,)), dma((3,)), dma((3,)), dma((devices - 1,)), dma((devices - 1,)), dma((2,)),
        ],
        compiler_params=pltpu.CompilerParams(
            collective_id=cid, has_side_effects=True, vmem_limit_bytes=60 << 20
        ),
        cost_estimate=lasting(125),
    )(
        g_own, q, kv, segq, codes, full, logs, cosine, sine, tok, gain, resid_grad, residual,
        grads, down_in, mix, output_part, tokens_all, q_full, k_full, v_full,
    )


def final_kernel(
    n_ctx, small, output_part, grads, gate_keep, gate_came, down_keep, down_came,
    swapped, output_grad, small_sum,
    halves, landed, rest, rest_landed, last, last_landed, turned, output_in, small_in,
    send_half, recv_half, send_deep, recv_deep, send_out, recv_out, send_small, recv_small,
    send_swap, recv_swap, load, stay,
):
    c, f = lax.axis_index("ctx"), lax.axis_index("fsdp")
    me, plane, rank = c * 4 + f, lax.div(c, 2), lax.rem(c, 2) * 4 + f
    planes = n_ctx // 2
    half, quarter = planes // 2, planes // 4
    barrier = pltpu.get_barrier_semaphore()
    peers = [(i, k) for i in range(n_ctx) for k in range(4) if i or k]
    for dc, df in peers:
        pl.semaphore_signal(
            barrier, inc=1, device_id=(flip(c, dc), flip(f, df)), device_id_type=MESH
        )
    first, second = lax.rem(plane, 2), lax.rem(lax.div(plane, 2), 2)
    loads = [
        pltpu.make_async_copy(source, target, load.at[i])
        for i, (source, target) in enumerate(
            (
                (down_keep, rest.at[2]),
                (down_came, rest_landed.at[2]),
                (gate_keep, rest.at[0]),
                (gate_came, rest_landed.at[0]),
                (grads.at[1, pl.ds(first * half, half)], halves),
                (output_part.at[plane], output_in.at[plane]),
                (small.at[me], small_in.at[me]),
            )
        )
    ]
    for copy in loads:
        copy.start()
    pl.semaphore_wait(barrier, len(peers))

    def over(source, target, sent, came, bit):
        return pltpu.make_async_remote_copy(
            source, target, sent, came, device_id=(flip(c, 2 * bit), f), device_id_type=MESH
        )

    up_first = [
        over(
            grads.at[1, pl.ds((1 - first) * half, half), e], landed.at[:, e],
            send_half.at[0, e], recv_half.at[0, e], 1,
        )
        for e in range(OWN)
    ]
    for copy in up_first:
        copy.start()
    outputs = []
    for i in range(1, planes):
        outputs.append(
            pltpu.make_async_remote_copy(
                output_part.at[flip(plane, i)], output_in.at[plane], send_out.at[i - 1], recv_out.at[i - 1],
                device_id=(flip(c, 2 * i), f), device_id_type=MESH,
            )
        )
    smalls = []
    for number, (i, k) in enumerate(peers):
        peer_c, peer_f = flip(c, i), flip(f, k)
        smalls.append(
            pltpu.make_async_remote_copy(
                small.at[peer_c * 4 + peer_f], small_in.at[me], send_small.at[number], recv_small.at[number],
                device_id=(peer_c, peer_f), device_id_type=MESH,
            )
        )
    for copy in outputs + smalls:
        copy.start()

    def plus(mine, came):
        return (mine.astype(F32) + came.astype(F32)).astype(BF16)

    swaps, sent = [], []

    def finish(m, e):
        count, bit, number = quarter, 4, 0
        for at in range(quarter):
            rest[m, at, e] = plus(rest[m, at, e], rest_landed[m, at, e])
        mine = rest.at[m, :, e]
        while count > 1:
            count //= 2
            chosen = lax.rem(lax.div(plane, bit), 2)
            came = last_landed.at[m, number, pl.ds(0, count), e]
            copy = over(
                mine.at[pl.ds((1 - chosen) * count, count)], came,
                send_deep.at[2 * m + number, e], recv_deep.at[2 * m + number, e], bit,
            )
            copy.start()
            copy.wait_recv()
            sent.append(copy)
            for at in range(count):
                last[m, number, at, e] = plus(mine[chosen * count + at], came[at])
            mine, bit, number = last.at[m, number, :, e], bit * 2, number + 1
        rows = turned.shape[3]
        across = mine[0].astype(F32).T
        for r in range(RANKS):
            turned[m, r, e] = across[r * rows : (r + 1) * rows].astype(BF16)
        for i in range(RANKS):
            source, target = turned.at[m, flip(rank, i), e], swapped.at[rank, m, e]
            if i:
                copy = pltpu.make_async_remote_copy(
                    source, target, send_swap.at[m * OWN + e, i], recv_swap.at[m * OWN + e, i],
                    device_id=(flip(c, i // 4), flip(f, i % 4)), device_id_type=MESH,
                )
            else:
                copy = pltpu.make_async_copy(source, target, stay.at[m * OWN + e])
            copy.start()
            swaps.append(copy)

    for copy in loads:
        copy.wait()
    for e in range(OWN):
        finish(2, e)
    up_second = []
    for e in range(OWN):
        up_first[e].wait_recv()
        for at in range(half):
            halves[at, e] = plus(halves[at, e], landed[at, e])
        up_second.append(
            over(
                halves.at[pl.ds((1 - second) * quarter, quarter), e], rest_landed.at[1, :, e],
                send_half.at[1, e], recv_half.at[1, e], 2,
            )
        )
        up_second[e].start()
        for at in range(quarter):
            rest[1, at, e] = halves[second * quarter + at, e]
        finish(0, e)
    for copy in outputs + smalls:
        copy.wait_recv()
    made = output_in[0].astype(F32)
    for i in range(1, planes):
        made = made + output_in[i].astype(F32)
    output_grad[...] = made
    small_sum[...] = jnp.sum(small_in[...], axis=0)
    for e in range(OWN):
        up_second[e].wait_recv()
        finish(1, e)
    for copy in swaps:
        copy.wait()
    for copy in smalls + outputs + sent + up_first + up_second:
        copy.wait_send()


def final_sums(cid, n_ctx, small, output_part, grads, gate_keep, gate_came, down_keep, down_came):
    anywhere = pl.BlockSpec(memory_space=pl.ANY)
    inside = pl.BlockSpec(memory_space=pltpu.VMEM)
    dma = pltpu.SemaphoreType.DMA
    devices, planes = n_ctx * 4, n_ctx // 2
    slab, piece = D // devices, grads.shape[2:]
    half, quarter = (planes // 2,) + piece, (planes // 4,) + piece
    deep = (3, 2, max(planes // 8, 1)) + piece
    return pl.pallas_call(
        functools.partial(final_kernel, n_ctx),
        name="final_sums",
        out_shape=[
            jax.ShapeDtypeStruct((RANKS, 3, OWN, slab, FF), BF16),
            jax.ShapeDtypeStruct((slab, D), F32),
            jax.ShapeDtypeStruct(small.shape[1:], F32),
        ],
        in_specs=[anywhere] * 7,
        out_specs=[anywhere] + [inside] * 2,
        scratch_shapes=[
            pltpu.VMEM(half, BF16),
            pltpu.VMEM(half, BF16),
            pltpu.VMEM((3,) + quarter, BF16),
            pltpu.VMEM((3,) + quarter, BF16),
            pltpu.VMEM(deep if planes > 4 else (1, 1, 1, 1, 8, 128), BF16),
            pltpu.VMEM(deep if planes > 4 else (1, 1, 1, 1, 8, 128), BF16),
            pltpu.VMEM((3, RANKS, OWN, slab, FF), BF16),
            pltpu.VMEM((planes, slab, D), BF16),
            pltpu.VMEM(small.shape, F32),
            dma((2, OWN)), dma((2, OWN)), dma((6, OWN)), dma((6, OWN)),
            dma((planes - 1,)), dma((planes - 1,)), dma((devices - 1,)), dma((devices - 1,)),
            dma((3 * OWN, RANKS)), dma((3 * OWN, RANKS)), dma((7,)), dma((3 * OWN,)),
        ],
        compiler_params=pltpu.CompilerParams(
            collective_id=cid, has_side_effects=True, vmem_limit_bytes=56 << 20
        ),
        cost_estimate=lasting(80),
    )(small, output_part, grads, gate_keep, gate_came, down_keep, down_came)


def rope_tables(positions):
    half_dim = HEAD_SIZE // 2
    frequency = ROPE_BASE ** (-jnp.arange(half_dim, dtype=F32) * 2.0 / HEAD_SIZE)
    angle = positions.astype(F32)[:, None] * frequency[None, :]
    angle = jnp.concatenate([angle, angle], axis=1)
    return (jnp.cos(angle), jnp.sin(angle))


def heads_out(field, per):
    field = field.reshape(SEQS, BLOCK, KEY_VALUE_HEADS, per, HEAD_SIZE)
    return field.transpose(2, 3, 1, 0, 4).reshape(KEY_VALUE_HEADS, per, BLOCK, SEQS * HEAD_SIZE)


def heads_in(field):
    per = field.shape[1]
    field = field.reshape(KEY_VALUE_HEADS, per, BLOCK, SEQS, HEAD_SIZE)
    return field.transpose(3, 2, 0, 1, 4).reshape(SEQS, BLOCK, KEY_VALUE_HEADS * per * HEAD_SIZE)


def on_device(
    n_ctx,
    n_fsdp,
    tokens,
    segments,
    valid,
    expert_ids,
    slot_order,
    cotangent,
    norm1_gain,
    w_query,
    key_weight,
    value_weight,
    w_output,
    norm2_gain,
    w_router,
    w_gate,
    w_up,
    w_down,
):
    parts = n_ctx // KEY_VALUE_HEADS
    replicas = n_ctx // 2
    full_len = segments.shape[1]
    c_index, f_index = lax.axis_index("ctx"), lax.axis_index("fsdp")
    pair = lax.rem(c_index, 2)
    rank = pair * n_fsdp + f_index
    part = lax.rem(c_index, parts)
    head = lax.div(c_index, parts)
    positions = c_index * BLOCK + jnp.arange(BLOCK, dtype=jnp.int32)

    tokens_all = lax.all_gather(tokens, "ctx", axis=0, tiled=False)
    small = jnp.concatenate(
        [
            norm1_gain[None],
            norm2_gain[None],
            w_router.T,
            jnp.zeros((SMALL - EXPERTS - 2, D // n_fsdp), BF16),
        ],
        axis=0,
    )
    packs = [
        lax.dynamic_slice_in_dim(w, pair * (EXPERTS // 2), EXPERTS // 2, 1)
        .reshape(D // n_fsdp, n_fsdp, OWN, FF)
        .transpose(1, 2, 0, 3)
        for w in (w_gate, w_up, w_down)
    ]
    inputs_f = tokens.astype(F32)
    scale_one = lax.rsqrt(jnp.mean(inputs_f * inputs_f, axis=-1, keepdims=True) + EPS)
    segq = segments.reshape(SEQS, KEY_VALUE_HEADS, parts, BLOCK)
    segq = lax.dynamic_index_in_dim(segq, part, 2, keepdims=False).transpose(1, 0, 2)[..., None]
    codes = jnp.where(valid > 0, segments, -1)
    codes = codes.reshape(SEQS, full_len // KEYS, KEYS).transpose(1, 0, 2)
    all_cosine, all_sine = rope_tables(jnp.arange(full_len, dtype=jnp.int32))
    all_cosine = jnp.tile(all_cosine, (1, 2)).reshape(n_ctx, BLOCK, 2 * HEAD_SIZE)
    all_sine = jnp.tile(all_sine, (1, 2)).reshape(n_ctx, BLOCK, 2 * HEAD_SIZE)
    (
        normed_in, small_all, full_query, full_key, full_value, q_all, kv_all, head_full, head_logs,
        attn_heads, full_output, own_gate, own_up, own_down,
    ) = attention_forward(
        0, parts, n_ctx, tokens.reshape(SEQS * BLOCK, D), small, w_query, key_weight, value_weight,
        w_output, packs,
        lax.dynamic_index_in_dim(all_cosine, c_index, 0, keepdims=False),
        lax.dynamic_index_in_dim(all_sine, c_index, 0, keepdims=False),
        segq, codes,
    )
    gain_first = small_all[:, 0].reshape(D).astype(F32)
    gain_second = small_all[:, 1].reshape(D).astype(F32)
    full_router = small_all[:, 2 : 2 + EXPERTS].transpose(1, 0, 2).reshape(EXPERTS, D)
    full_output = full_output.reshape(D, D)
    attn_out = heads_in(attn_heads)
    attn_proj = jnp.einsum("sgq,dq->sgd", attn_out, full_output, preferred_element_type=F32)
    residual = inputs_f + attn_proj
    scale_two = lax.rsqrt(jnp.mean(residual * residual, axis=-1, keepdims=True) + EPS)
    normed_mid = (residual * scale_two * gain_second).astype(BF16)

    logits = jnp.einsum("sgd,ed->sge", normed_mid, full_router, preferred_element_type=F32)
    picked = jnp.any(expert_ids[..., None] == jnp.arange(EXPERTS, dtype=jnp.int32), axis=2)
    before = (slot_order[:, None, :] < slot_order[:, :, None]).astype(BF16)
    place = jnp.matmul(before, picked.astype(BF16), preferred_element_type=F32)
    is_kept = picked & (place < CAP)
    chosen = jnp.where(picked, logits, MASKED)
    raised = jnp.where(picked, jnp.exp(chosen - jnp.max(chosen, axis=-1, keepdims=True)), 0.0)
    gates = raised / jnp.sum(raised, axis=-1, keepdims=True)
    payload = jnp.concatenate(
        [
            normed_mid,
            jnp.where(is_kept, place, -1.0).astype(BF16),
            gates.astype(BF16),
            jnp.zeros((SEQS, BLOCK, 128 - 2 * EXPERTS), BF16),
        ],
        axis=2,
    )
    back, mix_part, own_grads, down_first, down_early = run_experts(
        2, replicas, payload.reshape(SEQS * BLOCK, PAY), cotangent.reshape(SEQS * BLOCK, D),
        (own_gate, own_up, own_down), tokens_all
    )

    back = back.reshape(SEQS, BLOCK, D + 128)
    grad_gates = jnp.where(is_kept, back[..., D : D + EXPERTS], 0.0)
    grad_chosen = gates * (grad_gates - jnp.sum(gates * grad_gates, axis=-1, keepdims=True))
    grad_logits = grad_chosen.astype(BF16)
    grad_mid = back[..., :D] + jnp.einsum(
        "sge,ed->sgd", grad_logits, full_router, preferred_element_type=F32
    )
    grad_router = jnp.einsum("sgd,sge->de", normed_mid, grad_logits, preferred_element_type=F32)

    grad_f = cotangent.astype(F32)
    weighted_two = gain_second * grad_mid
    grad_gain_second = jnp.sum(grad_mid * residual * scale_two, axis=(0, 1))
    cube_two = scale_two * scale_two * scale_two
    grad_resid = (
        grad_f
        + scale_two * weighted_two
        - residual * cube_two * jnp.mean(weighted_two * residual, axis=-1, keepdims=True)
    )
    grad_resid_low = grad_resid.astype(BF16)
    grad_attn = jnp.einsum("sgd,dq->sgq", grad_resid_low, full_output, preferred_element_type=F32)
    grad_attn = grad_attn.astype(BF16)
    grad_output_w = jnp.einsum("sgd,sgq->dq", grad_resid_low, attn_out, preferred_element_type=F32)
    rows = D // (n_ctx * n_fsdp)
    output_part = grad_output_w.astype(BF16).reshape(replicas, 2, 2, 2, rows, D)

    (
        input_grad, layer_out, gain_grad, output_sum, _, gate_keep, gate_came, down_keep, down_came, _,
        head_grads,
    ) = attention_backward(
        6, parts, n_ctx, down_early, heads_out(grad_attn, REP), q_all, kv_all, segq, codes, head_full, head_logs,
        all_cosine, all_sine, tokens.reshape(SEQS * BLOCK, D), gain_first[None],
        grad_resid.reshape(SEQS * BLOCK, D), residual.reshape(SEQS * BLOCK, D), own_grads, down_first, mix_part, output_part,
        tokens_all.reshape(n_ctx, SEQS * BLOCK, D), full_query, full_key, full_value,
    )
    input_grad = input_grad.reshape(SEQS, BLOCK, D)
    layer_out = layer_out.reshape(SEQS, BLOCK, D)
    amount = rows * (EXPERTS + 2)
    tiles = -(-amount // 1024) * 8
    small_grads = jnp.concatenate([grad_router, gain_grad.T, grad_gain_second[:, None]], axis=1)
    small_grads = jnp.pad(
        small_grads.reshape(n_ctx * n_fsdp, amount), ((0, 0), (0, tiles * 128 - amount))
    ).reshape(n_ctx * n_fsdp, tiles, 128)
    swapped, output_grad, small_sum = final_sums(
        9, n_ctx, small_grads, output_sum, own_grads, gate_keep, gate_came, down_keep, down_came
    )
    small_sum = small_sum.reshape(tiles * 128)[:amount].reshape(rows, EXPERTS + 2)
    head_grads = head_grads.reshape(KEY_VALUE_HEADS, parts * n_fsdp, rows, (REP + 2) * HEAD_SIZE)
    own_gain = lax.dynamic_slice_in_dim(gain_first, (c_index * n_fsdp + f_index) * rows, rows, 0)
    head_grads = jnp.sum(head_grads.astype(F32), axis=1).transpose(1, 0, 2) * own_gain[:, None, None]
    query_grad = head_grads[..., : REP * HEAD_SIZE].reshape(rows, D)
    key_grad = head_grads[..., REP * HEAD_SIZE : (REP + 1) * HEAD_SIZE].reshape(rows, -1)
    value_grad = head_grads[..., (REP + 1) * HEAD_SIZE :].reshape(rows, -1)

    def by_row(matrix):
        return swapped[:, matrix].transpose(2, 0, 1, 3).reshape(rows, EXPERTS, FF).astype(F32)

    return (
        layer_out,
        input_grad,
        small_sum[:, EXPERTS],
        query_grad,
        key_grad,
        value_grad,
        output_grad,
        small_sum[:, EXPERTS + 1],
        small_sum[:, :EXPERTS],
        by_row(0),
        by_row(1),
        by_row(2),
    )


def solution(mesh):
    placed = (
        P("fsdp", "ctx", None),
        P("fsdp", None),
        P("fsdp", None),
        P("fsdp", "ctx", None),
        P("fsdp", "ctx"),
        P("fsdp", "ctx", None),
        P("fsdp"),
        P("fsdp", None),
        P("fsdp", None),
        P("fsdp", None),
        P("fsdp", None),
        P("fsdp"),
        P("fsdp", None),
        P("fsdp", None, None),
        P("fsdp", None, None),
        P("fsdp", None, None),
    )
    return jax.shard_map(
        functools.partial(on_device, mesh.shape["ctx"], mesh.shape["fsdp"]),
        mesh=mesh,
        in_specs=placed,
        out_specs=(
            P("fsdp", "ctx", None),
            P("fsdp", "ctx", None),
            P(("ctx", "fsdp")),
            P(("ctx", "fsdp"), None),
            P(("ctx", "fsdp"), None),
            P(("ctx", "fsdp"), None),
            P(("ctx", "fsdp"), None),
            P(("ctx", "fsdp")),
            P(("ctx", "fsdp"), None),
            P(("ctx", "fsdp"), None, None),
            P(("ctx", "fsdp"), None, None),
            P(("ctx", "fsdp"), None, None),
        ),
        check_vma=False,
    )
```

```python
import functools

import jax
import jax.numpy as jnp
from jax import lax
from jax.experimental import pallas as pl
from jax.experimental.pallas import tpu as pltpu
from jax.sharding import PartitionSpec as P

D = 1536
QUERY_HEADS = 24
KEY_VALUE_HEADS = 8
REP = QUERY_HEADS // KEY_VALUE_HEADS
HEAD_SIZE = 64
FF = 512
EXPERTS = 16
CAP = 80
RANKS = 8
OWN = EXPERTS // RANKS
SEQS = 2
BLOCK = 128
KEYS = 256

EPS = 1e-05
ROPE_BASE = 10000.0
MASKED = -1e30
SCALE = HEAD_SIZE ** (-0.5)
MESH = pl.DeviceIdType.MESH
BF16 = jnp.bfloat16
F32 = jnp.float32


def flip(index, constant):
    result, bit = index, 1
    while bit <= constant:
        if constant & bit:
            result = result + bit - 2 * bit * lax.rem(lax.div(index, bit), 2)
        bit *= 2
    return result


def lasting(microseconds):
    return pl.CostEstimate(flops=0, bytes_accessed=int(microseconds * 3.3e6), transcendentals=0)


PAY = D + 128
GROUPS = 4
ROWS = GROUPS * CAP


def other_chip(c, f, k):
    pair, x = lax.div(k, 2), lax.rem(k, 2)
    return (
        c + pair * (1 - 2 * lax.rem(c, 2)),
        f + 2 * x * (1 - 2 * lax.rem(lax.div(f, 2), 2)),
    )


def plane_order(replicas):
    order = [0]
    while len(order) < replicas:
        order = [2 * i for i in order] + [2 * i + 1 for i in order]
    return order


def experts_kernel(
    replicas, pay, cot, gate_own, up_own, down_own, after,
    back, mix, grads, down_came, pay_in, cot_in,
    weights, total, pay_now, cot_now, xs, gs, eo, gi, hid, dgate, dup, disp, comb,
    own, out, sib, ret, mix_now,
    send_first, recv_first, send_fwd, recv_fwd, send_sib, recv_sib, send_chip, recv_chip,
    load_w, load, store, piece_sem, send_down, recv_down,
):
    c, f = lax.axis_index("ctx"), lax.axis_index("fsdp")
    rank = lax.rem(c, 2) * 4 + f
    sibling = (c, flip(f, 1))
    barrier = pltpu.get_barrier_semaphore()
    pl.semaphore_signal(barrier, inc=1, device_id=sibling, device_id_type=MESH)
    for k in range(1, 4):
        pl.semaphore_signal(barrier, inc=1, device_id=other_chip(c, f, k), device_id_type=MESH)
    apart = len(grads.shape) == 5
    if apart:
        pl.semaphore_signal(barrier, inc=1, device_id=(flip(c, 2), f), device_id_type=MESH)
    bring = []
    for m, own_weight in enumerate((gate_own, up_own, down_own)):
        bring.append(pltpu.make_async_copy(own_weight, weights.at[m], load_w.at[m]))
        bring[-1].start()
    pl.semaphore_wait(barrier, 5 if apart else 4)
    sources, landed = (pay, cot), (pay_in, cot_in)

    def push(k, a):
        slot = 1 if k == 0 else 2 * k
        return pltpu.make_async_remote_copy(
            sources[a], landed[a].at[slot - 1], send_first.at[k, a], recv_first.at[k, a],
            device_id=sibling if k == 0 else other_chip(c, f, k), device_id_type=MESH,
        )

    def forward(k, a):
        return pltpu.make_async_remote_copy(
            landed[a].at[2 * k - 1], landed[a].at[2 * k], send_fwd.at[k - 1, a], recv_fwd.at[k - 1, a],
            device_id=sibling, device_id_type=MESH,
        )

    def to_sibling(k):
        return pltpu.make_async_remote_copy(
            out.at[lax.rem(k, 2)], sib.at[k], send_sib.at[k], recv_sib.at[k],
            device_id=sibling, device_id_type=MESH,
        )

    def to_chip(k):
        return pltpu.make_async_remote_copy(
            sib.at[k], ret.at[k - 1], send_chip.at[k - 1], recv_chip.at[k - 1],
            device_id=other_chip(c, f, k), device_id_type=MESH,
        )

    def store_mix(k, s):
        return pltpu.make_async_copy(mix_now.at[s], mix.at[2 * k + s], store.at[s])

    for k, a in ((0, 0), (0, 1), (1, 0), (2, 0), (1, 1), (2, 1), (3, 0), (3, 1)):
        push(k, a).start()

    def clear(i, carry):
        total[lax.div(i, OWN), lax.rem(i, OWN)] = jnp.zeros((FF, D), F32)
        return carry

    lax.fori_loop(0, 3 * OWN, clear, 0)
    lane = lax.broadcasted_iota(jnp.int32, (BLOCK, 128), 1)
    wide = lax.broadcasted_iota(jnp.int32, (BLOCK, 2 * BLOCK), 1).astype(F32)
    both = lax.broadcasted_iota(jnp.int32, (BLOCK, OWN * CAP), 1)

    def chunk(k, carry):
        now = (pay_now, cot_now)

        def fetch(a, s, source):
            copy = pltpu.make_async_copy(source, now[a].at[s], load.at[a, s])
            copy.start()
            return copy

        @pl.when(k == 0)
        def _():
            copies = [fetch(a, 0, sources[a]) for a in range(2)]
            for a in range(2):
                push(0, a).wait_recv()
            copies += [fetch(a, 1, landed[a].at[0]) for a in range(2)]
            for copy in copies:
                copy.wait()
            for copy in bring:
                copy.wait()

        @pl.when(k > 0)
        def _():
            for a in range(2):
                pltpu.make_async_remote_copy(
                    sources[a], landed[a].at[2 * k - 1], send_first.at[k, a], recv_first.at[k, a],
                    device_id=other_chip(c, f, k), device_id_type=MESH,
                ).wait_recv()
                forward(k, a).start()
            copies = [fetch(a, 0, landed[a].at[2 * k - 1]) for a in range(2)]
            for a in range(2):
                forward(k, a).wait_recv()
            copies += [fetch(a, 1, landed[a].at[2 * k]) for a in range(2)]
            for copy in copies:
                copy.wait()

        for g in range(GROUPS):
            s, at = g // 2, (g % 2) * BLOCK
            tail = pay_now[s, at : at + BLOCK, D:].astype(F32)

            def column(index):
                return jnp.sum(jnp.where(lane == index, tail, 0.0), axis=1, keepdims=True)

            table = jnp.zeros((BLOCK, 2 * BLOCK), F32)
            gated = jnp.zeros((BLOCK, 2 * BLOCK), F32)
            for e in range(OWN):
                place = column(rank * OWN + e)
                place = jnp.where(place < 0.0, -1000.0, place + e * CAP)
                here = wide == place
                table = jnp.where(here, 1.0, table)
                gated = jnp.where(here, column(EXPERTS + rank * OWN + e), gated)
            table, gated = table.astype(BF16), gated.astype(BF16)
            disp[g] = table
            comb[g] = gated
            for weight, source, keep in (
                (table, pay_now[s, at : at + BLOCK, :D], xs),
                (gated, cot_now[s, at : at + BLOCK], gs),
            ):
                moved = lax.dot_general(
                    weight, source, (((0,), (0,)), ((), ())), preferred_element_type=F32
                ).astype(BF16)
                for e in range(OWN):
                    keep[e, g * CAP : (g + 1) * CAP] = moved[e * CAP : (e + 1) * CAP]

        def expert(e, carry):
            at = pl.multiple_of(e * CAP, 16)
            gate_pre = jnp.dot(xs[e], weights[0, e], preferred_element_type=F32)
            up_pre = jnp.dot(xs[e], weights[1, e], preferred_element_type=F32)
            sigmoid = 1.0 / (1.0 + jnp.exp(-gate_pre))
            activated = gate_pre * sigmoid
            hidden = (activated * up_pre).astype(BF16)
            hid[e] = hidden
            made = lax.dot_general(
                hidden, weights[2, e], (((1,), (1,)), ((), ())), preferred_element_type=F32
            ).astype(BF16)
            for g in range(GROUPS):
                eo[pl.ds(pl.multiple_of(g * OWN * CAP + at, 16), CAP)] = made[g * CAP : (g + 1) * CAP]
            grad_hidden = jnp.dot(gs[e], weights[2, e], preferred_element_type=F32)
            slope = sigmoid * (1.0 + gate_pre * (1.0 - sigmoid))
            grad_gate = (grad_hidden * up_pre * slope).astype(BF16)
            grad_up = (grad_hidden * activated).astype(BF16)
            dgate[e] = grad_gate
            dup[e] = grad_up
            made = lax.dot_general(
                grad_gate, weights[0, e], (((1,), (1,)), ((), ())), preferred_element_type=F32
            )
            made = made + lax.dot_general(
                grad_up, weights[1, e], (((1,), (1,)), ((), ())), preferred_element_type=F32
            )
            made = made.astype(BF16)
            for g in range(GROUPS):
                gi[pl.ds(pl.multiple_of(g * OWN * CAP + at, 16), CAP)] = made[g * CAP : (g + 1) * CAP]
            return carry

        lax.fori_loop(0, OWN, expert, 0)

        @pl.when(k > 0)
        def _():
            for s in range(2):
                store_mix(k - 1, s).wait()

        @pl.when(k > 1)
        def _():
            to_sibling(k - 2).wait_send()

        parity = lax.rem(k, 2)
        for g in range(GROUPS):
            s, at = g // 2, (g % 2) * BLOCK
            slots = pl.ds(g * OWN * CAP, OWN * CAP)
            made = eo[slots]
            mix_now[s, at : at + BLOCK] = jnp.dot(
                comb[g][:, : OWN * CAP], made, preferred_element_type=F32
            ).astype(BF16)
            table = disp[g][:, : OWN * CAP]
            grad_mid = jnp.dot(table, gi[slots], preferred_element_type=F32).astype(BF16)
            met = lax.dot_general(
                cot_now[s, at : at + BLOCK], made, (((1,), (1,)), ((), ())), preferred_element_type=F32
            ) * table.astype(F32)
            values = jnp.zeros((BLOCK, 128), F32)
            for e in range(OWN):
                inside = (both >= e * CAP) & (both < (e + 1) * CAP)
                value = jnp.sum(jnp.where(inside, met, 0.0), axis=1, keepdims=True)
                values = jnp.where(lane == rank * OWN + e, value, values)
            target = own if s == 0 else out
            target[parity, at : at + BLOCK, :D] = grad_mid
            target[parity, at : at + BLOCK, D:] = values.astype(BF16)
        to_sibling(k).start()
        for s in range(2):
            store_mix(k, s).start()

        def weight_grads(e, carry):
            for m, (left, right) in enumerate(((dgate, xs), (dup, xs), (hid, gs))):
                total[m, e] += lax.dot_general(
                    left[e], right[e], (((0,), (0,)), ((), ())), preferred_element_type=F32
                )
            return carry

        lax.fori_loop(0, OWN, weight_grads, 0)
        to_sibling(k).wait_recv()
        sib[k] = (sib[k].astype(F32) + own[parity].astype(F32)).astype(BF16)

        @pl.when(k > 0)
        def _():
            to_chip(k).start()

        return carry

    lax.fori_loop(0, 4, chunk, 0)
    for s in range(2):
        store_mix(3, s).wait()
    stages = (eo, gi)
    pending = []
    if apart:
        half = replicas // 2
        down_first = pltpu.make_async_remote_copy(
            grads.at[2, pl.ds((1 - lax.rem(lax.div(c, 2), 2)) * half, half)], down_came,
            send_down, recv_down, device_id=(flip(c, 2), f), device_id_type=MESH,
        )
    for i in range(3 * OWN):
        m, e = (2, 0, 1)[i // OWN], i % OWN
        if i >= 2:
            for copy in pending[i - 2]:
                copy.wait()
        if i == OWN + 1 and apart:
            down_first.start()
        stages[i % 2][:FF] = total[m, e].astype(BF16)
        pending.append([])
        if not apart:
            pending[i].append(
                pltpu.make_async_copy(stages[i % 2].at[:FF], grads.at[m, e], piece_sem.at[i % 2, 0])
            )
        else:
            width = D // replicas
            for at, plane in enumerate(plane_order(replicas)):
                pending[i].append(
                    pltpu.make_async_copy(
                        stages[i % 2].at[:FF, plane * width : (plane + 1) * width],
                        grads.at[m, at, e],
                        piece_sem.at[i % 2, at],
                    )
                )
        for copy in pending[i]:
            copy.start()
    for copy in pending[-2] + pending[-1]:
        copy.wait()
    for k in (2, 3):
        to_sibling(k).wait_send()
    for k in range(4):
        for a in range(2):
            push(k, a).wait_send()
            if k:
                forward(k, a).wait_send()
    for k in range(1, 4):
        to_chip(k).wait_recv()
    back[...] = (sib[0].astype(F32) + ret[0].astype(F32)) + (ret[1].astype(F32) + ret[2].astype(F32))
    for k in range(1, 4):
        to_chip(k).wait_send()
    if apart:
        down_first.wait()


def run_experts(cid, replicas, pay, cot, owns, after):
    width = D // replicas
    apart = width % 128 == 0
    tokens = SEQS * BLOCK
    anywhere = pl.BlockSpec(memory_space=pl.ANY)
    inside = pl.BlockSpec(memory_space=pltpu.VMEM)
    dma = pltpu.SemaphoreType.DMA
    back, mix, grads, down_came, _, _ = pl.pallas_call(
        functools.partial(experts_kernel, replicas),
        name="experts",
        out_shape=[
            jax.ShapeDtypeStruct((tokens, PAY), F32),
            jax.ShapeDtypeStruct((RANKS, tokens, D), BF16),
            jax.ShapeDtypeStruct((3, replicas, OWN, FF, width) if apart else (3, OWN, FF, D), BF16),
            jax.ShapeDtypeStruct((replicas // 2, OWN, FF, width) if apart else (8, 128), BF16),
            jax.ShapeDtypeStruct((RANKS - 1, tokens, PAY), BF16),
            jax.ShapeDtypeStruct((RANKS - 1, tokens, D), BF16),
        ],
        in_specs=[anywhere] * 6,
        out_specs=[inside] + [anywhere] * 5,
        scratch_shapes=[
            pltpu.VMEM((3, OWN, D, FF), BF16),
            pltpu.VMEM((3, OWN, FF, D), F32),
            pltpu.VMEM((2, tokens, PAY), BF16),
            pltpu.VMEM((2, tokens, D), BF16),
            pltpu.VMEM((OWN, ROWS, D), BF16),
            pltpu.VMEM((OWN, ROWS, D), BF16),
            pltpu.VMEM((OWN * ROWS, D), BF16),
            pltpu.VMEM((OWN * ROWS, D), BF16),
            pltpu.VMEM((OWN, ROWS, FF), BF16),
            pltpu.VMEM((OWN, ROWS, FF), BF16),
            pltpu.VMEM((OWN, ROWS, FF), BF16),
            pltpu.VMEM((GROUPS, BLOCK, 2 * BLOCK), BF16),
            pltpu.VMEM((GROUPS, BLOCK, 2 * BLOCK), BF16),
            pltpu.VMEM((2, tokens, PAY), BF16),
            pltpu.VMEM((2, tokens, PAY), BF16),
            pltpu.VMEM((4, tokens, PAY), BF16),
            pltpu.VMEM((3, tokens, PAY), BF16),
            pltpu.VMEM((2, tokens, D), BF16),
            dma((4, 2)), dma((4, 2)), dma((3, 2)), dma((3, 2)),
            dma((4,)), dma((4,)), dma((3,)), dma((3,)),
            dma((4,)), dma((2, 2)), dma((2,)), dma((2, replicas)), dma, dma,
        ],
        compiler_params=pltpu.CompilerParams(
            collective_id=cid, has_side_effects=True, vmem_limit_bytes=63 << 20
        ),
        cost_estimate=lasting(110),
    )(pay, cot, *owns, after)
    if not apart:
        grads = grads.reshape(3, OWN, FF, replicas, width).transpose(0, 3, 1, 2, 4)
        grads = grads[:, jnp.array(plane_order(replicas))]
    return back, mix, grads, down_came, apart


def half_masks(dtype):
    lane = lax.broadcasted_iota(jnp.int32, (1, 2 * HEAD_SIZE), 1)
    low = (lane < HEAD_SIZE).astype(F32)
    return low.astype(dtype), (1.0 - low).astype(dtype)


def allowed_at(block, step, segq, keycode):
    token = block * BLOCK + lax.broadcasted_iota(jnp.int32, (BLOCK, KEYS), 0)
    key = step * KEYS + lax.broadcasted_iota(jnp.int32, (BLOCK, KEYS), 1)
    return ((segq == keycode) & (key < token)) | (key == token)


SMALL = 32


def turn(field, cosine, sine):
    half = HEAD_SIZE // 2
    lane = lax.broadcasted_iota(jnp.int32, field.shape, field.ndim - 1)
    up = pltpu.roll(field, 2 * HEAD_SIZE - half, field.ndim - 1)
    down = pltpu.roll(field, half, field.ndim - 1)
    return field * cosine + jnp.where(lax.rem(lane, HEAD_SIZE) < half, -up, down) * sine


def attention_forward_kernel(
    parts, n_ctx, tok, small, w_q, w_k, w_v, w_o, pack0, pack1, pack2, cos_ref, sin_ref, seg_ref, code_ref,
    normed, small_all, q_full, k_full, v_full, q_ref, kv_ref, full_ref, log_ref, o_back, o_full,
    gate_own, up_own, down_own,
    acc, q_pack, kv_pack, o_buf, own_buf,
    send_w, recv_w, send_s, recv_s, send_e, recv_e, send_q, recv_q, send_kv, recv_kv, send_o, recv_o, here,
):
    c, f = lax.axis_index("ctx"), lax.axis_index("fsdp")
    head, part, pair = lax.div(c, parts), lax.rem(c, parts), lax.rem(c, 2)
    rows = D // 4
    half = rows // 2
    wide = 2 * HEAD_SIZE
    barrier = pltpu.get_barrier_semaphore()
    peers = [(i, 0) for i in range(1, n_ctx)] + [(0, k) for k in range(1, 4)]
    for dc, df in peers:
        pl.semaphore_signal(
            barrier, inc=1, device_id=(flip(c, dc), flip(f, df)), device_id_type=MESH
        )
    shards = (w_q, w_k, w_v, w_o)
    fulls = (q_full, k_full, v_full, o_full)
    packs, owns = (pack0, pack1, pack2), (gate_own, up_own, down_own)
    my_rows = pl.ds(pl.multiple_of(f * rows, rows), rows)
    local = [pltpu.make_async_copy(shards[a], fulls[a].at[f], here.at[a]) for a in range(4)]
    local += [pltpu.make_async_copy(small, small_all.at[f], here.at[4])]
    local += [pltpu.make_async_copy(packs[m].at[f], own_buf.at[m], here.at[5 + m]) for m in range(3)]
    for copy in local:
        copy.start()
    pl.semaphore_wait(barrier, len(peers))
    near = pl.ds(pl.multiple_of(pair * half, half), half)
    far = pl.ds(pl.multiple_of((1 - pair) * half, half), half)
    sibling, over_x, over_pair = (c, flip(f, 1)), (c, flip(f, 2)), (flip(c, 1), f)

    def weight(a, kind):
        beyond = flip(f, 2)
        source, target, device = (
            (shards[a], fulls[a].at[f], sibling),
            (shards[a].at[near], fulls[a].at[f, near], over_x),
            (fulls[a].at[beyond, near], fulls[a].at[beyond, near], sibling),
            (fulls[a].at[beyond, near], fulls[a].at[beyond, near], over_pair),
            (fulls[a].at[beyond, far], fulls[a].at[beyond, far], sibling),
        )[kind]
        return pltpu.make_async_remote_copy(
            source, target, send_w.at[a, kind], recv_w.at[a, kind], device_id=device, device_id_type=MESH
        )

    smalls = [
        pltpu.make_async_remote_copy(
            small, small_all.at[f], send_s.at[i - 1], recv_s.at[i - 1],
            device_id=(c, flip(f, i)), device_id_type=MESH,
        )
        for i in range(1, 4)
    ]
    for copy in smalls:
        copy.start()
    for a in range(4):
        weight(a, 1).start()
        weight(a, 0).start()
    experts = [
        pltpu.make_async_remote_copy(
            packs[m].at[flip(f, i)], owns[m].at[:, my_rows], send_e.at[i - 1, m], recv_e.at[i - 1, m],
            device_id=(c, flip(f, i)), device_id_type=MESH,
        )
        for m in range(3)
        for i in range(1, 4)
    ]
    for copy in experts:
        copy.start()

    x = tok[...].astype(F32)
    scale = lax.rsqrt(jnp.mean(x * x, axis=1, keepdims=True) + EPS)
    for copy in smalls:
        copy.wait_recv()
    local[4].wait()
    for b in range(4):
        columns = slice(b * rows, (b + 1) * rows)
        normed[:, columns] = (x[:, columns] * scale * small_all[b, :1].astype(F32)).astype(BF16)

    def project(b, first):
        block = normed[:, pl.ds(pl.multiple_of(b * rows, rows), rows)]
        at = 0
        for a in range(3):
            width = fulls[a].shape[2]
            made = jnp.dot(block, fulls[a][b], preferred_element_type=F32)
            acc[:, at : at + width] = made if first else acc[:, at : at + width] + made
            at += width

    for a in range(3):
        local[a].wait()
    stores = []
    for m in range(3):
        local[5 + m].wait()
        stores.append(pltpu.make_async_copy(own_buf.at[m], owns[m].at[:, my_rows], here.at[5 + m]))
        stores[m].start()
    project(f, True)
    for a in range(3):
        weight(a, 0).wait_recv()
    project(flip(f, 1), False)
    for a in range(3):
        weight(a, 1).wait_recv()
        weight(a, 2).start()
        weight(a, 3).start()
    for a in range(3):
        weight(a, 3).wait_recv()
        weight(a, 4).start()
    project(flip(f, 2), False)
    for a in range(3):
        weight(a, 2).wait_recv()
        weight(a, 4).wait_recv()
    project(flip(f, 3), False)

    lane = lax.broadcasted_iota(jnp.int32, (BLOCK, wide), 1)
    low = lane < HEAD_SIZE
    cosine, sine = cos_ref[...], sin_ref[...]
    for m in range((QUERY_HEADS + 2 * KEY_VALUE_HEADS) // 2):
        pieces = []
        for s in range(SEQS):
            piece = acc[s * BLOCK : (s + 1) * BLOCK, m * wide : (m + 1) * wide]
            pieces.append(turn(piece, cosine, sine) if m < (QUERY_HEADS + KEY_VALUE_HEADS) // 2 else piece)
        even = jnp.where(low, pieces[0], pltpu.roll(pieces[1], HEAD_SIZE, 1)).astype(BF16)
        odd = jnp.where(low, pltpu.roll(pieces[0], HEAD_SIZE, 1), pieces[1]).astype(BF16)
        for h, value in ((2 * m, even), (2 * m + 1, odd)):
            if h < QUERY_HEADS:
                q_pack[h // REP, h % REP] = value
            else:
                h -= QUERY_HEADS
                kv_pack[h % KEY_VALUE_HEADS, h // KEY_VALUE_HEADS] = value

    q_stays = pltpu.make_async_copy(q_pack.at[head], q_ref.at[head], here.at[8])
    kv_stays = pltpu.make_async_copy(kv_pack.at[head], kv_ref.at[c], here.at[9])
    q_stays.start()
    kv_stays.start()
    to_heads = []
    for i in range(1, n_ctx):
        peer = flip(c, i)
        moves = [(kv_pack.at[lax.div(peer, parts)], kv_ref.at[c], send_kv.at[i - 1], recv_kv.at[i - 1])]
        if i % parts == 0:
            number = i // parts - 1
            moves.append(
                (q_pack.at[lax.div(peer, parts)], q_ref.at[head], send_q.at[number], recv_q.at[number])
            )
        for source, target, sent, came in moves:
            copy = pltpu.make_async_remote_copy(
                source, target, sent, came, device_id=(peer, f), device_id_type=MESH
            )
            copy.start()
            to_heads.append(copy)
    weight(3, 1).wait_recv()
    weight(3, 2).start()
    weight(3, 3).start()
    q_stays.wait()
    kv_stays.wait()
    for copy in to_heads:
        copy.wait_recv()

    count = REP * BLOCK
    halves = half_masks(BF16)
    across = lax.broadcasted_iota(jnp.int32, (count, wide), 1)

    def out_back(j):
        return pltpu.make_async_remote_copy(
            o_buf.at[j], o_back.at[head], send_o.at[j], recv_o.at[head],
            device_id=(j * parts + part, f), device_id_type=MESH,
        )

    def out_stays(j):
        return pltpu.make_async_copy(o_buf.at[j], o_back.at[head], here.at[10])

    def one_block(j, nothing):
        block = j * parts + part
        q = q_ref[j].reshape(count, wide)
        queries = [q * half for half in halves]

        def step(number, carry):
            k = kv_ref[pl.ds(2 * number, 2), 0].reshape(KEYS, wide)
            v = kv_ref[pl.ds(2 * number, 2), 1].reshape(KEYS, wide)
            codes = code_ref[number]
            after = []
            for s in range(SEQS):
                largest, total, out = carry[s]
                mask = allowed_at(block, number, seg_ref[j, s], codes[s : s + 1])
                scores = lax.dot_general(
                    queries[s], k, (((1,), (1,)), ((), ())), preferred_element_type=F32
                )
                scores = jnp.where(mask[None], scores.reshape(REP, BLOCK, KEYS) * SCALE, MASKED)
                scores = scores.reshape(count, KEYS)
                new = jnp.maximum(largest, jnp.max(scores, axis=1, keepdims=True))
                probs = jnp.exp(scores - new)
                shrink = jnp.exp(largest - new)
                total = total * shrink + jnp.sum(probs, axis=1, keepdims=True)
                out = out * shrink + jnp.dot(probs.astype(BF16), v, preferred_element_type=F32)
                after.append((new, total, out))
            return tuple(after)

        start = (
            jnp.full((count, 1), MASKED, F32),
            jnp.zeros((count, 1), F32),
            jnp.zeros((count, wide), F32),
        )
        done = lax.fori_loop(0, lax.div(block, 2) + 1, step, (start,) * SEQS)
        outs, logs = [], []
        for largest, total, out in done:
            outs.append(out / total)
            logs.append(jnp.broadcast_to(largest + jnp.log(total), (count, wide)))
        out = jnp.where(across < HEAD_SIZE, outs[0], outs[1])
        full_ref[j] = out.reshape(REP, BLOCK, wide)
        log_ref[j] = jnp.where(across < HEAD_SIZE, logs[0], logs[1]).reshape(REP, BLOCK, wide)
        o_buf[j] = out.astype(BF16).reshape(REP, BLOCK, wide)

        @pl.when(j != head)
        def _():
            out_back(j).start()

        @pl.when(j == head)
        def _():
            out_stays(j).start()

        return nothing

    lax.fori_loop(0, KEY_VALUE_HEADS, one_block, 0)
    weight(3, 3).wait_recv()
    weight(3, 4).start()

    def came_out(h, nothing):
        @pl.when(h != head)
        def _():
            pltpu.make_async_remote_copy(
                o_buf.at[h], o_back.at[h], send_o.at[h], recv_o.at[h],
                device_id=(h * parts + part, f), device_id_type=MESH,
            ).wait()

        @pl.when(h == head)
        def _():
            out_stays(h).wait()

        return nothing

    lax.fori_loop(0, KEY_VALUE_HEADS, came_out, 0)
    for kind in (0, 2, 4):
        weight(3, kind).wait_recv()
    local[3].wait()
    for copy in stores:
        copy.wait()
    for copy in experts:
        copy.wait()
    for copy in smalls + to_heads:
        copy.wait_send()
    for a in range(4):
        for kind in range(5):
            weight(a, kind).wait_send()


def attention_forward(
    cid, parts, n_ctx, tok, small, w_q, w_k, w_v, w_o, packs, cosine, sine, segq, codes
):
    wide = 2 * HEAD_SIZE
    anywhere = pl.BlockSpec(memory_space=pl.ANY)
    inside = pl.BlockSpec(memory_space=pltpu.VMEM)
    dma = pltpu.SemaphoreType.DMA
    heads = (KEY_VALUE_HEADS, REP, BLOCK, wide)
    keys = (n_ctx, 2, BLOCK, wide)
    others = max(n_ctx // parts - 1, 1)
    columns = w_q.shape[1] + w_k.shape[1] + w_v.shape[1]
    own = jax.ShapeDtypeStruct((OWN, D, FF), BF16)

    def full(x):
        return jax.ShapeDtypeStruct((4,) + x.shape, BF16)

    return pl.pallas_call(
        functools.partial(attention_forward_kernel, parts, n_ctx),
        name="attention_forward",
        out_shape=[
            jax.ShapeDtypeStruct(tok.shape, BF16),
            full(small), full(w_q), full(w_k), full(w_v),
            jax.ShapeDtypeStruct(heads, BF16),
            jax.ShapeDtypeStruct(keys, BF16),
            jax.ShapeDtypeStruct(heads, F32),
            jax.ShapeDtypeStruct(heads, F32),
            jax.ShapeDtypeStruct(heads, BF16),
            full(w_o), own, own, own,
        ],
        in_specs=[inside] + [anywhere] * 8 + [inside] * 4,
        out_specs=[inside] * 9 + [anywhere, inside] + [anywhere] * 3,
        scratch_shapes=[
            pltpu.VMEM((SEQS * BLOCK, columns), F32),
            pltpu.VMEM(heads, BF16),
            pltpu.VMEM((KEY_VALUE_HEADS, 2, BLOCK, wide), BF16),
            pltpu.VMEM(heads, BF16),
            pltpu.VMEM((3,) + packs[0].shape[1:], BF16),
            dma((4, 5)), dma((4, 5)), dma((3,)), dma((3,)), dma((3, 3)), dma((3, 3)),
            dma((others,)), dma((others,)), dma((n_ctx - 1,)), dma((n_ctx - 1,)),
            dma((KEY_VALUE_HEADS,)), dma((KEY_VALUE_HEADS,)), dma((11,)),
        ],
        compiler_params=pltpu.CompilerParams(
            collective_id=cid, has_side_effects=True, vmem_limit_bytes=56 << 20
        ),
        cost_estimate=lasting(130),
    )(tok, small, w_q, w_k, w_v, w_o, *packs, cosine, sine, segq, codes)


def turn_back(field, cosine, sine):
    half = HEAD_SIZE // 2
    lane = lax.broadcasted_iota(jnp.int32, field.shape, field.ndim - 1)
    up = pltpu.roll(field, 2 * HEAD_SIZE - half, field.ndim - 1)
    down = pltpu.roll(field, half, field.ndim - 1)
    turned = jnp.where(lax.rem(lane, HEAD_SIZE) < half, -up, down)
    return field * cosine - turned * sine


def attention_backward_kernel(
    parts, n_ctx, early, g_own, q_ref, kv_ref, seg_ref, code_ref, full_ref, log_ref, cos_ref, sin_ref,
    tok, gain, resid_grad, residual, grads, down_in, mix, output_part, tokens_all, q_full, k_full, v_full,
    input_grad, layer_out, gain_grad, output_sum, gate_first, gate_keep, gate_came, gate_other, down_keep, down_came,
    mix_in, head_in, g_ref, total, kept, came, dq_ref, dkv_ref, dq_back, dkv_back, w_q, w_k, w_v, grad_qkv, grad_in,
    token_buf, field, head_acc, head_out, head_core, head_x, output_keep, output_came, output_x, output_pair,
    send_g, recv_g, send_q, recv_q, send_kv, recv_kv, send_mix, recv_mix, send_half, recv_half, here,
    send_out, recv_out, send_head, recv_head, load_t,
):
    c, f = lax.axis_index("ctx"), lax.axis_index("fsdp")
    head, part = lax.div(c, parts), lax.rem(c, parts)
    rows = REP * BLOCK
    wide = 2 * HEAD_SIZE
    barrier = pltpu.get_barrier_semaphore()
    peers = [(i, k) for i in range(n_ctx) for k in range(4) if i or k]
    for dc, df in peers:
        pl.semaphore_signal(
            barrier, inc=1, device_id=(flip(c, dc), flip(f, df)), device_id_type=MESH
        )
    pair, x_bit, core_bit = lax.rem(c, 2), lax.div(f, 2), lax.rem(f, 2)
    loads = [
        pltpu.make_async_copy(source, target, here.at[5 + i])
        for i, (source, target) in enumerate(
            (
                (q_full, w_q), (k_full, w_k), (v_full, w_v),
                (output_part.at[:, :, :, core_bit], output_keep),
            )
        )
    ]

    def bring(b):
        return pltpu.make_async_copy(
            tokens_all.at[b], token_buf.at[lax.rem(b, 2)], load_t.at[lax.rem(b, 2)]
        )

    for copy in loads + [bring(0), bring(1)]:
        copy.start()
    first = pltpu.make_async_copy(g_own.at[head], g_ref.at[head], here.at[0])
    first.start()
    pl.semaphore_wait(barrier, len(peers))
    to_heads = []
    for number, i in enumerate(range(parts, n_ctx, parts)):
        to_heads.append(
            pltpu.make_async_remote_copy(
                g_own.at[lax.div(flip(c, i), parts)], g_ref.at[head],
                send_g.at[number], recv_g.at[number],
                device_id=(flip(c, i), f), device_id_type=MESH,
            )
        )
        to_heads[-1].start()
    half = grads.shape[1] // 2
    quarter = half // 2
    mine = lax.rem(lax.div(c, 2), 2)
    second = lax.rem(lax.div(c, 4), 2)

    def halving(matrix, target, number):
        return pltpu.make_async_remote_copy(
            grads.at[matrix, pl.ds((1 - mine) * half, half)], target,
            send_half.at[number], recv_half.at[number],
            device_id=(flip(c, 2), f), device_id_type=MESH,
        )

    down_halving, gate_halving = halving(2, came, 0), halving(0, gate_first, 1)
    arriving = pltpu.make_async_copy(down_in, came, here.at[10]) if early else down_halving
    arriving.start()
    keeping = pltpu.make_async_copy(grads.at[2, pl.ds(mine * half, half)], kept, here.at[3])
    keeping.start()
    output_stages = [
        pltpu.make_async_remote_copy(
            source, target, send_out.at[i], recv_out.at[i], device_id=device, device_id_type=MESH
        )
        for i, (source, target, device) in enumerate(
            (
                (output_part.at[:, :, :, 1 - core_bit], output_came, (c, flip(f, 1))),
                (output_keep.at[:, :, 1 - x_bit], output_x, (c, flip(f, 2))),
                (output_x.at[:, 1 - pair], output_pair, (flip(c, 1), f)),
            )
        )
    ]
    output_stages[0].start()
    returns = []
    for i in range(1, RANKS):
        returns.append(
            pltpu.make_async_remote_copy(
                mix.at[i], mix_in.at[i - 1], send_mix.at[i - 1], recv_mix.at[i - 1],
                device_id=(flip(c, i // 4), flip(f, i % 4)), device_id_type=MESH,
            )
        )
        returns[-1].start()
    def plus(mine, came):
        return (mine.astype(F32) + came.astype(F32)).astype(BF16)

    def second_halving(keep, target, number, later=None):
        def add(i, nothing):
            at, e = lax.div(i, OWN), lax.rem(i, OWN)
            kept[at, e] = plus(kept[at, e], came[at, e])
            return nothing

        lax.fori_loop(0, half * OWN, add, 0)
        source = kept.at[pl.ds((1 - second) * quarter, quarter)]
        if later is not None:
            source, target = source.at[:, 0], target.at[:, 0]
            rest = pltpu.make_async_copy(
                kept.at[pl.ds((1 - second) * quarter, quarter), 1], later, here.at[3]
            )
            rest.start()
            rest.wait()
        going = pltpu.make_async_remote_copy(
            source, target, send_half.at[number], recv_half.at[number],
            device_id=(flip(c, 4), f), device_id_type=MESH,
        )
        going.start()
        staying = pltpu.make_async_copy(kept.at[pl.ds(second * quarter, quarter)], keep, here.at[4])
        staying.start()
        return going, staying

    if early:
        keeping.wait()
        arriving.wait()
        down_second, leaving = second_halving(down_keep, down_came, 2)
    gate_halving.start()
    total[...] = jnp.zeros_like(total)
    first.wait()
    for copy in to_heads:
        copy.wait_recv()
    halves = half_masks(BF16)
    lane = lax.broadcasted_iota(jnp.int32, (rows, wide), 1)

    def query_back(j):
        return pltpu.make_async_remote_copy(
            dq_ref.at[j], dq_back.at[head], send_q.at[j], recv_q.at[head],
            device_id=(j * parts + part, f), device_id_type=MESH,
        )

    def key_back(b):
        return pltpu.make_async_remote_copy(
            dkv_ref.at[b], dkv_back.at[c], send_kv.at[b], recv_kv.at[c],
            device_id=(b, f), device_id_type=MESH,
        )

    def query_stays(j):
        return pltpu.make_async_copy(dq_ref.at[j], dq_back.at[head], here.at[1])

    def key_stays(b):
        return pltpu.make_async_copy(dkv_ref.at[b], dkv_back.at[c], here.at[2])

    def one_block(j, nothing):
        block = j * parts + part
        q = q_ref[j].reshape(rows, wide)
        g = g_ref[j].reshape(rows, wide)
        queries = [q * half for half in halves]
        partial = [g * half for half in halves]
        product = g.astype(F32) * full_ref[j].reshape(rows, wide)
        logs = log_ref[j].reshape(rows, wide)
        log_total = [logs[:, :1], logs[:, HEAD_SIZE : HEAD_SIZE + 1]]
        inner = [jnp.sum(product * half, axis=1, keepdims=True) for half in half_masks(F32)]

        def step(number, carry):
            k = kv_ref[pl.ds(2 * number, 2), 0].reshape(KEYS, wide)
            v = kv_ref[pl.ds(2 * number, 2), 1].reshape(KEYS, wide)
            codes = code_ref[number]
            after = []
            dk = jnp.zeros((KEYS, wide), F32)
            dv = jnp.zeros((KEYS, wide), F32)
            for s in range(SEQS):
                mask = allowed_at(block, number, seg_ref[j, s], codes[s : s + 1])
                scores = lax.dot_general(
                    queries[s], k, (((1,), (1,)), ((), ())), preferred_element_type=F32
                )
                scores = jnp.where(mask[None], scores.reshape(REP, BLOCK, KEYS) * SCALE, MASKED)
                probs = jnp.exp(scores.reshape(rows, KEYS) - log_total[s])
                grad_probs = lax.dot_general(
                    partial[s], v, (((1,), (1,)), ((), ())), preferred_element_type=F32
                )
                grad_scores = (probs * (grad_probs - inner[s])).astype(BF16)
                dv = dv + lax.dot_general(
                    probs.astype(BF16), partial[s], (((0,), (0,)), ((), ())), preferred_element_type=F32
                )
                dk = dk + lax.dot_general(
                    grad_scores, queries[s], (((0,), (0,)), ((), ())), preferred_element_type=F32
                )
                after.append(carry[s] + jnp.dot(grad_scores, k, preferred_element_type=F32))
            total[pl.ds(2 * number, 2), 0] += dk.reshape(2, BLOCK, wide)
            total[pl.ds(2 * number, 2), 1] += dv.reshape(2, BLOCK, wide)
            return tuple(after)

        start = jnp.zeros((rows, wide), F32)
        done = lax.fori_loop(0, lax.div(block, 2) + 1, step, (start,) * SEQS)
        dq = (jnp.where(lane < HEAD_SIZE, done[0], done[1]) * SCALE).reshape(REP, BLOCK, wide)
        dq_ref[j] = turn_back(dq, cos_ref[block][None], sin_ref[block][None]).astype(BF16)

        @pl.when(j != head)
        def _():
            query_back(j).start()

        @pl.when(j == head)
        def _():
            query_stays(j).start()

        return nothing

    lax.fori_loop(0, KEY_VALUE_HEADS, one_block, 0)

    def finish(b, nothing):
        dkv_ref[b, 0] = turn_back(total[b, 0] * SCALE, cos_ref[b], sin_ref[b]).astype(BF16)
        dkv_ref[b, 1] = total[b, 1].astype(BF16)

        @pl.when(b != c)
        def _():
            key_back(b).start()

        @pl.when(b == c)
        def _():
            key_stays(b).start()

        return nothing

    lax.fori_loop(0, n_ctx, finish, 0)
    if not early:
        keeping.wait()
        down_halving.wait_recv()
        down_second, leaving = second_halving(down_keep, down_came, 2)

    planes = output_keep.shape[0]

    loads[3].wait()
    output_stages[0].wait_recv()

    def cores(i, nothing):
        r, p, x = lax.div(i, 4), lax.rem(lax.div(i, 2), 2), lax.rem(i, 2)
        output_keep[r, p, x] = plus(output_keep[r, p, x], output_came[r, p, x])
        return nothing

    lax.fori_loop(0, planes * 4, cores, 0)
    output_stages[1].start()

    low = lax.broadcasted_iota(jnp.int32, (BLOCK, wide), 1) < HEAD_SIZE

    def side_by_side(even, odd):
        even, odd = even.astype(F32), odd.astype(F32)
        return (
            jnp.where(low, even, pltpu.roll(odd, HEAD_SIZE, 1)),
            jnp.where(low, pltpu.roll(even, HEAD_SIZE, 1), odd),
        )

    head_acc[...] = jnp.zeros_like(head_acc)

    def head_weights(b, nothing):
        bring(b).wait()
        block = token_buf[lax.rem(b, 2)]
        wide_block = block.astype(F32)
        scales = lax.rsqrt(jnp.mean(wide_block * wide_block, axis=1, keepdims=True) + EPS)
        j = lax.div(b, parts)
        have = jnp.where(lax.rem(b, parts) == part, 1.0, 0.0)
        heads = [dq_ref[j, r].astype(F32) * have for r in range(REP)] + [dkv_ref[b, 0], dkv_ref[b, 1]]
        heads.append(jnp.zeros((BLOCK, wide), F32))
        for m in range((REP + 3) // 2):
            for s, value in enumerate(side_by_side(heads[2 * m], heads[2 * m + 1])):
                at = slice(s * BLOCK, (s + 1) * BLOCK)
                field[at, m * wide : (m + 1) * wide] = (value * scales[at]).astype(BF16)
        head_acc[...] += lax.dot_general(
            block, field[...], (((0,), (0,)), ((), ())), preferred_element_type=F32
        )

        @pl.when(b + 2 < n_ctx)
        def _():
            bring(b + 2).start()

        return nothing

    lax.fori_loop(0, n_ctx, head_weights, 0)
    slab = D // (n_ctx * 4)
    for d in range(n_ctx * 4):
        head_out[d // 4, d // 2 % 2, d % 2] = head_acc[
            d * slab : (d + 1) * slab, : head_out.shape[4]
        ].astype(BF16)
    head_stages = [
        pltpu.make_async_remote_copy(
            source, target, send_head.at[i], recv_head.at[i], device_id=device, device_id_type=MESH
        )
        for i, (source, target, device) in enumerate(
            (
                (head_out.at[:, :, 1 - core_bit], head_core, (c, flip(f, 1))),
                (head_core.at[:, 1 - x_bit], head_x, (c, flip(f, 2))),
            )
        )
    ]
    head_stages[0].start()
    down_second.wait_send()
    leaving.wait()
    gate_halving.wait_recv()
    refill = [
        pltpu.make_async_copy(grads.at[0, pl.ds(mine * half, half)], kept, here.at[3]),
        pltpu.make_async_copy(gate_first, came, here.at[10]),
    ]
    for copy in refill:
        copy.start()
    for copy in refill:
        copy.wait()
    gate_second, leaving = second_halving(gate_keep, gate_came, 3, gate_other)

    head_stages[0].wait_recv()

    def head_cores(i, nothing):
        d, x = lax.div(i, 2), lax.rem(i, 2)
        head_core[d, x] = plus(head_out[d, x, core_bit], head_core[d, x])
        return nothing

    lax.fori_loop(0, n_ctx * 2, head_cores, 0)
    head_stages[1].start()

    def came_query(h, nothing):
        @pl.when(h != head)
        def _():
            pltpu.make_async_remote_copy(
                dq_ref.at[h], dq_back.at[h], send_q.at[h], recv_q.at[h],
                device_id=(h * parts + part, f), device_id_type=MESH,
            ).wait()

        @pl.when(h == head)
        def _():
            query_stays(h).wait()

        return nothing

    def came_key(b, nothing):
        @pl.when(b != c)
        def _():
            pltpu.make_async_remote_copy(
                dkv_ref.at[b], dkv_back.at[b], send_kv.at[b], recv_kv.at[b],
                device_id=(b, f), device_id_type=MESH,
            ).wait()

        @pl.when(b == c)
        def _():
            key_stays(b).wait()

        return nothing

    lax.fori_loop(0, KEY_VALUE_HEADS, came_query, 0)
    lax.fori_loop(0, n_ctx, came_key, 0)

    def head_of(h):
        if h < QUERY_HEADS:
            return dq_back[h // REP, h % REP]
        kind, h = (h - QUERY_HEADS) // KEY_VALUE_HEADS, (h - QUERY_HEADS) % KEY_VALUE_HEADS
        value = dkv_back[h * parts, kind]
        if parts > 1:
            value = value.astype(F32)
            for p in range(1, parts):
                value = value + dkv_back[h * parts + p, kind].astype(F32)
        return value

    head_stages[1].wait_recv()

    def head_over_x(d, nothing):
        head_x[d] = plus(head_core[d, x_bit], head_x[d])
        return nothing

    lax.fori_loop(0, n_ctx, head_over_x, 0)
    head_stays = pltpu.make_async_copy(head_x.at[c], head_in.at[c], here.at[9])
    head_stays.start()
    to_all = []
    for i in range(1, n_ctx):
        to_all.append(
            pltpu.make_async_remote_copy(
                head_x.at[flip(c, i)], head_in.at[c], send_head.at[1 + i], recv_head.at[1 + i],
                device_id=(flip(c, i), f), device_id_type=MESH,
            )
        )
        to_all[-1].start()
    for m in range((QUERY_HEADS + 2 * KEY_VALUE_HEADS) // 2):
        for s, value in enumerate(side_by_side(head_of(2 * m), head_of(2 * m + 1))):
            grad_qkv[s * BLOCK : (s + 1) * BLOCK, m * wide : (m + 1) * wide] = value.astype(BF16)
    for copy in loads[:3]:
        copy.wait()
    depth = D // 4
    for b in range(4):
        made, at = 0.0, 0
        for weight in (w_q, w_k, w_v):
            width = weight.shape[2]
            made = made + lax.dot_general(
                grad_qkv[:, at : at + width], weight[b], (((1,), (1,)), ((), ())),
                preferred_element_type=F32,
            )
            at += width
        grad_in[:, b * depth : (b + 1) * depth] = made
    x = tok[...].astype(F32)
    scale = lax.rsqrt(jnp.mean(x * x, axis=1, keepdims=True) + EPS)
    gain_grad[...] = jnp.sum(grad_in[...] * x * scale, axis=0, keepdims=True)
    weighted = grad_in[...] * gain[...]
    input_grad[...] = (
        resid_grad[...]
        + scale * weighted
        - x * (scale * scale * scale) * jnp.mean(weighted * x, axis=1, keepdims=True)
    ).astype(BF16)

    staying = pltpu.make_async_copy(residual, grad_in, here.at[8])
    staying.start()
    staying.wait()

    def share(i):
        return pltpu.make_async_copy(
            mix_in.at[i - 1] if i else mix.at[0], token_buf.at[i % 2], load_t.at[i % 2]
        )

    share(0).start()
    for i in range(RANKS):
        if i + 1 < RANKS:
            returns[i].wait_recv()
            share(i + 1).start()
        share(i).wait()
        grad_in[...] += token_buf[i % 2].astype(F32)
    layer_out[...] = grad_in[...].astype(BF16)

    output_stages[1].wait_recv()

    def over_x(i, nothing):
        r, p = lax.div(i, 2), lax.rem(i, 2)
        output_x[r, p] = plus(output_keep[r, p, x_bit], output_x[r, p])
        return nothing

    lax.fori_loop(0, planes * 2, over_x, 0)
    output_stages[2].start()
    output_stages[2].wait_recv()

    def over_pair(r, nothing):
        output_sum[r] = plus(output_x[r, pair], output_pair[r])
        return nothing

    lax.fori_loop(0, planes, over_pair, 0)
    for copy in to_heads:
        copy.wait_send()
    for copy in to_all + [gate_second, leaving, head_stays]:
        copy.wait()
    down_second.wait_recv()
    for copy in returns + output_stages + head_stages + [gate_halving] + ([] if early else [down_halving]):
        copy.wait_send()


def attention_backward(
    cid, parts, n_ctx, early, g_own, q, kv, segq, codes, full, logs, cosine, sine,
    tok, gain, resid_grad, residual, grads, down_in, mix, output_part, tokens_all, q_full, k_full, v_full,
):
    wide = 2 * HEAD_SIZE
    anywhere = pl.BlockSpec(memory_space=pl.ANY)
    inside = pl.BlockSpec(memory_space=pltpu.VMEM)
    dma = pltpu.SemaphoreType.DMA
    others = max(n_ctx // parts - 1, 1)
    devices, planes = n_ctx * 4, n_ctx // 2
    slab, head_width = D // devices, (REP + 2) * HEAD_SIZE
    half = (grads.shape[1] // 2,) + grads.shape[2:]
    quarter = (grads.shape[1] // 4,) + grads.shape[2:]
    columns = q_full.shape[2] + k_full.shape[2] + v_full.shape[2]
    return pl.pallas_call(
        functools.partial(attention_backward_kernel, parts, n_ctx, early),
        name="attention_backward",
        out_shape=[
            jax.ShapeDtypeStruct(tok.shape, BF16),
            jax.ShapeDtypeStruct(tok.shape, BF16),
            jax.ShapeDtypeStruct((1, D), F32),
            jax.ShapeDtypeStruct((planes, slab, D), BF16),
            jax.ShapeDtypeStruct(half, BF16),
            jax.ShapeDtypeStruct(quarter, BF16),
            jax.ShapeDtypeStruct(quarter, BF16),
            jax.ShapeDtypeStruct(quarter[:1] + quarter[2:], BF16),
            jax.ShapeDtypeStruct(quarter, BF16),
            jax.ShapeDtypeStruct(quarter, BF16),
            jax.ShapeDtypeStruct((RANKS - 1,) + mix.shape[1:], BF16),
            jax.ShapeDtypeStruct((n_ctx, slab, head_width), BF16),
        ],
        in_specs=[anywhere] + [inside] * 11 + [anywhere] * 9,
        out_specs=[inside] * 4 + [anywhere] * 8,
        scratch_shapes=[
            pltpu.VMEM(q.shape, BF16),
            pltpu.VMEM((n_ctx, 2, BLOCK, wide), F32),
            pltpu.VMEM(half, BF16),
            pltpu.VMEM(half, BF16),
            pltpu.VMEM(q.shape, BF16),
            pltpu.VMEM(kv.shape, BF16),
            pltpu.VMEM(q.shape, BF16),
            pltpu.VMEM(kv.shape, BF16),
            pltpu.VMEM(q_full.shape, BF16),
            pltpu.VMEM(k_full.shape, BF16),
            pltpu.VMEM(v_full.shape, BF16),
            pltpu.VMEM((SEQS * BLOCK, columns), BF16),
            pltpu.VMEM((SEQS * BLOCK, D), F32),
            pltpu.VMEM((2, SEQS * BLOCK, D), BF16),
            pltpu.VMEM((SEQS * BLOCK, 3 * wide), BF16),
            pltpu.VMEM((D, 3 * wide), F32),
            pltpu.VMEM((n_ctx, 2, 2, slab, head_width), BF16),
            pltpu.VMEM((n_ctx, 2, slab, head_width), BF16),
            pltpu.VMEM((n_ctx, slab, head_width), BF16),
            pltpu.VMEM((planes, 2, 2, slab, D), BF16),
            pltpu.VMEM((planes, 2, 2, slab, D), BF16),
            pltpu.VMEM((planes, 2, slab, D), BF16),
            pltpu.VMEM((planes, slab, D), BF16),
            dma((others,)), dma((others,)), dma((KEY_VALUE_HEADS,)), dma((KEY_VALUE_HEADS,)),
            dma((n_ctx,)), dma((n_ctx,)), dma((RANKS - 1,)), dma((RANKS - 1,)), dma((4,)), dma((4,)),
            dma((11,)), dma((3,)), dma((3,)), dma((n_ctx + 1,)), dma((n_ctx + 1,)), dma((2,)),
        ],
        compiler_params=pltpu.CompilerParams(
            collective_id=cid, has_side_effects=True, vmem_limit_bytes=62 << 20
        ),
        cost_estimate=lasting(125),
    )(
        g_own, q, kv, segq, codes, full, logs, cosine, sine, tok, gain, resid_grad, residual,
        grads, down_in, mix, output_part, tokens_all, q_full, k_full, v_full,
    )


def final_kernel(
    n_ctx, small, output_part, grads, gate_keep, gate_came, gate_other, down_keep, down_came,
    swapped, output_grad, small_sum,
    halves, landed, rest, rest_landed, last, last_landed, turned, output_in, small_in,
    send_half, recv_half, send_deep, recv_deep, send_out, recv_out, send_small, recv_small,
    send_swap, recv_swap, load, stay,
):
    c, f = lax.axis_index("ctx"), lax.axis_index("fsdp")
    me, plane, rank = c * 4 + f, lax.div(c, 2), lax.rem(c, 2) * 4 + f
    planes = n_ctx // 2
    half, quarter = planes // 2, planes // 4
    barrier = pltpu.get_barrier_semaphore()
    peers = [(i, k) for i in range(n_ctx) for k in range(4) if i or k]
    for dc, df in peers:
        pl.semaphore_signal(
            barrier, inc=1, device_id=(flip(c, dc), flip(f, df)), device_id_type=MESH
        )
    first, second = lax.rem(plane, 2), lax.rem(lax.div(plane, 2), 2)
    loads = [
        pltpu.make_async_copy(source, target, load.at[i])
        for i, (source, target) in enumerate(
            (
                (down_keep, rest.at[2]),
                (down_came, rest_landed.at[2]),
                (gate_keep, rest.at[0]),
                (gate_came.at[:, 0], rest_landed.at[0, :, 0]),
                (grads.at[1, pl.ds(first * half, half)], halves),
                (output_part.at[plane], output_in.at[plane]),
                (small.at[me], small_in.at[me]),
            )
        )
    ]
    for copy in loads:
        copy.start()
    pl.semaphore_wait(barrier, len(peers))

    def over(source, target, sent, came, bit):
        return pltpu.make_async_remote_copy(
            source, target, sent, came, device_id=(flip(c, 2 * bit), f), device_id_type=MESH
        )

    up_first = [
        over(
            grads.at[1, pl.ds((1 - first) * half, half), e], landed.at[:, e],
            send_half.at[0, e], recv_half.at[0, e], 1,
        )
        for e in range(OWN)
    ]
    gate_second = over(gate_other, rest_landed.at[0, :, 1], send_half.at[2, 1], recv_half.at[2, 1], 2)
    for copy in [gate_second] + up_first:
        copy.start()
    outputs = []
    for i in range(1, planes):
        outputs.append(
            pltpu.make_async_remote_copy(
                output_part.at[flip(plane, i)], output_in.at[plane], send_out.at[i - 1], recv_out.at[i - 1],
                device_id=(flip(c, 2 * i), f), device_id_type=MESH,
            )
        )
    smalls = []
    for number, (i, k) in enumerate(peers):
        peer_c, peer_f = flip(c, i), flip(f, k)
        smalls.append(
            pltpu.make_async_remote_copy(
                small.at[peer_c * 4 + peer_f], small_in.at[me], send_small.at[number], recv_small.at[number],
                device_id=(peer_c, peer_f), device_id_type=MESH,
            )
        )
    for copy in outputs + smalls:
        copy.start()

    def plus(mine, came):
        return (mine.astype(F32) + came.astype(F32)).astype(BF16)

    swaps, sent = [], []

    def finish(m, e):
        count, bit, number = quarter, 4, 0
        for at in range(quarter):
            rest[m, at, e] = plus(rest[m, at, e], rest_landed[m, at, e])
        mine = rest.at[m, :, e]
        while count > 1:
            count //= 2
            chosen = lax.rem(lax.div(plane, bit), 2)
            came = last_landed.at[m, number, pl.ds(0, count), e]
            copy = over(
                mine.at[pl.ds((1 - chosen) * count, count)], came,
                send_deep.at[2 * m + number, e], recv_deep.at[2 * m + number, e], bit,
            )
            copy.start()
            copy.wait_recv()
            sent.append(copy)
            for at in range(count):
                last[m, number, at, e] = plus(mine[chosen * count + at], came[at])
            mine, bit, number = last.at[m, number, :, e], bit * 2, number + 1
        rows = turned.shape[3]
        across = mine[0].astype(F32).T
        for r in range(RANKS):
            turned[m, r, e] = across[r * rows : (r + 1) * rows].astype(BF16)
        for i in range(RANKS):
            source, target = turned.at[m, flip(rank, i), e], swapped.at[rank, m, e]
            if i:
                copy = pltpu.make_async_remote_copy(
                    source, target, send_swap.at[m * OWN + e, i], recv_swap.at[m * OWN + e, i],
                    device_id=(flip(c, i // 4), flip(f, i % 4)), device_id_type=MESH,
                )
            else:
                copy = pltpu.make_async_copy(source, target, stay.at[m * OWN + e])
            copy.start()
            swaps.append(copy)

    for copy in loads:
        copy.wait()
    for e in range(OWN):
        finish(2, e)
    finish(0, 0)
    up_second = []
    for e in range(OWN):
        up_first[e].wait_recv()
        for at in range(half):
            halves[at, e] = plus(halves[at, e], landed[at, e])
        up_second.append(
            over(
                halves.at[pl.ds((1 - second) * quarter, quarter), e], rest_landed.at[1, :, e],
                send_half.at[1, e], recv_half.at[1, e], 2,
            )
        )
        up_second[e].start()
        for at in range(quarter):
            rest[1, at, e] = halves[second * quarter + at, e]
    gate_second.wait_recv()
    finish(0, 1)
    for copy in outputs + smalls:
        copy.wait_recv()
    made = output_in[0].astype(F32)
    for i in range(1, planes):
        made = made + output_in[i].astype(F32)
    output_grad[...] = made
    small_sum[...] = jnp.sum(small_in[...], axis=0)
    for e in range(OWN):
        up_second[e].wait_recv()
        finish(1, e)
    for copy in swaps:
        copy.wait()
    for copy in smalls + outputs + sent + up_first + up_second + [gate_second]:
        copy.wait_send()


def final_sums(
    cid, n_ctx, small, output_part, grads, gate_keep, gate_came, gate_other, down_keep, down_came
):
    anywhere = pl.BlockSpec(memory_space=pl.ANY)
    inside = pl.BlockSpec(memory_space=pltpu.VMEM)
    dma = pltpu.SemaphoreType.DMA
    devices, planes = n_ctx * 4, n_ctx // 2
    slab, piece = D // devices, grads.shape[2:]
    half, quarter = (planes // 2,) + piece, (planes // 4,) + piece
    deep = (3, 2, max(planes // 8, 1)) + piece
    return pl.pallas_call(
        functools.partial(final_kernel, n_ctx),
        name="final_sums",
        out_shape=[
            jax.ShapeDtypeStruct((RANKS, 3, OWN, slab, FF), BF16),
            jax.ShapeDtypeStruct((slab, D), F32),
            jax.ShapeDtypeStruct(small.shape[1:], F32),
        ],
        in_specs=[anywhere] * 8,
        out_specs=[anywhere] + [inside] * 2,
        scratch_shapes=[
            pltpu.VMEM(half, BF16),
            pltpu.VMEM(half, BF16),
            pltpu.VMEM((3,) + quarter, BF16),
            pltpu.VMEM((3,) + quarter, BF16),
            pltpu.VMEM(deep if planes > 4 else (1, 1, 1, 1, 8, 128), BF16),
            pltpu.VMEM(deep if planes > 4 else (1, 1, 1, 1, 8, 128), BF16),
            pltpu.VMEM((3, RANKS, OWN, slab, FF), BF16),
            pltpu.VMEM((planes, slab, D), BF16),
            pltpu.VMEM(small.shape, F32),
            dma((3, OWN)), dma((3, OWN)), dma((6, OWN)), dma((6, OWN)),
            dma((planes - 1,)), dma((planes - 1,)), dma((devices - 1,)), dma((devices - 1,)),
            dma((3 * OWN, RANKS)), dma((3 * OWN, RANKS)), dma((7,)), dma((3 * OWN,)),
        ],
        compiler_params=pltpu.CompilerParams(
            collective_id=cid, has_side_effects=True, vmem_limit_bytes=56 << 20
        ),
        cost_estimate=lasting(80),
    )(small, output_part, grads, gate_keep, gate_came, gate_other, down_keep, down_came)


def rope_tables(positions):
    half_dim = HEAD_SIZE // 2
    frequency = ROPE_BASE ** (-jnp.arange(half_dim, dtype=F32) * 2.0 / HEAD_SIZE)
    angle = positions.astype(F32)[:, None] * frequency[None, :]
    angle = jnp.concatenate([angle, angle], axis=1)
    return (jnp.cos(angle), jnp.sin(angle))


def heads_out(field, per):
    field = field.reshape(SEQS, BLOCK, KEY_VALUE_HEADS, per, HEAD_SIZE)
    return field.transpose(2, 3, 1, 0, 4).reshape(KEY_VALUE_HEADS, per, BLOCK, SEQS * HEAD_SIZE)


def heads_in(field):
    per = field.shape[1]
    field = field.reshape(KEY_VALUE_HEADS, per, BLOCK, SEQS, HEAD_SIZE)
    return field.transpose(3, 2, 0, 1, 4).reshape(SEQS, BLOCK, KEY_VALUE_HEADS * per * HEAD_SIZE)


def on_device(
    n_ctx,
    n_fsdp,
    tokens,
    segments,
    valid,
    expert_ids,
    slot_order,
    cotangent,
    norm1_gain,
    w_query,
    key_weight,
    value_weight,
    w_output,
    norm2_gain,
    w_router,
    w_gate,
    w_up,
    w_down,
):
    parts = n_ctx // KEY_VALUE_HEADS
    replicas = n_ctx // 2
    full_len = segments.shape[1]
    c_index, f_index = lax.axis_index("ctx"), lax.axis_index("fsdp")
    pair = lax.rem(c_index, 2)
    rank = pair * n_fsdp + f_index
    part = lax.rem(c_index, parts)
    head = lax.div(c_index, parts)
    positions = c_index * BLOCK + jnp.arange(BLOCK, dtype=jnp.int32)

    tokens_all = lax.all_gather(tokens, "ctx", axis=0, tiled=False)
    small = jnp.concatenate(
        [
            norm1_gain[None],
            norm2_gain[None],
            w_router.T,
            jnp.zeros((SMALL - EXPERTS - 2, D // n_fsdp), BF16),
        ],
        axis=0,
    )
    packs = [
        lax.dynamic_slice_in_dim(w, pair * (EXPERTS // 2), EXPERTS // 2, 1)
        .reshape(D // n_fsdp, n_fsdp, OWN, FF)
        .transpose(1, 2, 0, 3)
        for w in (w_gate, w_up, w_down)
    ]
    inputs_f = tokens.astype(F32)
    scale_one = lax.rsqrt(jnp.mean(inputs_f * inputs_f, axis=-1, keepdims=True) + EPS)
    segq = segments.reshape(SEQS, KEY_VALUE_HEADS, parts, BLOCK)
    segq = lax.dynamic_index_in_dim(segq, part, 2, keepdims=False).transpose(1, 0, 2)[..., None]
    codes = jnp.where(valid > 0, segments, -1)
    codes = codes.reshape(SEQS, full_len // KEYS, KEYS).transpose(1, 0, 2)
    all_cosine, all_sine = rope_tables(jnp.arange(full_len, dtype=jnp.int32))
    all_cosine = jnp.tile(all_cosine, (1, 2)).reshape(n_ctx, BLOCK, 2 * HEAD_SIZE)
    all_sine = jnp.tile(all_sine, (1, 2)).reshape(n_ctx, BLOCK, 2 * HEAD_SIZE)
    (
        normed_in, small_all, full_query, full_key, full_value, q_all, kv_all, head_full, head_logs,
        attn_heads, full_output, own_gate, own_up, own_down,
    ) = attention_forward(
        0, parts, n_ctx, tokens.reshape(SEQS * BLOCK, D), small, w_query, key_weight, value_weight,
        w_output, packs,
        lax.dynamic_index_in_dim(all_cosine, c_index, 0, keepdims=False),
        lax.dynamic_index_in_dim(all_sine, c_index, 0, keepdims=False),
        segq, codes,
    )
    gain_first = small_all[:, 0].reshape(D).astype(F32)
    gain_second = small_all[:, 1].reshape(D).astype(F32)
    full_router = small_all[:, 2 : 2 + EXPERTS].transpose(1, 0, 2).reshape(EXPERTS, D)
    full_output = full_output.reshape(D, D)
    attn_out = heads_in(attn_heads)
    attn_proj = jnp.einsum("sgq,dq->sgd", attn_out, full_output, preferred_element_type=F32)
    residual = inputs_f + attn_proj
    scale_two = lax.rsqrt(jnp.mean(residual * residual, axis=-1, keepdims=True) + EPS)
    normed_mid = (residual * scale_two * gain_second).astype(BF16)

    logits = jnp.einsum("sgd,ed->sge", normed_mid, full_router, preferred_element_type=F32)
    picked = jnp.any(expert_ids[..., None] == jnp.arange(EXPERTS, dtype=jnp.int32), axis=2)
    before = (slot_order[:, None, :] < slot_order[:, :, None]).astype(BF16)
    place = jnp.matmul(before, picked.astype(BF16), preferred_element_type=F32)
    is_kept = picked & (place < CAP)
    chosen = jnp.where(picked, logits, MASKED)
    raised = jnp.where(picked, jnp.exp(chosen - jnp.max(chosen, axis=-1, keepdims=True)), 0.0)
    gates = raised / jnp.sum(raised, axis=-1, keepdims=True)
    payload = jnp.concatenate(
        [
            normed_mid,
            jnp.where(is_kept, place, -1.0).astype(BF16),
            gates.astype(BF16),
            jnp.zeros((SEQS, BLOCK, 128 - 2 * EXPERTS), BF16),
        ],
        axis=2,
    )
    back, mix_part, own_grads, down_first, down_early = run_experts(
        2, replicas, payload.reshape(SEQS * BLOCK, PAY), cotangent.reshape(SEQS * BLOCK, D),
        (own_gate, own_up, own_down), tokens_all
    )

    back = back.reshape(SEQS, BLOCK, D + 128)
    grad_gates = jnp.where(is_kept, back[..., D : D + EXPERTS], 0.0)
    grad_chosen = gates * (grad_gates - jnp.sum(gates * grad_gates, axis=-1, keepdims=True))
    grad_logits = grad_chosen.astype(BF16)
    grad_mid = back[..., :D] + jnp.einsum(
        "sge,ed->sgd", grad_logits, full_router, preferred_element_type=F32
    )
    grad_router = jnp.einsum("sgd,sge->de", normed_mid, grad_logits, preferred_element_type=F32)

    grad_f = cotangent.astype(F32)
    weighted_two = gain_second * grad_mid
    grad_gain_second = jnp.sum(grad_mid * residual * scale_two, axis=(0, 1))
    cube_two = scale_two * scale_two * scale_two
    grad_resid = (
        grad_f
        + scale_two * weighted_two
        - residual * cube_two * jnp.mean(weighted_two * residual, axis=-1, keepdims=True)
    )
    grad_resid_low = grad_resid.astype(BF16)
    grad_attn = jnp.einsum("sgd,dq->sgq", grad_resid_low, full_output, preferred_element_type=F32)
    grad_attn = grad_attn.astype(BF16)
    grad_output_w = jnp.einsum("sgd,sgq->dq", grad_resid_low, attn_out, preferred_element_type=F32)
    rows = D // (n_ctx * n_fsdp)
    output_part = grad_output_w.astype(BF16).reshape(replicas, 2, 2, 2, rows, D)

    (
        input_grad, layer_out, gain_grad, output_sum, _, gate_keep, gate_came, gate_other, down_keep, down_came,
        _, head_grads,
    ) = attention_backward(
        6, parts, n_ctx, down_early, heads_out(grad_attn, REP), q_all, kv_all, segq, codes, head_full, head_logs,
        all_cosine, all_sine, tokens.reshape(SEQS * BLOCK, D), gain_first[None],
        grad_resid.reshape(SEQS * BLOCK, D), residual.reshape(SEQS * BLOCK, D), own_grads, down_first, mix_part, output_part,
        tokens_all.reshape(n_ctx, SEQS * BLOCK, D), full_query, full_key, full_value,
    )
    input_grad = input_grad.reshape(SEQS, BLOCK, D)
    layer_out = layer_out.reshape(SEQS, BLOCK, D)
    amount = rows * (EXPERTS + 2)
    tiles = -(-amount // 1024) * 8
    small_grads = jnp.concatenate([grad_router, gain_grad.T, grad_gain_second[:, None]], axis=1)
    small_grads = jnp.pad(
        small_grads.reshape(n_ctx * n_fsdp, amount), ((0, 0), (0, tiles * 128 - amount))
    ).reshape(n_ctx * n_fsdp, tiles, 128)
    swapped, output_grad, small_sum = final_sums(
        9, n_ctx, small_grads, output_sum, own_grads, gate_keep, gate_came, gate_other, down_keep, down_came
    )
    small_sum = small_sum.reshape(tiles * 128)[:amount].reshape(rows, EXPERTS + 2)
    head_grads = head_grads.reshape(KEY_VALUE_HEADS, parts, rows, (REP + 2) * HEAD_SIZE)
    own_gain = lax.dynamic_slice_in_dim(gain_first, (c_index * n_fsdp + f_index) * rows, rows, 0)
    head_grads = jnp.sum(head_grads.astype(F32), axis=1).transpose(1, 0, 2) * own_gain[:, None, None]
    query_grad = head_grads[..., : REP * HEAD_SIZE].reshape(rows, D)
    key_grad = head_grads[..., REP * HEAD_SIZE : (REP + 1) * HEAD_SIZE].reshape(rows, -1)
    value_grad = head_grads[..., (REP + 1) * HEAD_SIZE :].reshape(rows, -1)

    def by_row(matrix):
        return swapped[:, matrix].transpose(2, 0, 1, 3).reshape(rows, EXPERTS, FF).astype(F32)

    return (
        layer_out,
        input_grad,
        small_sum[:, EXPERTS],
        query_grad,
        key_grad,
        value_grad,
        output_grad,
        small_sum[:, EXPERTS + 1],
        small_sum[:, :EXPERTS],
        by_row(0),
        by_row(1),
        by_row(2),
    )


def solution(mesh):
    placed = (
        P("fsdp", "ctx", None),
        P("fsdp", None),
        P("fsdp", None),
        P("fsdp", "ctx", None),
        P("fsdp", "ctx"),
        P("fsdp", "ctx", None),
        P("fsdp"),
        P("fsdp", None),
        P("fsdp", None),
        P("fsdp", None),
        P("fsdp", None),
        P("fsdp"),
        P("fsdp", None),
        P("fsdp", None, None),
        P("fsdp", None, None),
        P("fsdp", None, None),
    )
    return jax.shard_map(
        functools.partial(on_device, mesh.shape["ctx"], mesh.shape["fsdp"]),
        mesh=mesh,
        in_specs=placed,
        out_specs=(
            P("fsdp", "ctx", None),
            P("fsdp", "ctx", None),
            P(("ctx", "fsdp")),
            P(("ctx", "fsdp"), None),
            P(("ctx", "fsdp"), None),
            P(("ctx", "fsdp"), None),
            P(("ctx", "fsdp"), None),
            P(("ctx", "fsdp")),
            P(("ctx", "fsdp"), None),
            P(("ctx", "fsdp"), None, None),
            P(("ctx", "fsdp"), None, None),
            P(("ctx", "fsdp"), None, None),
        ),
        check_vma=False,
    )
```

```python
import functools

import jax
import jax.numpy as jnp
from jax import lax
from jax.experimental import pallas as pl
from jax.experimental.pallas import tpu as pltpu
from jax.sharding import PartitionSpec as P

D = 1536
QUERY_HEADS = 24
KEY_VALUE_HEADS = 8
REP = QUERY_HEADS // KEY_VALUE_HEADS
HEAD_SIZE = 64
FF = 512
EXPERTS = 16
CAP = 80
RANKS = 8
OWN = EXPERTS // RANKS
SEQS = 2
BLOCK = 128
KEYS = 256

EPS = 1e-05
ROPE_BASE = 10000.0
MASKED = -1e30
SCALE = HEAD_SIZE ** (-0.5)
MESH = pl.DeviceIdType.MESH
BF16 = jnp.bfloat16
F32 = jnp.float32


def flip(index, constant):
    result, bit = index, 1
    while bit <= constant:
        if constant & bit:
            result = result + bit - 2 * bit * lax.rem(lax.div(index, bit), 2)
        bit *= 2
    return result


def lasting(microseconds):
    return pl.CostEstimate(flops=0, bytes_accessed=int(microseconds * 3.3e6), transcendentals=0)


PAY = D + 128
GROUPS = 4
ROWS = GROUPS * CAP


def other_chip(c, f, k):
    pair, x = lax.div(k, 2), lax.rem(k, 2)
    return (
        c + pair * (1 - 2 * lax.rem(c, 2)),
        f + 2 * x * (1 - 2 * lax.rem(lax.div(f, 2), 2)),
    )


def plane_order(replicas):
    order = [0]
    while len(order) < replicas:
        order = [2 * i for i in order] + [2 * i + 1 for i in order]
    return order


def experts_kernel(
    replicas, pay, cot, gate_own, up_own, down_own, after,
    back, mix, grads, down_came, pay_in, cot_in,
    weights, total, pay_now, cot_now, xs, gs, eo, gi, hid, dgate, dup, disp, comb,
    own, out, sib, ret, mix_now,
    send_first, recv_first, send_fwd, recv_fwd, send_sib, recv_sib, send_chip, recv_chip,
    load_w, load, store, piece_sem, send_down, recv_down,
):
    c, f = lax.axis_index("ctx"), lax.axis_index("fsdp")
    rank = lax.rem(c, 2) * 4 + f
    sibling = (c, flip(f, 1))
    barrier = pltpu.get_barrier_semaphore()
    pl.semaphore_signal(barrier, inc=1, device_id=sibling, device_id_type=MESH)
    for k in range(1, 4):
        pl.semaphore_signal(barrier, inc=1, device_id=other_chip(c, f, k), device_id_type=MESH)
    apart = len(grads.shape) == 5
    if apart:
        pl.semaphore_signal(barrier, inc=1, device_id=(flip(c, 2), f), device_id_type=MESH)
    bring = []
    for m, own_weight in enumerate((gate_own, up_own, down_own)):
        bring.append(pltpu.make_async_copy(own_weight, weights.at[m], load_w.at[m]))
        bring[-1].start()
    pl.semaphore_wait(barrier, 5 if apart else 4)
    sources, landed = (pay, cot), (pay_in, cot_in)

    def push(k, a):
        slot = 1 if k == 0 else 2 * k
        return pltpu.make_async_remote_copy(
            sources[a], landed[a].at[slot - 1], send_first.at[k, a], recv_first.at[k, a],
            device_id=sibling if k == 0 else other_chip(c, f, k), device_id_type=MESH,
        )

    def forward(k, a):
        return pltpu.make_async_remote_copy(
            landed[a].at[2 * k - 1], landed[a].at[2 * k], send_fwd.at[k - 1, a], recv_fwd.at[k - 1, a],
            device_id=sibling, device_id_type=MESH,
        )

    def to_sibling(k):
        return pltpu.make_async_remote_copy(
            out.at[lax.rem(k, 2)], sib.at[k], send_sib.at[k], recv_sib.at[k],
            device_id=sibling, device_id_type=MESH,
        )

    def to_chip(k):
        return pltpu.make_async_remote_copy(
            sib.at[k], ret.at[k - 1], send_chip.at[k - 1], recv_chip.at[k - 1],
            device_id=other_chip(c, f, k), device_id_type=MESH,
        )

    def store_mix(k, s):
        return pltpu.make_async_copy(mix_now.at[s], mix.at[2 * k + s], store.at[s])

    for k, a in ((0, 0), (0, 1), (1, 0), (2, 0), (1, 1), (2, 1), (3, 0), (3, 1)):
        push(k, a).start()

    def clear(i, carry):
        total[lax.div(i, OWN), lax.rem(i, OWN)] = jnp.zeros((FF, D), F32)
        return carry

    lax.fori_loop(0, 3 * OWN, clear, 0)
    lane = lax.broadcasted_iota(jnp.int32, (BLOCK, 128), 1)
    wide = lax.broadcasted_iota(jnp.int32, (BLOCK, 2 * BLOCK), 1).astype(F32)
    both = lax.broadcasted_iota(jnp.int32, (BLOCK, OWN * CAP), 1)

    def chunk(k, carry):
        now = (pay_now, cot_now)

        def fetch(a, s, source):
            copy = pltpu.make_async_copy(source, now[a].at[s], load.at[a, s])
            copy.start()
            return copy

        @pl.when(k == 0)
        def _():
            copies = [fetch(a, 0, sources[a]) for a in range(2)]
            for a in range(2):
                push(0, a).wait_recv()
            copies += [fetch(a, 1, landed[a].at[0]) for a in range(2)]
            for copy in copies:
                copy.wait()
            for copy in bring:
                copy.wait()

        @pl.when(k > 0)
        def _():
            for a in range(2):
                pltpu.make_async_remote_copy(
                    sources[a], landed[a].at[2 * k - 1], send_first.at[k, a], recv_first.at[k, a],
                    device_id=other_chip(c, f, k), device_id_type=MESH,
                ).wait_recv()
                forward(k, a).start()
            copies = [fetch(a, 0, landed[a].at[2 * k - 1]) for a in range(2)]
            for a in range(2):
                forward(k, a).wait_recv()
            copies += [fetch(a, 1, landed[a].at[2 * k]) for a in range(2)]
            for copy in copies:
                copy.wait()

        for g in range(GROUPS):
            s, at = g // 2, (g % 2) * BLOCK
            tail = pay_now[s, at : at + BLOCK, D:].astype(F32)

            def column(index):
                return jnp.sum(jnp.where(lane == index, tail, 0.0), axis=1, keepdims=True)

            table = jnp.zeros((BLOCK, 2 * BLOCK), F32)
            gated = jnp.zeros((BLOCK, 2 * BLOCK), F32)
            for e in range(OWN):
                place = column(rank * OWN + e)
                place = jnp.where(place < 0.0, -1000.0, place + e * CAP)
                here = wide == place
                table = jnp.where(here, 1.0, table)
                gated = jnp.where(here, column(EXPERTS + rank * OWN + e), gated)
            table, gated = table.astype(BF16), gated.astype(BF16)
            disp[g] = table
            comb[g] = gated
            for weight, source, keep in (
                (table, pay_now[s, at : at + BLOCK, :D], xs),
                (gated, cot_now[s, at : at + BLOCK], gs),
            ):
                moved = lax.dot_general(
                    weight, source, (((0,), (0,)), ((), ())), preferred_element_type=F32
                ).astype(BF16)
                for e in range(OWN):
                    keep[e, g * CAP : (g + 1) * CAP] = moved[e * CAP : (e + 1) * CAP]

        def expert(e, carry):
            at = pl.multiple_of(e * CAP, 16)
            gate_pre = jnp.dot(xs[e], weights[0, e], preferred_element_type=F32)
            up_pre = jnp.dot(xs[e], weights[1, e], preferred_element_type=F32)
            sigmoid = 1.0 / (1.0 + jnp.exp(-gate_pre))
            activated = gate_pre * sigmoid
            hidden = (activated * up_pre).astype(BF16)
            hid[e] = hidden
            made = lax.dot_general(
                hidden, weights[2, e], (((1,), (1,)), ((), ())), preferred_element_type=F32
            ).astype(BF16)
            for g in range(GROUPS):
                eo[pl.ds(pl.multiple_of(g * OWN * CAP + at, 16), CAP)] = made[g * CAP : (g + 1) * CAP]
            grad_hidden = jnp.dot(gs[e], weights[2, e], preferred_element_type=F32)
            slope = sigmoid * (1.0 + gate_pre * (1.0 - sigmoid))
            grad_gate = (grad_hidden * up_pre * slope).astype(BF16)
            grad_up = (grad_hidden * activated).astype(BF16)
            dgate[e] = grad_gate
            dup[e] = grad_up
            made = lax.dot_general(
                grad_gate, weights[0, e], (((1,), (1,)), ((), ())), preferred_element_type=F32
            )
            made = made + lax.dot_general(
                grad_up, weights[1, e], (((1,), (1,)), ((), ())), preferred_element_type=F32
            )
            made = made.astype(BF16)
            for g in range(GROUPS):
                gi[pl.ds(pl.multiple_of(g * OWN * CAP + at, 16), CAP)] = made[g * CAP : (g + 1) * CAP]
            return carry

        lax.fori_loop(0, OWN, expert, 0)

        @pl.when(k > 0)
        def _():
            for s in range(2):
                store_mix(k - 1, s).wait()

        @pl.when(k > 1)
        def _():
            to_sibling(k - 2).wait_send()

        parity = lax.rem(k, 2)
        for g in range(GROUPS):
            s, at = g // 2, (g % 2) * BLOCK
            slots = pl.ds(g * OWN * CAP, OWN * CAP)
            made = eo[slots]
            mix_now[s, at : at + BLOCK] = jnp.dot(
                comb[g][:, : OWN * CAP], made, preferred_element_type=F32
            ).astype(BF16)
            table = disp[g][:, : OWN * CAP]
            grad_mid = jnp.dot(table, gi[slots], preferred_element_type=F32).astype(BF16)
            met = lax.dot_general(
                cot_now[s, at : at + BLOCK], made, (((1,), (1,)), ((), ())), preferred_element_type=F32
            ) * table.astype(F32)
            values = jnp.zeros((BLOCK, 128), F32)
            for e in range(OWN):
                inside = (both >= e * CAP) & (both < (e + 1) * CAP)
                value = jnp.sum(jnp.where(inside, met, 0.0), axis=1, keepdims=True)
                values = jnp.where(lane == rank * OWN + e, value, values)
            target = own if s == 0 else out
            target[parity, at : at + BLOCK, :D] = grad_mid
            target[parity, at : at + BLOCK, D:] = values.astype(BF16)
        to_sibling(k).start()
        for s in range(2):
            store_mix(k, s).start()

        def weight_grads(e, carry):
            for m, (left, right) in enumerate(((dgate, xs), (dup, xs), (hid, gs))):
                total[m, e] += lax.dot_general(
                    left[e], right[e], (((0,), (0,)), ((), ())), preferred_element_type=F32
                )
            return carry

        lax.fori_loop(0, OWN, weight_grads, 0)
        to_sibling(k).wait_recv()
        sib[k] = (sib[k].astype(F32) + own[parity].astype(F32)).astype(BF16)

        @pl.when(k > 0)
        def _():
            to_chip(k).start()

        return carry

    lax.fori_loop(0, 4, chunk, 0)
    for s in range(2):
        store_mix(3, s).wait()
    stages = (eo, gi)
    pending = []
    if apart:
        half = replicas // 2
        down_first = pltpu.make_async_remote_copy(
            grads.at[2, pl.ds((1 - lax.rem(lax.div(c, 2), 2)) * half, half)], down_came,
            send_down, recv_down, device_id=(flip(c, 2), f), device_id_type=MESH,
        )
    for i in range(3 * OWN):
        m, e = (2, 0, 1)[i // OWN], i % OWN
        if i >= 2:
            for copy in pending[i - 2]:
                copy.wait()
        if i == OWN + 1 and apart:
            down_first.start()
        stages[i % 2][:FF] = total[m, e].astype(BF16)
        pending.append([])
        if not apart:
            pending[i].append(
                pltpu.make_async_copy(stages[i % 2].at[:FF], grads.at[m, e], piece_sem.at[i % 2, 0])
            )
        else:
            width = D // replicas
            for at, plane in enumerate(plane_order(replicas)):
                pending[i].append(
                    pltpu.make_async_copy(
                        stages[i % 2].at[:FF, plane * width : (plane + 1) * width],
                        grads.at[m, at, e],
                        piece_sem.at[i % 2, at],
                    )
                )
        for copy in pending[i]:
            copy.start()
    for copy in pending[-2] + pending[-1]:
        copy.wait()
    for k in (2, 3):
        to_sibling(k).wait_send()
    for k in range(4):
        for a in range(2):
            push(k, a).wait_send()
            if k:
                forward(k, a).wait_send()
    for k in range(1, 4):
        to_chip(k).wait_recv()
    back[...] = (sib[0].astype(F32) + ret[0].astype(F32)) + (ret[1].astype(F32) + ret[2].astype(F32))
    for k in range(1, 4):
        to_chip(k).wait_send()
    if apart:
        down_first.wait()


def run_experts(cid, replicas, pay, cot, owns, after):
    width = D // replicas
    apart = width % 128 == 0
    tokens = SEQS * BLOCK
    anywhere = pl.BlockSpec(memory_space=pl.ANY)
    inside = pl.BlockSpec(memory_space=pltpu.VMEM)
    dma = pltpu.SemaphoreType.DMA
    back, mix, grads, down_came, _, _ = pl.pallas_call(
        functools.partial(experts_kernel, replicas),
        name="experts",
        out_shape=[
            jax.ShapeDtypeStruct((tokens, PAY), F32),
            jax.ShapeDtypeStruct((RANKS, tokens, D), BF16),
            jax.ShapeDtypeStruct((3, replicas, OWN, FF, width) if apart else (3, OWN, FF, D), BF16),
            jax.ShapeDtypeStruct((replicas // 2, OWN, FF, width) if apart else (8, 128), BF16),
            jax.ShapeDtypeStruct((RANKS - 1, tokens, PAY), BF16),
            jax.ShapeDtypeStruct((RANKS - 1, tokens, D), BF16),
        ],
        in_specs=[anywhere] * 6,
        out_specs=[inside] + [anywhere] * 5,
        scratch_shapes=[
            pltpu.VMEM((3, OWN, D, FF), BF16),
            pltpu.VMEM((3, OWN, FF, D), F32),
            pltpu.VMEM((2, tokens, PAY), BF16),
            pltpu.VMEM((2, tokens, D), BF16),
            pltpu.VMEM((OWN, ROWS, D), BF16),
            pltpu.VMEM((OWN, ROWS, D), BF16),
            pltpu.VMEM((OWN * ROWS, D), BF16),
            pltpu.VMEM((OWN * ROWS, D), BF16),
            pltpu.VMEM((OWN, ROWS, FF), BF16),
            pltpu.VMEM((OWN, ROWS, FF), BF16),
            pltpu.VMEM((OWN, ROWS, FF), BF16),
            pltpu.VMEM((GROUPS, BLOCK, 2 * BLOCK), BF16),
            pltpu.VMEM((GROUPS, BLOCK, 2 * BLOCK), BF16),
            pltpu.VMEM((2, tokens, PAY), BF16),
            pltpu.VMEM((2, tokens, PAY), BF16),
            pltpu.VMEM((4, tokens, PAY), BF16),
            pltpu.VMEM((3, tokens, PAY), BF16),
            pltpu.VMEM((2, tokens, D), BF16),
            dma((4, 2)), dma((4, 2)), dma((3, 2)), dma((3, 2)),
            dma((4,)), dma((4,)), dma((3,)), dma((3,)),
            dma((4,)), dma((2, 2)), dma((2,)), dma((2, replicas)), dma, dma,
        ],
        compiler_params=pltpu.CompilerParams(
            collective_id=cid, has_side_effects=True, vmem_limit_bytes=63 << 20
        ),
        cost_estimate=lasting(110),
    )(pay, cot, *owns, after)
    if not apart:
        grads = grads.reshape(3, OWN, FF, replicas, width).transpose(0, 3, 1, 2, 4)
        grads = grads[:, jnp.array(plane_order(replicas))]
    return back, mix, grads, down_came, apart


def half_masks(dtype):
    lane = lax.broadcasted_iota(jnp.int32, (1, 2 * HEAD_SIZE), 1)
    low = (lane < HEAD_SIZE).astype(F32)
    return low.astype(dtype), (1.0 - low).astype(dtype)


def allowed_at(block, step, segq, keycode):
    token = block * BLOCK + lax.broadcasted_iota(jnp.int32, (BLOCK, KEYS), 0)
    key = step * KEYS + lax.broadcasted_iota(jnp.int32, (BLOCK, KEYS), 1)
    return ((segq == keycode) & (key < token)) | (key == token)


SMALL = 32


def turn(field, cosine, sine):
    half = HEAD_SIZE // 2
    lane = lax.broadcasted_iota(jnp.int32, field.shape, field.ndim - 1)
    up = pltpu.roll(field, 2 * HEAD_SIZE - half, field.ndim - 1)
    down = pltpu.roll(field, half, field.ndim - 1)
    return field * cosine + jnp.where(lax.rem(lane, HEAD_SIZE) < half, -up, down) * sine


def attention_forward_kernel(
    parts, n_ctx, tok, small, w_q, w_k, w_v, w_o, near_q, near_k, near_v, pack0, pack1, pack2, cos_ref, sin_ref, seg_ref, code_ref,
    normed, small_all, q_full, k_full, v_full, q_ref, kv_ref, full_ref, log_ref, o_back, o_full,
    gate_own, up_own, down_own,
    acc, q_pack, kv_pack, o_buf, own_buf,
    send_w, recv_w, send_s, recv_s, send_e, recv_e, send_q, recv_q, send_kv, recv_kv, send_o, recv_o, here,
):
    c, f = lax.axis_index("ctx"), lax.axis_index("fsdp")
    head, part, pair = lax.div(c, parts), lax.rem(c, parts), lax.rem(c, 2)
    rows = D // 4
    half = rows // 2
    wide = 2 * HEAD_SIZE
    barrier = pltpu.get_barrier_semaphore()
    peers = [(i, 0) for i in range(1, n_ctx)] + [(0, k) for k in range(1, 4)]
    for dc, df in peers:
        pl.semaphore_signal(
            barrier, inc=1, device_id=(flip(c, dc), flip(f, df)), device_id_type=MESH
        )
    shards = (w_q, w_k, w_v, w_o)
    fulls = (q_full, k_full, v_full, o_full)
    packs, owns = (pack0, pack1, pack2), (gate_own, up_own, down_own)
    my_rows = pl.ds(pl.multiple_of(f * rows, rows), rows)
    local = [pltpu.make_async_copy(shards[a], fulls[a].at[f], here.at[a]) for a in range(4)]
    local += [pltpu.make_async_copy(small, small_all.at[f], here.at[4])]
    local += [pltpu.make_async_copy(packs[m].at[f], own_buf.at[m], here.at[5 + m]) for m in range(3)]
    for copy in local:
        copy.start()
    pl.semaphore_wait(barrier, len(peers))
    near = pl.ds(pl.multiple_of(pair * half, half), half)
    far = pl.ds(pl.multiple_of((1 - pair) * half, half), half)
    sibling, over_x, over_pair = (c, flip(f, 1)), (c, flip(f, 2)), (flip(c, 1), f)
    nears = (near_q, near_k, near_v)
    crossed = [
        pltpu.make_async_copy(nears[a], fulls[a].at[flip(f, 2), near], here.at[11 + a]) for a in range(3)
    ]
    for copy in crossed:
        copy.start()

    def weight(a, kind):
        beyond = flip(f, 2)
        brought = nears[a] if a < 3 else fulls[a].at[beyond, near]
        source, target, device = (
            (shards[a], fulls[a].at[f], sibling),
            (shards[a].at[near], fulls[a].at[f, near], over_x),
            (brought, fulls[a].at[beyond, near], sibling),
            (brought, fulls[a].at[beyond, near], over_pair),
            (fulls[a].at[beyond, far], fulls[a].at[beyond, far], sibling),
        )[kind]
        return pltpu.make_async_remote_copy(
            source, target, send_w.at[a, kind], recv_w.at[a, kind], device_id=device, device_id_type=MESH
        )

    smalls = [
        pltpu.make_async_remote_copy(
            small, small_all.at[f], send_s.at[i - 1], recv_s.at[i - 1],
            device_id=(c, flip(f, i)), device_id_type=MESH,
        )
        for i in range(1, 4)
    ]
    for copy in smalls:
        copy.start()
    for a in range(4):
        for kind in (3, 0, 2) if a < 3 else (1, 0):
            weight(a, kind).start()
    experts = [
        pltpu.make_async_remote_copy(
            packs[m].at[flip(f, i)], owns[m].at[:, my_rows], send_e.at[i - 1, m], recv_e.at[i - 1, m],
            device_id=(c, flip(f, i)), device_id_type=MESH,
        )
        for m in range(3)
        for i in range(1, 4)
    ]
    for copy in experts:
        copy.start()

    x = tok[...].astype(F32)
    scale = lax.rsqrt(jnp.mean(x * x, axis=1, keepdims=True) + EPS)
    for copy in smalls:
        copy.wait_recv()
    local[4].wait()
    for b in range(4):
        columns = slice(b * rows, (b + 1) * rows)
        normed[:, columns] = (x[:, columns] * scale * small_all[b, :1].astype(F32)).astype(BF16)

    def project(b, first):
        block = normed[:, pl.ds(pl.multiple_of(b * rows, rows), rows)]
        at = 0
        for a in range(3):
            width = fulls[a].shape[2]
            made = jnp.dot(block, fulls[a][b], preferred_element_type=F32)
            acc[:, at : at + width] = made if first else acc[:, at : at + width] + made
            at += width

    for a in range(3):
        local[a].wait()
    stores = []
    for m in range(3):
        local[5 + m].wait()
        stores.append(pltpu.make_async_copy(own_buf.at[m], owns[m].at[:, my_rows], here.at[5 + m]))
        stores[m].start()
    project(f, True)
    for a in range(3):
        weight(a, 0).wait_recv()
    project(flip(f, 1), False)
    for a in range(3):
        weight(a, 3).wait_recv()
        weight(a, 4).start()
        crossed[a].wait()
    project(flip(f, 2), False)
    for a in range(3):
        weight(a, 2).wait_recv()
        weight(a, 4).wait_recv()
    project(flip(f, 3), False)

    lane = lax.broadcasted_iota(jnp.int32, (BLOCK, wide), 1)
    low = lane < HEAD_SIZE
    cosine, sine = cos_ref[...], sin_ref[...]
    for m in range((QUERY_HEADS + 2 * KEY_VALUE_HEADS) // 2):
        pieces = []
        for s in range(SEQS):
            piece = acc[s * BLOCK : (s + 1) * BLOCK, m * wide : (m + 1) * wide]
            pieces.append(turn(piece, cosine, sine) if m < (QUERY_HEADS + KEY_VALUE_HEADS) // 2 else piece)
        even = jnp.where(low, pieces[0], pltpu.roll(pieces[1], HEAD_SIZE, 1)).astype(BF16)
        odd = jnp.where(low, pltpu.roll(pieces[0], HEAD_SIZE, 1), pieces[1]).astype(BF16)
        for h, value in ((2 * m, even), (2 * m + 1, odd)):
            if h < QUERY_HEADS:
                q_pack[h // REP, h % REP] = value
            else:
                h -= QUERY_HEADS
                kv_pack[h % KEY_VALUE_HEADS, h // KEY_VALUE_HEADS] = value

    q_stays = pltpu.make_async_copy(q_pack.at[head], q_ref.at[head], here.at[8])
    kv_stays = pltpu.make_async_copy(kv_pack.at[head], kv_ref.at[c], here.at[9])
    q_stays.start()
    kv_stays.start()
    to_heads = []
    for i in range(1, n_ctx):
        peer = flip(c, i)
        moves = [(kv_pack.at[lax.div(peer, parts)], kv_ref.at[c], send_kv.at[i - 1], recv_kv.at[i - 1])]
        if i % parts == 0:
            number = i // parts - 1
            moves.append(
                (q_pack.at[lax.div(peer, parts)], q_ref.at[head], send_q.at[number], recv_q.at[number])
            )
        for source, target, sent, came in moves:
            copy = pltpu.make_async_remote_copy(
                source, target, sent, came, device_id=(peer, f), device_id_type=MESH
            )
            copy.start()
            to_heads.append(copy)
    weight(3, 1).wait_recv()
    weight(3, 2).start()
    weight(3, 3).start()
    q_stays.wait()
    kv_stays.wait()
    for copy in to_heads:
        copy.wait_recv()

    count = REP * BLOCK
    halves = half_masks(BF16)
    across = lax.broadcasted_iota(jnp.int32, (count, wide), 1)

    def out_back(j):
        return pltpu.make_async_remote_copy(
            o_buf.at[j], o_back.at[head], send_o.at[j], recv_o.at[head],
            device_id=(j * parts + part, f), device_id_type=MESH,
        )

    def out_stays(j):
        return pltpu.make_async_copy(o_buf.at[j], o_back.at[head], here.at[10])

    def one_block(j, nothing):
        block = j * parts + part
        q = q_ref[j].reshape(count, wide)
        queries = [q * half for half in halves]

        def step(number, carry):
            k = kv_ref[pl.ds(2 * number, 2), 0].reshape(KEYS, wide)
            v = kv_ref[pl.ds(2 * number, 2), 1].reshape(KEYS, wide)
            codes = code_ref[number]
            after = []
            for s in range(SEQS):
                largest, total, out = carry[s]
                mask = allowed_at(block, number, seg_ref[j, s], codes[s : s + 1])
                scores = lax.dot_general(
                    queries[s], k, (((1,), (1,)), ((), ())), preferred_element_type=F32
                )
                scores = jnp.where(mask[None], scores.reshape(REP, BLOCK, KEYS) * SCALE, MASKED)
                scores = scores.reshape(count, KEYS)
                new = jnp.maximum(largest, jnp.max(scores, axis=1, keepdims=True))
                probs = jnp.exp(scores - new)
                shrink = jnp.exp(largest - new)
                total = total * shrink + jnp.sum(probs, axis=1, keepdims=True)
                out = out * shrink + jnp.dot(probs.astype(BF16), v, preferred_element_type=F32)
                after.append((new, total, out))
            return tuple(after)

        start = (
            jnp.full((count, 1), MASKED, F32),
            jnp.zeros((count, 1), F32),
            jnp.zeros((count, wide), F32),
        )
        done = lax.fori_loop(0, lax.div(block, 2) + 1, step, (start,) * SEQS)
        outs, logs = [], []
        for largest, total, out in done:
            outs.append(out / total)
            logs.append(jnp.broadcast_to(largest + jnp.log(total), (count, wide)))
        out = jnp.where(across < HEAD_SIZE, outs[0], outs[1])
        full_ref[j] = out.reshape(REP, BLOCK, wide)
        log_ref[j] = jnp.where(across < HEAD_SIZE, logs[0], logs[1]).reshape(REP, BLOCK, wide)
        o_buf[j] = out.astype(BF16).reshape(REP, BLOCK, wide)

        @pl.when(j != head)
        def _():
            out_back(j).start()

        @pl.when(j == head)
        def _():
            out_stays(j).start()

        return nothing

    lax.fori_loop(0, KEY_VALUE_HEADS, one_block, 0)
    weight(3, 3).wait_recv()
    weight(3, 4).start()

    def came_out(h, nothing):
        @pl.when(h != head)
        def _():
            pltpu.make_async_remote_copy(
                o_buf.at[h], o_back.at[h], send_o.at[h], recv_o.at[h],
                device_id=(h * parts + part, f), device_id_type=MESH,
            ).wait()

        @pl.when(h == head)
        def _():
            out_stays(h).wait()

        return nothing

    lax.fori_loop(0, KEY_VALUE_HEADS, came_out, 0)
    for kind in (0, 2, 4):
        weight(3, kind).wait_recv()
    local[3].wait()
    for copy in stores:
        copy.wait()
    for copy in experts:
        copy.wait()
    for copy in smalls + to_heads:
        copy.wait_send()
    for a in range(4):
        for kind in (0, 2, 3, 4) if a < 3 else range(5):
            weight(a, kind).wait_send()


def attention_forward(
    cid, parts, n_ctx, tok, small, w_q, w_k, w_v, w_o, nears, packs, cosine, sine, segq, codes
):
    wide = 2 * HEAD_SIZE
    anywhere = pl.BlockSpec(memory_space=pl.ANY)
    inside = pl.BlockSpec(memory_space=pltpu.VMEM)
    dma = pltpu.SemaphoreType.DMA
    heads = (KEY_VALUE_HEADS, REP, BLOCK, wide)
    keys = (n_ctx, 2, BLOCK, wide)
    others = max(n_ctx // parts - 1, 1)
    columns = w_q.shape[1] + w_k.shape[1] + w_v.shape[1]
    own = jax.ShapeDtypeStruct((OWN, D, FF), BF16)

    def full(x):
        return jax.ShapeDtypeStruct((4,) + x.shape, BF16)

    return pl.pallas_call(
        functools.partial(attention_forward_kernel, parts, n_ctx),
        name="attention_forward",
        out_shape=[
            jax.ShapeDtypeStruct(tok.shape, BF16),
            full(small), full(w_q), full(w_k), full(w_v),
            jax.ShapeDtypeStruct(heads, BF16),
            jax.ShapeDtypeStruct(keys, BF16),
            jax.ShapeDtypeStruct(heads, F32),
            jax.ShapeDtypeStruct(heads, F32),
            jax.ShapeDtypeStruct(heads, BF16),
            full(w_o), own, own, own,
        ],
        in_specs=[inside] + [anywhere] * 11 + [inside] * 4,
        out_specs=[inside] * 9 + [anywhere, inside] + [anywhere] * 3,
        scratch_shapes=[
            pltpu.VMEM((SEQS * BLOCK, columns), F32),
            pltpu.VMEM(heads, BF16),
            pltpu.VMEM((KEY_VALUE_HEADS, 2, BLOCK, wide), BF16),
            pltpu.VMEM(heads, BF16),
            pltpu.VMEM((3,) + packs[0].shape[1:], BF16),
            dma((4, 5)), dma((4, 5)), dma((3,)), dma((3,)), dma((3, 3)), dma((3, 3)),
            dma((others,)), dma((others,)), dma((n_ctx - 1,)), dma((n_ctx - 1,)),
            dma((KEY_VALUE_HEADS,)), dma((KEY_VALUE_HEADS,)), dma((14,)),
        ],
        compiler_params=pltpu.CompilerParams(
            collective_id=cid, has_side_effects=True, vmem_limit_bytes=56 << 20
        ),
        cost_estimate=lasting(130),
    )(tok, small, w_q, w_k, w_v, w_o, *nears, *packs, cosine, sine, segq, codes)


def turn_back(field, cosine, sine):
    half = HEAD_SIZE // 2
    lane = lax.broadcasted_iota(jnp.int32, field.shape, field.ndim - 1)
    up = pltpu.roll(field, 2 * HEAD_SIZE - half, field.ndim - 1)
    down = pltpu.roll(field, half, field.ndim - 1)
    turned = jnp.where(lax.rem(lane, HEAD_SIZE) < half, -up, down)
    return field * cosine - turned * sine


def attention_backward_kernel(
    parts, n_ctx, early, g_own, q_ref, kv_ref, seg_ref, code_ref, full_ref, log_ref, cos_ref, sin_ref,
    tok, gain, resid_grad, residual, grads, down_in, mix, output_part, tokens_all, q_full, k_full, v_full,
    input_grad, layer_out, gain_grad, output_sum, gate_first, gate_keep, gate_came, gate_other, down_keep, down_came,
    mix_core, mix_in, head_in, g_ref, total, kept, came, dq_ref, dkv_ref, dq_back, dkv_back, w_q, w_k, w_v, grad_qkv, grad_in,
    token_buf, field, head_acc, head_out, head_core, head_x, output_keep, output_came, output_x, output_pair,
    send_g, recv_g, send_q, recv_q, send_kv, recv_kv, send_mix, recv_mix, send_half, recv_half, here,
    send_out, recv_out, send_head, recv_head, load_t,
):
    c, f = lax.axis_index("ctx"), lax.axis_index("fsdp")
    head, part = lax.div(c, parts), lax.rem(c, parts)
    rows = REP * BLOCK
    wide = 2 * HEAD_SIZE
    barrier = pltpu.get_barrier_semaphore()
    peers = [(i, k) for i in range(n_ctx) for k in range(4) if i or k]
    for dc, df in peers:
        pl.semaphore_signal(
            barrier, inc=1, device_id=(flip(c, dc), flip(f, df)), device_id_type=MESH
        )
    pair, x_bit, core_bit = lax.rem(c, 2), lax.div(f, 2), lax.rem(f, 2)
    loads = [
        pltpu.make_async_copy(source, target, here.at[5 + i])
        for i, (source, target) in enumerate(
            (
                (q_full, w_q), (k_full, w_k), (v_full, w_v),
                (output_part.at[:, :, :, core_bit], output_keep),
            )
        )
    ]

    def bring(b):
        return pltpu.make_async_copy(
            tokens_all.at[b], token_buf.at[lax.rem(b, 2)], load_t.at[lax.rem(b, 2)]
        )

    for copy in loads[1:]:
        copy.start()
    first = pltpu.make_async_copy(g_own.at[head], g_ref.at[head], here.at[0])
    first.start()
    pl.semaphore_wait(barrier, len(peers))
    to_heads = []
    for number, i in enumerate(range(parts, n_ctx, parts)):
        to_heads.append(
            pltpu.make_async_remote_copy(
                g_own.at[lax.div(flip(c, i), parts)], g_ref.at[head],
                send_g.at[number], recv_g.at[number],
                device_id=(flip(c, i), f), device_id_type=MESH,
            )
        )
        to_heads[-1].start()
    half = grads.shape[1] // 2
    quarter = half // 2
    mine = lax.rem(lax.div(c, 2), 2)
    second = lax.rem(lax.div(c, 4), 2)

    def halving(matrix, target, number):
        return pltpu.make_async_remote_copy(
            grads.at[matrix, pl.ds((1 - mine) * half, half)], target,
            send_half.at[number], recv_half.at[number],
            device_id=(flip(c, 2), f), device_id_type=MESH,
        )

    down_halving, gate_halving = halving(2, came, 0), halving(0, gate_first, 1)
    arriving = pltpu.make_async_copy(down_in, came, here.at[10]) if early else down_halving
    arriving.start()
    keeping = pltpu.make_async_copy(grads.at[2, pl.ds(mine * half, half)], kept, here.at[3])
    keeping.start()
    output_stages = [
        pltpu.make_async_remote_copy(
            source, target, send_out.at[i], recv_out.at[i], device_id=device, device_id_type=MESH
        )
        for i, (source, target, device) in enumerate(
            (
                (output_part.at[:, :, :, 1 - core_bit], output_came, (c, flip(f, 1))),
                (output_keep.at[:, :, 1 - x_bit], output_x, (c, flip(f, 2))),
                (output_x.at[:, 1 - pair], output_pair, (flip(c, 1), f)),
            )
        )
    ]
    output_stages[0].start()
    to_core = [
        pltpu.make_async_remote_copy(
            mix.at[2 * k + 1], mix_core.at[k], send_mix.at[k], recv_mix.at[k],
            device_id=(c, flip(f, 1)), device_id_type=MESH,
        )
        for k in range(4)
    ]
    for copy in to_core:
        copy.start()

    def plus(mine, came):
        return (mine.astype(F32) + came.astype(F32)).astype(BF16)

    def second_halving(keep, target, number, later=None):
        def add(i, nothing):
            at, e = lax.div(i, OWN), lax.rem(i, OWN)
            kept[at, e] = plus(kept[at, e], came[at, e])
            return nothing

        lax.fori_loop(0, half * OWN, add, 0)
        source = kept.at[pl.ds((1 - second) * quarter, quarter)]
        if later is not None:
            source, target = source.at[:, 0], target.at[:, 0]
            rest = pltpu.make_async_copy(
                kept.at[pl.ds((1 - second) * quarter, quarter), 1], later, here.at[3]
            )
            rest.start()
            rest.wait()
        going = pltpu.make_async_remote_copy(
            source, target, send_half.at[number], recv_half.at[number],
            device_id=(flip(c, 4), f), device_id_type=MESH,
        )
        going.start()
        staying = pltpu.make_async_copy(kept.at[pl.ds(second * quarter, quarter)], keep, here.at[4])
        staying.start()
        return going, staying

    if early:
        keeping.wait()
        arriving.wait()
        down_second, leaving = second_halving(down_keep, down_came, 2)
    gate_halving.start()
    shares = w_q.at[:, pl.ds(0, SEQS * BLOCK)]
    for k in range(4):
        pair_in = [
            pltpu.make_async_copy(mix.at[2 * k], token_buf.at[0], load_t.at[0]),
            pltpu.make_async_copy(mix_core.at[k], token_buf.at[1], load_t.at[1]),
        ]
        pair_in[0].start()
        to_core[k].wait_recv()
        pair_in[1].start()
        for copy in pair_in:
            copy.wait()
        shares[k] = plus(token_buf[0], token_buf[1])
    own_share = pltpu.make_async_copy(shares.at[0], mix_in.at[0], here.at[5])
    own_share.start()
    returns = [
        pltpu.make_async_remote_copy(
            shares.at[k], mix_in.at[k], send_mix.at[3 + k], recv_mix.at[3 + k],
            device_id=(flip(c, k // 2), flip(f, 2 * (k % 2))), device_id_type=MESH,
        )
        for k in range(1, 4)
    ]
    for copy in returns:
        copy.start()
    for b in range(2):
        bring(b).start()
    total[...] = jnp.zeros_like(total)
    first.wait()
    for copy in to_heads:
        copy.wait_recv()
    halves = half_masks(BF16)
    lane = lax.broadcasted_iota(jnp.int32, (rows, wide), 1)

    def query_back(j):
        return pltpu.make_async_remote_copy(
            dq_ref.at[j], dq_back.at[head], send_q.at[j], recv_q.at[head],
            device_id=(j * parts + part, f), device_id_type=MESH,
        )

    def key_back(b):
        return pltpu.make_async_remote_copy(
            dkv_ref.at[b], dkv_back.at[c], send_kv.at[b], recv_kv.at[c],
            device_id=(b, f), device_id_type=MESH,
        )

    def query_stays(j):
        return pltpu.make_async_copy(dq_ref.at[j], dq_back.at[head], here.at[1])

    def key_stays(b):
        return pltpu.make_async_copy(dkv_ref.at[b], dkv_back.at[c], here.at[2])

    def one_block(j, nothing):
        block = j * parts + part
        q = q_ref[j].reshape(rows, wide)
        g = g_ref[j].reshape(rows, wide)
        queries = [q * half for half in halves]
        partial = [g * half for half in halves]
        product = g.astype(F32) * full_ref[j].reshape(rows, wide)
        logs = log_ref[j].reshape(rows, wide)
        log_total = [logs[:, :1], logs[:, HEAD_SIZE : HEAD_SIZE + 1]]
        inner = [jnp.sum(product * half, axis=1, keepdims=True) for half in half_masks(F32)]

        def step(number, carry):
            k = kv_ref[pl.ds(2 * number, 2), 0].reshape(KEYS, wide)
            v = kv_ref[pl.ds(2 * number, 2), 1].reshape(KEYS, wide)
            codes = code_ref[number]
            after = []
            dk = jnp.zeros((KEYS, wide), F32)
            dv = jnp.zeros((KEYS, wide), F32)
            for s in range(SEQS):
                mask = allowed_at(block, number, seg_ref[j, s], codes[s : s + 1])
                scores = lax.dot_general(
                    queries[s], k, (((1,), (1,)), ((), ())), preferred_element_type=F32
                )
                scores = jnp.where(mask[None], scores.reshape(REP, BLOCK, KEYS) * SCALE, MASKED)
                probs = jnp.exp(scores.reshape(rows, KEYS) - log_total[s])
                grad_probs = lax.dot_general(
                    partial[s], v, (((1,), (1,)), ((), ())), preferred_element_type=F32
                )
                grad_scores = (probs * (grad_probs - inner[s])).astype(BF16)
                dv = dv + lax.dot_general(
                    probs.astype(BF16), partial[s], (((0,), (0,)), ((), ())), preferred_element_type=F32
                )
                dk = dk + lax.dot_general(
                    grad_scores, queries[s], (((0,), (0,)), ((), ())), preferred_element_type=F32
                )
                after.append(carry[s] + jnp.dot(grad_scores, k, preferred_element_type=F32))
            total[pl.ds(2 * number, 2), 0] += dk.reshape(2, BLOCK, wide)
            total[pl.ds(2 * number, 2), 1] += dv.reshape(2, BLOCK, wide)
            return tuple(after)

        start = jnp.zeros((rows, wide), F32)
        done = lax.fori_loop(0, lax.div(block, 2) + 1, step, (start,) * SEQS)
        dq = (jnp.where(lane < HEAD_SIZE, done[0], done[1]) * SCALE).reshape(REP, BLOCK, wide)
        dq_ref[j] = turn_back(dq, cos_ref[block][None], sin_ref[block][None]).astype(BF16)

        @pl.when(j != head)
        def _():
            query_back(j).start()

        @pl.when(j == head)
        def _():
            query_stays(j).start()

        return nothing

    lax.fori_loop(0, KEY_VALUE_HEADS, one_block, 0)

    def finish(b, nothing):
        dkv_ref[b, 0] = turn_back(total[b, 0] * SCALE, cos_ref[b], sin_ref[b]).astype(BF16)
        dkv_ref[b, 1] = total[b, 1].astype(BF16)

        @pl.when(b != c)
        def _():
            key_back(b).start()

        @pl.when(b == c)
        def _():
            key_stays(b).start()

        return nothing

    lax.fori_loop(0, n_ctx, finish, 0)
    if not early:
        keeping.wait()
        down_halving.wait_recv()
        down_second, leaving = second_halving(down_keep, down_came, 2)

    planes = output_keep.shape[0]

    loads[3].wait()
    output_stages[0].wait_recv()

    def cores(i, nothing):
        r, p, x = lax.div(i, 4), lax.rem(lax.div(i, 2), 2), lax.rem(i, 2)
        output_keep[r, p, x] = plus(output_keep[r, p, x], output_came[r, p, x])
        return nothing

    lax.fori_loop(0, planes * 4, cores, 0)
    output_stages[1].start()

    low = lax.broadcasted_iota(jnp.int32, (BLOCK, wide), 1) < HEAD_SIZE

    def side_by_side(even, odd):
        even, odd = even.astype(F32), odd.astype(F32)
        return (
            jnp.where(low, even, pltpu.roll(odd, HEAD_SIZE, 1)),
            jnp.where(low, pltpu.roll(even, HEAD_SIZE, 1), odd),
        )

    head_acc[...] = jnp.zeros_like(head_acc)

    def head_weights(b, nothing):
        bring(b).wait()
        block = token_buf[lax.rem(b, 2)]
        wide_block = block.astype(F32)
        scales = lax.rsqrt(jnp.mean(wide_block * wide_block, axis=1, keepdims=True) + EPS)
        j = lax.div(b, parts)
        have = jnp.where(lax.rem(b, parts) == part, 1.0, 0.0)
        heads = [dq_ref[j, r].astype(F32) * have for r in range(REP)] + [dkv_ref[b, 0], dkv_ref[b, 1]]
        heads.append(jnp.zeros((BLOCK, wide), F32))
        for m in range((REP + 3) // 2):
            for s, value in enumerate(side_by_side(heads[2 * m], heads[2 * m + 1])):
                at = slice(s * BLOCK, (s + 1) * BLOCK)
                field[at, m * wide : (m + 1) * wide] = (value * scales[at]).astype(BF16)
        head_acc[...] += lax.dot_general(
            block, field[...], (((0,), (0,)), ((), ())), preferred_element_type=F32
        )

        @pl.when(b + 2 < n_ctx)
        def _():
            bring(b + 2).start()

        return nothing

    lax.fori_loop(0, n_ctx, head_weights, 0)
    slab = D // (n_ctx * 4)
    for d in range(n_ctx * 4):
        head_out[d // 4, d // 2 % 2, d % 2] = head_acc[
            d * slab : (d + 1) * slab, : head_out.shape[4]
        ].astype(BF16)
    head_stages = [
        pltpu.make_async_remote_copy(
            source, target, send_head.at[i], recv_head.at[i], device_id=device, device_id_type=MESH
        )
        for i, (source, target, device) in enumerate(
            (
                (head_out.at[:, :, 1 - core_bit], head_core, (c, flip(f, 1))),
                (head_core.at[:, 1 - x_bit], head_x, (c, flip(f, 2))),
            )
        )
    ]
    head_stages[0].start()
    for copy in returns:
        copy.wait_send()
    own_share.wait()
    loads[0].start()
    down_second.wait_send()
    leaving.wait()
    gate_halving.wait_recv()
    refill = [
        pltpu.make_async_copy(grads.at[0, pl.ds(mine * half, half)], kept, here.at[3]),
        pltpu.make_async_copy(gate_first, came, here.at[10]),
    ]
    for copy in refill:
        copy.start()
    for copy in refill:
        copy.wait()
    gate_second, leaving = second_halving(gate_keep, gate_came, 3, gate_other)

    head_stages[0].wait_recv()

    def head_cores(i, nothing):
        d, x = lax.div(i, 2), lax.rem(i, 2)
        head_core[d, x] = plus(head_out[d, x, core_bit], head_core[d, x])
        return nothing

    lax.fori_loop(0, n_ctx * 2, head_cores, 0)
    head_stages[1].start()

    def came_query(h, nothing):
        @pl.when(h != head)
        def _():
            pltpu.make_async_remote_copy(
                dq_ref.at[h], dq_back.at[h], send_q.at[h], recv_q.at[h],
                device_id=(h * parts + part, f), device_id_type=MESH,
            ).wait()

        @pl.when(h == head)
        def _():
            query_stays(h).wait()

        return nothing

    def came_key(b, nothing):
        @pl.when(b != c)
        def _():
            pltpu.make_async_remote_copy(
                dkv_ref.at[b], dkv_back.at[b], send_kv.at[b], recv_kv.at[b],
                device_id=(b, f), device_id_type=MESH,
            ).wait()

        @pl.when(b == c)
        def _():
            key_stays(b).wait()

        return nothing

    lax.fori_loop(0, KEY_VALUE_HEADS, came_query, 0)
    lax.fori_loop(0, n_ctx, came_key, 0)

    def head_of(h):
        if h < QUERY_HEADS:
            return dq_back[h // REP, h % REP]
        kind, h = (h - QUERY_HEADS) // KEY_VALUE_HEADS, (h - QUERY_HEADS) % KEY_VALUE_HEADS
        value = dkv_back[h * parts, kind]
        if parts > 1:
            value = value.astype(F32)
            for p in range(1, parts):
                value = value + dkv_back[h * parts + p, kind].astype(F32)
        return value

    head_stages[1].wait_recv()

    def head_over_x(d, nothing):
        head_x[d] = plus(head_core[d, x_bit], head_x[d])
        return nothing

    lax.fori_loop(0, n_ctx, head_over_x, 0)
    head_stays = pltpu.make_async_copy(head_x.at[c], head_in.at[c], here.at[9])
    head_stays.start()
    to_all = []
    for i in range(1, n_ctx):
        to_all.append(
            pltpu.make_async_remote_copy(
                head_x.at[flip(c, i)], head_in.at[c], send_head.at[1 + i], recv_head.at[1 + i],
                device_id=(flip(c, i), f), device_id_type=MESH,
            )
        )
        to_all[-1].start()
    for m in range((QUERY_HEADS + 2 * KEY_VALUE_HEADS) // 2):
        for s, value in enumerate(side_by_side(head_of(2 * m), head_of(2 * m + 1))):
            grad_qkv[s * BLOCK : (s + 1) * BLOCK, m * wide : (m + 1) * wide] = value.astype(BF16)
    for copy in loads[:3]:
        copy.wait()
    depth = D // 4
    for b in range(4):
        made, at = 0.0, 0
        for weight in (w_q, w_k, w_v):
            width = weight.shape[2]
            made = made + lax.dot_general(
                grad_qkv[:, at : at + width], weight[b], (((1,), (1,)), ((), ())),
                preferred_element_type=F32,
            )
            at += width
        grad_in[:, b * depth : (b + 1) * depth] = made
    x = tok[...].astype(F32)
    scale = lax.rsqrt(jnp.mean(x * x, axis=1, keepdims=True) + EPS)
    gain_grad[...] = jnp.sum(grad_in[...] * x * scale, axis=0, keepdims=True)
    weighted = grad_in[...] * gain[...]
    input_grad[...] = (
        resid_grad[...]
        + scale * weighted
        - x * (scale * scale * scale) * jnp.mean(weighted * x, axis=1, keepdims=True)
    ).astype(BF16)

    staying = pltpu.make_async_copy(residual, grad_in, here.at[8])
    staying.start()
    staying.wait()

    def share(k):
        return pltpu.make_async_copy(mix_in.at[k], token_buf.at[k % 2], load_t.at[k % 2])

    share(0).start()
    for k in range(4):
        if k < 3:
            returns[k].wait_recv()
            share(k + 1).start()
        share(k).wait()
        grad_in[...] += token_buf[k % 2].astype(F32)
    layer_out[...] = grad_in[...].astype(BF16)

    output_stages[1].wait_recv()

    def over_x(i, nothing):
        r, p = lax.div(i, 2), lax.rem(i, 2)
        output_x[r, p] = plus(output_keep[r, p, x_bit], output_x[r, p])
        return nothing

    lax.fori_loop(0, planes * 2, over_x, 0)
    output_stages[2].start()
    output_stages[2].wait_recv()

    def over_pair(r, nothing):
        output_sum[r] = plus(output_x[r, pair], output_pair[r])
        return nothing

    lax.fori_loop(0, planes, over_pair, 0)
    for copy in to_heads:
        copy.wait_send()
    for copy in to_all + [gate_second, leaving, head_stays]:
        copy.wait()
    down_second.wait_recv()
    for copy in to_core + output_stages + head_stages + [gate_halving] + ([] if early else [down_halving]):
        copy.wait_send()


def attention_backward(
    cid, parts, n_ctx, early, g_own, q, kv, segq, codes, full, logs, cosine, sine,
    tok, gain, resid_grad, residual, grads, down_in, mix, output_part, tokens_all, q_full, k_full, v_full,
):
    wide = 2 * HEAD_SIZE
    anywhere = pl.BlockSpec(memory_space=pl.ANY)
    inside = pl.BlockSpec(memory_space=pltpu.VMEM)
    dma = pltpu.SemaphoreType.DMA
    others = max(n_ctx // parts - 1, 1)
    devices, planes = n_ctx * 4, n_ctx // 2
    slab, head_width = D // devices, (REP + 2) * HEAD_SIZE
    half = (grads.shape[1] // 2,) + grads.shape[2:]
    quarter = (grads.shape[1] // 4,) + grads.shape[2:]
    columns = q_full.shape[2] + k_full.shape[2] + v_full.shape[2]
    return pl.pallas_call(
        functools.partial(attention_backward_kernel, parts, n_ctx, early),
        name="attention_backward",
        out_shape=[
            jax.ShapeDtypeStruct(tok.shape, BF16),
            jax.ShapeDtypeStruct(tok.shape, BF16),
            jax.ShapeDtypeStruct((1, D), F32),
            jax.ShapeDtypeStruct((planes, slab, D), BF16),
            jax.ShapeDtypeStruct(half, BF16),
            jax.ShapeDtypeStruct(quarter, BF16),
            jax.ShapeDtypeStruct(quarter, BF16),
            jax.ShapeDtypeStruct(quarter[:1] + quarter[2:], BF16),
            jax.ShapeDtypeStruct(quarter, BF16),
            jax.ShapeDtypeStruct(quarter, BF16),
            jax.ShapeDtypeStruct((4,) + mix.shape[1:], BF16),
            jax.ShapeDtypeStruct((4,) + mix.shape[1:], BF16),
            jax.ShapeDtypeStruct((n_ctx, slab, head_width), BF16),
        ],
        in_specs=[anywhere] + [inside] * 11 + [anywhere] * 9,
        out_specs=[inside] * 4 + [anywhere] * 9,
        scratch_shapes=[
            pltpu.VMEM(q.shape, BF16),
            pltpu.VMEM((n_ctx, 2, BLOCK, wide), F32),
            pltpu.VMEM(half, BF16),
            pltpu.VMEM(half, BF16),
            pltpu.VMEM(q.shape, BF16),
            pltpu.VMEM(kv.shape, BF16),
            pltpu.VMEM(q.shape, BF16),
            pltpu.VMEM(kv.shape, BF16),
            pltpu.VMEM(q_full.shape, BF16),
            pltpu.VMEM(k_full.shape, BF16),
            pltpu.VMEM(v_full.shape, BF16),
            pltpu.VMEM((SEQS * BLOCK, columns), BF16),
            pltpu.VMEM((SEQS * BLOCK, D), F32),
            pltpu.VMEM((2, SEQS * BLOCK, D), BF16),
            pltpu.VMEM((SEQS * BLOCK, 3 * wide), BF16),
            pltpu.VMEM((D, 3 * wide), F32),
            pltpu.VMEM((n_ctx, 2, 2, slab, head_width), BF16),
            pltpu.VMEM((n_ctx, 2, slab, head_width), BF16),
            pltpu.VMEM((n_ctx, slab, head_width), BF16),
            pltpu.VMEM((planes, 2, 2, slab, D), BF16),
            pltpu.VMEM((planes, 2, 2, slab, D), BF16),
            pltpu.VMEM((planes, 2, slab, D), BF16),
            pltpu.VMEM((planes, slab, D), BF16),
            dma((others,)), dma((others,)), dma((KEY_VALUE_HEADS,)), dma((KEY_VALUE_HEADS,)),
            dma((n_ctx,)), dma((n_ctx,)), dma((RANKS - 1,)), dma((RANKS - 1,)), dma((4,)), dma((4,)),
            dma((11,)), dma((3,)), dma((3,)), dma((n_ctx + 1,)), dma((n_ctx + 1,)), dma((2,)),
        ],
        compiler_params=pltpu.CompilerParams(
            collective_id=cid, has_side_effects=True, vmem_limit_bytes=62 << 20
        ),
        cost_estimate=lasting(125),
    )(
        g_own, q, kv, segq, codes, full, logs, cosine, sine, tok, gain, resid_grad, residual,
        grads, down_in, mix, output_part, tokens_all, q_full, k_full, v_full,
    )


def final_kernel(
    n_ctx, small, output_part, grads, gate_keep, gate_came, gate_other, down_keep, down_came,
    swapped, output_grad, small_sum,
    halves, landed, rest, rest_landed, last, last_landed, turned, output_in, small_in,
    send_half, recv_half, send_deep, recv_deep, send_out, recv_out, send_small, recv_small,
    send_swap, recv_swap, load, stay,
):
    c, f = lax.axis_index("ctx"), lax.axis_index("fsdp")
    me, plane, rank = c * 4 + f, lax.div(c, 2), lax.rem(c, 2) * 4 + f
    planes = n_ctx // 2
    half, quarter = planes // 2, planes // 4
    barrier = pltpu.get_barrier_semaphore()
    peers = [(i, k) for i in range(n_ctx) for k in range(4) if i or k]
    for dc, df in peers:
        pl.semaphore_signal(
            barrier, inc=1, device_id=(flip(c, dc), flip(f, df)), device_id_type=MESH
        )
    first, second = lax.rem(plane, 2), lax.rem(lax.div(plane, 2), 2)
    loads = [
        pltpu.make_async_copy(source, target, load.at[i])
        for i, (source, target) in enumerate(
            (
                (down_keep, rest.at[2]),
                (down_came, rest_landed.at[2]),
                (gate_keep, rest.at[0]),
                (gate_came.at[:, 0], rest_landed.at[0, :, 0]),
                (grads.at[1, pl.ds(first * half, half)], halves),
                (output_part.at[plane], output_in.at[plane]),
                (small.at[me], small_in.at[me]),
            )
        )
    ]
    for copy in loads:
        copy.start()
    pl.semaphore_wait(barrier, len(peers))

    def over(source, target, sent, came, bit):
        return pltpu.make_async_remote_copy(
            source, target, sent, came, device_id=(flip(c, 2 * bit), f), device_id_type=MESH
        )

    up_first = [
        over(
            grads.at[1, pl.ds((1 - first) * half, half), e], landed.at[:, e],
            send_half.at[0, e], recv_half.at[0, e], 1,
        )
        for e in range(OWN)
    ]
    gate_second = over(gate_other, rest_landed.at[0, :, 1], send_half.at[2, 1], recv_half.at[2, 1], 2)
    for copy in [gate_second] + up_first:
        copy.start()
    outputs = []
    for i in range(1, planes):
        outputs.append(
            pltpu.make_async_remote_copy(
                output_part.at[flip(plane, i)], output_in.at[plane], send_out.at[i - 1], recv_out.at[i - 1],
                device_id=(flip(c, 2 * i), f), device_id_type=MESH,
            )
        )
    smalls = []
    for number, (i, k) in enumerate(peers):
        peer_c, peer_f = flip(c, i), flip(f, k)
        smalls.append(
            pltpu.make_async_remote_copy(
                small.at[peer_c * 4 + peer_f], small_in.at[me], send_small.at[number], recv_small.at[number],
                device_id=(peer_c, peer_f), device_id_type=MESH,
            )
        )
    for copy in outputs + smalls:
        copy.start()

    def plus(mine, came):
        return (mine.astype(F32) + came.astype(F32)).astype(BF16)

    swaps, sent = [], []

    def finish(m, e):
        count, bit, number = quarter, 4, 0
        for at in range(quarter):
            rest[m, at, e] = plus(rest[m, at, e], rest_landed[m, at, e])
        mine = rest.at[m, :, e]
        while count > 1:
            count //= 2
            chosen = lax.rem(lax.div(plane, bit), 2)
            came = last_landed.at[m, number, pl.ds(0, count), e]
            copy = over(
                mine.at[pl.ds((1 - chosen) * count, count)], came,
                send_deep.at[2 * m + number, e], recv_deep.at[2 * m + number, e], bit,
            )
            copy.start()
            copy.wait_recv()
            sent.append(copy)
            for at in range(count):
                last[m, number, at, e] = plus(mine[chosen * count + at], came[at])
            mine, bit, number = last.at[m, number, :, e], bit * 2, number + 1
        rows = turned.shape[3]
        across = mine[0].astype(F32).T
        for r in range(RANKS):
            turned[m, r, e] = across[r * rows : (r + 1) * rows].astype(BF16)
        for i in range(RANKS):
            source, target = turned.at[m, flip(rank, i), e], swapped.at[rank, m, e]
            if i:
                copy = pltpu.make_async_remote_copy(
                    source, target, send_swap.at[m * OWN + e, i], recv_swap.at[m * OWN + e, i],
                    device_id=(flip(c, i // 4), flip(f, i % 4)), device_id_type=MESH,
                )
            else:
                copy = pltpu.make_async_copy(source, target, stay.at[m * OWN + e])
            copy.start()
            swaps.append(copy)

    for copy in loads:
        copy.wait()
    for e in range(OWN):
        finish(2, e)
    finish(0, 0)
    up_second = []
    for e in range(OWN):
        up_first[e].wait_recv()
        for at in range(half):
            halves[at, e] = plus(halves[at, e], landed[at, e])
        up_second.append(
            over(
                halves.at[pl.ds((1 - second) * quarter, quarter), e], rest_landed.at[1, :, e],
                send_half.at[1, e], recv_half.at[1, e], 2,
            )
        )
        up_second[e].start()
        for at in range(quarter):
            rest[1, at, e] = halves[second * quarter + at, e]
    gate_second.wait_recv()
    finish(0, 1)
    for copy in outputs + smalls:
        copy.wait_recv()
    made = output_in[0].astype(F32)
    for i in range(1, planes):
        made = made + output_in[i].astype(F32)
    output_grad[...] = made
    small_sum[...] = jnp.sum(small_in[...], axis=0)
    for e in range(OWN):
        up_second[e].wait_recv()
        finish(1, e)
    for copy in swaps:
        copy.wait()
    for copy in smalls + outputs + sent + up_first + up_second + [gate_second]:
        copy.wait_send()


def final_sums(
    cid, n_ctx, small, output_part, grads, gate_keep, gate_came, gate_other, down_keep, down_came
):
    anywhere = pl.BlockSpec(memory_space=pl.ANY)
    inside = pl.BlockSpec(memory_space=pltpu.VMEM)
    dma = pltpu.SemaphoreType.DMA
    devices, planes = n_ctx * 4, n_ctx // 2
    slab, piece = D // devices, grads.shape[2:]
    half, quarter = (planes // 2,) + piece, (planes // 4,) + piece
    deep = (3, 2, max(planes // 8, 1)) + piece
    return pl.pallas_call(
        functools.partial(final_kernel, n_ctx),
        name="final_sums",
        out_shape=[
            jax.ShapeDtypeStruct((RANKS, 3, OWN, slab, FF), BF16),
            jax.ShapeDtypeStruct((slab, D), F32),
            jax.ShapeDtypeStruct(small.shape[1:], F32),
        ],
        in_specs=[anywhere] * 8,
        out_specs=[anywhere] + [inside] * 2,
        scratch_shapes=[
            pltpu.VMEM(half, BF16),
            pltpu.VMEM(half, BF16),
            pltpu.VMEM((3,) + quarter, BF16),
            pltpu.VMEM((3,) + quarter, BF16),
            pltpu.VMEM(deep if planes > 4 else (1, 1, 1, 1, 8, 128), BF16),
            pltpu.VMEM(deep if planes > 4 else (1, 1, 1, 1, 8, 128), BF16),
            pltpu.VMEM((3, RANKS, OWN, slab, FF), BF16),
            pltpu.VMEM((planes, slab, D), BF16),
            pltpu.VMEM(small.shape, F32),
            dma((3, OWN)), dma((3, OWN)), dma((6, OWN)), dma((6, OWN)),
            dma((planes - 1,)), dma((planes - 1,)), dma((devices - 1,)), dma((devices - 1,)),
            dma((3 * OWN, RANKS)), dma((3 * OWN, RANKS)), dma((7,)), dma((3 * OWN,)),
        ],
        compiler_params=pltpu.CompilerParams(
            collective_id=cid, has_side_effects=True, vmem_limit_bytes=56 << 20
        ),
        cost_estimate=lasting(80),
    )(small, output_part, grads, gate_keep, gate_came, gate_other, down_keep, down_came)


def rope_tables(positions):
    half_dim = HEAD_SIZE // 2
    frequency = ROPE_BASE ** (-jnp.arange(half_dim, dtype=F32) * 2.0 / HEAD_SIZE)
    angle = positions.astype(F32)[:, None] * frequency[None, :]
    angle = jnp.concatenate([angle, angle], axis=1)
    return (jnp.cos(angle), jnp.sin(angle))


def heads_out(field, per):
    field = field.reshape(SEQS, BLOCK, KEY_VALUE_HEADS, per, HEAD_SIZE)
    return field.transpose(2, 3, 1, 0, 4).reshape(KEY_VALUE_HEADS, per, BLOCK, SEQS * HEAD_SIZE)


def heads_in(field):
    per = field.shape[1]
    field = field.reshape(KEY_VALUE_HEADS, per, BLOCK, SEQS, HEAD_SIZE)
    return field.transpose(3, 2, 0, 1, 4).reshape(SEQS, BLOCK, KEY_VALUE_HEADS * per * HEAD_SIZE)


def on_device(
    n_ctx,
    n_fsdp,
    tokens,
    segments,
    valid,
    expert_ids,
    slot_order,
    cotangent,
    norm1_gain,
    w_query,
    key_weight,
    value_weight,
    w_output,
    norm2_gain,
    w_router,
    w_gate,
    w_up,
    w_down,
):
    parts = n_ctx // KEY_VALUE_HEADS
    replicas = n_ctx // 2
    full_len = segments.shape[1]
    c_index, f_index = lax.axis_index("ctx"), lax.axis_index("fsdp")
    pair = lax.rem(c_index, 2)
    rank = pair * n_fsdp + f_index
    part = lax.rem(c_index, parts)
    head = lax.div(c_index, parts)
    positions = c_index * BLOCK + jnp.arange(BLOCK, dtype=jnp.int32)

    span = D // n_fsdp // 2
    nears = [
        lax.ppermute(
            lax.dynamic_slice_in_dim(w, pair * span, span, 0), "fsdp", [(a, a ^ 2) for a in range(n_fsdp)]
        )
        for w in (w_query, key_weight, value_weight)
    ]
    tokens_all = lax.all_gather(tokens, "ctx", axis=0, tiled=False)
    small = jnp.concatenate(
        [
            norm1_gain[None],
            norm2_gain[None],
            w_router.T,
            jnp.zeros((SMALL - EXPERTS - 2, D // n_fsdp), BF16),
        ],
        axis=0,
    )
    packs = [
        lax.dynamic_slice_in_dim(w, pair * (EXPERTS // 2), EXPERTS // 2, 1)
        .reshape(D // n_fsdp, n_fsdp, OWN, FF)
        .transpose(1, 2, 0, 3)
        for w in (w_gate, w_up, w_down)
    ]
    inputs_f = tokens.astype(F32)
    scale_one = lax.rsqrt(jnp.mean(inputs_f * inputs_f, axis=-1, keepdims=True) + EPS)
    segq = segments.reshape(SEQS, KEY_VALUE_HEADS, parts, BLOCK)
    segq = lax.dynamic_index_in_dim(segq, part, 2, keepdims=False).transpose(1, 0, 2)[..., None]
    codes = jnp.where(valid > 0, segments, -1)
    codes = codes.reshape(SEQS, full_len // KEYS, KEYS).transpose(1, 0, 2)
    all_cosine, all_sine = rope_tables(jnp.arange(full_len, dtype=jnp.int32))
    all_cosine = jnp.tile(all_cosine, (1, 2)).reshape(n_ctx, BLOCK, 2 * HEAD_SIZE)
    all_sine = jnp.tile(all_sine, (1, 2)).reshape(n_ctx, BLOCK, 2 * HEAD_SIZE)
    (
        normed_in, small_all, full_query, full_key, full_value, q_all, kv_all, head_full, head_logs,
        attn_heads, full_output, own_gate, own_up, own_down,
    ) = attention_forward(
        0, parts, n_ctx, tokens.reshape(SEQS * BLOCK, D), small, w_query, key_weight, value_weight,
        w_output, nears, packs,
        lax.dynamic_index_in_dim(all_cosine, c_index, 0, keepdims=False),
        lax.dynamic_index_in_dim(all_sine, c_index, 0, keepdims=False),
        segq, codes,
    )
    gain_first = small_all[:, 0].reshape(D).astype(F32)
    gain_second = small_all[:, 1].reshape(D).astype(F32)
    full_router = small_all[:, 2 : 2 + EXPERTS].transpose(1, 0, 2).reshape(EXPERTS, D)
    full_output = full_output.reshape(D, D)
    attn_out = heads_in(attn_heads)
    attn_proj = jnp.einsum("sgq,dq->sgd", attn_out, full_output, preferred_element_type=F32)
    residual = inputs_f + attn_proj
    scale_two = lax.rsqrt(jnp.mean(residual * residual, axis=-1, keepdims=True) + EPS)
    normed_mid = (residual * scale_two * gain_second).astype(BF16)

    logits = jnp.einsum("sgd,ed->sge", normed_mid, full_router, preferred_element_type=F32)
    picked = jnp.any(expert_ids[..., None] == jnp.arange(EXPERTS, dtype=jnp.int32), axis=2)
    before = (slot_order[:, None, :] < slot_order[:, :, None]).astype(BF16)
    place = jnp.matmul(before, picked.astype(BF16), preferred_element_type=F32)
    is_kept = picked & (place < CAP)
    chosen = jnp.where(picked, logits, MASKED)
    raised = jnp.where(picked, jnp.exp(chosen - jnp.max(chosen, axis=-1, keepdims=True)), 0.0)
    gates = raised / jnp.sum(raised, axis=-1, keepdims=True)
    payload = jnp.concatenate(
        [
            normed_mid,
            jnp.where(is_kept, place, -1.0).astype(BF16),
            gates.astype(BF16),
            jnp.zeros((SEQS, BLOCK, 128 - 2 * EXPERTS), BF16),
        ],
        axis=2,
    )
    back, mix_part, own_grads, down_first, down_early = run_experts(
        2, replicas, payload.reshape(SEQS * BLOCK, PAY), cotangent.reshape(SEQS * BLOCK, D),
        (own_gate, own_up, own_down), tokens_all
    )

    back = back.reshape(SEQS, BLOCK, D + 128)
    grad_gates = jnp.where(is_kept, back[..., D : D + EXPERTS], 0.0)
    grad_chosen = gates * (grad_gates - jnp.sum(gates * grad_gates, axis=-1, keepdims=True))
    grad_logits = grad_chosen.astype(BF16)
    grad_mid = back[..., :D] + jnp.einsum(
        "sge,ed->sgd", grad_logits, full_router, preferred_element_type=F32
    )
    grad_router = jnp.einsum("sgd,sge->de", normed_mid, grad_logits, preferred_element_type=F32)

    grad_f = cotangent.astype(F32)
    weighted_two = gain_second * grad_mid
    grad_gain_second = jnp.sum(grad_mid * residual * scale_two, axis=(0, 1))
    cube_two = scale_two * scale_two * scale_two
    grad_resid = (
        grad_f
        + scale_two * weighted_two
        - residual * cube_two * jnp.mean(weighted_two * residual, axis=-1, keepdims=True)
    )
    grad_resid_low = grad_resid.astype(BF16)
    grad_attn = jnp.einsum("sgd,dq->sgq", grad_resid_low, full_output, preferred_element_type=F32)
    grad_attn = grad_attn.astype(BF16)
    grad_output_w = jnp.einsum("sgd,sgq->dq", grad_resid_low, attn_out, preferred_element_type=F32)
    rows = D // (n_ctx * n_fsdp)
    output_part = grad_output_w.astype(BF16).reshape(replicas, 2, 2, 2, rows, D)

    (
        input_grad, layer_out, gain_grad, output_sum, _, gate_keep, gate_came, gate_other, down_keep, down_came,
        _, _, head_grads,
    ) = attention_backward(
        6, parts, n_ctx, down_early, heads_out(grad_attn, REP), q_all, kv_all, segq, codes, head_full, head_logs,
        all_cosine, all_sine, tokens.reshape(SEQS * BLOCK, D), gain_first[None],
        grad_resid.reshape(SEQS * BLOCK, D), residual.reshape(SEQS * BLOCK, D), own_grads, down_first, mix_part, output_part,
        tokens_all.reshape(n_ctx, SEQS * BLOCK, D), full_query, full_key, full_value,
    )
    input_grad = input_grad.reshape(SEQS, BLOCK, D)
    layer_out = layer_out.reshape(SEQS, BLOCK, D)
    amount = rows * (EXPERTS + 2)
    tiles = -(-amount // 1024) * 8
    small_grads = jnp.concatenate([grad_router, gain_grad.T, grad_gain_second[:, None]], axis=1)
    small_grads = jnp.pad(
        small_grads.reshape(n_ctx * n_fsdp, amount), ((0, 0), (0, tiles * 128 - amount))
    ).reshape(n_ctx * n_fsdp, tiles, 128)
    swapped, output_grad, small_sum = final_sums(
        9, n_ctx, small_grads, output_sum, own_grads, gate_keep, gate_came, gate_other, down_keep, down_came
    )
    small_sum = small_sum.reshape(tiles * 128)[:amount].reshape(rows, EXPERTS + 2)
    head_grads = head_grads.reshape(KEY_VALUE_HEADS, parts, rows, (REP + 2) * HEAD_SIZE)
    own_gain = lax.dynamic_slice_in_dim(gain_first, (c_index * n_fsdp + f_index) * rows, rows, 0)
    head_grads = jnp.sum(head_grads.astype(F32), axis=1).transpose(1, 0, 2) * own_gain[:, None, None]
    query_grad = head_grads[..., : REP * HEAD_SIZE].reshape(rows, D)
    key_grad = head_grads[..., REP * HEAD_SIZE : (REP + 1) * HEAD_SIZE].reshape(rows, -1)
    value_grad = head_grads[..., (REP + 1) * HEAD_SIZE :].reshape(rows, -1)

    def by_row(matrix):
        return swapped[:, matrix].transpose(2, 0, 1, 3).reshape(rows, EXPERTS, FF).astype(F32)

    return (
        layer_out,
        input_grad,
        small_sum[:, EXPERTS],
        query_grad,
        key_grad,
        value_grad,
        output_grad,
        small_sum[:, EXPERTS + 1],
        small_sum[:, :EXPERTS],
        by_row(0),
        by_row(1),
        by_row(2),
    )


def solution(mesh):
    placed = (
        P("fsdp", "ctx", None),
        P("fsdp", None),
        P("fsdp", None),
        P("fsdp", "ctx", None),
        P("fsdp", "ctx"),
        P("fsdp", "ctx", None),
        P("fsdp"),
        P("fsdp", None),
        P("fsdp", None),
        P("fsdp", None),
        P("fsdp", None),
        P("fsdp"),
        P("fsdp", None),
        P("fsdp", None, None),
        P("fsdp", None, None),
        P("fsdp", None, None),
    )
    return jax.shard_map(
        functools.partial(on_device, mesh.shape["ctx"], mesh.shape["fsdp"]),
        mesh=mesh,
        in_specs=placed,
        out_specs=(
            P("fsdp", "ctx", None),
            P("fsdp", "ctx", None),
            P(("ctx", "fsdp")),
            P(("ctx", "fsdp"), None),
            P(("ctx", "fsdp"), None),
            P(("ctx", "fsdp"), None),
            P(("ctx", "fsdp"), None),
            P(("ctx", "fsdp")),
            P(("ctx", "fsdp"), None),
            P(("ctx", "fsdp"), None, None),
            P(("ctx", "fsdp"), None, None),
            P(("ctx", "fsdp"), None, None),
        ),
        check_vma=False,
    )
```

```python
import functools

import jax
import jax.numpy as jnp
from jax import lax
from jax.experimental import pallas as pl
from jax.experimental.pallas import tpu as pltpu
from jax.sharding import PartitionSpec as P

D = 1536
QUERY_HEADS = 24
KEY_VALUE_HEADS = 8
REP = QUERY_HEADS // KEY_VALUE_HEADS
HEAD_SIZE = 64
FF = 512
EXPERTS = 16
CAP = 80
RANKS = 8
OWN = EXPERTS // RANKS
SEQS = 2
BLOCK = 128
KEYS = 256

EPS = 1e-05
ROPE_BASE = 10000.0
MASKED = -1e30
SCALE = HEAD_SIZE ** (-0.5)
MESH = pl.DeviceIdType.MESH
BF16 = jnp.bfloat16
F32 = jnp.float32


def flip(index, constant):
    result, bit = index, 1
    while bit <= constant:
        if constant & bit:
            result = result + bit - 2 * bit * lax.rem(lax.div(index, bit), 2)
        bit *= 2
    return result


def lasting(microseconds):
    return pl.CostEstimate(flops=0, bytes_accessed=int(microseconds * 3.3e6), transcendentals=0)


PAY = D + 128
GROUPS = 4
ROWS = GROUPS * CAP


def other_chip(c, f, k):
    pair, x = lax.div(k, 2), lax.rem(k, 2)
    return (
        c + pair * (1 - 2 * lax.rem(c, 2)),
        f + 2 * x * (1 - 2 * lax.rem(lax.div(f, 2), 2)),
    )


def plane_order(replicas):
    order = [0]
    while len(order) < replicas:
        order = [2 * i for i in order] + [2 * i + 1 for i in order]
    return order


def experts_kernel(
    replicas, pay, cot, gate_own, up_own, down_own, after,
    back, mix, grads, down_came, pay_in, cot_in,
    weights, total, pay_now, cot_now, xs, gs, eo, gi, hid, dgate, dup, disp, comb,
    own, out, sib, ret, mix_now,
    send_first, recv_first, send_fwd, recv_fwd, send_sib, recv_sib, send_chip, recv_chip,
    load_w, load, store, piece_sem, send_down, recv_down,
):
    c, f = lax.axis_index("ctx"), lax.axis_index("fsdp")
    rank = lax.rem(c, 2) * 4 + f
    sibling = (c, flip(f, 1))
    barrier = pltpu.get_barrier_semaphore()
    pl.semaphore_signal(barrier, inc=1, device_id=sibling, device_id_type=MESH)
    for k in range(1, 4):
        pl.semaphore_signal(barrier, inc=1, device_id=other_chip(c, f, k), device_id_type=MESH)
    apart = len(grads.shape) == 5
    if apart:
        pl.semaphore_signal(barrier, inc=1, device_id=(flip(c, 2), f), device_id_type=MESH)
    bring = []
    for m, own_weight in enumerate((gate_own, up_own, down_own)):
        bring.append(pltpu.make_async_copy(own_weight, weights.at[m], load_w.at[m]))
        bring[-1].start()
    pl.semaphore_wait(barrier, 5 if apart else 4)
    sources, landed = (pay, cot), (pay_in, cot_in)

    def push(k, a):
        slot = 1 if k == 0 else 2 * k
        return pltpu.make_async_remote_copy(
            sources[a], landed[a].at[slot - 1], send_first.at[k, a], recv_first.at[k, a],
            device_id=sibling if k == 0 else other_chip(c, f, k), device_id_type=MESH,
        )

    def forward(k, a):
        return pltpu.make_async_remote_copy(
            landed[a].at[2 * k - 1], landed[a].at[2 * k], send_fwd.at[k - 1, a], recv_fwd.at[k - 1, a],
            device_id=sibling, device_id_type=MESH,
        )

    def to_sibling(k):
        return pltpu.make_async_remote_copy(
            out.at[lax.rem(k, 2)], sib.at[k], send_sib.at[k], recv_sib.at[k],
            device_id=sibling, device_id_type=MESH,
        )

    def to_chip(k):
        return pltpu.make_async_remote_copy(
            sib.at[k], ret.at[k - 1], send_chip.at[k - 1], recv_chip.at[k - 1],
            device_id=other_chip(c, f, k), device_id_type=MESH,
        )

    def store_mix(k, s):
        return pltpu.make_async_copy(mix_now.at[s], mix.at[2 * k + s], store.at[s])

    for k, a in ((0, 0), (0, 1), (1, 0), (2, 0), (1, 1), (2, 1), (3, 0), (3, 1)):
        push(k, a).start()

    def clear(i, carry):
        total[lax.div(i, OWN), lax.rem(i, OWN)] = jnp.zeros((FF, D), F32)
        return carry

    lax.fori_loop(0, 3 * OWN, clear, 0)
    lane = lax.broadcasted_iota(jnp.int32, (BLOCK, 128), 1)
    wide = lax.broadcasted_iota(jnp.int32, (BLOCK, 2 * BLOCK), 1).astype(F32)
    both = lax.broadcasted_iota(jnp.int32, (BLOCK, OWN * CAP), 1)

    def chunk(k, carry):
        now = (pay_now, cot_now)

        def fetch(a, s, source):
            copy = pltpu.make_async_copy(source, now[a].at[s], load.at[a, s])
            copy.start()
            return copy

        def arrived(chip):
            for a in range(2):
                push(chip, a).wait_recv()
                forward(chip, a).start()

        def fetch_chip(chip):
            for a in range(2):
                fetch(a, 0, landed[a].at[2 * chip - 1])
            for a in range(2):
                forward(chip, a).wait_recv()
                fetch(a, 1, landed[a].at[2 * chip])

        @pl.when(k == 0)
        def _():
            copies = [fetch(a, 0, sources[a]) for a in range(2)]
            for a in range(2):
                push(0, a).wait_recv()
            copies += [fetch(a, 1, landed[a].at[0]) for a in range(2)]
            for copy in copies:
                copy.wait()
            for copy in bring:
                copy.wait()

        @pl.when(k == 1)
        def _():
            arrived(1)
            arrived(2)
            fetch_chip(1)

        @pl.when(k > 0)
        def _():
            for a in range(2):
                for s in range(2):
                    pltpu.make_async_copy(landed[a].at[2 * k - 1 + s], now[a].at[s], load.at[a, s]).wait()

        for g in range(GROUPS):
            s, at = g // 2, (g % 2) * BLOCK
            tail = pay_now[s, at : at + BLOCK, D:].astype(F32)

            def column(index):
                return jnp.sum(jnp.where(lane == index, tail, 0.0), axis=1, keepdims=True)

            table = jnp.zeros((BLOCK, 2 * BLOCK), F32)
            gated = jnp.zeros((BLOCK, 2 * BLOCK), F32)
            for e in range(OWN):
                place = column(rank * OWN + e)
                place = jnp.where(place < 0.0, -1000.0, place + e * CAP)
                here = wide == place
                table = jnp.where(here, 1.0, table)
                gated = jnp.where(here, column(EXPERTS + rank * OWN + e), gated)
            table, gated = table.astype(BF16), gated.astype(BF16)
            disp[g] = table
            comb[g] = gated
            for weight, source, keep in (
                (table, pay_now[s, at : at + BLOCK, :D], xs),
                (gated, cot_now[s, at : at + BLOCK], gs),
            ):
                moved = lax.dot_general(
                    weight, source, (((0,), (0,)), ((), ())), preferred_element_type=F32
                ).astype(BF16)
                for e in range(OWN):
                    keep[e, g * CAP : (g + 1) * CAP] = moved[e * CAP : (e + 1) * CAP]

        def expert(e, carry):
            at = pl.multiple_of(e * CAP, 16)
            gate_pre = jnp.dot(xs[e], weights[0, e], preferred_element_type=F32)
            up_pre = jnp.dot(xs[e], weights[1, e], preferred_element_type=F32)
            sigmoid = 1.0 / (1.0 + jnp.exp(-gate_pre))
            activated = gate_pre * sigmoid
            hidden = (activated * up_pre).astype(BF16)
            hid[e] = hidden
            made = lax.dot_general(
                hidden, weights[2, e], (((1,), (1,)), ((), ())), preferred_element_type=F32
            ).astype(BF16)
            for g in range(GROUPS):
                eo[pl.ds(pl.multiple_of(g * OWN * CAP + at, 16), CAP)] = made[g * CAP : (g + 1) * CAP]
            grad_hidden = jnp.dot(gs[e], weights[2, e], preferred_element_type=F32)
            slope = sigmoid * (1.0 + gate_pre * (1.0 - sigmoid))
            grad_gate = (grad_hidden * up_pre * slope).astype(BF16)
            grad_up = (grad_hidden * activated).astype(BF16)
            dgate[e] = grad_gate
            dup[e] = grad_up
            made = lax.dot_general(
                grad_gate, weights[0, e], (((1,), (1,)), ((), ())), preferred_element_type=F32
            )
            made = made + lax.dot_general(
                grad_up, weights[1, e], (((1,), (1,)), ((), ())), preferred_element_type=F32
            )
            made = made.astype(BF16)
            for g in range(GROUPS):
                gi[pl.ds(pl.multiple_of(g * OWN * CAP + at, 16), CAP)] = made[g * CAP : (g + 1) * CAP]
            return carry

        lax.fori_loop(0, OWN, expert, 0)

        @pl.when(k > 0)
        def _():
            for s in range(2):
                store_mix(k - 1, s).wait()

        @pl.when(k > 1)
        def _():
            to_sibling(k - 2).wait_send()

        parity = lax.rem(k, 2)
        for g in range(GROUPS):
            s, at = g // 2, (g % 2) * BLOCK
            slots = pl.ds(g * OWN * CAP, OWN * CAP)
            made = eo[slots]
            mix_now[s, at : at + BLOCK] = jnp.dot(
                comb[g][:, : OWN * CAP], made, preferred_element_type=F32
            ).astype(BF16)
            table = disp[g][:, : OWN * CAP]
            grad_mid = jnp.dot(table, gi[slots], preferred_element_type=F32).astype(BF16)
            met = lax.dot_general(
                cot_now[s, at : at + BLOCK], made, (((1,), (1,)), ((), ())), preferred_element_type=F32
            ) * table.astype(F32)
            values = jnp.zeros((BLOCK, 128), F32)
            for e in range(OWN):
                inside = (both >= e * CAP) & (both < (e + 1) * CAP)
                value = jnp.sum(jnp.where(inside, met, 0.0), axis=1, keepdims=True)
                values = jnp.where(lane == rank * OWN + e, value, values)
            target = own if s == 0 else out
            target[parity, at : at + BLOCK, :D] = grad_mid
            target[parity, at : at + BLOCK, D:] = values.astype(BF16)
        to_sibling(k).start()
        for s in range(2):
            store_mix(k, s).start()

        @pl.when(k == 1)
        def _():
            fetch_chip(2)

        @pl.when(k == 2)
        def _():
            arrived(3)
            fetch_chip(3)

        def weight_grads(e, carry):
            for m, (left, right) in enumerate(((dgate, xs), (dup, xs), (hid, gs))):
                total[m, e] += lax.dot_general(
                    left[e], right[e], (((0,), (0,)), ((), ())), preferred_element_type=F32
                )
            return carry

        lax.fori_loop(0, OWN, weight_grads, 0)
        to_sibling(k).wait_recv()
        sib[k] = (sib[k].astype(F32) + own[parity].astype(F32)).astype(BF16)

        @pl.when(k > 0)
        def _():
            to_chip(k).start()

        return carry

    lax.fori_loop(0, 4, chunk, 0)
    for s in range(2):
        store_mix(3, s).wait()
    stages = (eo, gi)
    pending = []
    if apart:
        half = replicas // 2
        down_first = pltpu.make_async_remote_copy(
            grads.at[2, pl.ds((1 - lax.rem(lax.div(c, 2), 2)) * half, half)], down_came,
            send_down, recv_down, device_id=(flip(c, 2), f), device_id_type=MESH,
        )
    for i in range(3 * OWN):
        m, e = (2, 0, 1)[i // OWN], i % OWN
        if i >= 2:
            for copy in pending[i - 2]:
                copy.wait()
        if i == OWN + 1 and apart:
            down_first.start()
        stages[i % 2][:FF] = total[m, e].astype(BF16)
        pending.append([])
        if not apart:
            pending[i].append(
                pltpu.make_async_copy(stages[i % 2].at[:FF], grads.at[m, e], piece_sem.at[i % 2, 0])
            )
        else:
            width = D // replicas
            for at, plane in enumerate(plane_order(replicas)):
                pending[i].append(
                    pltpu.make_async_copy(
                        stages[i % 2].at[:FF, plane * width : (plane + 1) * width],
                        grads.at[m, at, e],
                        piece_sem.at[i % 2, at],
                    )
                )
        for copy in pending[i]:
            copy.start()
    for copy in pending[-2] + pending[-1]:
        copy.wait()
    for k in (2, 3):
        to_sibling(k).wait_send()
    for k in range(4):
        for a in range(2):
            push(k, a).wait_send()
            if k:
                forward(k, a).wait_send()
    for k in range(1, 4):
        to_chip(k).wait_recv()
    back[...] = (sib[0].astype(F32) + ret[0].astype(F32)) + (ret[1].astype(F32) + ret[2].astype(F32))
    for k in range(1, 4):
        to_chip(k).wait_send()
    if apart:
        down_first.wait()


def run_experts(cid, replicas, pay, cot, owns, after):
    width = D // replicas
    apart = width % 128 == 0
    tokens = SEQS * BLOCK
    anywhere = pl.BlockSpec(memory_space=pl.ANY)
    inside = pl.BlockSpec(memory_space=pltpu.VMEM)
    dma = pltpu.SemaphoreType.DMA
    back, mix, grads, down_came, _, _ = pl.pallas_call(
        functools.partial(experts_kernel, replicas),
        name="experts",
        out_shape=[
            jax.ShapeDtypeStruct((tokens, PAY), F32),
            jax.ShapeDtypeStruct((RANKS, tokens, D), BF16),
            jax.ShapeDtypeStruct((3, replicas, OWN, FF, width) if apart else (3, OWN, FF, D), BF16),
            jax.ShapeDtypeStruct((replicas // 2, OWN, FF, width) if apart else (8, 128), BF16),
            jax.ShapeDtypeStruct((RANKS - 1, tokens, PAY), BF16),
            jax.ShapeDtypeStruct((RANKS - 1, tokens, D), BF16),
        ],
        in_specs=[anywhere] * 6,
        out_specs=[inside] + [anywhere] * 5,
        scratch_shapes=[
            pltpu.VMEM((3, OWN, D, FF), BF16),
            pltpu.VMEM((3, OWN, FF, D), F32),
            pltpu.VMEM((2, tokens, PAY), BF16),
            pltpu.VMEM((2, tokens, D), BF16),
            pltpu.VMEM((OWN, ROWS, D), BF16),
            pltpu.VMEM((OWN, ROWS, D), BF16),
            pltpu.VMEM((OWN * ROWS, D), BF16),
            pltpu.VMEM((OWN * ROWS, D), BF16),
            pltpu.VMEM((OWN, ROWS, FF), BF16),
            pltpu.VMEM((OWN, ROWS, FF), BF16),
            pltpu.VMEM((OWN, ROWS, FF), BF16),
            pltpu.VMEM((GROUPS, BLOCK, 2 * BLOCK), BF16),
            pltpu.VMEM((GROUPS, BLOCK, 2 * BLOCK), BF16),
            pltpu.VMEM((2, tokens, PAY), BF16),
            pltpu.VMEM((2, tokens, PAY), BF16),
            pltpu.VMEM((4, tokens, PAY), BF16),
            pltpu.VMEM((3, tokens, PAY), BF16),
            pltpu.VMEM((2, tokens, D), BF16),
            dma((4, 2)), dma((4, 2)), dma((3, 2)), dma((3, 2)),
            dma((4,)), dma((4,)), dma((3,)), dma((3,)),
            dma((4,)), dma((2, 2)), dma((2,)), dma((2, replicas)), dma, dma,
        ],
        compiler_params=pltpu.CompilerParams(
            collective_id=cid, has_side_effects=True, vmem_limit_bytes=63 << 20
        ),
        cost_estimate=lasting(110),
    )(pay, cot, *owns, after)
    if not apart:
        grads = grads.reshape(3, OWN, FF, replicas, width).transpose(0, 3, 1, 2, 4)
        grads = grads[:, jnp.array(plane_order(replicas))]
    return back, mix, grads, down_came, apart


def half_masks(dtype):
    lane = lax.broadcasted_iota(jnp.int32, (1, 2 * HEAD_SIZE), 1)
    low = (lane < HEAD_SIZE).astype(F32)
    return low.astype(dtype), (1.0 - low).astype(dtype)


def allowed_at(block, step, segq, keycode):
    token = block * BLOCK + lax.broadcasted_iota(jnp.int32, (BLOCK, KEYS), 0)
    key = step * KEYS + lax.broadcasted_iota(jnp.int32, (BLOCK, KEYS), 1)
    return ((segq == keycode) & (key < token)) | (key == token)


SMALL = 32


def turn(field, cosine, sine):
    half = HEAD_SIZE // 2
    lane = lax.broadcasted_iota(jnp.int32, field.shape, field.ndim - 1)
    up = pltpu.roll(field, 2 * HEAD_SIZE - half, field.ndim - 1)
    down = pltpu.roll(field, half, field.ndim - 1)
    return field * cosine + jnp.where(lax.rem(lane, HEAD_SIZE) < half, -up, down) * sine


def attention_forward_kernel(
    parts, n_ctx, tok, small, w_q, w_k, w_v, w_o, near_q, near_k, near_v, pack0, pack1, pack2, cos_ref, sin_ref, seg_ref, code_ref,
    normed, small_all, q_full, k_full, v_full, q_ref, kv_ref, full_ref, log_ref, o_back, o_full,
    gate_own, up_own, down_own,
    acc, q_pack, kv_pack, o_buf, own_buf,
    send_w, recv_w, send_s, recv_s, send_e, recv_e, send_q, recv_q, send_kv, recv_kv, send_o, recv_o, here,
):
    c, f = lax.axis_index("ctx"), lax.axis_index("fsdp")
    head, part, pair = lax.div(c, parts), lax.rem(c, parts), lax.rem(c, 2)
    rows = D // 4
    half = rows // 2
    wide = 2 * HEAD_SIZE
    barrier = pltpu.get_barrier_semaphore()
    peers = [(i, 0) for i in range(1, n_ctx)] + [(0, k) for k in range(1, 4)]
    for dc, df in peers:
        pl.semaphore_signal(
            barrier, inc=1, device_id=(flip(c, dc), flip(f, df)), device_id_type=MESH
        )
    shards = (w_q, w_k, w_v, w_o)
    fulls = (q_full, k_full, v_full, o_full)
    packs, owns = (pack0, pack1, pack2), (gate_own, up_own, down_own)
    my_rows = pl.ds(pl.multiple_of(f * rows, rows), rows)
    local = [pltpu.make_async_copy(shards[a], fulls[a].at[f], here.at[a]) for a in range(4)]
    local += [pltpu.make_async_copy(small, small_all.at[f], here.at[4])]
    local += [pltpu.make_async_copy(packs[m].at[f], own_buf.at[m], here.at[5 + m]) for m in range(3)]
    for copy in local:
        copy.start()
    pl.semaphore_wait(barrier, len(peers))
    near = pl.ds(pl.multiple_of(pair * half, half), half)
    far = pl.ds(pl.multiple_of((1 - pair) * half, half), half)
    sibling, over_x, over_pair = (c, flip(f, 1)), (c, flip(f, 2)), (flip(c, 1), f)
    nears = (near_q, near_k, near_v)
    crossed = [
        pltpu.make_async_copy(nears[a], fulls[a].at[flip(f, 2), near], here.at[11 + a]) for a in range(3)
    ]
    for copy in crossed:
        copy.start()

    def weight(a, kind):
        beyond = flip(f, 2)
        brought = nears[a] if a < 3 else fulls[a].at[beyond, near]
        source, target, device = (
            (shards[a], fulls[a].at[f], sibling),
            (shards[a].at[near], fulls[a].at[f, near], over_x),
            (brought, fulls[a].at[beyond, near], sibling),
            (brought, fulls[a].at[beyond, near], over_pair),
            (fulls[a].at[beyond, far], fulls[a].at[beyond, far], sibling),
        )[kind]
        return pltpu.make_async_remote_copy(
            source, target, send_w.at[a, kind], recv_w.at[a, kind], device_id=device, device_id_type=MESH
        )

    smalls = [
        pltpu.make_async_remote_copy(
            small, small_all.at[f], send_s.at[i - 1], recv_s.at[i - 1],
            device_id=(c, flip(f, i)), device_id_type=MESH,
        )
        for i in range(1, 4)
    ]
    for copy in smalls:
        copy.start()
    for a in range(4):
        for kind in (3, 0, 2) if a < 3 else (1, 0):
            weight(a, kind).start()
    experts = [
        pltpu.make_async_remote_copy(
            packs[m].at[flip(f, i)], owns[m].at[:, my_rows], send_e.at[i - 1, m], recv_e.at[i - 1, m],
            device_id=(c, flip(f, i)), device_id_type=MESH,
        )
        for m in range(3)
        for i in range(1, 4)
    ]
    for copy in experts:
        copy.start()

    x = tok[...].astype(F32)
    scale = lax.rsqrt(jnp.mean(x * x, axis=1, keepdims=True) + EPS)
    for copy in smalls:
        copy.wait_recv()
    local[4].wait()
    for b in range(4):
        columns = slice(b * rows, (b + 1) * rows)
        normed[:, columns] = (x[:, columns] * scale * small_all[b, :1].astype(F32)).astype(BF16)

    def project(b, first):
        block = normed[:, pl.ds(pl.multiple_of(b * rows, rows), rows)]
        at = 0
        for a in range(3):
            width = fulls[a].shape[2]
            made = jnp.dot(block, fulls[a][b], preferred_element_type=F32)
            acc[:, at : at + width] = made if first else acc[:, at : at + width] + made
            at += width

    for a in range(3):
        local[a].wait()
    stores = []
    for m in range(3):
        local[5 + m].wait()
        stores.append(pltpu.make_async_copy(own_buf.at[m], owns[m].at[:, my_rows], here.at[5 + m]))
        stores[m].start()
    project(f, True)
    for a in range(3):
        weight(a, 0).wait_recv()
    project(flip(f, 1), False)
    for a in range(3):
        weight(a, 3).wait_recv()
        weight(a, 4).start()
        crossed[a].wait()
    project(flip(f, 2), False)
    for a in range(3):
        weight(a, 2).wait_recv()
        weight(a, 4).wait_recv()
    project(flip(f, 3), False)

    lane = lax.broadcasted_iota(jnp.int32, (BLOCK, wide), 1)
    low = lane < HEAD_SIZE
    cosine, sine = cos_ref[...], sin_ref[...]
    for m in range((QUERY_HEADS + 2 * KEY_VALUE_HEADS) // 2):
        pieces = []
        for s in range(SEQS):
            piece = acc[s * BLOCK : (s + 1) * BLOCK, m * wide : (m + 1) * wide]
            pieces.append(turn(piece, cosine, sine) if m < (QUERY_HEADS + KEY_VALUE_HEADS) // 2 else piece)
        even = jnp.where(low, pieces[0], pltpu.roll(pieces[1], HEAD_SIZE, 1)).astype(BF16)
        odd = jnp.where(low, pltpu.roll(pieces[0], HEAD_SIZE, 1), pieces[1]).astype(BF16)
        for h, value in ((2 * m, even), (2 * m + 1, odd)):
            if h < QUERY_HEADS:
                q_pack[h // REP, h % REP] = value
            else:
                h -= QUERY_HEADS
                kv_pack[h % KEY_VALUE_HEADS, h // KEY_VALUE_HEADS] = value

    q_stays = pltpu.make_async_copy(q_pack.at[head], q_ref.at[head], here.at[8])
    kv_stays = pltpu.make_async_copy(kv_pack.at[head], kv_ref.at[c], here.at[9])
    q_stays.start()
    kv_stays.start()
    to_heads = []
    for i in range(1, n_ctx):
        peer = flip(c, i)
        moves = [(kv_pack.at[lax.div(peer, parts)], kv_ref.at[c], send_kv.at[i - 1], recv_kv.at[i - 1])]
        if i % parts == 0:
            number = i // parts - 1
            moves.append(
                (q_pack.at[lax.div(peer, parts)], q_ref.at[head], send_q.at[number], recv_q.at[number])
            )
        for source, target, sent, came in moves:
            copy = pltpu.make_async_remote_copy(
                source, target, sent, came, device_id=(peer, f), device_id_type=MESH
            )
            copy.start()
            to_heads.append(copy)
    weight(3, 1).wait_recv()
    weight(3, 2).start()
    weight(3, 3).start()
    q_stays.wait()
    kv_stays.wait()
    for copy in to_heads:
        copy.wait_recv()

    count = REP * BLOCK
    halves = half_masks(BF16)
    across = lax.broadcasted_iota(jnp.int32, (count, wide), 1)

    def out_back(j):
        return pltpu.make_async_remote_copy(
            o_buf.at[j], o_back.at[head], send_o.at[j], recv_o.at[head],
            device_id=(j * parts + part, f), device_id_type=MESH,
        )

    def out_stays(j):
        return pltpu.make_async_copy(o_buf.at[j], o_back.at[head], here.at[10])

    def one_block(j, nothing):
        block = j * parts + part
        q = q_ref[j].reshape(count, wide)
        queries = [q * half for half in halves]

        def step(number, carry):
            k = kv_ref[pl.ds(2 * number, 2), 0].reshape(KEYS, wide)
            v = kv_ref[pl.ds(2 * number, 2), 1].reshape(KEYS, wide)
            codes = code_ref[number]
            after = []
            for s in range(SEQS):
                largest, total, out = carry[s]
                mask = allowed_at(block, number, seg_ref[j, s], codes[s : s + 1])
                scores = lax.dot_general(
                    queries[s], k, (((1,), (1,)), ((), ())), preferred_element_type=F32
                )
                scores = jnp.where(mask[None], scores.reshape(REP, BLOCK, KEYS) * SCALE, MASKED)
                scores = scores.reshape(count, KEYS)
                new = jnp.maximum(largest, jnp.max(scores, axis=1, keepdims=True))
                probs = jnp.exp(scores - new)
                shrink = jnp.exp(largest - new)
                total = total * shrink + jnp.sum(probs, axis=1, keepdims=True)
                out = out * shrink + jnp.dot(probs.astype(BF16), v, preferred_element_type=F32)
                after.append((new, total, out))
            return tuple(after)

        start = (
            jnp.full((count, 1), MASKED, F32),
            jnp.zeros((count, 1), F32),
            jnp.zeros((count, wide), F32),
        )
        done = lax.fori_loop(0, lax.div(block, 2) + 1, step, (start,) * SEQS)
        outs, logs = [], []
        for largest, total, out in done:
            outs.append(out / total)
            logs.append(jnp.broadcast_to(largest + jnp.log(total), (count, wide)))
        out = jnp.where(across < HEAD_SIZE, outs[0], outs[1])
        full_ref[j] = out.reshape(REP, BLOCK, wide)
        log_ref[j] = jnp.where(across < HEAD_SIZE, logs[0], logs[1]).reshape(REP, BLOCK, wide)
        o_buf[j] = out.astype(BF16).reshape(REP, BLOCK, wide)

        @pl.when(j != head)
        def _():
            out_back(j).start()

        @pl.when(j == head)
        def _():
            out_stays(j).start()

        return nothing

    lax.fori_loop(0, KEY_VALUE_HEADS, one_block, 0)
    weight(3, 3).wait_recv()
    weight(3, 4).start()

    def came_out(h, nothing):
        @pl.when(h != head)
        def _():
            pltpu.make_async_remote_copy(
                o_buf.at[h], o_back.at[h], send_o.at[h], recv_o.at[h],
                device_id=(h * parts + part, f), device_id_type=MESH,
            ).wait()

        @pl.when(h == head)
        def _():
            out_stays(h).wait()

        return nothing

    lax.fori_loop(0, KEY_VALUE_HEADS, came_out, 0)
    for kind in (0, 2, 4):
        weight(3, kind).wait_recv()
    local[3].wait()
    for copy in stores:
        copy.wait()
    for copy in experts:
        copy.wait()
    for copy in smalls + to_heads:
        copy.wait_send()
    for a in range(4):
        for kind in (0, 2, 3, 4) if a < 3 else range(5):
            weight(a, kind).wait_send()


def attention_forward(
    cid, parts, n_ctx, tok, small, w_q, w_k, w_v, w_o, nears, packs, cosine, sine, segq, codes
):
    wide = 2 * HEAD_SIZE
    anywhere = pl.BlockSpec(memory_space=pl.ANY)
    inside = pl.BlockSpec(memory_space=pltpu.VMEM)
    dma = pltpu.SemaphoreType.DMA
    heads = (KEY_VALUE_HEADS, REP, BLOCK, wide)
    keys = (n_ctx, 2, BLOCK, wide)
    others = max(n_ctx // parts - 1, 1)
    columns = w_q.shape[1] + w_k.shape[1] + w_v.shape[1]
    own = jax.ShapeDtypeStruct((OWN, D, FF), BF16)

    def full(x):
        return jax.ShapeDtypeStruct((4,) + x.shape, BF16)

    return pl.pallas_call(
        functools.partial(attention_forward_kernel, parts, n_ctx),
        name="attention_forward",
        out_shape=[
            jax.ShapeDtypeStruct(tok.shape, BF16),
            full(small), full(w_q), full(w_k), full(w_v),
            jax.ShapeDtypeStruct(heads, BF16),
            jax.ShapeDtypeStruct(keys, BF16),
            jax.ShapeDtypeStruct(heads, F32),
            jax.ShapeDtypeStruct(heads, F32),
            jax.ShapeDtypeStruct(heads, BF16),
            full(w_o), own, own, own,
        ],
        in_specs=[inside] + [anywhere] * 11 + [inside] * 4,
        out_specs=[inside] * 9 + [anywhere, inside] + [anywhere] * 3,
        scratch_shapes=[
            pltpu.VMEM((SEQS * BLOCK, columns), F32),
            pltpu.VMEM(heads, BF16),
            pltpu.VMEM((KEY_VALUE_HEADS, 2, BLOCK, wide), BF16),
            pltpu.VMEM(heads, BF16),
            pltpu.VMEM((3,) + packs[0].shape[1:], BF16),
            dma((4, 5)), dma((4, 5)), dma((3,)), dma((3,)), dma((3, 3)), dma((3, 3)),
            dma((others,)), dma((others,)), dma((n_ctx - 1,)), dma((n_ctx - 1,)),
            dma((KEY_VALUE_HEADS,)), dma((KEY_VALUE_HEADS,)), dma((14,)),
        ],
        compiler_params=pltpu.CompilerParams(
            collective_id=cid, has_side_effects=True, vmem_limit_bytes=56 << 20
        ),
        cost_estimate=lasting(130),
    )(tok, small, w_q, w_k, w_v, w_o, *nears, *packs, cosine, sine, segq, codes)


def turn_back(field, cosine, sine):
    half = HEAD_SIZE // 2
    lane = lax.broadcasted_iota(jnp.int32, field.shape, field.ndim - 1)
    up = pltpu.roll(field, 2 * HEAD_SIZE - half, field.ndim - 1)
    down = pltpu.roll(field, half, field.ndim - 1)
    turned = jnp.where(lax.rem(lane, HEAD_SIZE) < half, -up, down)
    return field * cosine - turned * sine


def attention_backward_kernel(
    parts, n_ctx, early, g_own, q_ref, kv_ref, seg_ref, code_ref, full_ref, log_ref, cos_ref, sin_ref,
    tok, gain, resid_grad, residual, grads, down_in, mix, output_part, tokens_all, q_full, k_full, v_full,
    input_grad, layer_out, gain_grad, output_sum, gate_first, gate_keep, gate_came, gate_other, up_came, down_keep, down_came,
    mix_core, mix_in, head_in, g_ref, total, kept, came, dq_ref, dkv_ref, dq_back, dkv_back, w_q, w_k, w_v, grad_qkv, grad_in,
    token_buf, field, head_acc, head_out, head_core, head_x, output_keep, output_came, output_x, output_pair,
    send_g, recv_g, send_q, recv_q, send_kv, recv_kv, send_mix, recv_mix, send_half, recv_half, here,
    send_out, recv_out, send_head, recv_head, load_t,
):
    c, f = lax.axis_index("ctx"), lax.axis_index("fsdp")
    head, part = lax.div(c, parts), lax.rem(c, parts)
    rows = REP * BLOCK
    wide = 2 * HEAD_SIZE
    barrier = pltpu.get_barrier_semaphore()
    peers = [(i, k) for i in range(n_ctx) for k in range(4) if i or k]
    for dc, df in peers:
        pl.semaphore_signal(
            barrier, inc=1, device_id=(flip(c, dc), flip(f, df)), device_id_type=MESH
        )
    pair, x_bit, core_bit = lax.rem(c, 2), lax.div(f, 2), lax.rem(f, 2)
    loads = [
        pltpu.make_async_copy(source, target, here.at[5 + i])
        for i, (source, target) in enumerate(
            (
                (q_full, w_q), (k_full, w_k), (v_full, w_v),
                (output_part.at[:, :, :, core_bit], output_keep),
            )
        )
    ]

    def bring(b):
        return pltpu.make_async_copy(
            tokens_all.at[b], token_buf.at[lax.rem(b, 2)], load_t.at[lax.rem(b, 2)]
        )

    for copy in loads[1:]:
        copy.start()
    first = pltpu.make_async_copy(g_own.at[head], g_ref.at[head], here.at[0])
    first.start()
    pl.semaphore_wait(barrier, len(peers))
    to_heads = []
    for number, i in enumerate(range(parts, n_ctx, parts)):
        to_heads.append(
            pltpu.make_async_remote_copy(
                g_own.at[lax.div(flip(c, i), parts)], g_ref.at[head],
                send_g.at[number], recv_g.at[number],
                device_id=(flip(c, i), f), device_id_type=MESH,
            )
        )
        to_heads[-1].start()
    half = grads.shape[1] // 2
    quarter = half // 2
    mine = lax.rem(lax.div(c, 2), 2)
    second = lax.rem(lax.div(c, 4), 2)

    def halving(matrix, target, number):
        return pltpu.make_async_remote_copy(
            grads.at[matrix, pl.ds((1 - mine) * half, half)], target,
            send_half.at[number], recv_half.at[number],
            device_id=(flip(c, 2), f), device_id_type=MESH,
        )

    down_halving, gate_halving = halving(2, came, 0), halving(0, gate_first, 1)
    arriving = pltpu.make_async_copy(down_in, came, here.at[10]) if early else down_halving
    arriving.start()
    up_halving = pltpu.make_async_remote_copy(
        grads.at[1, pl.ds((1 - mine) * half, half), 0], up_came, send_half.at[4], recv_half.at[4],
        device_id=(flip(c, 2), f), device_id_type=MESH,
    )
    keeping = pltpu.make_async_copy(grads.at[2, pl.ds(mine * half, half)], kept, here.at[3])
    keeping.start()
    output_stages = [
        pltpu.make_async_remote_copy(
            source, target, send_out.at[i], recv_out.at[i], device_id=device, device_id_type=MESH
        )
        for i, (source, target, device) in enumerate(
            (
                (output_part.at[:, :, :, 1 - core_bit], output_came, (c, flip(f, 1))),
                (output_keep.at[:, :, 1 - x_bit], output_x, (c, flip(f, 2))),
                (output_x.at[:, 1 - pair], output_pair, (flip(c, 1), f)),
            )
        )
    ]
    output_stages[0].start()
    to_core = [
        pltpu.make_async_remote_copy(
            mix.at[2 * k + 1], mix_core.at[k], send_mix.at[k], recv_mix.at[k],
            device_id=(c, flip(f, 1)), device_id_type=MESH,
        )
        for k in range(4)
    ]
    for copy in to_core:
        copy.start()

    def plus(mine, came):
        return (mine.astype(F32) + came.astype(F32)).astype(BF16)

    def second_halving(keep, target, number, later=None):
        def add(i, nothing):
            at, e = lax.div(i, OWN), lax.rem(i, OWN)
            kept[at, e] = plus(kept[at, e], came[at, e])
            return nothing

        lax.fori_loop(0, half * OWN, add, 0)
        source = kept.at[pl.ds((1 - second) * quarter, quarter)]
        if later is not None:
            source, target = source.at[:, 0], target.at[:, 0]
            rest = pltpu.make_async_copy(
                kept.at[pl.ds((1 - second) * quarter, quarter), 1], later, here.at[3]
            )
            rest.start()
            rest.wait()
        going = pltpu.make_async_remote_copy(
            source, target, send_half.at[number], recv_half.at[number],
            device_id=(flip(c, 4), f), device_id_type=MESH,
        )
        going.start()
        staying = pltpu.make_async_copy(kept.at[pl.ds(second * quarter, quarter)], keep, here.at[4])
        staying.start()
        return going, staying

    if early:
        keeping.wait()
        arriving.wait()
        down_second, leaving = second_halving(down_keep, down_came, 2)
    gate_halving.start()
    shares = w_q.at[:, pl.ds(0, SEQS * BLOCK)]
    for k in range(4):
        pair_in = [
            pltpu.make_async_copy(mix.at[2 * k], token_buf.at[0], load_t.at[0]),
            pltpu.make_async_copy(mix_core.at[k], token_buf.at[1], load_t.at[1]),
        ]
        pair_in[0].start()
        to_core[k].wait_recv()
        pair_in[1].start()
        for copy in pair_in:
            copy.wait()
        shares[k] = plus(token_buf[0], token_buf[1])
    own_share = pltpu.make_async_copy(shares.at[0], mix_in.at[0], here.at[5])
    own_share.start()
    returns = [
        pltpu.make_async_remote_copy(
            shares.at[k], mix_in.at[k], send_mix.at[3 + k], recv_mix.at[3 + k],
            device_id=(flip(c, k // 2), flip(f, 2 * (k % 2))), device_id_type=MESH,
        )
        for k in range(1, 4)
    ]
    for copy in returns:
        copy.start()
    for b in range(2):
        bring(b).start()
    total[...] = jnp.zeros_like(total)
    first.wait()
    for copy in to_heads:
        copy.wait_recv()
    halves = half_masks(BF16)
    lane = lax.broadcasted_iota(jnp.int32, (rows, wide), 1)

    def query_back(j):
        return pltpu.make_async_remote_copy(
            dq_ref.at[j], dq_back.at[head], send_q.at[j], recv_q.at[head],
            device_id=(j * parts + part, f), device_id_type=MESH,
        )

    def key_back(b):
        return pltpu.make_async_remote_copy(
            dkv_ref.at[b], dkv_back.at[c], send_kv.at[b], recv_kv.at[c],
            device_id=(b, f), device_id_type=MESH,
        )

    def query_stays(j):
        return pltpu.make_async_copy(dq_ref.at[j], dq_back.at[head], here.at[1])

    def key_stays(b):
        return pltpu.make_async_copy(dkv_ref.at[b], dkv_back.at[c], here.at[2])

    def one_block(j, nothing):
        block = j * parts + part
        q = q_ref[j].reshape(rows, wide)
        g = g_ref[j].reshape(rows, wide)
        queries = [q * half for half in halves]
        partial = [g * half for half in halves]
        product = g.astype(F32) * full_ref[j].reshape(rows, wide)
        logs = log_ref[j].reshape(rows, wide)
        log_total = [logs[:, :1], logs[:, HEAD_SIZE : HEAD_SIZE + 1]]
        inner = [jnp.sum(product * half, axis=1, keepdims=True) for half in half_masks(F32)]

        def step(number, carry):
            k = kv_ref[pl.ds(2 * number, 2), 0].reshape(KEYS, wide)
            v = kv_ref[pl.ds(2 * number, 2), 1].reshape(KEYS, wide)
            codes = code_ref[number]
            after = []
            dk = jnp.zeros((KEYS, wide), F32)
            dv = jnp.zeros((KEYS, wide), F32)
            for s in range(SEQS):
                mask = allowed_at(block, number, seg_ref[j, s], codes[s : s + 1])
                scores = lax.dot_general(
                    queries[s], k, (((1,), (1,)), ((), ())), preferred_element_type=F32
                )
                scores = jnp.where(mask[None], scores.reshape(REP, BLOCK, KEYS) * SCALE, MASKED)
                probs = jnp.exp(scores.reshape(rows, KEYS) - log_total[s])
                grad_probs = lax.dot_general(
                    partial[s], v, (((1,), (1,)), ((), ())), preferred_element_type=F32
                )
                grad_scores = (probs * (grad_probs - inner[s])).astype(BF16)
                dv = dv + lax.dot_general(
                    probs.astype(BF16), partial[s], (((0,), (0,)), ((), ())), preferred_element_type=F32
                )
                dk = dk + lax.dot_general(
                    grad_scores, queries[s], (((0,), (0,)), ((), ())), preferred_element_type=F32
                )
                after.append(carry[s] + jnp.dot(grad_scores, k, preferred_element_type=F32))
            total[pl.ds(2 * number, 2), 0] += dk.reshape(2, BLOCK, wide)
            total[pl.ds(2 * number, 2), 1] += dv.reshape(2, BLOCK, wide)
            return tuple(after)

        start = jnp.zeros((rows, wide), F32)
        done = lax.fori_loop(0, lax.div(block, 2) + 1, step, (start,) * SEQS)
        dq = (jnp.where(lane < HEAD_SIZE, done[0], done[1]) * SCALE).reshape(REP, BLOCK, wide)
        dq_ref[j] = turn_back(dq, cos_ref[block][None], sin_ref[block][None]).astype(BF16)

        @pl.when(j != head)
        def _():
            query_back(j).start()

        @pl.when(j == head)
        def _():
            query_stays(j).start()

        return nothing

    lax.fori_loop(0, KEY_VALUE_HEADS, one_block, 0)

    def finish(b, nothing):
        dkv_ref[b, 0] = turn_back(total[b, 0] * SCALE, cos_ref[b], sin_ref[b]).astype(BF16)
        dkv_ref[b, 1] = total[b, 1].astype(BF16)

        @pl.when(b != c)
        def _():
            key_back(b).start()

        @pl.when(b == c)
        def _():
            key_stays(b).start()

        return nothing

    lax.fori_loop(0, n_ctx, finish, 0)
    up_halving.start()
    if not early:
        keeping.wait()
        down_halving.wait_recv()
        down_second, leaving = second_halving(down_keep, down_came, 2)

    planes = output_keep.shape[0]

    loads[3].wait()
    output_stages[0].wait_recv()

    def cores(i, nothing):
        r, p, x = lax.div(i, 4), lax.rem(lax.div(i, 2), 2), lax.rem(i, 2)
        output_keep[r, p, x] = plus(output_keep[r, p, x], output_came[r, p, x])
        return nothing

    lax.fori_loop(0, planes * 4, cores, 0)
    output_stages[1].start()

    low = lax.broadcasted_iota(jnp.int32, (BLOCK, wide), 1) < HEAD_SIZE

    def side_by_side(even, odd):
        even, odd = even.astype(F32), odd.astype(F32)
        return (
            jnp.where(low, even, pltpu.roll(odd, HEAD_SIZE, 1)),
            jnp.where(low, pltpu.roll(even, HEAD_SIZE, 1), odd),
        )

    head_acc[...] = jnp.zeros_like(head_acc)

    def head_weights(b, nothing):
        bring(b).wait()
        block = token_buf[lax.rem(b, 2)]
        wide_block = block.astype(F32)
        scales = lax.rsqrt(jnp.mean(wide_block * wide_block, axis=1, keepdims=True) + EPS)
        j = lax.div(b, parts)
        have = jnp.where(lax.rem(b, parts) == part, 1.0, 0.0)
        heads = [dq_ref[j, r].astype(F32) * have for r in range(REP)] + [dkv_ref[b, 0], dkv_ref[b, 1]]
        heads.append(jnp.zeros((BLOCK, wide), F32))
        for m in range((REP + 3) // 2):
            for s, value in enumerate(side_by_side(heads[2 * m], heads[2 * m + 1])):
                at = slice(s * BLOCK, (s + 1) * BLOCK)
                field[at, m * wide : (m + 1) * wide] = (value * scales[at]).astype(BF16)
        head_acc[...] += lax.dot_general(
            block, field[...], (((0,), (0,)), ((), ())), preferred_element_type=F32
        )

        @pl.when(b + 2 < n_ctx)
        def _():
            bring(b + 2).start()

        return nothing

    lax.fori_loop(0, n_ctx, head_weights, 0)
    slab = D // (n_ctx * 4)
    for d in range(n_ctx * 4):
        head_out[d // 4, d // 2 % 2, d % 2] = head_acc[
            d * slab : (d + 1) * slab, : head_out.shape[4]
        ].astype(BF16)
    head_stages = [
        pltpu.make_async_remote_copy(
            source, target, send_head.at[i], recv_head.at[i], device_id=device, device_id_type=MESH
        )
        for i, (source, target, device) in enumerate(
            (
                (head_out.at[:, :, 1 - core_bit], head_core, (c, flip(f, 1))),
                (head_core.at[:, 1 - x_bit], head_x, (c, flip(f, 2))),
            )
        )
    ]
    head_stages[0].start()
    for copy in returns:
        copy.wait_send()
    own_share.wait()
    loads[0].start()
    down_second.wait_send()
    leaving.wait()
    gate_halving.wait_recv()
    refill = [
        pltpu.make_async_copy(grads.at[0, pl.ds(mine * half, half)], kept, here.at[3]),
        pltpu.make_async_copy(gate_first, came, here.at[10]),
    ]
    for copy in refill:
        copy.start()
    for copy in refill:
        copy.wait()
    gate_second, leaving = second_halving(gate_keep, gate_came, 3, gate_other)

    head_stages[0].wait_recv()

    def head_cores(i, nothing):
        d, x = lax.div(i, 2), lax.rem(i, 2)
        head_core[d, x] = plus(head_out[d, x, core_bit], head_core[d, x])
        return nothing

    lax.fori_loop(0, n_ctx * 2, head_cores, 0)
    head_stages[1].start()

    def came_query(h, nothing):
        @pl.when(h != head)
        def _():
            pltpu.make_async_remote_copy(
                dq_ref.at[h], dq_back.at[h], send_q.at[h], recv_q.at[h],
                device_id=(h * parts + part, f), device_id_type=MESH,
            ).wait()

        @pl.when(h == head)
        def _():
            query_stays(h).wait()

        return nothing

    def came_key(b, nothing):
        @pl.when(b != c)
        def _():
            pltpu.make_async_remote_copy(
                dkv_ref.at[b], dkv_back.at[b], send_kv.at[b], recv_kv.at[b],
                device_id=(b, f), device_id_type=MESH,
            ).wait()

        @pl.when(b == c)
        def _():
            key_stays(b).wait()

        return nothing

    lax.fori_loop(0, KEY_VALUE_HEADS, came_query, 0)
    lax.fori_loop(0, n_ctx, came_key, 0)

    def head_of(h):
        if h < QUERY_HEADS:
            return dq_back[h // REP, h % REP]
        kind, h = (h - QUERY_HEADS) // KEY_VALUE_HEADS, (h - QUERY_HEADS) % KEY_VALUE_HEADS
        value = dkv_back[h * parts, kind]
        if parts > 1:
            value = value.astype(F32)
            for p in range(1, parts):
                value = value + dkv_back[h * parts + p, kind].astype(F32)
        return value

    head_stages[1].wait_recv()

    def head_over_x(d, nothing):
        head_x[d] = plus(head_core[d, x_bit], head_x[d])
        return nothing

    lax.fori_loop(0, n_ctx, head_over_x, 0)
    head_stays = pltpu.make_async_copy(head_x.at[c], head_in.at[c], here.at[9])
    head_stays.start()
    to_all = []
    for i in range(1, n_ctx):
        to_all.append(
            pltpu.make_async_remote_copy(
                head_x.at[flip(c, i)], head_in.at[c], send_head.at[1 + i], recv_head.at[1 + i],
                device_id=(flip(c, i), f), device_id_type=MESH,
            )
        )
        to_all[-1].start()
    for m in range((QUERY_HEADS + 2 * KEY_VALUE_HEADS) // 2):
        for s, value in enumerate(side_by_side(head_of(2 * m), head_of(2 * m + 1))):
            grad_qkv[s * BLOCK : (s + 1) * BLOCK, m * wide : (m + 1) * wide] = value.astype(BF16)
    for copy in loads[:3]:
        copy.wait()
    depth = D // 4
    for b in range(4):
        made, at = 0.0, 0
        for weight in (w_q, w_k, w_v):
            width = weight.shape[2]
            made = made + lax.dot_general(
                grad_qkv[:, at : at + width], weight[b], (((1,), (1,)), ((), ())),
                preferred_element_type=F32,
            )
            at += width
        grad_in[:, b * depth : (b + 1) * depth] = made
    x = tok[...].astype(F32)
    scale = lax.rsqrt(jnp.mean(x * x, axis=1, keepdims=True) + EPS)
    gain_grad[...] = jnp.sum(grad_in[...] * x * scale, axis=0, keepdims=True)
    weighted = grad_in[...] * gain[...]
    input_grad[...] = (
        resid_grad[...]
        + scale * weighted
        - x * (scale * scale * scale) * jnp.mean(weighted * x, axis=1, keepdims=True)
    ).astype(BF16)

    staying = pltpu.make_async_copy(residual, grad_in, here.at[8])
    staying.start()
    staying.wait()

    def share(k):
        return pltpu.make_async_copy(mix_in.at[k], token_buf.at[k % 2], load_t.at[k % 2])

    share(0).start()
    for k in range(4):
        if k < 3:
            returns[k].wait_recv()
            share(k + 1).start()
        share(k).wait()
        grad_in[...] += token_buf[k % 2].astype(F32)
    layer_out[...] = grad_in[...].astype(BF16)

    output_stages[1].wait_recv()

    def over_x(i, nothing):
        r, p = lax.div(i, 2), lax.rem(i, 2)
        output_x[r, p] = plus(output_keep[r, p, x_bit], output_x[r, p])
        return nothing

    lax.fori_loop(0, planes * 2, over_x, 0)
    output_stages[2].start()
    output_stages[2].wait_recv()

    def over_pair(r, nothing):
        output_sum[r] = plus(output_x[r, pair], output_pair[r])
        return nothing

    lax.fori_loop(0, planes, over_pair, 0)
    for copy in to_heads:
        copy.wait_send()
    for copy in to_all + [gate_second, up_halving, leaving, head_stays]:
        copy.wait()
    down_second.wait_recv()
    for copy in to_core + output_stages + head_stages + [gate_halving] + ([] if early else [down_halving]):
        copy.wait_send()


def attention_backward(
    cid, parts, n_ctx, early, g_own, q, kv, segq, codes, full, logs, cosine, sine,
    tok, gain, resid_grad, residual, grads, down_in, mix, output_part, tokens_all, q_full, k_full, v_full,
):
    wide = 2 * HEAD_SIZE
    anywhere = pl.BlockSpec(memory_space=pl.ANY)
    inside = pl.BlockSpec(memory_space=pltpu.VMEM)
    dma = pltpu.SemaphoreType.DMA
    others = max(n_ctx // parts - 1, 1)
    devices, planes = n_ctx * 4, n_ctx // 2
    slab, head_width = D // devices, (REP + 2) * HEAD_SIZE
    half = (grads.shape[1] // 2,) + grads.shape[2:]
    quarter = (grads.shape[1] // 4,) + grads.shape[2:]
    columns = q_full.shape[2] + k_full.shape[2] + v_full.shape[2]
    return pl.pallas_call(
        functools.partial(attention_backward_kernel, parts, n_ctx, early),
        name="attention_backward",
        out_shape=[
            jax.ShapeDtypeStruct(tok.shape, BF16),
            jax.ShapeDtypeStruct(tok.shape, BF16),
            jax.ShapeDtypeStruct((1, D), F32),
            jax.ShapeDtypeStruct((planes, slab, D), BF16),
            jax.ShapeDtypeStruct(half, BF16),
            jax.ShapeDtypeStruct(quarter, BF16),
            jax.ShapeDtypeStruct(quarter, BF16),
            jax.ShapeDtypeStruct(quarter[:1] + quarter[2:], BF16),
            jax.ShapeDtypeStruct(half[:1] + half[2:], BF16),
            jax.ShapeDtypeStruct(quarter, BF16),
            jax.ShapeDtypeStruct(quarter, BF16),
            jax.ShapeDtypeStruct((4,) + mix.shape[1:], BF16),
            jax.ShapeDtypeStruct((4,) + mix.shape[1:], BF16),
            jax.ShapeDtypeStruct((n_ctx, slab, head_width), BF16),
        ],
        in_specs=[anywhere] + [inside] * 11 + [anywhere] * 9,
        out_specs=[inside] * 4 + [anywhere] * 10,
        scratch_shapes=[
            pltpu.VMEM(q.shape, BF16),
            pltpu.VMEM((n_ctx, 2, BLOCK, wide), F32),
            pltpu.VMEM(half, BF16),
            pltpu.VMEM(half, BF16),
            pltpu.VMEM(q.shape, BF16),
            pltpu.VMEM(kv.shape, BF16),
            pltpu.VMEM(q.shape, BF16),
            pltpu.VMEM(kv.shape, BF16),
            pltpu.VMEM(q_full.shape, BF16),
            pltpu.VMEM(k_full.shape, BF16),
            pltpu.VMEM(v_full.shape, BF16),
            pltpu.VMEM((SEQS * BLOCK, columns), BF16),
            pltpu.VMEM((SEQS * BLOCK, D), F32),
            pltpu.VMEM((2, SEQS * BLOCK, D), BF16),
            pltpu.VMEM((SEQS * BLOCK, 3 * wide), BF16),
            pltpu.VMEM((D, 3 * wide), F32),
            pltpu.VMEM((n_ctx, 2, 2, slab, head_width), BF16),
            pltpu.VMEM((n_ctx, 2, slab, head_width), BF16),
            pltpu.VMEM((n_ctx, slab, head_width), BF16),
            pltpu.VMEM((planes, 2, 2, slab, D), BF16),
            pltpu.VMEM((planes, 2, 2, slab, D), BF16),
            pltpu.VMEM((planes, 2, slab, D), BF16),
            pltpu.VMEM((planes, slab, D), BF16),
            dma((others,)), dma((others,)), dma((KEY_VALUE_HEADS,)), dma((KEY_VALUE_HEADS,)),
            dma((n_ctx,)), dma((n_ctx,)), dma((RANKS - 1,)), dma((RANKS - 1,)), dma((5,)), dma((5,)),
            dma((11,)), dma((3,)), dma((3,)), dma((n_ctx + 1,)), dma((n_ctx + 1,)), dma((2,)),
        ],
        compiler_params=pltpu.CompilerParams(
            collective_id=cid, has_side_effects=True, vmem_limit_bytes=62 << 20
        ),
        cost_estimate=lasting(125),
    )(
        g_own, q, kv, segq, codes, full, logs, cosine, sine, tok, gain, resid_grad, residual,
        grads, down_in, mix, output_part, tokens_all, q_full, k_full, v_full,
    )


def final_kernel(
    n_ctx, small, output_part, grads, gate_keep, gate_came, gate_other, up_came, down_keep, down_came,
    swapped, output_grad, small_sum,
    halves, landed, rest, rest_landed, last, last_landed, turned, output_in, small_in,
    send_half, recv_half, send_deep, recv_deep, send_out, recv_out, send_small, recv_small,
    send_swap, recv_swap, load, stay,
):
    c, f = lax.axis_index("ctx"), lax.axis_index("fsdp")
    me, plane, rank = c * 4 + f, lax.div(c, 2), lax.rem(c, 2) * 4 + f
    planes = n_ctx // 2
    half, quarter = planes // 2, planes // 4
    barrier = pltpu.get_barrier_semaphore()
    peers = [(i, k) for i in range(n_ctx) for k in range(4) if i or k]
    for dc, df in peers:
        pl.semaphore_signal(
            barrier, inc=1, device_id=(flip(c, dc), flip(f, df)), device_id_type=MESH
        )
    first, second = lax.rem(plane, 2), lax.rem(lax.div(plane, 2), 2)
    loads = [
        pltpu.make_async_copy(source, target, load.at[i])
        for i, (source, target) in enumerate(
            (
                (down_keep, rest.at[2]),
                (down_came, rest_landed.at[2]),
                (gate_keep, rest.at[0]),
                (gate_came.at[:, 0], rest_landed.at[0, :, 0]),
                (grads.at[1, pl.ds(first * half, half)], halves),
                (output_part.at[plane], output_in.at[plane]),
                (small.at[me], small_in.at[me]),
                (up_came, landed.at[:, 0]),
            )
        )
    ]
    for copy in loads:
        copy.start()
    pl.semaphore_wait(barrier, len(peers))

    def over(source, target, sent, came, bit):
        return pltpu.make_async_remote_copy(
            source, target, sent, came, device_id=(flip(c, 2 * bit), f), device_id_type=MESH
        )

    up_first = over(
        grads.at[1, pl.ds((1 - first) * half, half), 1], landed.at[:, 1],
        send_half.at[0, 1], recv_half.at[0, 1], 1,
    )
    gate_second = over(gate_other, rest_landed.at[0, :, 1], send_half.at[2, 1], recv_half.at[2, 1], 2)
    up_first.start()
    outputs = []
    for i in range(1, planes):
        outputs.append(
            pltpu.make_async_remote_copy(
                output_part.at[flip(plane, i)], output_in.at[plane], send_out.at[i - 1], recv_out.at[i - 1],
                device_id=(flip(c, 2 * i), f), device_id_type=MESH,
            )
        )
    smalls = []
    for number, (i, k) in enumerate(peers):
        peer_c, peer_f = flip(c, i), flip(f, k)
        smalls.append(
            pltpu.make_async_remote_copy(
                small.at[peer_c * 4 + peer_f], small_in.at[me], send_small.at[number], recv_small.at[number],
                device_id=(peer_c, peer_f), device_id_type=MESH,
            )
        )

    def plus(mine, came):
        return (mine.astype(F32) + came.astype(F32)).astype(BF16)

    swaps, sent = [], []

    def finish(m, e):
        count, bit, number = quarter, 4, 0
        for at in range(quarter):
            rest[m, at, e] = plus(rest[m, at, e], rest_landed[m, at, e])
        mine = rest.at[m, :, e]
        while count > 1:
            count //= 2
            chosen = lax.rem(lax.div(plane, bit), 2)
            came = last_landed.at[m, number, pl.ds(0, count), e]
            copy = over(
                mine.at[pl.ds((1 - chosen) * count, count)], came,
                send_deep.at[2 * m + number, e], recv_deep.at[2 * m + number, e], bit,
            )
            copy.start()
            copy.wait_recv()
            sent.append(copy)
            for at in range(count):
                last[m, number, at, e] = plus(mine[chosen * count + at], came[at])
            mine, bit, number = last.at[m, number, :, e], bit * 2, number + 1
        rows = turned.shape[3]
        across = mine[0].astype(F32).T
        for r in range(RANKS):
            turned[m, r, e] = across[r * rows : (r + 1) * rows].astype(BF16)
        for i in range(RANKS):
            source, target = turned.at[m, flip(rank, i), e], swapped.at[rank, m, e]
            if i:
                copy = pltpu.make_async_remote_copy(
                    source, target, send_swap.at[m * OWN + e, i], recv_swap.at[m * OWN + e, i],
                    device_id=(flip(c, i // 4), flip(f, i % 4)), device_id_type=MESH,
                )
            else:
                copy = pltpu.make_async_copy(source, target, stay.at[m * OWN + e])
            copy.start()
            swaps.append(copy)

    for copy in loads:
        copy.wait()
    up_second = []

    def second_of_up(e):
        for at in range(half):
            halves[at, e] = plus(halves[at, e], landed[at, e])
        up_second.append(
            over(
                halves.at[pl.ds((1 - second) * quarter, quarter), e], rest_landed.at[1, :, e],
                send_half.at[1, e], recv_half.at[1, e], 2,
            )
        )
        up_second[e].start()
        for at in range(quarter):
            rest[1, at, e] = halves[second * quarter + at, e]

    second_of_up(0)
    gate_second.start()
    for copy in outputs + smalls:
        copy.start()
    for e in range(OWN):
        finish(2, e)
    finish(0, 0)
    up_first.wait_recv()
    second_of_up(1)
    gate_second.wait_recv()
    finish(0, 1)
    for copy in outputs + smalls:
        copy.wait_recv()
    made = output_in[0].astype(F32)
    for i in range(1, planes):
        made = made + output_in[i].astype(F32)
    output_grad[...] = made
    small_sum[...] = jnp.sum(small_in[...], axis=0)
    for e in range(OWN):
        up_second[e].wait_recv()
        finish(1, e)
    for copy in swaps:
        copy.wait()
    for copy in smalls + outputs + sent + up_second + [up_first, gate_second]:
        copy.wait_send()


def final_sums(
    cid, n_ctx, small, output_part, grads, gate_keep, gate_came, gate_other, up_came, down_keep,
    down_came
):
    anywhere = pl.BlockSpec(memory_space=pl.ANY)
    inside = pl.BlockSpec(memory_space=pltpu.VMEM)
    dma = pltpu.SemaphoreType.DMA
    devices, planes = n_ctx * 4, n_ctx // 2
    slab, piece = D // devices, grads.shape[2:]
    half, quarter = (planes // 2,) + piece, (planes // 4,) + piece
    deep = (3, 2, max(planes // 8, 1)) + piece
    return pl.pallas_call(
        functools.partial(final_kernel, n_ctx),
        name="final_sums",
        out_shape=[
            jax.ShapeDtypeStruct((RANKS, 3, OWN, slab, FF), BF16),
            jax.ShapeDtypeStruct((slab, D), F32),
            jax.ShapeDtypeStruct(small.shape[1:], F32),
        ],
        in_specs=[anywhere] * 9,
        out_specs=[anywhere] + [inside] * 2,
        scratch_shapes=[
            pltpu.VMEM(half, BF16),
            pltpu.VMEM(half, BF16),
            pltpu.VMEM((3,) + quarter, BF16),
            pltpu.VMEM((3,) + quarter, BF16),
            pltpu.VMEM(deep if planes > 4 else (1, 1, 1, 1, 8, 128), BF16),
            pltpu.VMEM(deep if planes > 4 else (1, 1, 1, 1, 8, 128), BF16),
            pltpu.VMEM((3, RANKS, OWN, slab, FF), BF16),
            pltpu.VMEM((planes, slab, D), BF16),
            pltpu.VMEM(small.shape, F32),
            dma((3, OWN)), dma((3, OWN)), dma((6, OWN)), dma((6, OWN)),
            dma((planes - 1,)), dma((planes - 1,)), dma((devices - 1,)), dma((devices - 1,)),
            dma((3 * OWN, RANKS)), dma((3 * OWN, RANKS)), dma((8,)), dma((3 * OWN,)),
        ],
        compiler_params=pltpu.CompilerParams(
            collective_id=cid, has_side_effects=True, vmem_limit_bytes=56 << 20
        ),
        cost_estimate=lasting(80),
    )(small, output_part, grads, gate_keep, gate_came, gate_other, up_came, down_keep, down_came)


def rope_tables(positions):
    half_dim = HEAD_SIZE // 2
    frequency = ROPE_BASE ** (-jnp.arange(half_dim, dtype=F32) * 2.0 / HEAD_SIZE)
    angle = positions.astype(F32)[:, None] * frequency[None, :]
    angle = jnp.concatenate([angle, angle], axis=1)
    return (jnp.cos(angle), jnp.sin(angle))


def heads_out(field, per):
    field = field.reshape(SEQS, BLOCK, KEY_VALUE_HEADS, per, HEAD_SIZE)
    return field.transpose(2, 3, 1, 0, 4).reshape(KEY_VALUE_HEADS, per, BLOCK, SEQS * HEAD_SIZE)


def heads_in(field):
    per = field.shape[1]
    field = field.reshape(KEY_VALUE_HEADS, per, BLOCK, SEQS, HEAD_SIZE)
    return field.transpose(3, 2, 0, 1, 4).reshape(SEQS, BLOCK, KEY_VALUE_HEADS * per * HEAD_SIZE)


def on_device(
    n_ctx,
    n_fsdp,
    tokens,
    segments,
    valid,
    expert_ids,
    slot_order,
    cotangent,
    norm1_gain,
    w_query,
    key_weight,
    value_weight,
    w_output,
    norm2_gain,
    w_router,
    w_gate,
    w_up,
    w_down,
):
    parts = n_ctx // KEY_VALUE_HEADS
    replicas = n_ctx // 2
    full_len = segments.shape[1]
    c_index, f_index = lax.axis_index("ctx"), lax.axis_index("fsdp")
    pair = lax.rem(c_index, 2)
    rank = pair * n_fsdp + f_index
    part = lax.rem(c_index, parts)
    head = lax.div(c_index, parts)
    positions = c_index * BLOCK + jnp.arange(BLOCK, dtype=jnp.int32)

    span = D // n_fsdp // 2
    nears = [
        lax.ppermute(
            lax.dynamic_slice_in_dim(w, pair * span, span, 0), "fsdp", [(a, a ^ 2) for a in range(n_fsdp)]
        )
        for w in (w_query, key_weight, value_weight)
    ]
    tokens_all = lax.all_gather(tokens, "ctx", axis=0, tiled=False)
    small = jnp.concatenate(
        [
            norm1_gain[None],
            norm2_gain[None],
            w_router.T,
            jnp.zeros((SMALL - EXPERTS - 2, D // n_fsdp), BF16),
        ],
        axis=0,
    )
    packs = [
        lax.dynamic_slice_in_dim(w, pair * (EXPERTS // 2), EXPERTS // 2, 1)
        .reshape(D // n_fsdp, n_fsdp, OWN, FF)
        .transpose(1, 2, 0, 3)
        for w in (w_gate, w_up, w_down)
    ]
    inputs_f = tokens.astype(F32)
    scale_one = lax.rsqrt(jnp.mean(inputs_f * inputs_f, axis=-1, keepdims=True) + EPS)
    segq = segments.reshape(SEQS, KEY_VALUE_HEADS, parts, BLOCK)
    segq = lax.dynamic_index_in_dim(segq, part, 2, keepdims=False).transpose(1, 0, 2)[..., None]
    codes = jnp.where(valid > 0, segments, -1)
    codes = codes.reshape(SEQS, full_len // KEYS, KEYS).transpose(1, 0, 2)
    all_cosine, all_sine = rope_tables(jnp.arange(full_len, dtype=jnp.int32))
    all_cosine = jnp.tile(all_cosine, (1, 2)).reshape(n_ctx, BLOCK, 2 * HEAD_SIZE)
    all_sine = jnp.tile(all_sine, (1, 2)).reshape(n_ctx, BLOCK, 2 * HEAD_SIZE)
    (
        normed_in, small_all, full_query, full_key, full_value, q_all, kv_all, head_full, head_logs,
        attn_heads, full_output, own_gate, own_up, own_down,
    ) = attention_forward(
        0, parts, n_ctx, tokens.reshape(SEQS * BLOCK, D), small, w_query, key_weight, value_weight,
        w_output, nears, packs,
        lax.dynamic_index_in_dim(all_cosine, c_index, 0, keepdims=False),
        lax.dynamic_index_in_dim(all_sine, c_index, 0, keepdims=False),
        segq, codes,
    )
    gain_first = small_all[:, 0].reshape(D).astype(F32)
    gain_second = small_all[:, 1].reshape(D).astype(F32)
    full_router = small_all[:, 2 : 2 + EXPERTS].transpose(1, 0, 2).reshape(EXPERTS, D)
    full_output = full_output.reshape(D, D)
    attn_out = heads_in(attn_heads)
    attn_proj = jnp.einsum("sgq,dq->sgd", attn_out, full_output, preferred_element_type=F32)
    residual = inputs_f + attn_proj
    scale_two = lax.rsqrt(jnp.mean(residual * residual, axis=-1, keepdims=True) + EPS)
    normed_mid = (residual * scale_two * gain_second).astype(BF16)

    logits = jnp.einsum("sgd,ed->sge", normed_mid, full_router, preferred_element_type=F32)
    picked = jnp.any(expert_ids[..., None] == jnp.arange(EXPERTS, dtype=jnp.int32), axis=2)
    before = (slot_order[:, None, :] < slot_order[:, :, None]).astype(BF16)
    place = jnp.matmul(before, picked.astype(BF16), preferred_element_type=F32)
    is_kept = picked & (place < CAP)
    chosen = jnp.where(picked, logits, MASKED)
    raised = jnp.where(picked, jnp.exp(chosen - jnp.max(chosen, axis=-1, keepdims=True)), 0.0)
    gates = raised / jnp.sum(raised, axis=-1, keepdims=True)
    payload = jnp.concatenate(
        [
            normed_mid,
            jnp.where(is_kept, place, -1.0).astype(BF16),
            gates.astype(BF16),
            jnp.zeros((SEQS, BLOCK, 128 - 2 * EXPERTS), BF16),
        ],
        axis=2,
    )
    back, mix_part, own_grads, down_first, down_early = run_experts(
        2, replicas, payload.reshape(SEQS * BLOCK, PAY), cotangent.reshape(SEQS * BLOCK, D),
        (own_gate, own_up, own_down), tokens_all
    )

    back = back.reshape(SEQS, BLOCK, D + 128)
    grad_gates = jnp.where(is_kept, back[..., D : D + EXPERTS], 0.0)
    grad_chosen = gates * (grad_gates - jnp.sum(gates * grad_gates, axis=-1, keepdims=True))
    grad_logits = grad_chosen.astype(BF16)
    grad_mid = back[..., :D] + jnp.einsum(
        "sge,ed->sgd", grad_logits, full_router, preferred_element_type=F32
    )
    grad_router = jnp.einsum("sgd,sge->de", normed_mid, grad_logits, preferred_element_type=F32)

    grad_f = cotangent.astype(F32)
    weighted_two = gain_second * grad_mid
    grad_gain_second = jnp.sum(grad_mid * residual * scale_two, axis=(0, 1))
    cube_two = scale_two * scale_two * scale_two
    grad_resid = (
        grad_f
        + scale_two * weighted_two
        - residual * cube_two * jnp.mean(weighted_two * residual, axis=-1, keepdims=True)
    )
    grad_resid_low = grad_resid.astype(BF16)
    grad_attn = jnp.einsum("sgd,dq->sgq", grad_resid_low, full_output, preferred_element_type=F32)
    grad_attn = grad_attn.astype(BF16)
    grad_output_w = jnp.einsum("sgd,sgq->dq", grad_resid_low, attn_out, preferred_element_type=F32)
    rows = D // (n_ctx * n_fsdp)
    output_part = grad_output_w.astype(BF16).reshape(replicas, 2, 2, 2, rows, D)

    (
        input_grad, layer_out, gain_grad, output_sum, _, gate_keep, gate_came, gate_other, up_came, down_keep,
        down_came, _, _, head_grads,
    ) = attention_backward(
        6, parts, n_ctx, down_early, heads_out(grad_attn, REP), q_all, kv_all, segq, codes, head_full, head_logs,
        all_cosine, all_sine, tokens.reshape(SEQS * BLOCK, D), gain_first[None],
        grad_resid.reshape(SEQS * BLOCK, D), residual.reshape(SEQS * BLOCK, D), own_grads, down_first, mix_part, output_part,
        tokens_all.reshape(n_ctx, SEQS * BLOCK, D), full_query, full_key, full_value,
    )
    input_grad = input_grad.reshape(SEQS, BLOCK, D)
    layer_out = layer_out.reshape(SEQS, BLOCK, D)
    amount = rows * (EXPERTS + 2)
    tiles = -(-amount // 1024) * 8
    small_grads = jnp.concatenate([grad_router, gain_grad.T, grad_gain_second[:, None]], axis=1)
    small_grads = jnp.pad(
        small_grads.reshape(n_ctx * n_fsdp, amount), ((0, 0), (0, tiles * 128 - amount))
    ).reshape(n_ctx * n_fsdp, tiles, 128)
    swapped, output_grad, small_sum = final_sums(
        9, n_ctx, small_grads, output_sum, own_grads, gate_keep, gate_came, gate_other, up_came,
        down_keep, down_came,
    )
    small_sum = small_sum.reshape(tiles * 128)[:amount].reshape(rows, EXPERTS + 2)
    head_grads = head_grads.reshape(KEY_VALUE_HEADS, parts, rows, (REP + 2) * HEAD_SIZE)
    own_gain = lax.dynamic_slice_in_dim(gain_first, (c_index * n_fsdp + f_index) * rows, rows, 0)
    head_grads = jnp.sum(head_grads.astype(F32), axis=1).transpose(1, 0, 2) * own_gain[:, None, None]
    query_grad = head_grads[..., : REP * HEAD_SIZE].reshape(rows, D)
    key_grad = head_grads[..., REP * HEAD_SIZE : (REP + 1) * HEAD_SIZE].reshape(rows, -1)
    value_grad = head_grads[..., (REP + 1) * HEAD_SIZE :].reshape(rows, -1)

    def by_row(matrix):
        return swapped[:, matrix].transpose(2, 0, 1, 3).reshape(rows, EXPERTS, FF).astype(F32)

    return (
        layer_out,
        input_grad,
        small_sum[:, EXPERTS],
        query_grad,
        key_grad,
        value_grad,
        output_grad,
        small_sum[:, EXPERTS + 1],
        small_sum[:, :EXPERTS],
        by_row(0),
        by_row(1),
        by_row(2),
    )


def solution(mesh):
    placed = (
        P("fsdp", "ctx", None),
        P("fsdp", None),
        P("fsdp", None),
        P("fsdp", "ctx", None),
        P("fsdp", "ctx"),
        P("fsdp", "ctx", None),
        P("fsdp"),
        P("fsdp", None),
        P("fsdp", None),
        P("fsdp", None),
        P("fsdp", None),
        P("fsdp"),
        P("fsdp", None),
        P("fsdp", None, None),
        P("fsdp", None, None),
        P("fsdp", None, None),
    )
    return jax.shard_map(
        functools.partial(on_device, mesh.shape["ctx"], mesh.shape["fsdp"]),
        mesh=mesh,
        in_specs=placed,
        out_specs=(
            P("fsdp", "ctx", None),
            P("fsdp", "ctx", None),
            P(("ctx", "fsdp")),
            P(("ctx", "fsdp"), None),
            P(("ctx", "fsdp"), None),
            P(("ctx", "fsdp"), None),
            P(("ctx", "fsdp"), None),
            P(("ctx", "fsdp")),
            P(("ctx", "fsdp"), None),
            P(("ctx", "fsdp"), None, None),
            P(("ctx", "fsdp"), None, None),
            P(("ctx", "fsdp"), None, None),
        ),
        check_vma=False,
    )
```

```python
import functools

import jax
import jax.numpy as jnp
from jax import lax
from jax.experimental import pallas as pl
from jax.experimental.pallas import tpu as pltpu
from jax.sharding import PartitionSpec as P

D = 1536
QUERY_HEADS = 24
KEY_VALUE_HEADS = 8
REP = QUERY_HEADS // KEY_VALUE_HEADS
HEAD_SIZE = 64
FF = 512
EXPERTS = 16
CAP = 80
RANKS = 8
OWN = EXPERTS // RANKS
SEQS = 2
BLOCK = 128
KEYS = 256

EPS = 1e-05
ROPE_BASE = 10000.0
MASKED = -1e30
SCALE = HEAD_SIZE ** (-0.5)
MESH = pl.DeviceIdType.MESH
BF16 = jnp.bfloat16
F32 = jnp.float32


def flip(index, constant):
    result, bit = index, 1
    while bit <= constant:
        if constant & bit:
            result = result + bit - 2 * bit * lax.rem(lax.div(index, bit), 2)
        bit *= 2
    return result


def lasting(microseconds):
    return pl.CostEstimate(flops=0, bytes_accessed=int(microseconds * 3.3e6), transcendentals=0)


PAY = D + 128
GROUPS = 4
ROWS = GROUPS * CAP


def other_chip(c, f, k):
    pair, x = lax.div(k, 2), lax.rem(k, 2)
    return (
        c + pair * (1 - 2 * lax.rem(c, 2)),
        f + 2 * x * (1 - 2 * lax.rem(lax.div(f, 2), 2)),
    )


def plane_order(replicas):
    order = [0]
    while len(order) < replicas:
        order = [2 * i for i in order] + [2 * i + 1 for i in order]
    return order


def experts_kernel(
    replicas, pay, cot, gate_own, up_own, down_own, after,
    back, mix, grads, down_came, pay_in, cot_in,
    weights, total, pay_now, cot_now, xs, gs, eo, gi, hid, dgate, dup, disp, comb,
    own, out, sib, ret, mix_now,
    send_first, recv_first, send_fwd, recv_fwd, send_sib, recv_sib, send_chip, recv_chip,
    load_w, load, store, piece_sem, send_down, recv_down,
):
    c, f = lax.axis_index("ctx"), lax.axis_index("fsdp")
    rank = lax.rem(c, 2) * 4 + f
    sibling = (c, flip(f, 1))
    barrier = pltpu.get_barrier_semaphore()
    pl.semaphore_signal(barrier, inc=1, device_id=sibling, device_id_type=MESH)
    for k in range(1, 4):
        pl.semaphore_signal(barrier, inc=1, device_id=other_chip(c, f, k), device_id_type=MESH)
    apart = len(grads.shape) == 5
    if apart:
        pl.semaphore_signal(barrier, inc=1, device_id=(flip(c, 2), f), device_id_type=MESH)
    bring = []
    for m, own_weight in enumerate((gate_own, up_own, down_own)):
        bring.append(pltpu.make_async_copy(own_weight, weights.at[m], load_w.at[m]))
        bring[-1].start()
    pl.semaphore_wait(barrier, 5 if apart else 4)
    sources, landed = (pay, cot), (pay_in, cot_in)

    def push(k, a):
        slot = 1 if k == 0 else 2 * k
        return pltpu.make_async_remote_copy(
            sources[a], landed[a].at[slot - 1], send_first.at[k, a], recv_first.at[k, a],
            device_id=sibling if k == 0 else other_chip(c, f, k), device_id_type=MESH,
        )

    def forward(k, a):
        return pltpu.make_async_remote_copy(
            landed[a].at[2 * k - 1], landed[a].at[2 * k], send_fwd.at[k - 1, a], recv_fwd.at[k - 1, a],
            device_id=sibling, device_id_type=MESH,
        )

    def to_sibling(k):
        return pltpu.make_async_remote_copy(
            out.at[lax.rem(k, 2)], sib.at[k], send_sib.at[k], recv_sib.at[k],
            device_id=sibling, device_id_type=MESH,
        )

    def to_chip(k):
        return pltpu.make_async_remote_copy(
            sib.at[k], ret.at[k - 1], send_chip.at[k - 1], recv_chip.at[k - 1],
            device_id=other_chip(c, f, k), device_id_type=MESH,
        )

    def store_mix(k, s):
        return pltpu.make_async_copy(mix_now.at[s], mix.at[2 * k + s], store.at[s])

    for k, a in ((0, 0), (0, 1), (1, 0), (2, 0), (1, 1), (2, 1), (3, 0), (3, 1)):
        push(k, a).start()

    stages = (eo, gi)

    def leaving(m, e, stage):
        if not apart:
            return [pltpu.make_async_copy(stages[stage].at[:FF], grads.at[m, e], piece_sem.at[stage, 0])]
        width = D // replicas
        return [
            pltpu.make_async_copy(
                stages[stage].at[:FF, plane * width : (plane + 1) * width],
                grads.at[m, at, e],
                piece_sem.at[stage, at],
            )
            for at, plane in enumerate(plane_order(replicas))
        ]

    if apart:
        half = replicas // 2
        down_first = pltpu.make_async_remote_copy(
            grads.at[2, pl.ds((1 - lax.rem(lax.div(c, 2), 2)) * half, half)], down_came,
            send_down, recv_down, device_id=(flip(c, 2), f), device_id_type=MESH,
        )

    def clear(i, carry):
        total[lax.div(i, OWN), lax.rem(i, OWN)] = jnp.zeros((FF, D), F32)
        return carry

    lax.fori_loop(0, 3 * OWN, clear, 0)
    lane = lax.broadcasted_iota(jnp.int32, (BLOCK, 128), 1)
    wide = lax.broadcasted_iota(jnp.int32, (BLOCK, 2 * BLOCK), 1).astype(F32)
    both = lax.broadcasted_iota(jnp.int32, (BLOCK, OWN * CAP), 1)

    def chunk(k, carry):
        now = (pay_now, cot_now)

        def fetch(a, s, source):
            copy = pltpu.make_async_copy(source, now[a].at[s], load.at[a, s])
            copy.start()
            return copy

        def arrived(chip):
            for a in range(2):
                push(chip, a).wait_recv()
                forward(chip, a).start()

        def fetch_chip(chip):
            for a in range(2):
                fetch(a, 0, landed[a].at[2 * chip - 1])
            for a in range(2):
                forward(chip, a).wait_recv()
                fetch(a, 1, landed[a].at[2 * chip])

        @pl.when(k == 0)
        def _():
            copies = [fetch(a, 0, sources[a]) for a in range(2)]
            for a in range(2):
                push(0, a).wait_recv()
            copies += [fetch(a, 1, landed[a].at[0]) for a in range(2)]
            for copy in copies:
                copy.wait()
            for copy in bring:
                copy.wait()

        @pl.when(k == 1)
        def _():
            arrived(1)
            arrived(2)
            fetch_chip(1)

        @pl.when(k > 0)
        def _():
            for a in range(2):
                for s in range(2):
                    pltpu.make_async_copy(landed[a].at[2 * k - 1 + s], now[a].at[s], load.at[a, s]).wait()

        for g in range(GROUPS):
            s, at = g // 2, (g % 2) * BLOCK
            tail = pay_now[s, at : at + BLOCK, D:].astype(F32)

            def column(index):
                return jnp.sum(jnp.where(lane == index, tail, 0.0), axis=1, keepdims=True)

            table = jnp.zeros((BLOCK, 2 * BLOCK), F32)
            gated = jnp.zeros((BLOCK, 2 * BLOCK), F32)
            for e in range(OWN):
                place = column(rank * OWN + e)
                place = jnp.where(place < 0.0, -1000.0, place + e * CAP)
                here = wide == place
                table = jnp.where(here, 1.0, table)
                gated = jnp.where(here, column(EXPERTS + rank * OWN + e), gated)
            table, gated = table.astype(BF16), gated.astype(BF16)
            disp[g] = table
            comb[g] = gated
            for weight, source, keep in (
                (table, pay_now[s, at : at + BLOCK, :D], xs),
                (gated, cot_now[s, at : at + BLOCK], gs),
            ):
                moved = lax.dot_general(
                    weight, source, (((0,), (0,)), ((), ())), preferred_element_type=F32
                ).astype(BF16)
                for e in range(OWN):
                    keep[e, g * CAP : (g + 1) * CAP] = moved[e * CAP : (e + 1) * CAP]

        def expert(e, carry):
            at = pl.multiple_of(e * CAP, 16)
            gate_pre = jnp.dot(xs[e], weights[0, e], preferred_element_type=F32)
            up_pre = jnp.dot(xs[e], weights[1, e], preferred_element_type=F32)
            sigmoid = 1.0 / (1.0 + jnp.exp(-gate_pre))
            activated = gate_pre * sigmoid
            hidden = (activated * up_pre).astype(BF16)
            hid[e] = hidden
            made = lax.dot_general(
                hidden, weights[2, e], (((1,), (1,)), ((), ())), preferred_element_type=F32
            ).astype(BF16)
            for g in range(GROUPS):
                eo[pl.ds(pl.multiple_of(g * OWN * CAP + at, 16), CAP)] = made[g * CAP : (g + 1) * CAP]
            grad_hidden = jnp.dot(gs[e], weights[2, e], preferred_element_type=F32)
            slope = sigmoid * (1.0 + gate_pre * (1.0 - sigmoid))
            grad_gate = (grad_hidden * up_pre * slope).astype(BF16)
            grad_up = (grad_hidden * activated).astype(BF16)
            dgate[e] = grad_gate
            dup[e] = grad_up
            made = lax.dot_general(
                grad_gate, weights[0, e], (((1,), (1,)), ((), ())), preferred_element_type=F32
            )
            made = made + lax.dot_general(
                grad_up, weights[1, e], (((1,), (1,)), ((), ())), preferred_element_type=F32
            )
            made = made.astype(BF16)
            for g in range(GROUPS):
                gi[pl.ds(pl.multiple_of(g * OWN * CAP + at, 16), CAP)] = made[g * CAP : (g + 1) * CAP]
            return carry

        lax.fori_loop(0, OWN, expert, 0)

        @pl.when(k > 0)
        def _():
            for s in range(2):
                store_mix(k - 1, s).wait()

        @pl.when(k > 1)
        def _():
            to_sibling(k - 2).wait_send()

        parity = lax.rem(k, 2)
        for g in range(GROUPS):
            s, at = g // 2, (g % 2) * BLOCK
            slots = pl.ds(g * OWN * CAP, OWN * CAP)
            made = eo[slots]
            mix_now[s, at : at + BLOCK] = jnp.dot(
                comb[g][:, : OWN * CAP], made, preferred_element_type=F32
            ).astype(BF16)
            table = disp[g][:, : OWN * CAP]
            grad_mid = jnp.dot(table, gi[slots], preferred_element_type=F32).astype(BF16)
            met = lax.dot_general(
                cot_now[s, at : at + BLOCK], made, (((1,), (1,)), ((), ())), preferred_element_type=F32
            ) * table.astype(F32)
            values = jnp.zeros((BLOCK, 128), F32)
            for e in range(OWN):
                inside = (both >= e * CAP) & (both < (e + 1) * CAP)
                value = jnp.sum(jnp.where(inside, met, 0.0), axis=1, keepdims=True)
                values = jnp.where(lane == rank * OWN + e, value, values)
            target = own if s == 0 else out
            target[parity, at : at + BLOCK, :D] = grad_mid
            target[parity, at : at + BLOCK, D:] = values.astype(BF16)
        to_sibling(k).start()
        for s in range(2):
            store_mix(k, s).start()

        @pl.when(k == 1)
        def _():
            fetch_chip(2)

        @pl.when(k == 2)
        def _():
            arrived(3)
            fetch_chip(3)

        def down_grads(e, carry):
            total[2, e] += lax.dot_general(
                hid[e], gs[e], (((0,), (0,)), ((), ())), preferred_element_type=F32
            )
            return carry

        def other_grads(e, carry):
            for m, left in enumerate((dgate, dup)):
                total[m, e] += lax.dot_general(
                    left[e], xs[e], (((0,), (0,)), ((), ())), preferred_element_type=F32
                )
            return carry

        lax.fori_loop(0, OWN, down_grads, 0)

        @pl.when(k == 3)
        def _():
            for e in range(OWN):
                stages[e][:FF] = total[2, e].astype(BF16)
                for copy in leaving(2, e, e):
                    copy.start()

        lax.fori_loop(0, OWN, other_grads, 0)

        @pl.when(k == 3)
        def _():
            for e in range(OWN):
                for copy in leaving(2, e, e):
                    copy.wait()
            if apart:
                down_first.start()

        to_sibling(k).wait_recv()
        sib[k] = (sib[k].astype(F32) + own[parity].astype(F32)).astype(BF16)

        @pl.when(k > 0)
        def _():
            to_chip(k).start()

        return carry

    lax.fori_loop(0, 4, chunk, 0)
    for s in range(2):
        store_mix(3, s).wait()
    for i in range(2 * OWN):
        m, e = i // OWN, i % OWN
        if i >= 2:
            for copy in leaving((i - 2) // OWN, (i - 2) % OWN, i % 2):
                copy.wait()
        stages[i % 2][:FF] = total[m, e].astype(BF16)
        for copy in leaving(m, e, i % 2):
            copy.start()
    for i in (2 * OWN - 2, 2 * OWN - 1):
        for copy in leaving(i // OWN, i % OWN, i % 2):
            copy.wait()
    for k in (2, 3):
        to_sibling(k).wait_send()
    for k in range(4):
        for a in range(2):
            push(k, a).wait_send()
            if k:
                forward(k, a).wait_send()
    for k in range(1, 4):
        to_chip(k).wait_recv()
    back[...] = (sib[0].astype(F32) + ret[0].astype(F32)) + (ret[1].astype(F32) + ret[2].astype(F32))
    for k in range(1, 4):
        to_chip(k).wait_send()
    if apart:
        down_first.wait()


def run_experts(cid, replicas, pay, cot, owns, after):
    width = D // replicas
    apart = width % 128 == 0
    tokens = SEQS * BLOCK
    anywhere = pl.BlockSpec(memory_space=pl.ANY)
    inside = pl.BlockSpec(memory_space=pltpu.VMEM)
    dma = pltpu.SemaphoreType.DMA
    back, mix, grads, down_came, _, _ = pl.pallas_call(
        functools.partial(experts_kernel, replicas),
        name="experts",
        out_shape=[
            jax.ShapeDtypeStruct((tokens, PAY), F32),
            jax.ShapeDtypeStruct((RANKS, tokens, D), BF16),
            jax.ShapeDtypeStruct((3, replicas, OWN, FF, width) if apart else (3, OWN, FF, D), BF16),
            jax.ShapeDtypeStruct((replicas // 2, OWN, FF, width) if apart else (8, 128), BF16),
            jax.ShapeDtypeStruct((RANKS - 1, tokens, PAY), BF16),
            jax.ShapeDtypeStruct((RANKS - 1, tokens, D), BF16),
        ],
        in_specs=[anywhere] * 6,
        out_specs=[inside] + [anywhere] * 5,
        scratch_shapes=[
            pltpu.VMEM((3, OWN, D, FF), BF16),
            pltpu.VMEM((3, OWN, FF, D), F32),
            pltpu.VMEM((2, tokens, PAY), BF16),
            pltpu.VMEM((2, tokens, D), BF16),
            pltpu.VMEM((OWN, ROWS, D), BF16),
            pltpu.VMEM((OWN, ROWS, D), BF16),
            pltpu.VMEM((OWN * ROWS, D), BF16),
            pltpu.VMEM((OWN * ROWS, D), BF16),
            pltpu.VMEM((OWN, ROWS, FF), BF16),
            pltpu.VMEM((OWN, ROWS, FF), BF16),
            pltpu.VMEM((OWN, ROWS, FF), BF16),
            pltpu.VMEM((GROUPS, BLOCK, 2 * BLOCK), BF16),
            pltpu.VMEM((GROUPS, BLOCK, 2 * BLOCK), BF16),
            pltpu.VMEM((2, tokens, PAY), BF16),
            pltpu.VMEM((2, tokens, PAY), BF16),
            pltpu.VMEM((4, tokens, PAY), BF16),
            pltpu.VMEM((3, tokens, PAY), BF16),
            pltpu.VMEM((2, tokens, D), BF16),
            dma((4, 2)), dma((4, 2)), dma((3, 2)), dma((3, 2)),
            dma((4,)), dma((4,)), dma((3,)), dma((3,)),
            dma((4,)), dma((2, 2)), dma((2,)), dma((2, replicas)), dma, dma,
        ],
        compiler_params=pltpu.CompilerParams(
            collective_id=cid, has_side_effects=True, vmem_limit_bytes=63 << 20
        ),
        cost_estimate=lasting(110),
    )(pay, cot, *owns, after)
    if not apart:
        grads = grads.reshape(3, OWN, FF, replicas, width).transpose(0, 3, 1, 2, 4)
        grads = grads[:, jnp.array(plane_order(replicas))]
    return back, mix, grads, down_came, apart


def half_masks(dtype):
    lane = lax.broadcasted_iota(jnp.int32, (1, 2 * HEAD_SIZE), 1)
    low = (lane < HEAD_SIZE).astype(F32)
    return low.astype(dtype), (1.0 - low).astype(dtype)


def allowed_at(block, step, segq, keycode):
    token = block * BLOCK + lax.broadcasted_iota(jnp.int32, (BLOCK, KEYS), 0)
    key = step * KEYS + lax.broadcasted_iota(jnp.int32, (BLOCK, KEYS), 1)
    return ((segq == keycode) & (key < token)) | (key == token)


SMALL = 32


def turn(field, cosine, sine):
    half = HEAD_SIZE // 2
    lane = lax.broadcasted_iota(jnp.int32, field.shape, field.ndim - 1)
    up = pltpu.roll(field, 2 * HEAD_SIZE - half, field.ndim - 1)
    down = pltpu.roll(field, half, field.ndim - 1)
    return field * cosine + jnp.where(lax.rem(lane, HEAD_SIZE) < half, -up, down) * sine


def attention_forward_kernel(
    parts, n_ctx, tok, small, w_q, w_k, w_v, w_o, near_q, near_k, near_v, pack0, pack1, pack2, cos_ref, sin_ref, seg_ref, code_ref,
    normed, small_all, q_full, k_full, v_full, q_ref, kv_ref, full_ref, log_ref, o_back, o_full,
    gate_own, up_own, down_own,
    acc, q_pack, kv_pack, o_buf, own_buf,
    send_w, recv_w, send_s, recv_s, send_e, recv_e, send_q, recv_q, send_kv, recv_kv, send_o, recv_o, here,
    send_z, recv_z,
):
    c, f = lax.axis_index("ctx"), lax.axis_index("fsdp")
    head, part, pair = lax.div(c, parts), lax.rem(c, parts), lax.rem(c, 2)
    rows = D // 4
    half = rows // 2
    wide = 2 * HEAD_SIZE
    barrier = pltpu.get_barrier_semaphore()
    peers = [(i, 0) for i in range(1, n_ctx)] + [(0, k) for k in range(1, 4)]
    for dc, df in peers:
        pl.semaphore_signal(
            barrier, inc=1, device_id=(flip(c, dc), flip(f, df)), device_id_type=MESH
        )
    shards = (w_q, w_k, w_v, w_o)
    fulls = (q_full, k_full, v_full, o_full)
    packs, owns = (pack0, pack1, pack2), (gate_own, up_own, down_own)
    my_rows = pl.ds(pl.multiple_of(f * rows, rows), rows)
    local = [pltpu.make_async_copy(shards[a], fulls[a].at[f], here.at[a]) for a in range(4)]
    local += [pltpu.make_async_copy(small, small_all.at[f], here.at[4])]
    local += [pltpu.make_async_copy(packs[m].at[f], own_buf.at[m], here.at[5 + m]) for m in range(3)]
    for copy in local:
        copy.start()
    pl.semaphore_wait(barrier, len(peers))
    near = pl.ds(pl.multiple_of(pair * half, half), half)
    far = pl.ds(pl.multiple_of((1 - pair) * half, half), half)
    sibling, over_x, over_pair = (c, flip(f, 1)), (c, flip(f, 2)), (flip(c, 1), f)
    nears = (near_q, near_k, near_v)
    crossed = [
        pltpu.make_async_copy(nears[a], fulls[a].at[flip(f, 2), near], here.at[11 + a]) for a in range(3)
    ]
    for copy in crossed:
        copy.start()

    def weight(a, kind):
        beyond = flip(f, 2)
        brought = nears[a] if a < 3 else fulls[a].at[beyond, near]
        source, target, device = (
            (shards[a], fulls[a].at[f], sibling),
            (shards[a].at[near], fulls[a].at[f, near], over_x),
            (brought, fulls[a].at[beyond, near], sibling),
            (brought, fulls[a].at[beyond, near], over_pair),
            (fulls[a].at[beyond, far], fulls[a].at[beyond, far], sibling),
        )[kind]
        return pltpu.make_async_remote_copy(
            source, target, send_w.at[a, kind], recv_w.at[a, kind], device_id=device, device_id_type=MESH
        )

    smalls = [
        pltpu.make_async_remote_copy(
            small, small_all.at[f], send_s.at[i - 1], recv_s.at[i - 1],
            device_id=(c, flip(f, i)), device_id_type=MESH,
        )
        for i in range(1, 4)
    ]
    for copy in smalls:
        copy.start()
    for a in range(4):
        for kind in (3, 0, 2) if a < 3 else (1, 0):
            weight(a, kind).start()
    bit = lax.rem(lax.div(c, 2), 2)
    half_rows = pl.ds(pl.multiple_of(bit * half, half), half)

    def half_of(owner):
        return pl.ds(pl.multiple_of(owner * rows + bit * half, half), half)

    shared = [
        pltpu.make_async_remote_copy(
            packs[2].at[flip(f, i), :, half_rows], owns[2].at[:, half_of(f)],
            send_e.at[i - 1, 2], recv_e.at[i - 1, 2], device_id=(c, flip(f, i)), device_id_type=MESH,
        )
        for i in (2, 3)
    ]
    onward = [
        pltpu.make_async_remote_copy(
            owns[2].at[:, half_of(flip(f, i))], owns[2].at[:, half_of(flip(f, i))],
            send_z.at[i - 2], recv_z.at[i - 2], device_id=(flip(c, 2), f), device_id_type=MESH,
        )
        for i in (2, 3)
    ]
    experts = [
        pltpu.make_async_remote_copy(
            packs[m].at[flip(f, i)], owns[m].at[:, my_rows], send_e.at[i - 1, m], recv_e.at[i - 1, m],
            device_id=(c, flip(f, i)), device_id_type=MESH,
        )
        for m, i in ((2, 1), (0, 1), (0, 2), (0, 3), (1, 1), (1, 2), (1, 3))
    ]
    for copy in shared + experts:
        copy.start()

    x = tok[...].astype(F32)
    scale = lax.rsqrt(jnp.mean(x * x, axis=1, keepdims=True) + EPS)
    for copy in smalls:
        copy.wait_recv()
    local[4].wait()
    for b in range(4):
        columns = slice(b * rows, (b + 1) * rows)
        normed[:, columns] = (x[:, columns] * scale * small_all[b, :1].astype(F32)).astype(BF16)

    def project(b, first):
        block = normed[:, pl.ds(pl.multiple_of(b * rows, rows), rows)]
        at = 0
        for a in range(3):
            width = fulls[a].shape[2]
            made = jnp.dot(block, fulls[a][b], preferred_element_type=F32)
            acc[:, at : at + width] = made if first else acc[:, at : at + width] + made
            at += width

    for a in range(3):
        local[a].wait()
    stores = []
    for m in range(3):
        local[5 + m].wait()
        stores.append(pltpu.make_async_copy(own_buf.at[m], owns[m].at[:, my_rows], here.at[5 + m]))
        stores[m].start()
    project(f, True)
    for a in range(3):
        weight(a, 0).wait_recv()
    project(flip(f, 1), False)
    for a in range(3):
        weight(a, 3).wait_recv()
        weight(a, 4).start()
        crossed[a].wait()
    project(flip(f, 2), False)
    for a in range(3):
        weight(a, 2).wait_recv()
        weight(a, 4).wait_recv()
    project(flip(f, 3), False)

    lane = lax.broadcasted_iota(jnp.int32, (BLOCK, wide), 1)
    low = lane < HEAD_SIZE
    cosine, sine = cos_ref[...], sin_ref[...]
    for m in range((QUERY_HEADS + 2 * KEY_VALUE_HEADS) // 2):
        pieces = []
        for s in range(SEQS):
            piece = acc[s * BLOCK : (s + 1) * BLOCK, m * wide : (m + 1) * wide]
            pieces.append(turn(piece, cosine, sine) if m < (QUERY_HEADS + KEY_VALUE_HEADS) // 2 else piece)
        even = jnp.where(low, pieces[0], pltpu.roll(pieces[1], HEAD_SIZE, 1)).astype(BF16)
        odd = jnp.where(low, pltpu.roll(pieces[0], HEAD_SIZE, 1), pieces[1]).astype(BF16)
        for h, value in ((2 * m, even), (2 * m + 1, odd)):
            if h < QUERY_HEADS:
                q_pack[h // REP, h % REP] = value
            else:
                h -= QUERY_HEADS
                kv_pack[h % KEY_VALUE_HEADS, h // KEY_VALUE_HEADS] = value

    q_stays = pltpu.make_async_copy(q_pack.at[head], q_ref.at[head], here.at[8])
    kv_stays = pltpu.make_async_copy(kv_pack.at[head], kv_ref.at[c], here.at[9])
    q_stays.start()
    kv_stays.start()
    to_heads = []
    for i in range(1, n_ctx):
        peer = flip(c, i)
        moves = [(kv_pack.at[lax.div(peer, parts)], kv_ref.at[c], send_kv.at[i - 1], recv_kv.at[i - 1])]
        if i % parts == 0:
            number = i // parts - 1
            moves.append(
                (q_pack.at[lax.div(peer, parts)], q_ref.at[head], send_q.at[number], recv_q.at[number])
            )
        for source, target, sent, came in moves:
            copy = pltpu.make_async_remote_copy(
                source, target, sent, came, device_id=(peer, f), device_id_type=MESH
            )
            copy.start()
            to_heads.append(copy)
    weight(3, 1).wait_recv()
    weight(3, 2).start()
    weight(3, 3).start()
    q_stays.wait()
    kv_stays.wait()
    for copy in to_heads:
        copy.wait_recv()
    for came, goes in zip(shared, onward):
        came.wait_recv()
        goes.start()

    count = REP * BLOCK
    halves = half_masks(BF16)
    across = lax.broadcasted_iota(jnp.int32, (count, wide), 1)

    def out_back(j):
        return pltpu.make_async_remote_copy(
            o_buf.at[j], o_back.at[head], send_o.at[j], recv_o.at[head],
            device_id=(j * parts + part, f), device_id_type=MESH,
        )

    def out_stays(j):
        return pltpu.make_async_copy(o_buf.at[j], o_back.at[head], here.at[10])

    def one_block(j, nothing):
        block = j * parts + part
        q = q_ref[j].reshape(count, wide)
        queries = [q * half for half in halves]

        def step(number, carry):
            k = kv_ref[pl.ds(2 * number, 2), 0].reshape(KEYS, wide)
            v = kv_ref[pl.ds(2 * number, 2), 1].reshape(KEYS, wide)
            codes = code_ref[number]
            after = []
            for s in range(SEQS):
                largest, total, out = carry[s]
                mask = allowed_at(block, number, seg_ref[j, s], codes[s : s + 1])
                scores = lax.dot_general(
                    queries[s], k, (((1,), (1,)), ((), ())), preferred_element_type=F32
                )
                scores = jnp.where(mask[None], scores.reshape(REP, BLOCK, KEYS) * SCALE, MASKED)
                scores = scores.reshape(count, KEYS)
                new = jnp.maximum(largest, jnp.max(scores, axis=1, keepdims=True))
                probs = jnp.exp(scores - new)
                shrink = jnp.exp(largest - new)
                total = total * shrink + jnp.sum(probs, axis=1, keepdims=True)
                out = out * shrink + jnp.dot(probs.astype(BF16), v, preferred_element_type=F32)
                after.append((new, total, out))
            return tuple(after)

        start = (
            jnp.full((count, 1), MASKED, F32),
            jnp.zeros((count, 1), F32),
            jnp.zeros((count, wide), F32),
        )
        done = lax.fori_loop(0, lax.div(block, 2) + 1, step, (start,) * SEQS)
        outs, logs = [], []
        for largest, total, out in done:
            outs.append(out / total)
            logs.append(jnp.broadcast_to(largest + jnp.log(total), (count, wide)))
        out = jnp.where(across < HEAD_SIZE, outs[0], outs[1])
        full_ref[j] = out.reshape(REP, BLOCK, wide)
        log_ref[j] = jnp.where(across < HEAD_SIZE, logs[0], logs[1]).reshape(REP, BLOCK, wide)
        o_buf[j] = out.astype(BF16).reshape(REP, BLOCK, wide)

        @pl.when(j != head)
        def _():
            out_back(j).start()

        @pl.when(j == head)
        def _():
            out_stays(j).start()

        return nothing

    lax.fori_loop(0, KEY_VALUE_HEADS, one_block, 0)
    weight(3, 3).wait_recv()
    weight(3, 4).start()

    def came_out(h, nothing):
        @pl.when(h != head)
        def _():
            pltpu.make_async_remote_copy(
                o_buf.at[h], o_back.at[h], send_o.at[h], recv_o.at[h],
                device_id=(h * parts + part, f), device_id_type=MESH,
            ).wait()

        @pl.when(h == head)
        def _():
            out_stays(h).wait()

        return nothing

    lax.fori_loop(0, KEY_VALUE_HEADS, came_out, 0)
    for kind in (0, 2, 4):
        weight(3, kind).wait_recv()
    local[3].wait()
    for copy in stores:
        copy.wait()
    for copy in experts + onward:
        copy.wait()
    for copy in smalls + to_heads + shared:
        copy.wait_send()
    for a in range(4):
        for kind in (0, 2, 3, 4) if a < 3 else range(5):
            weight(a, kind).wait_send()


def attention_forward(
    cid, parts, n_ctx, tok, small, w_q, w_k, w_v, w_o, nears, packs, cosine, sine, segq, codes
):
    wide = 2 * HEAD_SIZE
    anywhere = pl.BlockSpec(memory_space=pl.ANY)
    inside = pl.BlockSpec(memory_space=pltpu.VMEM)
    dma = pltpu.SemaphoreType.DMA
    heads = (KEY_VALUE_HEADS, REP, BLOCK, wide)
    keys = (n_ctx, 2, BLOCK, wide)
    others = max(n_ctx // parts - 1, 1)
    columns = w_q.shape[1] + w_k.shape[1] + w_v.shape[1]
    own = jax.ShapeDtypeStruct((OWN, D, FF), BF16)

    def full(x):
        return jax.ShapeDtypeStruct((4,) + x.shape, BF16)

    return pl.pallas_call(
        functools.partial(attention_forward_kernel, parts, n_ctx),
        name="attention_forward",
        out_shape=[
            jax.ShapeDtypeStruct(tok.shape, BF16),
            full(small), full(w_q), full(w_k), full(w_v),
            jax.ShapeDtypeStruct(heads, BF16),
            jax.ShapeDtypeStruct(keys, BF16),
            jax.ShapeDtypeStruct(heads, F32),
            jax.ShapeDtypeStruct(heads, F32),
            jax.ShapeDtypeStruct(heads, BF16),
            full(w_o), own, own, own,
        ],
        in_specs=[inside] + [anywhere] * 11 + [inside] * 4,
        out_specs=[inside] * 9 + [anywhere, inside] + [anywhere] * 3,
        scratch_shapes=[
            pltpu.VMEM((SEQS * BLOCK, columns), F32),
            pltpu.VMEM(heads, BF16),
            pltpu.VMEM((KEY_VALUE_HEADS, 2, BLOCK, wide), BF16),
            pltpu.VMEM(heads, BF16),
            pltpu.VMEM((3,) + packs[0].shape[1:], BF16),
            dma((4, 5)), dma((4, 5)), dma((3,)), dma((3,)), dma((3, 3)), dma((3, 3)),
            dma((others,)), dma((others,)), dma((n_ctx - 1,)), dma((n_ctx - 1,)),
            dma((KEY_VALUE_HEADS,)), dma((KEY_VALUE_HEADS,)), dma((14,)), dma((2,)), dma((2,)),
        ],
        compiler_params=pltpu.CompilerParams(
            collective_id=cid, has_side_effects=True, vmem_limit_bytes=56 << 20
        ),
        cost_estimate=lasting(130),
    )(tok, small, w_q, w_k, w_v, w_o, *nears, *packs, cosine, sine, segq, codes)


def turn_back(field, cosine, sine):
    half = HEAD_SIZE // 2
    lane = lax.broadcasted_iota(jnp.int32, field.shape, field.ndim - 1)
    up = pltpu.roll(field, 2 * HEAD_SIZE - half, field.ndim - 1)
    down = pltpu.roll(field, half, field.ndim - 1)
    turned = jnp.where(lax.rem(lane, HEAD_SIZE) < half, -up, down)
    return field * cosine - turned * sine


def attention_backward_kernel(
    parts, n_ctx, early, g_own, q_ref, kv_ref, seg_ref, code_ref, full_ref, log_ref, cos_ref, sin_ref,
    tok, gain, resid_grad, residual, grads, down_in, mix, output_part, tokens_all, q_full, k_full, v_full,
    input_grad, layer_out, gain_grad, output_sum, gate_first, gate_keep, gate_came, gate_other, up_came, down_keep, down_came,
    mix_core, mix_in, head_in, g_ref, total, kept, came, dq_ref, dkv_ref, dq_back, dkv_back, w_q, w_k, w_v, grad_qkv, grad_in,
    token_buf, field, head_acc, head_out, head_core, head_x, output_keep, output_came, output_x, output_pair,
    send_g, recv_g, send_q, recv_q, send_kv, recv_kv, send_mix, recv_mix, send_half, recv_half, here,
    send_out, recv_out, send_head, recv_head, load_t,
):
    c, f = lax.axis_index("ctx"), lax.axis_index("fsdp")
    head, part = lax.div(c, parts), lax.rem(c, parts)
    rows = REP * BLOCK
    wide = 2 * HEAD_SIZE
    barrier = pltpu.get_barrier_semaphore()
    peers = [(i, k) for i in range(n_ctx) for k in range(4) if i or k]
    for dc, df in peers:
        pl.semaphore_signal(
            barrier, inc=1, device_id=(flip(c, dc), flip(f, df)), device_id_type=MESH
        )
    pair, x_bit, core_bit = lax.rem(c, 2), lax.div(f, 2), lax.rem(f, 2)
    loads = [
        pltpu.make_async_copy(source, target, here.at[5 + i])
        for i, (source, target) in enumerate(
            (
                (q_full, w_q), (k_full, w_k), (v_full, w_v),
                (output_part.at[:, :, :, core_bit], output_keep),
            )
        )
    ]

    def bring(b):
        return pltpu.make_async_copy(
            tokens_all.at[b], token_buf.at[lax.rem(b, 2)], load_t.at[lax.rem(b, 2)]
        )

    for copy in loads[1:]:
        copy.start()
    first = pltpu.make_async_copy(g_own.at[head], g_ref.at[head], here.at[0])
    first.start()
    pl.semaphore_wait(barrier, len(peers))
    to_heads = []
    for number, i in enumerate(range(parts, n_ctx, parts)):
        to_heads.append(
            pltpu.make_async_remote_copy(
                g_own.at[lax.div(flip(c, i), parts)], g_ref.at[head],
                send_g.at[number], recv_g.at[number],
                device_id=(flip(c, i), f), device_id_type=MESH,
            )
        )
        to_heads[-1].start()
    half = grads.shape[1] // 2
    quarter = half // 2
    mine = lax.rem(lax.div(c, 2), 2)
    second = lax.rem(lax.div(c, 4), 2)

    def halving(matrix, target, number):
        return pltpu.make_async_remote_copy(
            grads.at[matrix, pl.ds((1 - mine) * half, half)], target,
            send_half.at[number], recv_half.at[number],
            device_id=(flip(c, 2), f), device_id_type=MESH,
        )

    down_halving, gate_halving = halving(2, came, 0), halving(0, gate_first, 1)
    arriving = pltpu.make_async_copy(down_in, came, here.at[10]) if early else down_halving
    arriving.start()
    up_halving = pltpu.make_async_remote_copy(
        grads.at[1, pl.ds((1 - mine) * half, half), 0], up_came, send_half.at[4], recv_half.at[4],
        device_id=(flip(c, 2), f), device_id_type=MESH,
    )
    keeping = pltpu.make_async_copy(grads.at[2, pl.ds(mine * half, half)], kept, here.at[3])
    keeping.start()
    output_stages = [
        pltpu.make_async_remote_copy(
            source, target, send_out.at[i], recv_out.at[i], device_id=device, device_id_type=MESH
        )
        for i, (source, target, device) in enumerate(
            (
                (output_part.at[:, :, :, 1 - core_bit], output_came, (c, flip(f, 1))),
                (output_keep.at[:, :, 1 - x_bit], output_x, (c, flip(f, 2))),
                (output_x.at[:, 1 - pair], output_pair, (flip(c, 1), f)),
            )
        )
    ]
    output_stages[0].start()
    to_core = [
        pltpu.make_async_remote_copy(
            mix.at[2 * k + 1], mix_core.at[k], send_mix.at[k], recv_mix.at[k],
            device_id=(c, flip(f, 1)), device_id_type=MESH,
        )
        for k in range(4)
    ]
    for copy in to_core:
        copy.start()

    def plus(mine, came):
        return (mine.astype(F32) + came.astype(F32)).astype(BF16)

    def second_halving(keep, target, number, later=None):
        def add(i, nothing):
            at, e = lax.div(i, OWN), lax.rem(i, OWN)
            kept[at, e] = plus(kept[at, e], came[at, e])
            return nothing

        lax.fori_loop(0, half * OWN, add, 0)
        source = kept.at[pl.ds((1 - second) * quarter, quarter)]
        if later is not None:
            source, target = source.at[:, 0], target.at[:, 0]
            rest = pltpu.make_async_copy(
                kept.at[pl.ds((1 - second) * quarter, quarter), 1], later, here.at[3]
            )
            rest.start()
            rest.wait()
        going = pltpu.make_async_remote_copy(
            source, target, send_half.at[number], recv_half.at[number],
            device_id=(flip(c, 4), f), device_id_type=MESH,
        )
        going.start()
        staying = pltpu.make_async_copy(kept.at[pl.ds(second * quarter, quarter)], keep, here.at[4])
        staying.start()
        return going, staying

    if early:
        keeping.wait()
        arriving.wait()
        down_second, leaving = second_halving(down_keep, down_came, 2)
    gate_halving.start()
    shares = w_q.at[:, pl.ds(0, SEQS * BLOCK)]
    for k in range(4):
        pair_in = [
            pltpu.make_async_copy(mix.at[2 * k], token_buf.at[0], load_t.at[0]),
            pltpu.make_async_copy(mix_core.at[k], token_buf.at[1], load_t.at[1]),
        ]
        pair_in[0].start()
        to_core[k].wait_recv()
        pair_in[1].start()
        for copy in pair_in:
            copy.wait()
        shares[k] = plus(token_buf[0], token_buf[1])
    own_share = pltpu.make_async_copy(shares.at[0], mix_in.at[0], here.at[5])
    own_share.start()
    returns = [
        pltpu.make_async_remote_copy(
            shares.at[k], mix_in.at[k], send_mix.at[3 + k], recv_mix.at[3 + k],
            device_id=(flip(c, k // 2), flip(f, 2 * (k % 2))), device_id_type=MESH,
        )
        for k in range(1, 4)
    ]
    for copy in returns:
        copy.start()
    for b in range(2):
        bring(b).start()
    total[...] = jnp.zeros_like(total)
    first.wait()
    for copy in to_heads:
        copy.wait_recv()
    halves = half_masks(BF16)
    lane = lax.broadcasted_iota(jnp.int32, (rows, wide), 1)

    def query_back(j):
        return pltpu.make_async_remote_copy(
            dq_ref.at[j], dq_back.at[head], send_q.at[j], recv_q.at[head],
            device_id=(j * parts + part, f), device_id_type=MESH,
        )

    def key_back(b):
        return pltpu.make_async_remote_copy(
            dkv_ref.at[b], dkv_back.at[c], send_kv.at[b], recv_kv.at[c],
            device_id=(b, f), device_id_type=MESH,
        )

    def query_stays(j):
        return pltpu.make_async_copy(dq_ref.at[j], dq_back.at[head], here.at[1])

    def key_stays(b):
        return pltpu.make_async_copy(dkv_ref.at[b], dkv_back.at[c], here.at[2])

    def one_block(j, nothing):
        block = j * parts + part
        q = q_ref[j].reshape(rows, wide)
        g = g_ref[j].reshape(rows, wide)
        queries = [q * half for half in halves]
        partial = [g * half for half in halves]
        product = g.astype(F32) * full_ref[j].reshape(rows, wide)
        logs = log_ref[j].reshape(rows, wide)
        log_total = [logs[:, :1], logs[:, HEAD_SIZE : HEAD_SIZE + 1]]
        inner = [jnp.sum(product * half, axis=1, keepdims=True) for half in half_masks(F32)]

        def step(number, carry):
            k = kv_ref[pl.ds(2 * number, 2), 0].reshape(KEYS, wide)
            v = kv_ref[pl.ds(2 * number, 2), 1].reshape(KEYS, wide)
            codes = code_ref[number]
            after = []
            dk = jnp.zeros((KEYS, wide), F32)
            dv = jnp.zeros((KEYS, wide), F32)
            for s in range(SEQS):
                mask = allowed_at(block, number, seg_ref[j, s], codes[s : s + 1])
                scores = lax.dot_general(
                    queries[s], k, (((1,), (1,)), ((), ())), preferred_element_type=F32
                )
                scores = jnp.where(mask[None], scores.reshape(REP, BLOCK, KEYS) * SCALE, MASKED)
                probs = jnp.exp(scores.reshape(rows, KEYS) - log_total[s])
                grad_probs = lax.dot_general(
                    partial[s], v, (((1,), (1,)), ((), ())), preferred_element_type=F32
                )
                grad_scores = (probs * (grad_probs - inner[s])).astype(BF16)
                dv = dv + lax.dot_general(
                    probs.astype(BF16), partial[s], (((0,), (0,)), ((), ())), preferred_element_type=F32
                )
                dk = dk + lax.dot_general(
                    grad_scores, queries[s], (((0,), (0,)), ((), ())), preferred_element_type=F32
                )
                after.append(carry[s] + jnp.dot(grad_scores, k, preferred_element_type=F32))
            total[pl.ds(2 * number, 2), 0] += dk.reshape(2, BLOCK, wide)
            total[pl.ds(2 * number, 2), 1] += dv.reshape(2, BLOCK, wide)
            return tuple(after)

        start = jnp.zeros((rows, wide), F32)
        done = lax.fori_loop(0, lax.div(block, 2) + 1, step, (start,) * SEQS)
        dq = (jnp.where(lane < HEAD_SIZE, done[0], done[1]) * SCALE).reshape(REP, BLOCK, wide)
        dq_ref[j] = turn_back(dq, cos_ref[block][None], sin_ref[block][None]).astype(BF16)

        @pl.when(j != head)
        def _():
            query_back(j).start()

        @pl.when(j == head)
        def _():
            query_stays(j).start()

        return nothing

    lax.fori_loop(0, KEY_VALUE_HEADS, one_block, 0)

    def finish(b, nothing):
        dkv_ref[b, 0] = turn_back(total[b, 0] * SCALE, cos_ref[b], sin_ref[b]).astype(BF16)
        dkv_ref[b, 1] = total[b, 1].astype(BF16)

        @pl.when(b != c)
        def _():
            key_back(b).start()

        @pl.when(b == c)
        def _():
            key_stays(b).start()

        return nothing

    lax.fori_loop(0, n_ctx, finish, 0)
    up_halving.start()
    if not early:
        keeping.wait()
        down_halving.wait_recv()
        down_second, leaving = second_halving(down_keep, down_came, 2)

    planes = output_keep.shape[0]

    loads[3].wait()
    output_stages[0].wait_recv()

    def cores(i, nothing):
        r, p, x = lax.div(i, 4), lax.rem(lax.div(i, 2), 2), lax.rem(i, 2)
        output_keep[r, p, x] = plus(output_keep[r, p, x], output_came[r, p, x])
        return nothing

    lax.fori_loop(0, planes * 4, cores, 0)
    output_stages[1].start()

    low = lax.broadcasted_iota(jnp.int32, (BLOCK, wide), 1) < HEAD_SIZE

    def side_by_side(even, odd):
        even, odd = even.astype(F32), odd.astype(F32)
        return (
            jnp.where(low, even, pltpu.roll(odd, HEAD_SIZE, 1)),
            jnp.where(low, pltpu.roll(even, HEAD_SIZE, 1), odd),
        )

    head_acc[...] = jnp.zeros_like(head_acc)

    def head_weights(b, nothing):
        bring(b).wait()
        block = token_buf[lax.rem(b, 2)]
        wide_block = block.astype(F32)
        scales = lax.rsqrt(jnp.mean(wide_block * wide_block, axis=1, keepdims=True) + EPS)
        j = lax.div(b, parts)
        have = jnp.where(lax.rem(b, parts) == part, 1.0, 0.0)
        heads = [dq_ref[j, r].astype(F32) * have for r in range(REP)] + [dkv_ref[b, 0], dkv_ref[b, 1]]
        heads.append(jnp.zeros((BLOCK, wide), F32))
        for m in range((REP + 3) // 2):
            for s, value in enumerate(side_by_side(heads[2 * m], heads[2 * m + 1])):
                at = slice(s * BLOCK, (s + 1) * BLOCK)
                field[at, m * wide : (m + 1) * wide] = (value * scales[at]).astype(BF16)
        head_acc[...] += lax.dot_general(
            block, field[...], (((0,), (0,)), ((), ())), preferred_element_type=F32
        )

        @pl.when(b + 2 < n_ctx)
        def _():
            bring(b + 2).start()

        return nothing

    lax.fori_loop(0, n_ctx, head_weights, 0)
    slab = D // (n_ctx * 4)
    for d in range(n_ctx * 4):
        head_out[d // 4, d // 2 % 2, d % 2] = head_acc[
            d * slab : (d + 1) * slab, : head_out.shape[4]
        ].astype(BF16)
    head_stages = [
        pltpu.make_async_remote_copy(
            source, target, send_head.at[i], recv_head.at[i], device_id=device, device_id_type=MESH
        )
        for i, (source, target, device) in enumerate(
            (
                (head_out.at[:, :, 1 - core_bit], head_core, (c, flip(f, 1))),
                (head_core.at[:, 1 - x_bit], head_x, (c, flip(f, 2))),
            )
        )
    ]
    head_stages[0].start()
    for copy in returns:
        copy.wait_send()
    own_share.wait()
    loads[0].start()
    down_second.wait_send()
    leaving.wait()
    gate_halving.wait_recv()
    refill = [
        pltpu.make_async_copy(grads.at[0, pl.ds(mine * half, half)], kept, here.at[3]),
        pltpu.make_async_copy(gate_first, came, here.at[10]),
    ]
    for copy in refill:
        copy.start()
    for copy in refill:
        copy.wait()
    gate_second, leaving = second_halving(gate_keep, gate_came, 3, gate_other)

    head_stages[0].wait_recv()

    def head_cores(i, nothing):
        d, x = lax.div(i, 2), lax.rem(i, 2)
        head_core[d, x] = plus(head_out[d, x, core_bit], head_core[d, x])
        return nothing

    lax.fori_loop(0, n_ctx * 2, head_cores, 0)
    head_stages[1].start()

    def came_query(h, nothing):
        @pl.when(h != head)
        def _():
            pltpu.make_async_remote_copy(
                dq_ref.at[h], dq_back.at[h], send_q.at[h], recv_q.at[h],
                device_id=(h * parts + part, f), device_id_type=MESH,
            ).wait()

        @pl.when(h == head)
        def _():
            query_stays(h).wait()

        return nothing

    def came_key(b, nothing):
        @pl.when(b != c)
        def _():
            pltpu.make_async_remote_copy(
                dkv_ref.at[b], dkv_back.at[b], send_kv.at[b], recv_kv.at[b],
                device_id=(b, f), device_id_type=MESH,
            ).wait()

        @pl.when(b == c)
        def _():
            key_stays(b).wait()

        return nothing

    lax.fori_loop(0, KEY_VALUE_HEADS, came_query, 0)
    lax.fori_loop(0, n_ctx, came_key, 0)

    def head_of(h):
        if h < QUERY_HEADS:
            return dq_back[h // REP, h % REP]
        kind, h = (h - QUERY_HEADS) // KEY_VALUE_HEADS, (h - QUERY_HEADS) % KEY_VALUE_HEADS
        value = dkv_back[h * parts, kind]
        if parts > 1:
            value = value.astype(F32)
            for p in range(1, parts):
                value = value + dkv_back[h * parts + p, kind].astype(F32)
        return value

    head_stages[1].wait_recv()

    def head_over_x(d, nothing):
        head_x[d] = plus(head_core[d, x_bit], head_x[d])
        return nothing

    lax.fori_loop(0, n_ctx, head_over_x, 0)
    head_stays = pltpu.make_async_copy(head_x.at[c], head_in.at[c], here.at[9])
    head_stays.start()
    to_all = []
    for i in range(1, n_ctx):
        to_all.append(
            pltpu.make_async_remote_copy(
                head_x.at[flip(c, i)], head_in.at[c], send_head.at[1 + i], recv_head.at[1 + i],
                device_id=(flip(c, i), f), device_id_type=MESH,
            )
        )
        to_all[-1].start()
    for m in range((QUERY_HEADS + 2 * KEY_VALUE_HEADS) // 2):
        for s, value in enumerate(side_by_side(head_of(2 * m), head_of(2 * m + 1))):
            grad_qkv[s * BLOCK : (s + 1) * BLOCK, m * wide : (m + 1) * wide] = value.astype(BF16)
    for copy in loads[:3]:
        copy.wait()
    depth = D // 4
    for b in range(4):
        made, at = 0.0, 0
        for weight in (w_q, w_k, w_v):
            width = weight.shape[2]
            made = made + lax.dot_general(
                grad_qkv[:, at : at + width], weight[b], (((1,), (1,)), ((), ())),
                preferred_element_type=F32,
            )
            at += width
        grad_in[:, b * depth : (b + 1) * depth] = made
    x = tok[...].astype(F32)
    scale = lax.rsqrt(jnp.mean(x * x, axis=1, keepdims=True) + EPS)
    gain_grad[...] = jnp.sum(grad_in[...] * x * scale, axis=0, keepdims=True)
    weighted = grad_in[...] * gain[...]
    input_grad[...] = (
        resid_grad[...]
        + scale * weighted
        - x * (scale * scale * scale) * jnp.mean(weighted * x, axis=1, keepdims=True)
    ).astype(BF16)

    staying = pltpu.make_async_copy(residual, grad_in, here.at[8])
    staying.start()
    staying.wait()

    def share(k):
        return pltpu.make_async_copy(mix_in.at[k], token_buf.at[k % 2], load_t.at[k % 2])

    share(0).start()
    for k in range(4):
        if k < 3:
            returns[k].wait_recv()
            share(k + 1).start()
        share(k).wait()
        grad_in[...] += token_buf[k % 2].astype(F32)
    layer_out[...] = grad_in[...].astype(BF16)

    output_stages[1].wait_recv()

    def over_x(i, nothing):
        r, p = lax.div(i, 2), lax.rem(i, 2)
        output_x[r, p] = plus(output_keep[r, p, x_bit], output_x[r, p])
        return nothing

    lax.fori_loop(0, planes * 2, over_x, 0)
    output_stages[2].start()
    output_stages[2].wait_recv()

    def over_pair(r, nothing):
        output_sum[r] = plus(output_x[r, pair], output_pair[r])
        return nothing

    lax.fori_loop(0, planes, over_pair, 0)
    for copy in to_heads:
        copy.wait_send()
    for copy in to_all + [gate_second, up_halving, leaving, head_stays]:
        copy.wait()
    down_second.wait_recv()
    for copy in to_core + output_stages + head_stages + [gate_halving] + ([] if early else [down_halving]):
        copy.wait_send()


def attention_backward(
    cid, parts, n_ctx, early, g_own, q, kv, segq, codes, full, logs, cosine, sine,
    tok, gain, resid_grad, residual, grads, down_in, mix, output_part, tokens_all, q_full, k_full, v_full,
):
    wide = 2 * HEAD_SIZE
    anywhere = pl.BlockSpec(memory_space=pl.ANY)
    inside = pl.BlockSpec(memory_space=pltpu.VMEM)
    dma = pltpu.SemaphoreType.DMA
    others = max(n_ctx // parts - 1, 1)
    devices, planes = n_ctx * 4, n_ctx // 2
    slab, head_width = D // devices, (REP + 2) * HEAD_SIZE
    half = (grads.shape[1] // 2,) + grads.shape[2:]
    quarter = (grads.shape[1] // 4,) + grads.shape[2:]
    columns = q_full.shape[2] + k_full.shape[2] + v_full.shape[2]
    return pl.pallas_call(
        functools.partial(attention_backward_kernel, parts, n_ctx, early),
        name="attention_backward",
        out_shape=[
            jax.ShapeDtypeStruct(tok.shape, BF16),
            jax.ShapeDtypeStruct(tok.shape, BF16),
            jax.ShapeDtypeStruct((1, D), F32),
            jax.ShapeDtypeStruct((planes, slab, D), BF16),
            jax.ShapeDtypeStruct(half, BF16),
            jax.ShapeDtypeStruct(quarter, BF16),
            jax.ShapeDtypeStruct(quarter, BF16),
            jax.ShapeDtypeStruct(quarter[:1] + quarter[2:], BF16),
            jax.ShapeDtypeStruct(half[:1] + half[2:], BF16),
            jax.ShapeDtypeStruct(quarter, BF16),
            jax.ShapeDtypeStruct(quarter, BF16),
            jax.ShapeDtypeStruct((4,) + mix.shape[1:], BF16),
            jax.ShapeDtypeStruct((4,) + mix.shape[1:], BF16),
            jax.ShapeDtypeStruct((n_ctx, slab, head_width), BF16),
        ],
        in_specs=[anywhere] + [inside] * 11 + [anywhere] * 9,
        out_specs=[inside] * 4 + [anywhere] * 10,
        scratch_shapes=[
            pltpu.VMEM(q.shape, BF16),
            pltpu.VMEM((n_ctx, 2, BLOCK, wide), F32),
            pltpu.VMEM(half, BF16),
            pltpu.VMEM(half, BF16),
            pltpu.VMEM(q.shape, BF16),
            pltpu.VMEM(kv.shape, BF16),
            pltpu.VMEM(q.shape, BF16),
            pltpu.VMEM(kv.shape, BF16),
            pltpu.VMEM(q_full.shape, BF16),
            pltpu.VMEM(k_full.shape, BF16),
            pltpu.VMEM(v_full.shape, BF16),
            pltpu.VMEM((SEQS * BLOCK, columns), BF16),
            pltpu.VMEM((SEQS * BLOCK, D), F32),
            pltpu.VMEM((2, SEQS * BLOCK, D), BF16),
            pltpu.VMEM((SEQS * BLOCK, 3 * wide), BF16),
            pltpu.VMEM((D, 3 * wide), F32),
            pltpu.VMEM((n_ctx, 2, 2, slab, head_width), BF16),
            pltpu.VMEM((n_ctx, 2, slab, head_width), BF16),
            pltpu.VMEM((n_ctx, slab, head_width), BF16),
            pltpu.VMEM((planes, 2, 2, slab, D), BF16),
            pltpu.VMEM((planes, 2, 2, slab, D), BF16),
            pltpu.VMEM((planes, 2, slab, D), BF16),
            pltpu.VMEM((planes, slab, D), BF16),
            dma((others,)), dma((others,)), dma((KEY_VALUE_HEADS,)), dma((KEY_VALUE_HEADS,)),
            dma((n_ctx,)), dma((n_ctx,)), dma((RANKS - 1,)), dma((RANKS - 1,)), dma((5,)), dma((5,)),
            dma((11,)), dma((3,)), dma((3,)), dma((n_ctx + 1,)), dma((n_ctx + 1,)), dma((2,)),
        ],
        compiler_params=pltpu.CompilerParams(
            collective_id=cid, has_side_effects=True, vmem_limit_bytes=62 << 20
        ),
        cost_estimate=lasting(125),
    )(
        g_own, q, kv, segq, codes, full, logs, cosine, sine, tok, gain, resid_grad, residual,
        grads, down_in, mix, output_part, tokens_all, q_full, k_full, v_full,
    )


def final_kernel(
    n_ctx, small, output_part, grads, gate_keep, gate_came, gate_other, up_came, down_keep, down_came,
    swapped, output_grad, small_sum,
    halves, landed, rest, rest_landed, last, last_landed, turned, output_in, small_in,
    send_half, recv_half, send_deep, recv_deep, send_out, recv_out, send_small, recv_small,
    send_swap, recv_swap, load, stay,
):
    c, f = lax.axis_index("ctx"), lax.axis_index("fsdp")
    me, plane, rank = c * 4 + f, lax.div(c, 2), lax.rem(c, 2) * 4 + f
    planes = n_ctx // 2
    half, quarter = planes // 2, planes // 4
    barrier = pltpu.get_barrier_semaphore()
    peers = [(i, k) for i in range(n_ctx) for k in range(4) if i or k]
    for dc, df in peers:
        pl.semaphore_signal(
            barrier, inc=1, device_id=(flip(c, dc), flip(f, df)), device_id_type=MESH
        )
    first, second = lax.rem(plane, 2), lax.rem(lax.div(plane, 2), 2)
    loads = [
        pltpu.make_async_copy(source, target, load.at[i])
        for i, (source, target) in enumerate(
            (
                (down_keep, rest.at[2]),
                (down_came, rest_landed.at[2]),
                (gate_keep, rest.at[0]),
                (gate_came.at[:, 0], rest_landed.at[0, :, 0]),
                (grads.at[1, pl.ds(first * half, half)], halves),
                (output_part.at[plane], output_in.at[plane]),
                (small.at[me], small_in.at[me]),
                (up_came, landed.at[:, 0]),
            )
        )
    ]
    for copy in loads:
        copy.start()
    pl.semaphore_wait(barrier, len(peers))

    def over(source, target, sent, came, bit):
        return pltpu.make_async_remote_copy(
            source, target, sent, came, device_id=(flip(c, 2 * bit), f), device_id_type=MESH
        )

    up_first = over(
        grads.at[1, pl.ds((1 - first) * half, half), 1], landed.at[:, 1],
        send_half.at[0, 1], recv_half.at[0, 1], 1,
    )
    gate_second = over(gate_other, rest_landed.at[0, :, 1], send_half.at[2, 1], recv_half.at[2, 1], 2)
    up_first.start()
    outputs = []
    for i in range(1, planes):
        outputs.append(
            pltpu.make_async_remote_copy(
                output_part.at[flip(plane, i)], output_in.at[plane], send_out.at[i - 1], recv_out.at[i - 1],
                device_id=(flip(c, 2 * i), f), device_id_type=MESH,
            )
        )
    smalls = []
    for number, (i, k) in enumerate(peers):
        peer_c, peer_f = flip(c, i), flip(f, k)
        smalls.append(
            pltpu.make_async_remote_copy(
                small.at[peer_c * 4 + peer_f], small_in.at[me], send_small.at[number], recv_small.at[number],
                device_id=(peer_c, peer_f), device_id_type=MESH,
            )
        )

    def plus(mine, came):
        return (mine.astype(F32) + came.astype(F32)).astype(BF16)

    swaps, sent = [], []

    def finish(m, e):
        count, bit, number = quarter, 4, 0
        for at in range(quarter):
            rest[m, at, e] = plus(rest[m, at, e], rest_landed[m, at, e])
        mine = rest.at[m, :, e]
        while count > 1:
            count //= 2
            chosen = lax.rem(lax.div(plane, bit), 2)
            came = last_landed.at[m, number, pl.ds(0, count), e]
            copy = over(
                mine.at[pl.ds((1 - chosen) * count, count)], came,
                send_deep.at[2 * m + number, e], recv_deep.at[2 * m + number, e], bit,
            )
            copy.start()
            copy.wait_recv()
            sent.append(copy)
            for at in range(count):
                last[m, number, at, e] = plus(mine[chosen * count + at], came[at])
            mine, bit, number = last.at[m, number, :, e], bit * 2, number + 1
        rows = turned.shape[3]
        across = mine[0].astype(F32).T
        for r in range(RANKS):
            turned[m, r, e] = across[r * rows : (r + 1) * rows].astype(BF16)
        for i in range(RANKS):
            source, target = turned.at[m, flip(rank, i), e], swapped.at[rank, m, e]
            if i:
                copy = pltpu.make_async_remote_copy(
                    source, target, send_swap.at[m * OWN + e, i], recv_swap.at[m * OWN + e, i],
                    device_id=(flip(c, i // 4), flip(f, i % 4)), device_id_type=MESH,
                )
            else:
                copy = pltpu.make_async_copy(source, target, stay.at[m * OWN + e])
            copy.start()
            swaps.append(copy)

    for copy in loads:
        copy.wait()
    up_second = []

    def second_of_up(e):
        for at in range(half):
            halves[at, e] = plus(halves[at, e], landed[at, e])
        up_second.append(
            over(
                halves.at[pl.ds((1 - second) * quarter, quarter), e], rest_landed.at[1, :, e],
                send_half.at[1, e], recv_half.at[1, e], 2,
            )
        )
        up_second[e].start()
        for at in range(quarter):
            rest[1, at, e] = halves[second * quarter + at, e]

    second_of_up(0)
    gate_second.start()
    for copy in outputs + smalls:
        copy.start()
    for e in range(OWN):
        finish(2, e)
    finish(0, 0)
    up_first.wait_recv()
    second_of_up(1)
    gate_second.wait_recv()
    finish(0, 1)
    for copy in outputs + smalls:
        copy.wait_recv()
    made = output_in[0].astype(F32)
    for i in range(1, planes):
        made = made + output_in[i].astype(F32)
    output_grad[...] = made
    small_sum[...] = jnp.sum(small_in[...], axis=0)
    for e in range(OWN):
        up_second[e].wait_recv()
        finish(1, e)
    for copy in swaps:
        copy.wait()
    for copy in smalls + outputs + sent + up_second + [up_first, gate_second]:
        copy.wait_send()


def final_sums(
    cid, n_ctx, small, output_part, grads, gate_keep, gate_came, gate_other, up_came, down_keep,
    down_came
):
    anywhere = pl.BlockSpec(memory_space=pl.ANY)
    inside = pl.BlockSpec(memory_space=pltpu.VMEM)
    dma = pltpu.SemaphoreType.DMA
    devices, planes = n_ctx * 4, n_ctx // 2
    slab, piece = D // devices, grads.shape[2:]
    half, quarter = (planes // 2,) + piece, (planes // 4,) + piece
    deep = (3, 2, max(planes // 8, 1)) + piece
    return pl.pallas_call(
        functools.partial(final_kernel, n_ctx),
        name="final_sums",
        out_shape=[
            jax.ShapeDtypeStruct((RANKS, 3, OWN, slab, FF), BF16),
            jax.ShapeDtypeStruct((slab, D), F32),
            jax.ShapeDtypeStruct(small.shape[1:], F32),
        ],
        in_specs=[anywhere] * 9,
        out_specs=[anywhere] + [inside] * 2,
        scratch_shapes=[
            pltpu.VMEM(half, BF16),
            pltpu.VMEM(half, BF16),
            pltpu.VMEM((3,) + quarter, BF16),
            pltpu.VMEM((3,) + quarter, BF16),
            pltpu.VMEM(deep if planes > 4 else (1, 1, 1, 1, 8, 128), BF16),
            pltpu.VMEM(deep if planes > 4 else (1, 1, 1, 1, 8, 128), BF16),
            pltpu.VMEM((3, RANKS, OWN, slab, FF), BF16),
            pltpu.VMEM((planes, slab, D), BF16),
            pltpu.VMEM(small.shape, F32),
            dma((3, OWN)), dma((3, OWN)), dma((6, OWN)), dma((6, OWN)),
            dma((planes - 1,)), dma((planes - 1,)), dma((devices - 1,)), dma((devices - 1,)),
            dma((3 * OWN, RANKS)), dma((3 * OWN, RANKS)), dma((8,)), dma((3 * OWN,)),
        ],
        compiler_params=pltpu.CompilerParams(
            collective_id=cid, has_side_effects=True, vmem_limit_bytes=56 << 20
        ),
        cost_estimate=lasting(80),
    )(small, output_part, grads, gate_keep, gate_came, gate_other, up_came, down_keep, down_came)


def rope_tables(positions):
    half_dim = HEAD_SIZE // 2
    frequency = ROPE_BASE ** (-jnp.arange(half_dim, dtype=F32) * 2.0 / HEAD_SIZE)
    angle = positions.astype(F32)[:, None] * frequency[None, :]
    angle = jnp.concatenate([angle, angle], axis=1)
    return (jnp.cos(angle), jnp.sin(angle))


def heads_out(field, per):
    field = field.reshape(SEQS, BLOCK, KEY_VALUE_HEADS, per, HEAD_SIZE)
    return field.transpose(2, 3, 1, 0, 4).reshape(KEY_VALUE_HEADS, per, BLOCK, SEQS * HEAD_SIZE)


def heads_in(field):
    per = field.shape[1]
    field = field.reshape(KEY_VALUE_HEADS, per, BLOCK, SEQS, HEAD_SIZE)
    return field.transpose(3, 2, 0, 1, 4).reshape(SEQS, BLOCK, KEY_VALUE_HEADS * per * HEAD_SIZE)


def on_device(
    n_ctx,
    n_fsdp,
    tokens,
    segments,
    valid,
    expert_ids,
    slot_order,
    cotangent,
    norm1_gain,
    w_query,
    key_weight,
    value_weight,
    w_output,
    norm2_gain,
    w_router,
    w_gate,
    w_up,
    w_down,
):
    parts = n_ctx // KEY_VALUE_HEADS
    replicas = n_ctx // 2
    full_len = segments.shape[1]
    c_index, f_index = lax.axis_index("ctx"), lax.axis_index("fsdp")
    pair = lax.rem(c_index, 2)
    rank = pair * n_fsdp + f_index
    part = lax.rem(c_index, parts)
    head = lax.div(c_index, parts)
    positions = c_index * BLOCK + jnp.arange(BLOCK, dtype=jnp.int32)

    span = D // n_fsdp // 2
    nears = [
        lax.ppermute(
            lax.dynamic_slice_in_dim(w, pair * span, span, 0), "fsdp", [(a, a ^ 2) for a in range(n_fsdp)]
        )
        for w in (w_query, key_weight, value_weight)
    ]
    tokens_all = lax.all_gather(tokens, "ctx", axis=0, tiled=False)
    small = jnp.concatenate(
        [
            norm1_gain[None],
            norm2_gain[None],
            w_router.T,
            jnp.zeros((SMALL - EXPERTS - 2, D // n_fsdp), BF16),
        ],
        axis=0,
    )
    packs = [
        lax.dynamic_slice_in_dim(w, pair * (EXPERTS // 2), EXPERTS // 2, 1)
        .reshape(D // n_fsdp, n_fsdp, OWN, FF)
        .transpose(1, 2, 0, 3)
        for w in (w_gate, w_up, w_down)
    ]
    inputs_f = tokens.astype(F32)
    scale_one = lax.rsqrt(jnp.mean(inputs_f * inputs_f, axis=-1, keepdims=True) + EPS)
    segq = segments.reshape(SEQS, KEY_VALUE_HEADS, parts, BLOCK)
    segq = lax.dynamic_index_in_dim(segq, part, 2, keepdims=False).transpose(1, 0, 2)[..., None]
    codes = jnp.where(valid > 0, segments, -1)
    codes = codes.reshape(SEQS, full_len // KEYS, KEYS).transpose(1, 0, 2)
    all_cosine, all_sine = rope_tables(jnp.arange(full_len, dtype=jnp.int32))
    all_cosine = jnp.tile(all_cosine, (1, 2)).reshape(n_ctx, BLOCK, 2 * HEAD_SIZE)
    all_sine = jnp.tile(all_sine, (1, 2)).reshape(n_ctx, BLOCK, 2 * HEAD_SIZE)
    (
        normed_in, small_all, full_query, full_key, full_value, q_all, kv_all, head_full, head_logs,
        attn_heads, full_output, own_gate, own_up, own_down,
    ) = attention_forward(
        0, parts, n_ctx, tokens.reshape(SEQS * BLOCK, D), small, w_query, key_weight, value_weight,
        w_output, nears, packs,
        lax.dynamic_index_in_dim(all_cosine, c_index, 0, keepdims=False),
        lax.dynamic_index_in_dim(all_sine, c_index, 0, keepdims=False),
        segq, codes,
    )
    gain_first = small_all[:, 0].reshape(D).astype(F32)
    gain_second = small_all[:, 1].reshape(D).astype(F32)
    full_router = small_all[:, 2 : 2 + EXPERTS].transpose(1, 0, 2).reshape(EXPERTS, D)
    full_output = full_output.reshape(D, D)
    attn_out = heads_in(attn_heads)
    attn_proj = jnp.einsum("sgq,dq->sgd", attn_out, full_output, preferred_element_type=F32)
    residual = inputs_f + attn_proj
    scale_two = lax.rsqrt(jnp.mean(residual * residual, axis=-1, keepdims=True) + EPS)
    normed_mid = (residual * scale_two * gain_second).astype(BF16)

    logits = jnp.einsum("sgd,ed->sge", normed_mid, full_router, preferred_element_type=F32)
    picked = jnp.any(expert_ids[..., None] == jnp.arange(EXPERTS, dtype=jnp.int32), axis=2)
    before = (slot_order[:, None, :] < slot_order[:, :, None]).astype(BF16)
    place = jnp.matmul(before, picked.astype(BF16), preferred_element_type=F32)
    is_kept = picked & (place < CAP)
    chosen = jnp.where(picked, logits, MASKED)
    raised = jnp.where(picked, jnp.exp(chosen - jnp.max(chosen, axis=-1, keepdims=True)), 0.0)
    gates = raised / jnp.sum(raised, axis=-1, keepdims=True)
    payload = jnp.concatenate(
        [
            normed_mid,
            jnp.where(is_kept, place, -1.0).astype(BF16),
            gates.astype(BF16),
            jnp.zeros((SEQS, BLOCK, 128 - 2 * EXPERTS), BF16),
        ],
        axis=2,
    )
    back, mix_part, own_grads, down_first, down_early = run_experts(
        2, replicas, payload.reshape(SEQS * BLOCK, PAY), cotangent.reshape(SEQS * BLOCK, D),
        (own_gate, own_up, own_down), tokens_all
    )

    back = back.reshape(SEQS, BLOCK, D + 128)
    grad_gates = jnp.where(is_kept, back[..., D : D + EXPERTS], 0.0)
    grad_chosen = gates * (grad_gates - jnp.sum(gates * grad_gates, axis=-1, keepdims=True))
    grad_logits = grad_chosen.astype(BF16)
    grad_mid = back[..., :D] + jnp.einsum(
        "sge,ed->sgd", grad_logits, full_router, preferred_element_type=F32
    )
    grad_router = jnp.einsum("sgd,sge->de", normed_mid, grad_logits, preferred_element_type=F32)

    grad_f = cotangent.astype(F32)
    weighted_two = gain_second * grad_mid
    grad_gain_second = jnp.sum(grad_mid * residual * scale_two, axis=(0, 1))
    cube_two = scale_two * scale_two * scale_two
    grad_resid = (
        grad_f
        + scale_two * weighted_two
        - residual * cube_two * jnp.mean(weighted_two * residual, axis=-1, keepdims=True)
    )
    grad_resid_low = grad_resid.astype(BF16)
    grad_attn = jnp.einsum("sgd,dq->sgq", grad_resid_low, full_output, preferred_element_type=F32)
    grad_attn = grad_attn.astype(BF16)
    grad_output_w = jnp.einsum("sgd,sgq->dq", grad_resid_low, attn_out, preferred_element_type=F32)
    rows = D // (n_ctx * n_fsdp)
    output_part = grad_output_w.astype(BF16).reshape(replicas, 2, 2, 2, rows, D)

    (
        input_grad, layer_out, gain_grad, output_sum, _, gate_keep, gate_came, gate_other, up_came, down_keep,
        down_came, _, _, head_grads,
    ) = attention_backward(
        6, parts, n_ctx, down_early, heads_out(grad_attn, REP), q_all, kv_all, segq, codes, head_full, head_logs,
        all_cosine, all_sine, tokens.reshape(SEQS * BLOCK, D), gain_first[None],
        grad_resid.reshape(SEQS * BLOCK, D), residual.reshape(SEQS * BLOCK, D), own_grads, down_first, mix_part, output_part,
        tokens_all.reshape(n_ctx, SEQS * BLOCK, D), full_query, full_key, full_value,
    )
    input_grad = input_grad.reshape(SEQS, BLOCK, D)
    layer_out = layer_out.reshape(SEQS, BLOCK, D)
    amount = rows * (EXPERTS + 2)
    tiles = -(-amount // 1024) * 8
    small_grads = jnp.concatenate([grad_router, gain_grad.T, grad_gain_second[:, None]], axis=1)
    small_grads = jnp.pad(
        small_grads.reshape(n_ctx * n_fsdp, amount), ((0, 0), (0, tiles * 128 - amount))
    ).reshape(n_ctx * n_fsdp, tiles, 128)
    swapped, output_grad, small_sum = final_sums(
        9, n_ctx, small_grads, output_sum, own_grads, gate_keep, gate_came, gate_other, up_came,
        down_keep, down_came,
    )
    small_sum = small_sum.reshape(tiles * 128)[:amount].reshape(rows, EXPERTS + 2)
    head_grads = head_grads.reshape(KEY_VALUE_HEADS, parts, rows, (REP + 2) * HEAD_SIZE)
    own_gain = lax.dynamic_slice_in_dim(gain_first, (c_index * n_fsdp + f_index) * rows, rows, 0)
    head_grads = jnp.sum(head_grads.astype(F32), axis=1).transpose(1, 0, 2) * own_gain[:, None, None]
    query_grad = head_grads[..., : REP * HEAD_SIZE].reshape(rows, D)
    key_grad = head_grads[..., REP * HEAD_SIZE : (REP + 1) * HEAD_SIZE].reshape(rows, -1)
    value_grad = head_grads[..., (REP + 1) * HEAD_SIZE :].reshape(rows, -1)

    def by_row(matrix):
        return swapped[:, matrix].transpose(2, 0, 1, 3).reshape(rows, EXPERTS, FF).astype(F32)

    return (
        layer_out,
        input_grad,
        small_sum[:, EXPERTS],
        query_grad,
        key_grad,
        value_grad,
        output_grad,
        small_sum[:, EXPERTS + 1],
        small_sum[:, :EXPERTS],
        by_row(0),
        by_row(1),
        by_row(2),
    )


def solution(mesh):
    placed = (
        P("fsdp", "ctx", None),
        P("fsdp", None),
        P("fsdp", None),
        P("fsdp", "ctx", None),
        P("fsdp", "ctx"),
        P("fsdp", "ctx", None),
        P("fsdp"),
        P("fsdp", None),
        P("fsdp", None),
        P("fsdp", None),
        P("fsdp", None),
        P("fsdp"),
        P("fsdp", None),
        P("fsdp", None, None),
        P("fsdp", None, None),
        P("fsdp", None, None),
    )
    return jax.shard_map(
        functools.partial(on_device, mesh.shape["ctx"], mesh.shape["fsdp"]),
        mesh=mesh,
        in_specs=placed,
        out_specs=(
            P("fsdp", "ctx", None),
            P("fsdp", "ctx", None),
            P(("ctx", "fsdp")),
            P(("ctx", "fsdp"), None),
            P(("ctx", "fsdp"), None),
            P(("ctx", "fsdp"), None),
            P(("ctx", "fsdp"), None),
            P(("ctx", "fsdp")),
            P(("ctx", "fsdp"), None),
            P(("ctx", "fsdp"), None, None),
            P(("ctx", "fsdp"), None, None),
            P(("ctx", "fsdp"), None, None),
        ),
        check_vma=False,
    )
```

```python
import functools

import jax
import jax.numpy as jnp
from jax import lax
from jax.experimental import pallas as pl
from jax.experimental.pallas import tpu as pltpu
from jax.sharding import PartitionSpec as P

D = 1536
QUERY_HEADS = 24
KEY_VALUE_HEADS = 8
REP = QUERY_HEADS // KEY_VALUE_HEADS
HEAD_SIZE = 64
FF = 512
EXPERTS = 16
CAP = 80
RANKS = 8
OWN = EXPERTS // RANKS
SEQS = 2
BLOCK = 128
KEYS = 256

EPS = 1e-05
ROPE_BASE = 10000.0
MASKED = -1e30
SCALE = HEAD_SIZE ** (-0.5)
MESH = pl.DeviceIdType.MESH
BF16 = jnp.bfloat16
F32 = jnp.float32


def flip(index, constant):
    result, bit = index, 1
    while bit <= constant:
        if constant & bit:
            result = result + bit - 2 * bit * lax.rem(lax.div(index, bit), 2)
        bit *= 2
    return result


def lasting(microseconds):
    return pl.CostEstimate(flops=0, bytes_accessed=int(microseconds * 3.3e6), transcendentals=0)


PAY = D + 128
GROUPS = 4
ROWS = GROUPS * CAP


def other_chip(c, f, k):
    pair, x = lax.rem(k, 2), lax.div(k, 2)
    return (
        c + pair * (1 - 2 * lax.rem(c, 2)),
        f + 2 * x * (1 - 2 * lax.rem(lax.div(f, 2), 2)),
    )


def plane_order(replicas):
    order = [0]
    while len(order) < replicas:
        order = [2 * i for i in order] + [2 * i + 1 for i in order]
    return order


def experts_kernel(
    replicas, pay, cot, cot_pair, gate_own, up_own, down_own, after,
    back, mix, grads, down_came, pay_in, cot_in,
    weights, total, pay_now, cot_now, xs, gs, eo, gi, hid, dgate, dup, disp, comb,
    own, out, sib, ret, mix_now,
    send_first, recv_first, send_fwd, recv_fwd, send_sib, recv_sib, send_chip, recv_chip,
    load_w, load, store, piece_sem, send_down, recv_down,
):
    c, f = lax.axis_index("ctx"), lax.axis_index("fsdp")
    rank = lax.rem(c, 2) * 4 + f
    sibling = (c, flip(f, 1))
    barrier = pltpu.get_barrier_semaphore()
    pl.semaphore_signal(barrier, inc=1, device_id=sibling, device_id_type=MESH)
    for k in range(1, 4):
        pl.semaphore_signal(barrier, inc=1, device_id=other_chip(c, f, k), device_id_type=MESH)
    apart = len(grads.shape) == 5
    if apart:
        pl.semaphore_signal(barrier, inc=1, device_id=(flip(c, 2), f), device_id_type=MESH)
    bring = []
    for m, own_weight in enumerate((gate_own, up_own, down_own)):
        bring.append(pltpu.make_async_copy(own_weight, weights.at[m], load_w.at[m]))
        bring[-1].start()
    pl.semaphore_wait(barrier, 5 if apart else 4)
    sources, landed = (pay, cot), (pay_in, cot_in)

    def push(k, a):
        slot = 1 if k == 0 else 2 * k
        return pltpu.make_async_remote_copy(
            sources[a], landed[a].at[slot - 1], send_first.at[k, a], recv_first.at[k, a],
            device_id=sibling if k == 0 else other_chip(c, f, k), device_id_type=MESH,
        )

    def forward(k, a):
        return pltpu.make_async_remote_copy(
            landed[a].at[2 * k - 1], landed[a].at[2 * k], send_fwd.at[k - 1, a], recv_fwd.at[k - 1, a],
            device_id=sibling, device_id_type=MESH,
        )

    def to_sibling(k):
        return pltpu.make_async_remote_copy(
            out.at[lax.rem(k, 2)], sib.at[k], send_sib.at[k], recv_sib.at[k],
            device_id=sibling, device_id_type=MESH,
        )

    def to_chip(k):
        return pltpu.make_async_remote_copy(
            sib.at[k], ret.at[k - 1], send_chip.at[k - 1], recv_chip.at[k - 1],
            device_id=other_chip(c, f, k), device_id_type=MESH,
        )

    def store_mix(k, s):
        return pltpu.make_async_copy(mix_now.at[s], mix.at[2 * k + s], store.at[s])

    for k, a in ((0, 0), (0, 1), (1, 0), (2, 0), (2, 1), (3, 0), (3, 1)):
        push(k, a).start()

    def clear(i, carry):
        total[lax.div(i, OWN), lax.rem(i, OWN)] = jnp.zeros((FF, D), F32)
        return carry

    lax.fori_loop(0, 3 * OWN, clear, 0)
    lane = lax.broadcasted_iota(jnp.int32, (BLOCK, 128), 1)
    wide = lax.broadcasted_iota(jnp.int32, (BLOCK, 2 * BLOCK), 1).astype(F32)
    both = lax.broadcasted_iota(jnp.int32, (BLOCK, OWN * CAP), 1)

    def chunk(k, carry):
        now = (pay_now, cot_now)

        def fetch(a, s, source):
            copy = pltpu.make_async_copy(source, now[a].at[s], load.at[a, s])
            copy.start()
            return copy

        def arrived(chip):
            for a in range(1 if chip == 1 else 2):
                push(chip, a).wait_recv()
                forward(chip, a).start()

        def fetch_chip(chip):
            if chip == 1:
                for s in range(2):
                    fetch(1, s, cot_pair.at[s])
            among = range(1 if chip == 1 else 2)
            for a in among:
                fetch(a, 0, landed[a].at[2 * chip - 1])
            for a in among:
                forward(chip, a).wait_recv()
                fetch(a, 1, landed[a].at[2 * chip])

        @pl.when(k == 0)
        def _():
            copies = [fetch(a, 0, sources[a]) for a in range(2)]
            for a in range(2):
                push(0, a).wait_recv()
            copies += [fetch(a, 1, landed[a].at[0]) for a in range(2)]
            for copy in copies:
                copy.wait()
            for copy in bring:
                copy.wait()

        @pl.when(k == 1)
        def _():
            arrived(1)
            fetch_chip(1)

        @pl.when(k > 0)
        def _():
            for a in range(2):
                for s in range(2):
                    pltpu.make_async_copy(landed[a].at[2 * k - 1 + s], now[a].at[s], load.at[a, s]).wait()

        for g in range(GROUPS):
            s, at = g // 2, (g % 2) * BLOCK
            tail = pay_now[s, at : at + BLOCK, D:].astype(F32)

            def column(index):
                return jnp.sum(jnp.where(lane == index, tail, 0.0), axis=1, keepdims=True)

            table = jnp.zeros((BLOCK, 2 * BLOCK), F32)
            gated = jnp.zeros((BLOCK, 2 * BLOCK), F32)
            for e in range(OWN):
                place = column(rank * OWN + e)
                place = jnp.where(place < 0.0, -1000.0, place + e * CAP)
                here = wide == place
                table = jnp.where(here, 1.0, table)
                gated = jnp.where(here, column(EXPERTS + rank * OWN + e), gated)
            table, gated = table.astype(BF16), gated.astype(BF16)
            disp[g] = table
            comb[g] = gated
            for weight, source, keep in (
                (table, pay_now[s, at : at + BLOCK, :D], xs),
                (gated, cot_now[s, at : at + BLOCK], gs),
            ):
                moved = lax.dot_general(
                    weight, source, (((0,), (0,)), ((), ())), preferred_element_type=F32
                ).astype(BF16)
                for e in range(OWN):
                    keep[e, g * CAP : (g + 1) * CAP] = moved[e * CAP : (e + 1) * CAP]

        def expert(e, carry):
            at = pl.multiple_of(e * CAP, 16)
            gate_pre = jnp.dot(xs[e], weights[0, e], preferred_element_type=F32)
            up_pre = jnp.dot(xs[e], weights[1, e], preferred_element_type=F32)
            sigmoid = 1.0 / (1.0 + jnp.exp(-gate_pre))
            activated = gate_pre * sigmoid
            hidden = (activated * up_pre).astype(BF16)
            hid[e] = hidden
            made = lax.dot_general(
                hidden, weights[2, e], (((1,), (1,)), ((), ())), preferred_element_type=F32
            ).astype(BF16)
            for g in range(GROUPS):
                eo[pl.ds(pl.multiple_of(g * OWN * CAP + at, 16), CAP)] = made[g * CAP : (g + 1) * CAP]
            grad_hidden = jnp.dot(gs[e], weights[2, e], preferred_element_type=F32)
            slope = sigmoid * (1.0 + gate_pre * (1.0 - sigmoid))
            grad_gate = (grad_hidden * up_pre * slope).astype(BF16)
            grad_up = (grad_hidden * activated).astype(BF16)
            dgate[e] = grad_gate
            dup[e] = grad_up
            made = lax.dot_general(
                grad_gate, weights[0, e], (((1,), (1,)), ((), ())), preferred_element_type=F32
            )
            made = made + lax.dot_general(
                grad_up, weights[1, e], (((1,), (1,)), ((), ())), preferred_element_type=F32
            )
            made = made.astype(BF16)
            for g in range(GROUPS):
                gi[pl.ds(pl.multiple_of(g * OWN * CAP + at, 16), CAP)] = made[g * CAP : (g + 1) * CAP]
            return carry

        lax.fori_loop(0, OWN, expert, 0)

        @pl.when(k > 0)
        def _():
            for s in range(2):
                store_mix(k - 1, s).wait()

        @pl.when(k > 1)
        def _():
            to_sibling(k - 2).wait_send()

        parity = lax.rem(k, 2)
        for g in range(GROUPS):
            s, at = g // 2, (g % 2) * BLOCK
            slots = pl.ds(g * OWN * CAP, OWN * CAP)
            made = eo[slots]
            mix_now[s, at : at + BLOCK] = jnp.dot(
                comb[g][:, : OWN * CAP], made, preferred_element_type=F32
            ).astype(BF16)
            table = disp[g][:, : OWN * CAP]
            grad_mid = jnp.dot(table, gi[slots], preferred_element_type=F32).astype(BF16)
            met = lax.dot_general(
                cot_now[s, at : at + BLOCK], made, (((1,), (1,)), ((), ())), preferred_element_type=F32
            ) * table.astype(F32)
            values = jnp.zeros((BLOCK, 128), F32)
            for e in range(OWN):
                inside = (both >= e * CAP) & (both < (e + 1) * CAP)
                value = jnp.sum(jnp.where(inside, met, 0.0), axis=1, keepdims=True)
                values = jnp.where(lane == rank * OWN + e, value, values)
            target = own if s == 0 else out
            target[parity, at : at + BLOCK, :D] = grad_mid
            target[parity, at : at + BLOCK, D:] = values.astype(BF16)
        to_sibling(k).start()
        for s in range(2):
            store_mix(k, s).start()

        @pl.when(k == 1)
        def _():
            arrived(2)
            fetch_chip(2)

        @pl.when(k == 2)
        def _():
            arrived(3)
            fetch_chip(3)

        def weight_grads(e, carry):
            for m, (left, right) in enumerate(((dgate, xs), (dup, xs), (hid, gs))):
                total[m, e] += lax.dot_general(
                    left[e], right[e], (((0,), (0,)), ((), ())), preferred_element_type=F32
                )
            return carry

        lax.fori_loop(0, OWN, weight_grads, 0)
        to_sibling(k).wait_recv()
        sib[k] = (sib[k].astype(F32) + own[parity].astype(F32)).astype(BF16)

        @pl.when(k > 0)
        def _():
            to_chip(k).start()

        return carry

    lax.fori_loop(0, 4, chunk, 0)
    for s in range(2):
        store_mix(3, s).wait()
    stages = (eo, gi)
    pending = []
    if apart:
        half = replicas // 2
        down_first = pltpu.make_async_remote_copy(
            grads.at[2, pl.ds((1 - lax.rem(lax.div(c, 2), 2)) * half, half)], down_came,
            send_down, recv_down, device_id=(flip(c, 2), f), device_id_type=MESH,
        )
    for i in range(3 * OWN):
        m, e = (2, 0, 1)[i // OWN], i % OWN
        if i >= 2:
            for copy in pending[i - 2]:
                copy.wait()
        if i == OWN + 1 and apart:
            down_first.start()
        stages[i % 2][:FF] = total[m, e].astype(BF16)
        pending.append([])
        if not apart:
            pending[i].append(
                pltpu.make_async_copy(stages[i % 2].at[:FF], grads.at[m, e], piece_sem.at[i % 2, 0])
            )
        else:
            width = D // replicas
            for at, plane in enumerate(plane_order(replicas)):
                pending[i].append(
                    pltpu.make_async_copy(
                        stages[i % 2].at[:FF, plane * width : (plane + 1) * width],
                        grads.at[m, at, e],
                        piece_sem.at[i % 2, at],
                    )
                )
        for copy in pending[i]:
            copy.start()
    for copy in pending[-2] + pending[-1]:
        copy.wait()
    for k in (2, 3):
        to_sibling(k).wait_send()
    for k in range(4):
        for a in range(1 if k == 1 else 2):
            push(k, a).wait_send()
            if k:
                forward(k, a).wait_send()
    for k in range(1, 4):
        to_chip(k).wait_recv()
    back[...] = (sib[0].astype(F32) + ret[0].astype(F32)) + (ret[1].astype(F32) + ret[2].astype(F32))
    for k in range(1, 4):
        to_chip(k).wait_send()
    if apart:
        down_first.wait()


def run_experts(cid, replicas, pay, cot, cot_pair, owns, after):
    width = D // replicas
    apart = width % 128 == 0
    tokens = SEQS * BLOCK
    anywhere = pl.BlockSpec(memory_space=pl.ANY)
    inside = pl.BlockSpec(memory_space=pltpu.VMEM)
    dma = pltpu.SemaphoreType.DMA
    back, mix, grads, down_came, _, _ = pl.pallas_call(
        functools.partial(experts_kernel, replicas),
        name="experts",
        out_shape=[
            jax.ShapeDtypeStruct((tokens, PAY), F32),
            jax.ShapeDtypeStruct((RANKS, tokens, D), BF16),
            jax.ShapeDtypeStruct((3, replicas, OWN, FF, width) if apart else (3, OWN, FF, D), BF16),
            jax.ShapeDtypeStruct((replicas // 2, OWN, FF, width) if apart else (8, 128), BF16),
            jax.ShapeDtypeStruct((RANKS - 1, tokens, PAY), BF16),
            jax.ShapeDtypeStruct((RANKS - 1, tokens, D), BF16),
        ],
        in_specs=[anywhere] * 7,
        out_specs=[inside] + [anywhere] * 5,
        scratch_shapes=[
            pltpu.VMEM((3, OWN, D, FF), BF16),
            pltpu.VMEM((3, OWN, FF, D), F32),
            pltpu.VMEM((2, tokens, PAY), BF16),
            pltpu.VMEM((2, tokens, D), BF16),
            pltpu.VMEM((OWN, ROWS, D), BF16),
            pltpu.VMEM((OWN, ROWS, D), BF16),
            pltpu.VMEM((OWN * ROWS, D), BF16),
            pltpu.VMEM((OWN * ROWS, D), BF16),
            pltpu.VMEM((OWN, ROWS, FF), BF16),
            pltpu.VMEM((OWN, ROWS, FF), BF16),
            pltpu.VMEM((OWN, ROWS, FF), BF16),
            pltpu.VMEM((GROUPS, BLOCK, 2 * BLOCK), BF16),
            pltpu.VMEM((GROUPS, BLOCK, 2 * BLOCK), BF16),
            pltpu.VMEM((2, tokens, PAY), BF16),
            pltpu.VMEM((2, tokens, PAY), BF16),
            pltpu.VMEM((4, tokens, PAY), BF16),
            pltpu.VMEM((3, tokens, PAY), BF16),
            pltpu.VMEM((2, tokens, D), BF16),
            dma((4, 2)), dma((4, 2)), dma((3, 2)), dma((3, 2)),
            dma((4,)), dma((4,)), dma((3,)), dma((3,)),
            dma((4,)), dma((2, 2)), dma((2,)), dma((2, replicas)), dma, dma,
        ],
        compiler_params=pltpu.CompilerParams(
            collective_id=cid, has_side_effects=True, vmem_limit_bytes=63 << 20
        ),
        cost_estimate=lasting(110),
    )(pay, cot, cot_pair, *owns, after)
    if not apart:
        grads = grads.reshape(3, OWN, FF, replicas, width).transpose(0, 3, 1, 2, 4)
        grads = grads[:, jnp.array(plane_order(replicas))]
    return back, mix, grads, down_came, apart


def half_masks(dtype):
    lane = lax.broadcasted_iota(jnp.int32, (1, 2 * HEAD_SIZE), 1)
    low = (lane < HEAD_SIZE).astype(F32)
    return low.astype(dtype), (1.0 - low).astype(dtype)


def allowed_at(block, step, segq, keycode):
    token = block * BLOCK + lax.broadcasted_iota(jnp.int32, (BLOCK, KEYS), 0)
    key = step * KEYS + lax.broadcasted_iota(jnp.int32, (BLOCK, KEYS), 1)
    return ((segq == keycode) & (key < token)) | (key == token)


SMALL = 32


def turn(field, cosine, sine):
    half = HEAD_SIZE // 2
    lane = lax.broadcasted_iota(jnp.int32, field.shape, field.ndim - 1)
    up = pltpu.roll(field, 2 * HEAD_SIZE - half, field.ndim - 1)
    down = pltpu.roll(field, half, field.ndim - 1)
    return field * cosine + jnp.where(lax.rem(lane, HEAD_SIZE) < half, -up, down) * sine


def attention_forward_kernel(
    parts, n_ctx, tok, small, w_q, w_k, w_v, w_o, near_q, near_k, near_v, pack0, pack1, pack2, cot, cos_ref, sin_ref, seg_ref, code_ref,
    normed, small_all, q_full, k_full, v_full, q_ref, kv_ref, full_ref, log_ref, o_back, o_full,
    gate_own, up_own, down_own, cot_pair,
    acc, q_pack, kv_pack, o_buf, own_buf,
    send_w, recv_w, send_s, recv_s, send_e, recv_e, send_q, recv_q, send_kv, recv_kv, send_o, recv_o, here,
    send_c, recv_c,
):
    c, f = lax.axis_index("ctx"), lax.axis_index("fsdp")
    head, part, pair = lax.div(c, parts), lax.rem(c, parts), lax.rem(c, 2)
    rows = D // 4
    half = rows // 2
    wide = 2 * HEAD_SIZE
    barrier = pltpu.get_barrier_semaphore()
    peers = [(i, 0) for i in range(1, n_ctx)] + [(0, k) for k in range(1, 4)]
    for dc, df in peers:
        pl.semaphore_signal(
            barrier, inc=1, device_id=(flip(c, dc), flip(f, df)), device_id_type=MESH
        )
    shards = (w_q, w_k, w_v, w_o)
    fulls = (q_full, k_full, v_full, o_full)
    packs, owns = (pack0, pack1, pack2), (gate_own, up_own, down_own)
    my_rows = pl.ds(pl.multiple_of(f * rows, rows), rows)
    local = [pltpu.make_async_copy(shards[a], fulls[a].at[f], here.at[a]) for a in range(4)]
    local += [pltpu.make_async_copy(small, small_all.at[f], here.at[4])]
    local += [pltpu.make_async_copy(packs[m].at[f], own_buf.at[m], here.at[5 + m]) for m in range(3)]
    for copy in local:
        copy.start()
    pl.semaphore_wait(barrier, len(peers))
    near = pl.ds(pl.multiple_of(pair * half, half), half)
    far = pl.ds(pl.multiple_of((1 - pair) * half, half), half)
    sibling, over_x, over_pair = (c, flip(f, 1)), (c, flip(f, 2)), (flip(c, 1), f)
    nears = (near_q, near_k, near_v)
    crossed = [
        pltpu.make_async_copy(nears[a], fulls[a].at[flip(f, 2), near], here.at[11 + a]) for a in range(3)
    ]
    for copy in crossed:
        copy.start()

    def weight(a, kind):
        beyond = flip(f, 2)
        brought = nears[a] if a < 3 else fulls[a].at[beyond, near]
        source, target, device = (
            (shards[a], fulls[a].at[f], sibling),
            (shards[a].at[near], fulls[a].at[f, near], over_x),
            (brought, fulls[a].at[beyond, near], sibling),
            (brought, fulls[a].at[beyond, near], over_pair),
            (fulls[a].at[beyond, far], fulls[a].at[beyond, far], sibling),
        )[kind]
        return pltpu.make_async_remote_copy(
            source, target, send_w.at[a, kind], recv_w.at[a, kind], device_id=device, device_id_type=MESH
        )

    smalls = [
        pltpu.make_async_remote_copy(
            small, small_all.at[f], send_s.at[i - 1], recv_s.at[i - 1],
            device_id=(c, flip(f, i)), device_id_type=MESH,
        )
        for i in range(1, 4)
    ]
    for copy in smalls:
        copy.start()
    for a in range(4):
        for kind in (3, 0, 2) if a < 3 else (1, 0):
            weight(a, kind).start()
    experts = [
        pltpu.make_async_remote_copy(
            packs[m].at[flip(f, i)], owns[m].at[:, my_rows], send_e.at[i - 1, m], recv_e.at[i - 1, m],
            device_id=(c, flip(f, i)), device_id_type=MESH,
        )
        for m in range(3)
        for i in range(1, 4)
    ]
    for copy in experts:
        copy.start()

    cots = [
        pltpu.make_async_remote_copy(
            source, cot_pair.at[i], send_c.at[i], recv_c.at[i], device_id=device, device_id_type=MESH
        )
        for i, (source, device) in enumerate(((cot, over_pair), (cot_pair.at[0], sibling)))
    ]
    cots[0].start()
    x = tok[...].astype(F32)
    scale = lax.rsqrt(jnp.mean(x * x, axis=1, keepdims=True) + EPS)
    for copy in smalls:
        copy.wait_recv()
    local[4].wait()
    for b in range(4):
        columns = slice(b * rows, (b + 1) * rows)
        normed[:, columns] = (x[:, columns] * scale * small_all[b, :1].astype(F32)).astype(BF16)

    def project(b, first):
        block = normed[:, pl.ds(pl.multiple_of(b * rows, rows), rows)]
        at = 0
        for a in range(3):
            width = fulls[a].shape[2]
            made = jnp.dot(block, fulls[a][b], preferred_element_type=F32)
            acc[:, at : at + width] = made if first else acc[:, at : at + width] + made
            at += width

    for a in range(3):
        local[a].wait()
    stores = []
    for m in range(3):
        local[5 + m].wait()
        stores.append(pltpu.make_async_copy(own_buf.at[m], owns[m].at[:, my_rows], here.at[5 + m]))
        stores[m].start()
    project(f, True)
    for a in range(3):
        weight(a, 0).wait_recv()
    project(flip(f, 1), False)
    for a in range(3):
        weight(a, 3).wait_recv()
        weight(a, 4).start()
        crossed[a].wait()
    project(flip(f, 2), False)
    for a in range(3):
        weight(a, 2).wait_recv()
        weight(a, 4).wait_recv()
    project(flip(f, 3), False)

    lane = lax.broadcasted_iota(jnp.int32, (BLOCK, wide), 1)
    low = lane < HEAD_SIZE
    cosine, sine = cos_ref[...], sin_ref[...]
    for m in range((QUERY_HEADS + 2 * KEY_VALUE_HEADS) // 2):
        pieces = []
        for s in range(SEQS):
            piece = acc[s * BLOCK : (s + 1) * BLOCK, m * wide : (m + 1) * wide]
            pieces.append(turn(piece, cosine, sine) if m < (QUERY_HEADS + KEY_VALUE_HEADS) // 2 else piece)
        even = jnp.where(low, pieces[0], pltpu.roll(pieces[1], HEAD_SIZE, 1)).astype(BF16)
        odd = jnp.where(low, pltpu.roll(pieces[0], HEAD_SIZE, 1), pieces[1]).astype(BF16)
        for h, value in ((2 * m, even), (2 * m + 1, odd)):
            if h < QUERY_HEADS:
                q_pack[h // REP, h % REP] = value
            else:
                h -= QUERY_HEADS
                kv_pack[h % KEY_VALUE_HEADS, h // KEY_VALUE_HEADS] = value

    q_stays = pltpu.make_async_copy(q_pack.at[head], q_ref.at[head], here.at[8])
    kv_stays = pltpu.make_async_copy(kv_pack.at[head], kv_ref.at[c], here.at[9])
    q_stays.start()
    kv_stays.start()
    to_heads = []
    for i in range(1, n_ctx):
        peer = flip(c, i)
        moves = [(kv_pack.at[lax.div(peer, parts)], kv_ref.at[c], send_kv.at[i - 1], recv_kv.at[i - 1])]
        if i % parts == 0:
            number = i // parts - 1
            moves.append(
                (q_pack.at[lax.div(peer, parts)], q_ref.at[head], send_q.at[number], recv_q.at[number])
            )
        for source, target, sent, came in moves:
            copy = pltpu.make_async_remote_copy(
                source, target, sent, came, device_id=(peer, f), device_id_type=MESH
            )
            copy.start()
            to_heads.append(copy)
    weight(3, 1).wait_recv()
    weight(3, 2).start()
    weight(3, 3).start()
    q_stays.wait()
    kv_stays.wait()
    for copy in to_heads:
        copy.wait_recv()
    cots[0].wait_recv()
    cots[1].start()

    count = REP * BLOCK
    halves = half_masks(BF16)
    across = lax.broadcasted_iota(jnp.int32, (count, wide), 1)

    def out_back(j):
        return pltpu.make_async_remote_copy(
            o_buf.at[j], o_back.at[head], send_o.at[j], recv_o.at[head],
            device_id=(j * parts + part, f), device_id_type=MESH,
        )

    def out_stays(j):
        return pltpu.make_async_copy(o_buf.at[j], o_back.at[head], here.at[10])

    def one_block(j, nothing):
        block = j * parts + part
        q = q_ref[j].reshape(count, wide)
        queries = [q * half for half in halves]

        def step(number, carry):
            k = kv_ref[pl.ds(2 * number, 2), 0].reshape(KEYS, wide)
            v = kv_ref[pl.ds(2 * number, 2), 1].reshape(KEYS, wide)
            codes = code_ref[number]
            after = []
            for s in range(SEQS):
                largest, total, out = carry[s]
                mask = allowed_at(block, number, seg_ref[j, s], codes[s : s + 1])
                scores = lax.dot_general(
                    queries[s], k, (((1,), (1,)), ((), ())), preferred_element_type=F32
                )
                scores = jnp.where(mask[None], scores.reshape(REP, BLOCK, KEYS) * SCALE, MASKED)
                scores = scores.reshape(count, KEYS)
                new = jnp.maximum(largest, jnp.max(scores, axis=1, keepdims=True))
                probs = jnp.exp(scores - new)
                shrink = jnp.exp(largest - new)
                total = total * shrink + jnp.sum(probs, axis=1, keepdims=True)
                out = out * shrink + jnp.dot(probs.astype(BF16), v, preferred_element_type=F32)
                after.append((new, total, out))
            return tuple(after)

        start = (
            jnp.full((count, 1), MASKED, F32),
            jnp.zeros((count, 1), F32),
            jnp.zeros((count, wide), F32),
        )
        done = lax.fori_loop(0, lax.div(block, 2) + 1, step, (start,) * SEQS)
        outs, logs = [], []
        for largest, total, out in done:
            outs.append(out / total)
            logs.append(jnp.broadcast_to(largest + jnp.log(total), (count, wide)))
        out = jnp.where(across < HEAD_SIZE, outs[0], outs[1])
        full_ref[j] = out.reshape(REP, BLOCK, wide)
        log_ref[j] = jnp.where(across < HEAD_SIZE, logs[0], logs[1]).reshape(REP, BLOCK, wide)
        o_buf[j] = out.astype(BF16).reshape(REP, BLOCK, wide)

        @pl.when(j != head)
        def _():
            out_back(j).start()

        @pl.when(j == head)
        def _():
            out_stays(j).start()

        return nothing

    lax.fori_loop(0, KEY_VALUE_HEADS, one_block, 0)
    weight(3, 3).wait_recv()
    weight(3, 4).start()

    def came_out(h, nothing):
        @pl.when(h != head)
        def _():
            pltpu.make_async_remote_copy(
                o_buf.at[h], o_back.at[h], send_o.at[h], recv_o.at[h],
                device_id=(h * parts + part, f), device_id_type=MESH,
            ).wait()

        @pl.when(h == head)
        def _():
            out_stays(h).wait()

        return nothing

    lax.fori_loop(0, KEY_VALUE_HEADS, came_out, 0)
    for kind in (0, 2, 4):
        weight(3, kind).wait_recv()
    local[3].wait()
    for copy in stores:
        copy.wait()
    for copy in experts:
        copy.wait()
    cots[1].wait()
    for copy in smalls + to_heads + cots[:1]:
        copy.wait_send()
    for a in range(4):
        for kind in (0, 2, 3, 4) if a < 3 else range(5):
            weight(a, kind).wait_send()


def attention_forward(
    cid, parts, n_ctx, tok, small, w_q, w_k, w_v, w_o, nears, packs, cot, cosine, sine, segq, codes
):
    wide = 2 * HEAD_SIZE
    anywhere = pl.BlockSpec(memory_space=pl.ANY)
    inside = pl.BlockSpec(memory_space=pltpu.VMEM)
    dma = pltpu.SemaphoreType.DMA
    heads = (KEY_VALUE_HEADS, REP, BLOCK, wide)
    keys = (n_ctx, 2, BLOCK, wide)
    others = max(n_ctx // parts - 1, 1)
    columns = w_q.shape[1] + w_k.shape[1] + w_v.shape[1]
    own = jax.ShapeDtypeStruct((OWN, D, FF), BF16)

    def full(x):
        return jax.ShapeDtypeStruct((4,) + x.shape, BF16)

    return pl.pallas_call(
        functools.partial(attention_forward_kernel, parts, n_ctx),
        name="attention_forward",
        out_shape=[
            jax.ShapeDtypeStruct(tok.shape, BF16),
            full(small), full(w_q), full(w_k), full(w_v),
            jax.ShapeDtypeStruct(heads, BF16),
            jax.ShapeDtypeStruct(keys, BF16),
            jax.ShapeDtypeStruct(heads, F32),
            jax.ShapeDtypeStruct(heads, F32),
            jax.ShapeDtypeStruct(heads, BF16),
            full(w_o), own, own, own,
            jax.ShapeDtypeStruct((2,) + cot.shape, BF16),
        ],
        in_specs=[inside] + [anywhere] * 12 + [inside] * 4,
        out_specs=[inside] * 9 + [anywhere, inside] + [anywhere] * 4,
        scratch_shapes=[
            pltpu.VMEM((SEQS * BLOCK, columns), F32),
            pltpu.VMEM(heads, BF16),
            pltpu.VMEM((KEY_VALUE_HEADS, 2, BLOCK, wide), BF16),
            pltpu.VMEM(heads, BF16),
            pltpu.VMEM((3,) + packs[0].shape[1:], BF16),
            dma((4, 5)), dma((4, 5)), dma((3,)), dma((3,)), dma((3, 3)), dma((3, 3)),
            dma((others,)), dma((others,)), dma((n_ctx - 1,)), dma((n_ctx - 1,)),
            dma((KEY_VALUE_HEADS,)), dma((KEY_VALUE_HEADS,)), dma((14,)), dma((2,)), dma((2,)),
        ],
        compiler_params=pltpu.CompilerParams(
            collective_id=cid, has_side_effects=True, vmem_limit_bytes=56 << 20
        ),
        cost_estimate=lasting(130),
    )(tok, small, w_q, w_k, w_v, w_o, *nears, *packs, cot, cosine, sine, segq, codes)


def turn_back(field, cosine, sine):
    half = HEAD_SIZE // 2
    lane = lax.broadcasted_iota(jnp.int32, field.shape, field.ndim - 1)
    up = pltpu.roll(field, 2 * HEAD_SIZE - half, field.ndim - 1)
    down = pltpu.roll(field, half, field.ndim - 1)
    turned = jnp.where(lax.rem(lane, HEAD_SIZE) < half, -up, down)
    return field * cosine - turned * sine


def attention_backward_kernel(
    parts, n_ctx, early, g_own, q_ref, kv_ref, seg_ref, code_ref, full_ref, log_ref, cos_ref, sin_ref,
    tok, gain, resid_grad, residual, grads, down_in, mix, output_part, tokens_all, q_full, k_full, v_full,
    input_grad, layer_out, gain_grad, output_sum, gate_first, gate_keep, gate_came, gate_other, up_came, down_keep, down_came,
    mix_core, mix_in, head_in, g_ref, total, kept, came, dq_ref, dkv_ref, dq_back, dkv_back, w_q, w_k, w_v, grad_qkv, grad_in,
    token_buf, field, head_acc, head_out, head_core, head_x, output_keep, output_came, output_x, output_pair,
    send_g, recv_g, send_q, recv_q, send_kv, recv_kv, send_mix, recv_mix, send_half, recv_half, here,
    send_out, recv_out, send_head, recv_head, load_t,
):
    c, f = lax.axis_index("ctx"), lax.axis_index("fsdp")
    head, part = lax.div(c, parts), lax.rem(c, parts)
    rows = REP * BLOCK
    wide = 2 * HEAD_SIZE
    barrier = pltpu.get_barrier_semaphore()
    peers = [(i, k) for i in range(n_ctx) for k in range(4) if i or k]
    for dc, df in peers:
        pl.semaphore_signal(
            barrier, inc=1, device_id=(flip(c, dc), flip(f, df)), device_id_type=MESH
        )
    pair, x_bit, core_bit = lax.rem(c, 2), lax.div(f, 2), lax.rem(f, 2)
    loads = [
        pltpu.make_async_copy(source, target, here.at[5 + i])
        for i, (source, target) in enumerate(
            (
                (q_full, w_q), (k_full, w_k), (v_full, w_v),
                (output_part.at[:, :, :, core_bit], output_keep),
            )
        )
    ]

    def bring(b):
        return pltpu.make_async_copy(
            tokens_all.at[b], token_buf.at[lax.rem(b, 2)], load_t.at[lax.rem(b, 2)]
        )

    for copy in loads[1:]:
        copy.start()
    first = pltpu.make_async_copy(g_own.at[head], g_ref.at[head], here.at[0])
    first.start()
    pl.semaphore_wait(barrier, len(peers))
    to_heads = []
    for number, i in enumerate(range(parts, n_ctx, parts)):
        to_heads.append(
            pltpu.make_async_remote_copy(
                g_own.at[lax.div(flip(c, i), parts)], g_ref.at[head],
                send_g.at[number], recv_g.at[number],
                device_id=(flip(c, i), f), device_id_type=MESH,
            )
        )
        to_heads[-1].start()
    half = grads.shape[1] // 2
    quarter = half // 2
    mine = lax.rem(lax.div(c, 2), 2)
    second = lax.rem(lax.div(c, 4), 2)

    def halving(matrix, target, number):
        return pltpu.make_async_remote_copy(
            grads.at[matrix, pl.ds((1 - mine) * half, half)], target,
            send_half.at[number], recv_half.at[number],
            device_id=(flip(c, 2), f), device_id_type=MESH,
        )

    down_halving, gate_halving = halving(2, came, 0), halving(0, gate_first, 1)
    arriving = pltpu.make_async_copy(down_in, came, here.at[10]) if early else down_halving
    arriving.start()
    up_halving = pltpu.make_async_remote_copy(
        grads.at[1, pl.ds((1 - mine) * half, half), 0], up_came, send_half.at[4], recv_half.at[4],
        device_id=(flip(c, 2), f), device_id_type=MESH,
    )
    keeping = pltpu.make_async_copy(grads.at[2, pl.ds(mine * half, half)], kept, here.at[3])
    keeping.start()
    output_stages = [
        pltpu.make_async_remote_copy(
            source, target, send_out.at[i], recv_out.at[i], device_id=device, device_id_type=MESH
        )
        for i, (source, target, device) in enumerate(
            (
                (output_part.at[:, :, :, 1 - core_bit], output_came, (c, flip(f, 1))),
                (output_keep.at[:, :, 1 - x_bit], output_x, (c, flip(f, 2))),
                (output_x.at[:, 1 - pair], output_pair, (flip(c, 1), f)),
            )
        )
    ]
    output_stages[0].start()
    to_core = [
        pltpu.make_async_remote_copy(
            mix.at[2 * k + 1], mix_core.at[k], send_mix.at[k], recv_mix.at[k],
            device_id=(c, flip(f, 1)), device_id_type=MESH,
        )
        for k in range(4)
    ]
    for copy in to_core:
        copy.start()

    def plus(mine, came):
        return (mine.astype(F32) + came.astype(F32)).astype(BF16)

    def second_halving(keep, target, number, later=None):
        def add(i, nothing):
            at, e = lax.div(i, OWN), lax.rem(i, OWN)
            kept[at, e] = plus(kept[at, e], came[at, e])
            return nothing

        lax.fori_loop(0, half * OWN, add, 0)
        source = kept.at[pl.ds((1 - second) * quarter, quarter)]
        if later is not None:
            source, target = source.at[:, 0], target.at[:, 0]
            rest = pltpu.make_async_copy(
                kept.at[pl.ds((1 - second) * quarter, quarter), 1], later, here.at[3]
            )
            rest.start()
            rest.wait()
        going = pltpu.make_async_remote_copy(
            source, target, send_half.at[number], recv_half.at[number],
            device_id=(flip(c, 4), f), device_id_type=MESH,
        )
        going.start()
        staying = pltpu.make_async_copy(kept.at[pl.ds(second * quarter, quarter)], keep, here.at[4])
        staying.start()
        return going, staying

    if early:
        keeping.wait()
        arriving.wait()
        down_second, leaving = second_halving(down_keep, down_came, 2)
    gate_halving.start()
    shares = w_q.at[:, pl.ds(0, SEQS * BLOCK)]
    for k in range(4):
        pair_in = [
            pltpu.make_async_copy(mix.at[2 * k], token_buf.at[0], load_t.at[0]),
            pltpu.make_async_copy(mix_core.at[k], token_buf.at[1], load_t.at[1]),
        ]
        pair_in[0].start()
        to_core[k].wait_recv()
        pair_in[1].start()
        for copy in pair_in:
            copy.wait()
        shares[k] = plus(token_buf[0], token_buf[1])
    own_share = pltpu.make_async_copy(shares.at[0], mix_in.at[0], here.at[5])
    own_share.start()
    returns = [
        pltpu.make_async_remote_copy(
            shares.at[k], mix_in.at[k], send_mix.at[3 + k], recv_mix.at[3 + k],
            device_id=(flip(c, k % 2), flip(f, 2 * (k // 2))), device_id_type=MESH,
        )
        for k in range(1, 4)
    ]
    for copy in returns:
        copy.start()
    for b in range(2):
        bring(b).start()
    total[...] = jnp.zeros_like(total)
    first.wait()
    for copy in to_heads:
        copy.wait_recv()
    halves = half_masks(BF16)
    lane = lax.broadcasted_iota(jnp.int32, (rows, wide), 1)

    def query_back(j):
        return pltpu.make_async_remote_copy(
            dq_ref.at[j], dq_back.at[head], send_q.at[j], recv_q.at[head],
            device_id=(j * parts + part, f), device_id_type=MESH,
        )

    def key_back(b):
        return pltpu.make_async_remote_copy(
            dkv_ref.at[b], dkv_back.at[c], send_kv.at[b], recv_kv.at[c],
            device_id=(b, f), device_id_type=MESH,
        )

    def query_stays(j):
        return pltpu.make_async_copy(dq_ref.at[j], dq_back.at[head], here.at[1])

    def key_stays(b):
        return pltpu.make_async_copy(dkv_ref.at[b], dkv_back.at[c], here.at[2])

    def one_block(j, nothing):
        block = j * parts + part
        q = q_ref[j].reshape(rows, wide)
        g = g_ref[j].reshape(rows, wide)
        queries = [q * half for half in halves]
        partial = [g * half for half in halves]
        product = g.astype(F32) * full_ref[j].reshape(rows, wide)
        logs = log_ref[j].reshape(rows, wide)
        log_total = [logs[:, :1], logs[:, HEAD_SIZE : HEAD_SIZE + 1]]
        inner = [jnp.sum(product * half, axis=1, keepdims=True) for half in half_masks(F32)]

        def step(number, carry):
            k = kv_ref[pl.ds(2 * number, 2), 0].reshape(KEYS, wide)
            v = kv_ref[pl.ds(2 * number, 2), 1].reshape(KEYS, wide)
            codes = code_ref[number]
            after = []
            dk = jnp.zeros((KEYS, wide), F32)
            dv = jnp.zeros((KEYS, wide), F32)
            for s in range(SEQS):
                mask = allowed_at(block, number, seg_ref[j, s], codes[s : s + 1])
                scores = lax.dot_general(
                    queries[s], k, (((1,), (1,)), ((), ())), preferred_element_type=F32
                )
                scores = jnp.where(mask[None], scores.reshape(REP, BLOCK, KEYS) * SCALE, MASKED)
                probs = jnp.exp(scores.reshape(rows, KEYS) - log_total[s])
                grad_probs = lax.dot_general(
                    partial[s], v, (((1,), (1,)), ((), ())), preferred_element_type=F32
                )
                grad_scores = (probs * (grad_probs - inner[s])).astype(BF16)
                dv = dv + lax.dot_general(
                    probs.astype(BF16), partial[s], (((0,), (0,)), ((), ())), preferred_element_type=F32
                )
                dk = dk + lax.dot_general(
                    grad_scores, queries[s], (((0,), (0,)), ((), ())), preferred_element_type=F32
                )
                after.append(carry[s] + jnp.dot(grad_scores, k, preferred_element_type=F32))
            total[pl.ds(2 * number, 2), 0] += dk.reshape(2, BLOCK, wide)
            total[pl.ds(2 * number, 2), 1] += dv.reshape(2, BLOCK, wide)
            return tuple(after)

        start = jnp.zeros((rows, wide), F32)
        done = lax.fori_loop(0, lax.div(block, 2) + 1, step, (start,) * SEQS)
        dq = (jnp.where(lane < HEAD_SIZE, done[0], done[1]) * SCALE).reshape(REP, BLOCK, wide)
        dq_ref[j] = turn_back(dq, cos_ref[block][None], sin_ref[block][None]).astype(BF16)

        @pl.when(j != head)
        def _():
            query_back(j).start()

        @pl.when(j == head)
        def _():
            query_stays(j).start()

        return nothing

    lax.fori_loop(0, KEY_VALUE_HEADS, one_block, 0)

    def finish(b, nothing):
        dkv_ref[b, 0] = turn_back(total[b, 0] * SCALE, cos_ref[b], sin_ref[b]).astype(BF16)
        dkv_ref[b, 1] = total[b, 1].astype(BF16)

        @pl.when(b != c)
        def _():
            key_back(b).start()

        @pl.when(b == c)
        def _():
            key_stays(b).start()

        return nothing

    lax.fori_loop(0, n_ctx, finish, 0)
    up_halving.start()
    if not early:
        keeping.wait()
        down_halving.wait_recv()
        down_second, leaving = second_halving(down_keep, down_came, 2)

    planes = output_keep.shape[0]

    loads[3].wait()
    output_stages[0].wait_recv()

    def cores(i, nothing):
        r, p, x = lax.div(i, 4), lax.rem(lax.div(i, 2), 2), lax.rem(i, 2)
        output_keep[r, p, x] = plus(output_keep[r, p, x], output_came[r, p, x])
        return nothing

    lax.fori_loop(0, planes * 4, cores, 0)
    output_stages[1].start()

    low = lax.broadcasted_iota(jnp.int32, (BLOCK, wide), 1) < HEAD_SIZE

    def side_by_side(even, odd):
        even, odd = even.astype(F32), odd.astype(F32)
        return (
            jnp.where(low, even, pltpu.roll(odd, HEAD_SIZE, 1)),
            jnp.where(low, pltpu.roll(even, HEAD_SIZE, 1), odd),
        )

    head_acc[...] = jnp.zeros_like(head_acc)

    def head_weights(b, nothing):
        bring(b).wait()
        block = token_buf[lax.rem(b, 2)]
        wide_block = block.astype(F32)
        scales = lax.rsqrt(jnp.mean(wide_block * wide_block, axis=1, keepdims=True) + EPS)
        j = lax.div(b, parts)
        have = jnp.where(lax.rem(b, parts) == part, 1.0, 0.0)
        heads = [dq_ref[j, r].astype(F32) * have for r in range(REP)] + [dkv_ref[b, 0], dkv_ref[b, 1]]
        heads.append(jnp.zeros((BLOCK, wide), F32))
        for m in range((REP + 3) // 2):
            for s, value in enumerate(side_by_side(heads[2 * m], heads[2 * m + 1])):
                at = slice(s * BLOCK, (s + 1) * BLOCK)
                field[at, m * wide : (m + 1) * wide] = (value * scales[at]).astype(BF16)
        head_acc[...] += lax.dot_general(
            block, field[...], (((0,), (0,)), ((), ())), preferred_element_type=F32
        )

        @pl.when(b + 2 < n_ctx)
        def _():
            bring(b + 2).start()

        return nothing

    lax.fori_loop(0, n_ctx, head_weights, 0)
    slab = D // (n_ctx * 4)
    for d in range(n_ctx * 4):
        head_out[d // 4, d // 2 % 2, d % 2] = head_acc[
            d * slab : (d + 1) * slab, : head_out.shape[4]
        ].astype(BF16)
    head_stages = [
        pltpu.make_async_remote_copy(
            source, target, send_head.at[i], recv_head.at[i], device_id=device, device_id_type=MESH
        )
        for i, (source, target, device) in enumerate(
            (
                (head_out.at[:, :, 1 - core_bit], head_core, (c, flip(f, 1))),
                (head_core.at[:, 1 - x_bit], head_x, (c, flip(f, 2))),
            )
        )
    ]
    head_stages[0].start()
    for copy in returns:
        copy.wait_send()
    own_share.wait()
    loads[0].start()
    down_second.wait_send()
    leaving.wait()
    gate_halving.wait_recv()
    refill = [
        pltpu.make_async_copy(grads.at[0, pl.ds(mine * half, half)], kept, here.at[3]),
        pltpu.make_async_copy(gate_first, came, here.at[10]),
    ]
    for copy in refill:
        copy.start()
    for copy in refill:
        copy.wait()
    gate_second, leaving = second_halving(gate_keep, gate_came, 3, gate_other)

    head_stages[0].wait_recv()

    def head_cores(i, nothing):
        d, x = lax.div(i, 2), lax.rem(i, 2)
        head_core[d, x] = plus(head_out[d, x, core_bit], head_core[d, x])
        return nothing

    lax.fori_loop(0, n_ctx * 2, head_cores, 0)
    head_stages[1].start()

    def came_query(h, nothing):
        @pl.when(h != head)
        def _():
            pltpu.make_async_remote_copy(
                dq_ref.at[h], dq_back.at[h], send_q.at[h], recv_q.at[h],
                device_id=(h * parts + part, f), device_id_type=MESH,
            ).wait()

        @pl.when(h == head)
        def _():
            query_stays(h).wait()

        return nothing

    def came_key(b, nothing):
        @pl.when(b != c)
        def _():
            pltpu.make_async_remote_copy(
                dkv_ref.at[b], dkv_back.at[b], send_kv.at[b], recv_kv.at[b],
                device_id=(b, f), device_id_type=MESH,
            ).wait()

        @pl.when(b == c)
        def _():
            key_stays(b).wait()

        return nothing

    lax.fori_loop(0, KEY_VALUE_HEADS, came_query, 0)
    lax.fori_loop(0, n_ctx, came_key, 0)

    def head_of(h):
        if h < QUERY_HEADS:
            return dq_back[h // REP, h % REP]
        kind, h = (h - QUERY_HEADS) // KEY_VALUE_HEADS, (h - QUERY_HEADS) % KEY_VALUE_HEADS
        value = dkv_back[h * parts, kind]
        if parts > 1:
            value = value.astype(F32)
            for p in range(1, parts):
                value = value + dkv_back[h * parts + p, kind].astype(F32)
        return value

    head_stages[1].wait_recv()

    def head_over_x(d, nothing):
        head_x[d] = plus(head_core[d, x_bit], head_x[d])
        return nothing

    lax.fori_loop(0, n_ctx, head_over_x, 0)
    head_stays = pltpu.make_async_copy(head_x.at[c], head_in.at[c], here.at[9])
    head_stays.start()
    to_all = []
    for i in range(1, n_ctx):
        to_all.append(
            pltpu.make_async_remote_copy(
                head_x.at[flip(c, i)], head_in.at[c], send_head.at[1 + i], recv_head.at[1 + i],
                device_id=(flip(c, i), f), device_id_type=MESH,
            )
        )
        to_all[-1].start()
    for m in range((QUERY_HEADS + 2 * KEY_VALUE_HEADS) // 2):
        for s, value in enumerate(side_by_side(head_of(2 * m), head_of(2 * m + 1))):
            grad_qkv[s * BLOCK : (s + 1) * BLOCK, m * wide : (m + 1) * wide] = value.astype(BF16)
    for copy in loads[:3]:
        copy.wait()
    depth = D // 4
    for b in range(4):
        made, at = 0.0, 0
        for weight in (w_q, w_k, w_v):
            width = weight.shape[2]
            made = made + lax.dot_general(
                grad_qkv[:, at : at + width], weight[b], (((1,), (1,)), ((), ())),
                preferred_element_type=F32,
            )
            at += width
        grad_in[:, b * depth : (b + 1) * depth] = made
    x = tok[...].astype(F32)
    scale = lax.rsqrt(jnp.mean(x * x, axis=1, keepdims=True) + EPS)
    gain_grad[...] = jnp.sum(grad_in[...] * x * scale, axis=0, keepdims=True)
    weighted = grad_in[...] * gain[...]
    input_grad[...] = (
        resid_grad[...]
        + scale * weighted
        - x * (scale * scale * scale) * jnp.mean(weighted * x, axis=1, keepdims=True)
    ).astype(BF16)

    staying = pltpu.make_async_copy(residual, grad_in, here.at[8])
    staying.start()
    staying.wait()

    def share(k):
        return pltpu.make_async_copy(mix_in.at[k], token_buf.at[k % 2], load_t.at[k % 2])

    share(0).start()
    for k in range(4):
        if k < 3:
            returns[k].wait_recv()
            share(k + 1).start()
        share(k).wait()
        grad_in[...] += token_buf[k % 2].astype(F32)
    layer_out[...] = grad_in[...].astype(BF16)

    output_stages[1].wait_recv()

    def over_x(i, nothing):
        r, p = lax.div(i, 2), lax.rem(i, 2)
        output_x[r, p] = plus(output_keep[r, p, x_bit], output_x[r, p])
        return nothing

    lax.fori_loop(0, planes * 2, over_x, 0)
    output_stages[2].start()
    output_stages[2].wait_recv()

    def over_pair(r, nothing):
        output_sum[r] = plus(output_x[r, pair], output_pair[r])
        return nothing

    lax.fori_loop(0, planes, over_pair, 0)
    for copy in to_heads:
        copy.wait_send()
    for copy in to_all + [gate_second, up_halving, leaving, head_stays]:
        copy.wait()
    down_second.wait_recv()
    for copy in to_core + output_stages + head_stages + [gate_halving] + ([] if early else [down_halving]):
        copy.wait_send()


def attention_backward(
    cid, parts, n_ctx, early, g_own, q, kv, segq, codes, full, logs, cosine, sine,
    tok, gain, resid_grad, residual, grads, down_in, mix, output_part, tokens_all, q_full, k_full, v_full,
):
    wide = 2 * HEAD_SIZE
    anywhere = pl.BlockSpec(memory_space=pl.ANY)
    inside = pl.BlockSpec(memory_space=pltpu.VMEM)
    dma = pltpu.SemaphoreType.DMA
    others = max(n_ctx // parts - 1, 1)
    devices, planes = n_ctx * 4, n_ctx // 2
    slab, head_width = D // devices, (REP + 2) * HEAD_SIZE
    half = (grads.shape[1] // 2,) + grads.shape[2:]
    quarter = (grads.shape[1] // 4,) + grads.shape[2:]
    columns = q_full.shape[2] + k_full.shape[2] + v_full.shape[2]
    return pl.pallas_call(
        functools.partial(attention_backward_kernel, parts, n_ctx, early),
        name="attention_backward",
        out_shape=[
            jax.ShapeDtypeStruct(tok.shape, BF16),
            jax.ShapeDtypeStruct(tok.shape, BF16),
            jax.ShapeDtypeStruct((1, D), F32),
            jax.ShapeDtypeStruct((planes, slab, D), BF16),
            jax.ShapeDtypeStruct(half, BF16),
            jax.ShapeDtypeStruct(quarter, BF16),
            jax.ShapeDtypeStruct(quarter, BF16),
            jax.ShapeDtypeStruct(quarter[:1] + quarter[2:], BF16),
            jax.ShapeDtypeStruct(half[:1] + half[2:], BF16),
            jax.ShapeDtypeStruct(quarter, BF16),
            jax.ShapeDtypeStruct(quarter, BF16),
            jax.ShapeDtypeStruct((4,) + mix.shape[1:], BF16),
            jax.ShapeDtypeStruct((4,) + mix.shape[1:], BF16),
            jax.ShapeDtypeStruct((n_ctx, slab, head_width), BF16),
        ],
        in_specs=[anywhere] + [inside] * 11 + [anywhere] * 9,
        out_specs=[inside] * 4 + [anywhere] * 10,
        scratch_shapes=[
            pltpu.VMEM(q.shape, BF16),
            pltpu.VMEM((n_ctx, 2, BLOCK, wide), F32),
            pltpu.VMEM(half, BF16),
            pltpu.VMEM(half, BF16),
            pltpu.VMEM(q.shape, BF16),
            pltpu.VMEM(kv.shape, BF16),
            pltpu.VMEM(q.shape, BF16),
            pltpu.VMEM(kv.shape, BF16),
            pltpu.VMEM(q_full.shape, BF16),
            pltpu.VMEM(k_full.shape, BF16),
            pltpu.VMEM(v_full.shape, BF16),
            pltpu.VMEM((SEQS * BLOCK, columns), BF16),
            pltpu.VMEM((SEQS * BLOCK, D), F32),
            pltpu.VMEM((2, SEQS * BLOCK, D), BF16),
            pltpu.VMEM((SEQS * BLOCK, 3 * wide), BF16),
            pltpu.VMEM((D, 3 * wide), F32),
            pltpu.VMEM((n_ctx, 2, 2, slab, head_width), BF16),
            pltpu.VMEM((n_ctx, 2, slab, head_width), BF16),
            pltpu.VMEM((n_ctx, slab, head_width), BF16),
            pltpu.VMEM((planes, 2, 2, slab, D), BF16),
            pltpu.VMEM((planes, 2, 2, slab, D), BF16),
            pltpu.VMEM((planes, 2, slab, D), BF16),
            pltpu.VMEM((planes, slab, D), BF16),
            dma((others,)), dma((others,)), dma((KEY_VALUE_HEADS,)), dma((KEY_VALUE_HEADS,)),
            dma((n_ctx,)), dma((n_ctx,)), dma((RANKS - 1,)), dma((RANKS - 1,)), dma((5,)), dma((5,)),
            dma((11,)), dma((3,)), dma((3,)), dma((n_ctx + 1,)), dma((n_ctx + 1,)), dma((2,)),
        ],
        compiler_params=pltpu.CompilerParams(
            collective_id=cid, has_side_effects=True, vmem_limit_bytes=62 << 20
        ),
        cost_estimate=lasting(125),
    )(
        g_own, q, kv, segq, codes, full, logs, cosine, sine, tok, gain, resid_grad, residual,
        grads, down_in, mix, output_part, tokens_all, q_full, k_full, v_full,
    )


def final_kernel(
    n_ctx, small, output_part, grads, gate_keep, gate_came, gate_other, up_came, down_keep, down_came,
    swapped, output_grad, small_sum,
    halves, landed, rest, rest_landed, last, last_landed, turned, output_in, small_in,
    send_half, recv_half, send_deep, recv_deep, send_out, recv_out, send_small, recv_small,
    send_swap, recv_swap, load, stay,
):
    c, f = lax.axis_index("ctx"), lax.axis_index("fsdp")
    me, plane, rank = c * 4 + f, lax.div(c, 2), lax.rem(c, 2) * 4 + f
    planes = n_ctx // 2
    half, quarter = planes // 2, planes // 4
    barrier = pltpu.get_barrier_semaphore()
    peers = [(i, k) for i in range(n_ctx) for k in range(4) if i or k]
    for dc, df in peers:
        pl.semaphore_signal(
            barrier, inc=1, device_id=(flip(c, dc), flip(f, df)), device_id_type=MESH
        )
    first, second = lax.rem(plane, 2), lax.rem(lax.div(plane, 2), 2)
    loads = [
        pltpu.make_async_copy(source, target, load.at[i])
        for i, (source, target) in enumerate(
            (
                (down_keep, rest.at[2]),
                (down_came, rest_landed.at[2]),
                (gate_keep, rest.at[0]),
                (gate_came.at[:, 0], rest_landed.at[0, :, 0]),
                (grads.at[1, pl.ds(first * half, half)], halves),
                (output_part.at[plane], output_in.at[plane]),
                (small.at[me], small_in.at[me]),
                (up_came, landed.at[:, 0]),
            )
        )
    ]
    for copy in loads:
        copy.start()
    pl.semaphore_wait(barrier, len(peers))

    def over(source, target, sent, came, bit):
        return pltpu.make_async_remote_copy(
            source, target, sent, came, device_id=(flip(c, 2 * bit), f), device_id_type=MESH
        )

    up_first = over(
        grads.at[1, pl.ds((1 - first) * half, half), 1], landed.at[:, 1],
        send_half.at[0, 1], recv_half.at[0, 1], 1,
    )
    gate_second = over(gate_other, rest_landed.at[0, :, 1], send_half.at[2, 1], recv_half.at[2, 1], 2)
    up_first.start()
    outputs = []
    for i in range(1, planes):
        outputs.append(
            pltpu.make_async_remote_copy(
                output_part.at[flip(plane, i)], output_in.at[plane], send_out.at[i - 1], recv_out.at[i - 1],
                device_id=(flip(c, 2 * i), f), device_id_type=MESH,
            )
        )
    smalls = []
    for number, (i, k) in enumerate(peers):
        peer_c, peer_f = flip(c, i), flip(f, k)
        smalls.append(
            pltpu.make_async_remote_copy(
                small.at[peer_c * 4 + peer_f], small_in.at[me], send_small.at[number], recv_small.at[number],
                device_id=(peer_c, peer_f), device_id_type=MESH,
            )
        )

    def plus(mine, came):
        return (mine.astype(F32) + came.astype(F32)).astype(BF16)

    swaps, sent = [], []

    def finish(m, e):
        count, bit, number = quarter, 4, 0
        for at in range(quarter):
            rest[m, at, e] = plus(rest[m, at, e], rest_landed[m, at, e])
        mine = rest.at[m, :, e]
        while count > 1:
            count //= 2
            chosen = lax.rem(lax.div(plane, bit), 2)
            came = last_landed.at[m, number, pl.ds(0, count), e]
            copy = over(
                mine.at[pl.ds((1 - chosen) * count, count)], came,
                send_deep.at[2 * m + number, e], recv_deep.at[2 * m + number, e], bit,
            )
            copy.start()
            copy.wait_recv()
            sent.append(copy)
            for at in range(count):
                last[m, number, at, e] = plus(mine[chosen * count + at], came[at])
            mine, bit, number = last.at[m, number, :, e], bit * 2, number + 1
        rows = turned.shape[3]
        across = mine[0].astype(F32).T
        for r in range(RANKS):
            turned[m, r, e] = across[r * rows : (r + 1) * rows].astype(BF16)
        for i in range(RANKS):
            source, target = turned.at[m, flip(rank, i), e], swapped.at[rank, m, e]
            if i:
                copy = pltpu.make_async_remote_copy(
                    source, target, send_swap.at[m * OWN + e, i], recv_swap.at[m * OWN + e, i],
                    device_id=(flip(c, i // 4), flip(f, i % 4)), device_id_type=MESH,
                )
            else:
                copy = pltpu.make_async_copy(source, target, stay.at[m * OWN + e])
            copy.start()
            swaps.append(copy)

    for copy in loads:
        copy.wait()
    up_second = []

    def second_of_up(e):
        for at in range(half):
            halves[at, e] = plus(halves[at, e], landed[at, e])
        up_second.append(
            over(
                halves.at[pl.ds((1 - second) * quarter, quarter), e], rest_landed.at[1, :, e],
                send_half.at[1, e], recv_half.at[1, e], 2,
            )
        )
        up_second[e].start()
        for at in range(quarter):
            rest[1, at, e] = halves[second * quarter + at, e]

    second_of_up(0)
    gate_second.start()
    for copy in outputs + smalls:
        copy.start()
    for e in range(OWN):
        finish(2, e)
    finish(0, 0)
    up_first.wait_recv()
    second_of_up(1)
    gate_second.wait_recv()
    finish(0, 1)
    for copy in outputs + smalls:
        copy.wait_recv()
    made = output_in[0].astype(F32)
    for i in range(1, planes):
        made = made + output_in[i].astype(F32)
    output_grad[...] = made
    small_sum[...] = jnp.sum(small_in[...], axis=0)
    for e in range(OWN):
        up_second[e].wait_recv()
        finish(1, e)
    for copy in swaps:
        copy.wait()
    for copy in smalls + outputs + sent + up_second + [up_first, gate_second]:
        copy.wait_send()


def final_sums(
    cid, n_ctx, small, output_part, grads, gate_keep, gate_came, gate_other, up_came, down_keep,
    down_came
):
    anywhere = pl.BlockSpec(memory_space=pl.ANY)
    inside = pl.BlockSpec(memory_space=pltpu.VMEM)
    dma = pltpu.SemaphoreType.DMA
    devices, planes = n_ctx * 4, n_ctx // 2
    slab, piece = D // devices, grads.shape[2:]
    half, quarter = (planes // 2,) + piece, (planes // 4,) + piece
    deep = (3, 2, max(planes // 8, 1)) + piece
    return pl.pallas_call(
        functools.partial(final_kernel, n_ctx),
        name="final_sums",
        out_shape=[
            jax.ShapeDtypeStruct((RANKS, 3, OWN, slab, FF), BF16),
            jax.ShapeDtypeStruct((slab, D), F32),
            jax.ShapeDtypeStruct(small.shape[1:], F32),
        ],
        in_specs=[anywhere] * 9,
        out_specs=[anywhere] + [inside] * 2,
        scratch_shapes=[
            pltpu.VMEM(half, BF16),
            pltpu.VMEM(half, BF16),
            pltpu.VMEM((3,) + quarter, BF16),
            pltpu.VMEM((3,) + quarter, BF16),
            pltpu.VMEM(deep if planes > 4 else (1, 1, 1, 1, 8, 128), BF16),
            pltpu.VMEM(deep if planes > 4 else (1, 1, 1, 1, 8, 128), BF16),
            pltpu.VMEM((3, RANKS, OWN, slab, FF), BF16),
            pltpu.VMEM((planes, slab, D), BF16),
            pltpu.VMEM(small.shape, F32),
            dma((3, OWN)), dma((3, OWN)), dma((6, OWN)), dma((6, OWN)),
            dma((planes - 1,)), dma((planes - 1,)), dma((devices - 1,)), dma((devices - 1,)),
            dma((3 * OWN, RANKS)), dma((3 * OWN, RANKS)), dma((8,)), dma((3 * OWN,)),
        ],
        compiler_params=pltpu.CompilerParams(
            collective_id=cid, has_side_effects=True, vmem_limit_bytes=56 << 20
        ),
        cost_estimate=lasting(80),
    )(small, output_part, grads, gate_keep, gate_came, gate_other, up_came, down_keep, down_came)


def rope_tables(positions):
    half_dim = HEAD_SIZE // 2
    frequency = ROPE_BASE ** (-jnp.arange(half_dim, dtype=F32) * 2.0 / HEAD_SIZE)
    angle = positions.astype(F32)[:, None] * frequency[None, :]
    angle = jnp.concatenate([angle, angle], axis=1)
    return (jnp.cos(angle), jnp.sin(angle))


def heads_out(field, per):
    field = field.reshape(SEQS, BLOCK, KEY_VALUE_HEADS, per, HEAD_SIZE)
    return field.transpose(2, 3, 1, 0, 4).reshape(KEY_VALUE_HEADS, per, BLOCK, SEQS * HEAD_SIZE)


def heads_in(field):
    per = field.shape[1]
    field = field.reshape(KEY_VALUE_HEADS, per, BLOCK, SEQS, HEAD_SIZE)
    return field.transpose(3, 2, 0, 1, 4).reshape(SEQS, BLOCK, KEY_VALUE_HEADS * per * HEAD_SIZE)


def on_device(
    n_ctx,
    n_fsdp,
    tokens,
    segments,
    valid,
    expert_ids,
    slot_order,
    cotangent,
    norm1_gain,
    w_query,
    key_weight,
    value_weight,
    w_output,
    norm2_gain,
    w_router,
    w_gate,
    w_up,
    w_down,
):
    parts = n_ctx // KEY_VALUE_HEADS
    replicas = n_ctx // 2
    full_len = segments.shape[1]
    c_index, f_index = lax.axis_index("ctx"), lax.axis_index("fsdp")
    pair = lax.rem(c_index, 2)
    rank = pair * n_fsdp + f_index
    part = lax.rem(c_index, parts)
    head = lax.div(c_index, parts)
    positions = c_index * BLOCK + jnp.arange(BLOCK, dtype=jnp.int32)

    span = D // n_fsdp // 2
    nears = [
        lax.ppermute(
            lax.dynamic_slice_in_dim(w, pair * span, span, 0), "fsdp", [(a, a ^ 2) for a in range(n_fsdp)]
        )
        for w in (w_query, key_weight, value_weight)
    ]
    tokens_all = lax.all_gather(tokens, "ctx", axis=0, tiled=False)
    small = jnp.concatenate(
        [
            norm1_gain[None],
            norm2_gain[None],
            w_router.T,
            jnp.zeros((SMALL - EXPERTS - 2, D // n_fsdp), BF16),
        ],
        axis=0,
    )
    packs = [
        lax.dynamic_slice_in_dim(w, pair * (EXPERTS // 2), EXPERTS // 2, 1)
        .reshape(D // n_fsdp, n_fsdp, OWN, FF)
        .transpose(1, 2, 0, 3)
        for w in (w_gate, w_up, w_down)
    ]
    inputs_f = tokens.astype(F32)
    scale_one = lax.rsqrt(jnp.mean(inputs_f * inputs_f, axis=-1, keepdims=True) + EPS)
    segq = segments.reshape(SEQS, KEY_VALUE_HEADS, parts, BLOCK)
    segq = lax.dynamic_index_in_dim(segq, part, 2, keepdims=False).transpose(1, 0, 2)[..., None]
    codes = jnp.where(valid > 0, segments, -1)
    codes = codes.reshape(SEQS, full_len // KEYS, KEYS).transpose(1, 0, 2)
    all_cosine, all_sine = rope_tables(jnp.arange(full_len, dtype=jnp.int32))
    all_cosine = jnp.tile(all_cosine, (1, 2)).reshape(n_ctx, BLOCK, 2 * HEAD_SIZE)
    all_sine = jnp.tile(all_sine, (1, 2)).reshape(n_ctx, BLOCK, 2 * HEAD_SIZE)
    (
        normed_in, small_all, full_query, full_key, full_value, q_all, kv_all, head_full, head_logs,
        attn_heads, full_output, own_gate, own_up, own_down, cot_pair,
    ) = attention_forward(
        0, parts, n_ctx, tokens.reshape(SEQS * BLOCK, D), small, w_query, key_weight, value_weight,
        w_output, nears, packs, cotangent.reshape(SEQS * BLOCK, D),
        lax.dynamic_index_in_dim(all_cosine, c_index, 0, keepdims=False),
        lax.dynamic_index_in_dim(all_sine, c_index, 0, keepdims=False),
        segq, codes,
    )
    gain_first = small_all[:, 0].reshape(D).astype(F32)
    gain_second = small_all[:, 1].reshape(D).astype(F32)
    full_router = small_all[:, 2 : 2 + EXPERTS].transpose(1, 0, 2).reshape(EXPERTS, D)
    full_output = full_output.reshape(D, D)
    attn_out = heads_in(attn_heads)
    attn_proj = jnp.einsum("sgq,dq->sgd", attn_out, full_output, preferred_element_type=F32)
    residual = inputs_f + attn_proj
    scale_two = lax.rsqrt(jnp.mean(residual * residual, axis=-1, keepdims=True) + EPS)
    normed_mid = (residual * scale_two * gain_second).astype(BF16)

    logits = jnp.einsum("sgd,ed->sge", normed_mid, full_router, preferred_element_type=F32)
    picked = jnp.any(expert_ids[..., None] == jnp.arange(EXPERTS, dtype=jnp.int32), axis=2)
    before = (slot_order[:, None, :] < slot_order[:, :, None]).astype(BF16)
    place = jnp.matmul(before, picked.astype(BF16), preferred_element_type=F32)
    is_kept = picked & (place < CAP)
    chosen = jnp.where(picked, logits, MASKED)
    raised = jnp.where(picked, jnp.exp(chosen - jnp.max(chosen, axis=-1, keepdims=True)), 0.0)
    gates = raised / jnp.sum(raised, axis=-1, keepdims=True)
    payload = jnp.concatenate(
        [
            normed_mid,
            jnp.where(is_kept, place, -1.0).astype(BF16),
            gates.astype(BF16),
            jnp.zeros((SEQS, BLOCK, 128 - 2 * EXPERTS), BF16),
        ],
        axis=2,
    )
    back, mix_part, own_grads, down_first, down_early = run_experts(
        2, replicas, payload.reshape(SEQS * BLOCK, PAY), cotangent.reshape(SEQS * BLOCK, D), cot_pair,
        (own_gate, own_up, own_down), tokens_all
    )

    back = back.reshape(SEQS, BLOCK, D + 128)
    grad_gates = jnp.where(is_kept, back[..., D : D + EXPERTS], 0.0)
    grad_chosen = gates * (grad_gates - jnp.sum(gates * grad_gates, axis=-1, keepdims=True))
    grad_logits = grad_chosen.astype(BF16)
    grad_mid = back[..., :D] + jnp.einsum(
        "sge,ed->sgd", grad_logits, full_router, preferred_element_type=F32
    )
    grad_router = jnp.einsum("sgd,sge->de", normed_mid, grad_logits, preferred_element_type=F32)

    grad_f = cotangent.astype(F32)
    weighted_two = gain_second * grad_mid
    grad_gain_second = jnp.sum(grad_mid * residual * scale_two, axis=(0, 1))
    cube_two = scale_two * scale_two * scale_two
    grad_resid = (
        grad_f
        + scale_two * weighted_two
        - residual * cube_two * jnp.mean(weighted_two * residual, axis=-1, keepdims=True)
    )
    grad_resid_low = grad_resid.astype(BF16)
    grad_attn = jnp.einsum("sgd,dq->sgq", grad_resid_low, full_output, preferred_element_type=F32)
    grad_attn = grad_attn.astype(BF16)
    grad_output_w = jnp.einsum("sgd,sgq->dq", grad_resid_low, attn_out, preferred_element_type=F32)
    rows = D // (n_ctx * n_fsdp)
    output_part = grad_output_w.astype(BF16).reshape(replicas, 2, 2, 2, rows, D)

    (
        input_grad, layer_out, gain_grad, output_sum, _, gate_keep, gate_came, gate_other, up_came, down_keep,
        down_came, _, _, head_grads,
    ) = attention_backward(
        6, parts, n_ctx, down_early, heads_out(grad_attn, REP), q_all, kv_all, segq, codes, head_full, head_logs,
        all_cosine, all_sine, tokens.reshape(SEQS * BLOCK, D), gain_first[None],
        grad_resid.reshape(SEQS * BLOCK, D), residual.reshape(SEQS * BLOCK, D), own_grads, down_first, mix_part, output_part,
        tokens_all.reshape(n_ctx, SEQS * BLOCK, D), full_query, full_key, full_value,
    )
    input_grad = input_grad.reshape(SEQS, BLOCK, D)
    layer_out = layer_out.reshape(SEQS, BLOCK, D)
    amount = rows * (EXPERTS + 2)
    tiles = -(-amount // 1024) * 8
    small_grads = jnp.concatenate([grad_router, gain_grad.T, grad_gain_second[:, None]], axis=1)
    small_grads = jnp.pad(
        small_grads.reshape(n_ctx * n_fsdp, amount), ((0, 0), (0, tiles * 128 - amount))
    ).reshape(n_ctx * n_fsdp, tiles, 128)
    swapped, output_grad, small_sum = final_sums(
        9, n_ctx, small_grads, output_sum, own_grads, gate_keep, gate_came, gate_other, up_came,
        down_keep, down_came,
    )
    small_sum = small_sum.reshape(tiles * 128)[:amount].reshape(rows, EXPERTS + 2)
    head_grads = head_grads.reshape(KEY_VALUE_HEADS, parts, rows, (REP + 2) * HEAD_SIZE)
    own_gain = lax.dynamic_slice_in_dim(gain_first, (c_index * n_fsdp + f_index) * rows, rows, 0)
    head_grads = jnp.sum(head_grads.astype(F32), axis=1).transpose(1, 0, 2) * own_gain[:, None, None]
    query_grad = head_grads[..., : REP * HEAD_SIZE].reshape(rows, D)
    key_grad = head_grads[..., REP * HEAD_SIZE : (REP + 1) * HEAD_SIZE].reshape(rows, -1)
    value_grad = head_grads[..., (REP + 1) * HEAD_SIZE :].reshape(rows, -1)

    def by_row(matrix):
        return swapped[:, matrix].transpose(2, 0, 1, 3).reshape(rows, EXPERTS, FF).astype(F32)

    return (
        layer_out,
        input_grad,
        small_sum[:, EXPERTS],
        query_grad,
        key_grad,
        value_grad,
        output_grad,
        small_sum[:, EXPERTS + 1],
        small_sum[:, :EXPERTS],
        by_row(0),
        by_row(1),
        by_row(2),
    )


def solution(mesh):
    placed = (
        P("fsdp", "ctx", None),
        P("fsdp", None),
        P("fsdp", None),
        P("fsdp", "ctx", None),
        P("fsdp", "ctx"),
        P("fsdp", "ctx", None),
        P("fsdp"),
        P("fsdp", None),
        P("fsdp", None),
        P("fsdp", None),
        P("fsdp", None),
        P("fsdp"),
        P("fsdp", None),
        P("fsdp", None, None),
        P("fsdp", None, None),
        P("fsdp", None, None),
    )
    return jax.shard_map(
        functools.partial(on_device, mesh.shape["ctx"], mesh.shape["fsdp"]),
        mesh=mesh,
        in_specs=placed,
        out_specs=(
            P("fsdp", "ctx", None),
            P("fsdp", "ctx", None),
            P(("ctx", "fsdp")),
            P(("ctx", "fsdp"), None),
            P(("ctx", "fsdp"), None),
            P(("ctx", "fsdp"), None),
            P(("ctx", "fsdp"), None),
            P(("ctx", "fsdp")),
            P(("ctx", "fsdp"), None),
            P(("ctx", "fsdp"), None, None),
            P(("ctx", "fsdp"), None, None),
            P(("ctx", "fsdp"), None, None),
        ),
        check_vma=False,
    )
```

```python
import functools

import jax
import jax.numpy as jnp
from jax import lax
from jax.experimental import pallas as pl
from jax.experimental.pallas import tpu as pltpu
from jax.sharding import PartitionSpec as P

D = 1536
QUERY_HEADS = 24
KEY_VALUE_HEADS = 8
REP = QUERY_HEADS // KEY_VALUE_HEADS
HEAD_SIZE = 64
FF = 512
EXPERTS = 16
CAP = 80
RANKS = 8
OWN = EXPERTS // RANKS
SEQS = 2
BLOCK = 128
KEYS = 256

EPS = 1e-05
ROPE_BASE = 10000.0
MASKED = -1e30
SCALE = HEAD_SIZE ** (-0.5)
MESH = pl.DeviceIdType.MESH
BF16 = jnp.bfloat16
F32 = jnp.float32


def flip(index, constant):
    result, bit = index, 1
    while bit <= constant:
        if constant & bit:
            result = result + bit - 2 * bit * lax.rem(lax.div(index, bit), 2)
        bit *= 2
    return result


def lasting(microseconds):
    return pl.CostEstimate(flops=0, bytes_accessed=int(microseconds * 3.3e6), transcendentals=0)


PAY = D + 128
GROUPS = 4
ROWS = GROUPS * CAP


def other_chip(c, f, k):
    pair, x = lax.div(k, 2), lax.rem(k, 2)
    return (
        c + pair * (1 - 2 * lax.rem(c, 2)),
        f + 2 * x * (1 - 2 * lax.rem(lax.div(f, 2), 2)),
    )


def plane_order(replicas):
    order = [0]
    while len(order) < replicas:
        order = [2 * i for i in order] + [2 * i + 1 for i in order]
    return order


def experts_kernel(
    replicas, pay, cot, gate_own, up_own, down_own, after,
    back, mix, grads, down_came, pay_in, cot_in,
    weights, total, pay_now, cot_now, xs, gs, eo, gi, hid, dgate, dup, disp, comb,
    own, out, sib, ret, mix_now,
    send_first, recv_first, send_fwd, recv_fwd, send_sib, recv_sib, send_chip, recv_chip,
    load_w, load, store, piece_sem, send_down, recv_down,
):
    c, f = lax.axis_index("ctx"), lax.axis_index("fsdp")
    rank = lax.rem(c, 2) * 4 + f
    sibling = (c, flip(f, 1))
    barrier = pltpu.get_barrier_semaphore()
    pl.semaphore_signal(barrier, inc=1, device_id=sibling, device_id_type=MESH)
    for k in range(1, 4):
        pl.semaphore_signal(barrier, inc=1, device_id=other_chip(c, f, k), device_id_type=MESH)
    apart = len(grads.shape) == 5
    if apart:
        pl.semaphore_signal(barrier, inc=1, device_id=(flip(c, 2), f), device_id_type=MESH)
    bring = []
    for m, own_weight in enumerate((gate_own, up_own, down_own)):
        bring.append(pltpu.make_async_copy(own_weight, weights.at[m], load_w.at[m]))
        bring[-1].start()
    pl.semaphore_wait(barrier, 5 if apart else 4)
    sources, landed = (pay, cot), (pay_in, cot_in)

    def push(k, a):
        slot = 1 if k == 0 else 2 * k
        return pltpu.make_async_remote_copy(
            sources[a], landed[a].at[slot - 1], send_first.at[k, a], recv_first.at[k, a],
            device_id=sibling if k == 0 else other_chip(c, f, k), device_id_type=MESH,
        )

    def forward(k, a):
        return pltpu.make_async_remote_copy(
            landed[a].at[2 * k - 1], landed[a].at[2 * k], send_fwd.at[k - 1, a], recv_fwd.at[k - 1, a],
            device_id=sibling, device_id_type=MESH,
        )

    def to_sibling(k):
        return pltpu.make_async_remote_copy(
            out.at[lax.rem(k, 2)], sib.at[k], send_sib.at[k], recv_sib.at[k],
            device_id=sibling, device_id_type=MESH,
        )

    def to_chip(k):
        return pltpu.make_async_remote_copy(
            sib.at[k], ret.at[k - 1], send_chip.at[k - 1], recv_chip.at[k - 1],
            device_id=other_chip(c, f, k), device_id_type=MESH,
        )

    def store_mix(k, s):
        return pltpu.make_async_copy(mix_now.at[s], mix.at[2 * k + s], store.at[s])

    for k, a in ((0, 0), (0, 1), (1, 0), (2, 0), (1, 1), (2, 1), (3, 0), (3, 1)):
        push(k, a).start()

    stages = (eo, gi)

    def leaving(m, e, stage):
        if not apart:
            return [pltpu.make_async_copy(stages[stage].at[:FF], grads.at[m, e], piece_sem.at[stage, 0])]
        width = D // replicas
        return [
            pltpu.make_async_copy(
                stages[stage].at[:FF, plane * width : (plane + 1) * width],
                grads.at[m, at, e],
                piece_sem.at[stage, at],
            )
            for at, plane in enumerate(plane_order(replicas))
        ]

    if apart:
        half = replicas // 2
        down_first = pltpu.make_async_remote_copy(
            grads.at[2, pl.ds((1 - lax.rem(lax.div(c, 2), 2)) * half, half)], down_came,
            send_down, recv_down, device_id=(flip(c, 2), f), device_id_type=MESH,
        )

    def clear(i, carry):
        total[lax.div(i, OWN), lax.rem(i, OWN)] = jnp.zeros((FF, D), F32)
        return carry

    lax.fori_loop(0, 3 * OWN, clear, 0)
    lane = lax.broadcasted_iota(jnp.int32, (BLOCK, 128), 1)
    wide = lax.broadcasted_iota(jnp.int32, (BLOCK, 2 * BLOCK), 1).astype(F32)
    both = lax.broadcasted_iota(jnp.int32, (BLOCK, OWN * CAP), 1)

    def chunk(k, carry):
        now = (pay_now, cot_now)

        def fetch(a, s, source):
            copy = pltpu.make_async_copy(source, now[a].at[s], load.at[a, s])
            copy.start()
            return copy

        def arrived(chip):
            for a in range(2):
                push(chip, a).wait_recv()
                forward(chip, a).start()

        def fetch_chip(chip):
            for a in range(2):
                fetch(a, 0, landed[a].at[2 * chip - 1])
            for a in range(2):
                forward(chip, a).wait_recv()
                fetch(a, 1, landed[a].at[2 * chip])

        @pl.when(k == 0)
        def _():
            copies = [fetch(a, 0, sources[a]) for a in range(2)]
            for a in range(2):
                push(0, a).wait_recv()
            copies += [fetch(a, 1, landed[a].at[0]) for a in range(2)]
            for copy in copies:
                copy.wait()
            for copy in bring:
                copy.wait()

        @pl.when(k == 1)
        def _():
            arrived(1)
            arrived(2)
            fetch_chip(1)

        @pl.when(k > 0)
        def _():
            for a in range(2):
                for s in range(2):
                    pltpu.make_async_copy(landed[a].at[2 * k - 1 + s], now[a].at[s], load.at[a, s]).wait()

        for g in range(GROUPS):
            s, at = g // 2, (g % 2) * BLOCK
            tail = pay_now[s, at : at + BLOCK, D:].astype(F32)

            def column(index):
                return jnp.sum(jnp.where(lane == index, tail, 0.0), axis=1, keepdims=True)

            table = jnp.zeros((BLOCK, 2 * BLOCK), F32)
            gated = jnp.zeros((BLOCK, 2 * BLOCK), F32)
            for e in range(OWN):
                place = column(rank * OWN + e)
                place = jnp.where(place < 0.0, -1000.0, place + e * CAP)
                here = wide == place
                table = jnp.where(here, 1.0, table)
                gated = jnp.where(here, column(EXPERTS + rank * OWN + e), gated)
            table, gated = table.astype(BF16), gated.astype(BF16)
            disp[g] = table
            comb[g] = gated
            for weight, source, keep in (
                (table, pay_now[s, at : at + BLOCK, :D], xs),
                (gated, cot_now[s, at : at + BLOCK], gs),
            ):
                moved = lax.dot_general(
                    weight, source, (((0,), (0,)), ((), ())), preferred_element_type=F32
                ).astype(BF16)
                for e in range(OWN):
                    keep[e, g * CAP : (g + 1) * CAP] = moved[e * CAP : (e + 1) * CAP]

        def expert(e, carry):
            at = pl.multiple_of(e * CAP, 16)
            gate_pre = jnp.dot(xs[e], weights[0, e], preferred_element_type=F32)
            up_pre = jnp.dot(xs[e], weights[1, e], preferred_element_type=F32)
            sigmoid = 1.0 / (1.0 + jnp.exp(-gate_pre))
            activated = gate_pre * sigmoid
            hidden = (activated * up_pre).astype(BF16)
            hid[e] = hidden
            made = lax.dot_general(
                hidden, weights[2, e], (((1,), (1,)), ((), ())), preferred_element_type=F32
            ).astype(BF16)
            for g in range(GROUPS):
                eo[pl.ds(pl.multiple_of(g * OWN * CAP + at, 16), CAP)] = made[g * CAP : (g + 1) * CAP]
            grad_hidden = jnp.dot(gs[e], weights[2, e], preferred_element_type=F32)
            slope = sigmoid * (1.0 + gate_pre * (1.0 - sigmoid))
            grad_gate = (grad_hidden * up_pre * slope).astype(BF16)
            grad_up = (grad_hidden * activated).astype(BF16)
            dgate[e] = grad_gate
            dup[e] = grad_up
            made = lax.dot_general(
                grad_gate, weights[0, e], (((1,), (1,)), ((), ())), preferred_element_type=F32
            )
            made = made + lax.dot_general(
                grad_up, weights[1, e], (((1,), (1,)), ((), ())), preferred_element_type=F32
            )
            made = made.astype(BF16)
            for g in range(GROUPS):
                gi[pl.ds(pl.multiple_of(g * OWN * CAP + at, 16), CAP)] = made[g * CAP : (g + 1) * CAP]
            return carry

        lax.fori_loop(0, OWN, expert, 0)

        @pl.when(k > 0)
        def _():
            for s in range(2):
                store_mix(k - 1, s).wait()

        @pl.when(k > 1)
        def _():
            to_sibling(k - 2).wait_send()

        parity = lax.rem(k, 2)
        for g in range(GROUPS):
            s, at = g // 2, (g % 2) * BLOCK
            slots = pl.ds(g * OWN * CAP, OWN * CAP)
            made = eo[slots]
            mix_now[s, at : at + BLOCK] = jnp.dot(
                comb[g][:, : OWN * CAP], made, preferred_element_type=F32
            ).astype(BF16)
            table = disp[g][:, : OWN * CAP]
            grad_mid = jnp.dot(table, gi[slots], preferred_element_type=F32).astype(BF16)
            met = lax.dot_general(
                cot_now[s, at : at + BLOCK], made, (((1,), (1,)), ((), ())), preferred_element_type=F32
            ) * table.astype(F32)
            values = jnp.zeros((BLOCK, 128), F32)
            for e in range(OWN):
                inside = (both >= e * CAP) & (both < (e + 1) * CAP)
                value = jnp.sum(jnp.where(inside, met, 0.0), axis=1, keepdims=True)
                values = jnp.where(lane == rank * OWN + e, value, values)
            target = own if s == 0 else out
            target[parity, at : at + BLOCK, :D] = grad_mid
            target[parity, at : at + BLOCK, D:] = values.astype(BF16)
        to_sibling(k).start()
        for s in range(2):
            store_mix(k, s).start()

        @pl.when(k == 1)
        def _():
            fetch_chip(2)

        @pl.when(k == 2)
        def _():
            arrived(3)
            fetch_chip(3)

        def down_grads(e, carry):
            total[2, e] += lax.dot_general(
                hid[e], gs[e], (((0,), (0,)), ((), ())), preferred_element_type=F32
            )
            return carry

        def other_grads(e, carry):
            for m, left in enumerate((dgate, dup)):
                total[m, e] += lax.dot_general(
                    left[e], xs[e], (((0,), (0,)), ((), ())), preferred_element_type=F32
                )
            return carry

        lax.fori_loop(0, OWN, down_grads, 0)

        @pl.when(k == 3)
        def _():
            for e in range(OWN):
                stages[e][:FF] = total[2, e].astype(BF16)
                for copy in leaving(2, e, e):
                    copy.start()

        lax.fori_loop(0, OWN, other_grads, 0)

        @pl.when(k == 3)
        def _():
            for e in range(OWN):
                for copy in leaving(2, e, e):
                    copy.wait()
            if apart:
                down_first.start()

        to_sibling(k).wait_recv()
        sib[k] = (sib[k].astype(F32) + own[parity].astype(F32)).astype(BF16)

        @pl.when(k > 0)
        def _():
            to_chip(k).start()

        return carry

    lax.fori_loop(0, 4, chunk, 0)
    for s in range(2):
        store_mix(3, s).wait()
    for i in range(2 * OWN):
        m, e = i // OWN, i % OWN
        if i >= 2:
            for copy in leaving((i - 2) // OWN, (i - 2) % OWN, i % 2):
                copy.wait()
        stages[i % 2][:FF] = total[m, e].astype(BF16)
        for copy in leaving(m, e, i % 2):
            copy.start()
    for i in (2 * OWN - 2, 2 * OWN - 1):
        for copy in leaving(i // OWN, i % OWN, i % 2):
            copy.wait()
    for k in (2, 3):
        to_sibling(k).wait_send()
    for k in range(4):
        for a in range(2):
            push(k, a).wait_send()
            if k:
                forward(k, a).wait_send()
    for k in range(1, 4):
        to_chip(k).wait_recv()
    back[...] = (sib[0].astype(F32) + ret[0].astype(F32)) + (ret[1].astype(F32) + ret[2].astype(F32))
    for k in range(1, 4):
        to_chip(k).wait_send()
    if apart:
        down_first.wait()


def run_experts(cid, replicas, pay, cot, owns, after):
    width = D // replicas
    apart = width % 128 == 0
    tokens = SEQS * BLOCK
    anywhere = pl.BlockSpec(memory_space=pl.ANY)
    inside = pl.BlockSpec(memory_space=pltpu.VMEM)
    dma = pltpu.SemaphoreType.DMA
    back, mix, grads, down_came, _, _ = pl.pallas_call(
        functools.partial(experts_kernel, replicas),
        name="experts",
        out_shape=[
            jax.ShapeDtypeStruct((tokens, PAY), F32),
            jax.ShapeDtypeStruct((RANKS, tokens, D), BF16),
            jax.ShapeDtypeStruct((3, replicas, OWN, FF, width) if apart else (3, OWN, FF, D), BF16),
            jax.ShapeDtypeStruct((replicas // 2, OWN, FF, width) if apart else (8, 128), BF16),
            jax.ShapeDtypeStruct((RANKS - 1, tokens, PAY), BF16),
            jax.ShapeDtypeStruct((RANKS - 1, tokens, D), BF16),
        ],
        in_specs=[anywhere] * 6,
        out_specs=[inside] + [anywhere] * 5,
        scratch_shapes=[
            pltpu.VMEM((3, OWN, D, FF), BF16),
            pltpu.VMEM((3, OWN, FF, D), F32),
            pltpu.VMEM((2, tokens, PAY), BF16),
            pltpu.VMEM((2, tokens, D), BF16),
            pltpu.VMEM((OWN, ROWS, D), BF16),
            pltpu.VMEM((OWN, ROWS, D), BF16),
            pltpu.VMEM((OWN * ROWS, D), BF16),
            pltpu.VMEM((OWN * ROWS, D), BF16),
            pltpu.VMEM((OWN, ROWS, FF), BF16),
            pltpu.VMEM((OWN, ROWS, FF), BF16),
            pltpu.VMEM((OWN, ROWS, FF), BF16),
            pltpu.VMEM((GROUPS, BLOCK, 2 * BLOCK), BF16),
            pltpu.VMEM((GROUPS, BLOCK, 2 * BLOCK), BF16),
            pltpu.VMEM((2, tokens, PAY), BF16),
            pltpu.VMEM((2, tokens, PAY), BF16),
            pltpu.VMEM((4, tokens, PAY), BF16),
            pltpu.VMEM((3, tokens, PAY), BF16),
            pltpu.VMEM((2, tokens, D), BF16),
            dma((4, 2)), dma((4, 2)), dma((3, 2)), dma((3, 2)),
            dma((4,)), dma((4,)), dma((3,)), dma((3,)),
            dma((4,)), dma((2, 2)), dma((2,)), dma((2, replicas)), dma, dma,
        ],
        compiler_params=pltpu.CompilerParams(
            collective_id=cid, has_side_effects=True, vmem_limit_bytes=63 << 20
        ),
        cost_estimate=lasting(110),
    )(pay, cot, *owns, after)
    if not apart:
        grads = grads.reshape(3, OWN, FF, replicas, width).transpose(0, 3, 1, 2, 4)
        grads = grads[:, jnp.array(plane_order(replicas))]
    return back, mix, grads, down_came, apart


def half_masks(dtype):
    lane = lax.broadcasted_iota(jnp.int32, (1, 2 * HEAD_SIZE), 1)
    low = (lane < HEAD_SIZE).astype(F32)
    return low.astype(dtype), (1.0 - low).astype(dtype)


def allowed_at(block, step, segq, keycode):
    token = block * BLOCK + lax.broadcasted_iota(jnp.int32, (BLOCK, KEYS), 0)
    key = step * KEYS + lax.broadcasted_iota(jnp.int32, (BLOCK, KEYS), 1)
    return ((segq == keycode) & (key < token)) | (key == token)


SMALL = 32


def turn(field, cosine, sine):
    half = HEAD_SIZE // 2
    lane = lax.broadcasted_iota(jnp.int32, field.shape, field.ndim - 1)
    up = pltpu.roll(field, 2 * HEAD_SIZE - half, field.ndim - 1)
    down = pltpu.roll(field, half, field.ndim - 1)
    return field * cosine + jnp.where(lax.rem(lane, HEAD_SIZE) < half, -up, down) * sine


def attention_forward_kernel(
    parts, n_ctx, tok, small, w_q, w_k, w_v, w_o, near_q, near_k, near_v, pack0, pack1, pack2, cos_ref, sin_ref, seg_ref, code_ref,
    normed, small_all, q_full, k_full, v_full, q_ref, kv_ref, full_ref, log_ref, o_back, o_full,
    gate_own, up_own, down_own,
    acc, q_pack, kv_pack, o_buf, own_buf,
    send_w, recv_w, send_s, recv_s, send_e, recv_e, send_q, recv_q, send_kv, recv_kv, send_o, recv_o, here,
):
    c, f = lax.axis_index("ctx"), lax.axis_index("fsdp")
    head, part, pair = lax.div(c, parts), lax.rem(c, parts), lax.rem(c, 2)
    rows = D // 4
    half = rows // 2
    wide = 2 * HEAD_SIZE
    barrier = pltpu.get_barrier_semaphore()
    peers = [(i, 0) for i in range(1, n_ctx)] + [(0, k) for k in range(1, 4)]
    for dc, df in peers:
        pl.semaphore_signal(
            barrier, inc=1, device_id=(flip(c, dc), flip(f, df)), device_id_type=MESH
        )
    shards = (w_q, w_k, w_v, w_o)
    fulls = (q_full, k_full, v_full, o_full)
    packs, owns = (pack0, pack1, pack2), (gate_own, up_own, down_own)
    my_rows = pl.ds(pl.multiple_of(f * rows, rows), rows)
    local = [pltpu.make_async_copy(shards[a], fulls[a].at[f], here.at[a]) for a in range(4)]
    local += [pltpu.make_async_copy(small, small_all.at[f], here.at[4])]
    local += [pltpu.make_async_copy(packs[m].at[f], own_buf.at[m], here.at[5 + m]) for m in range(3)]
    for copy in local:
        copy.start()
    pl.semaphore_wait(barrier, len(peers))
    near = pl.ds(pl.multiple_of(pair * half, half), half)
    far = pl.ds(pl.multiple_of((1 - pair) * half, half), half)
    sibling, over_x, over_pair = (c, flip(f, 1)), (c, flip(f, 2)), (flip(c, 1), f)
    nears = (near_q, near_k, near_v)
    crossed = [
        pltpu.make_async_copy(nears[a], fulls[a].at[flip(f, 2), near], here.at[11 + a]) for a in range(3)
    ]
    for copy in crossed:
        copy.start()

    def weight(a, kind):
        beyond = flip(f, 2)
        brought = nears[a] if a < 3 else fulls[a].at[beyond, near]
        source, target, device = (
            (shards[a], fulls[a].at[f], sibling),
            (shards[a].at[near], fulls[a].at[f, near], over_x),
            (brought, fulls[a].at[beyond, near], sibling),
            (brought, fulls[a].at[beyond, near], over_pair),
            (fulls[a].at[beyond, far], fulls[a].at[beyond, far], sibling),
        )[kind]
        return pltpu.make_async_remote_copy(
            source, target, send_w.at[a, kind], recv_w.at[a, kind], device_id=device, device_id_type=MESH
        )

    smalls = [
        pltpu.make_async_remote_copy(
            small, small_all.at[f], send_s.at[i - 1], recv_s.at[i - 1],
            device_id=(c, flip(f, i)), device_id_type=MESH,
        )
        for i in range(1, 4)
    ]
    for copy in smalls:
        copy.start()
    for a in range(4):
        for kind in (3, 0, 2) if a < 3 else (1, 0):
            weight(a, kind).start()
    experts = [
        pltpu.make_async_remote_copy(
            packs[m].at[flip(f, i)], owns[m].at[:, my_rows], send_e.at[i - 1, m], recv_e.at[i - 1, m],
            device_id=(c, flip(f, i)), device_id_type=MESH,
        )
        for m in range(3)
        for i in range(1, 4)
    ]
    for copy in experts:
        copy.start()

    x = tok[...].astype(F32)
    scale = lax.rsqrt(jnp.mean(x * x, axis=1, keepdims=True) + EPS)
    for copy in smalls:
        copy.wait_recv()
    local[4].wait()
    for b in range(4):
        columns = slice(b * rows, (b + 1) * rows)
        normed[:, columns] = (x[:, columns] * scale * small_all[b, :1].astype(F32)).astype(BF16)

    def project(b, first):
        block = normed[:, pl.ds(pl.multiple_of(b * rows, rows), rows)]
        at = 0
        for a in range(3):
            width = fulls[a].shape[2]
            made = jnp.dot(block, fulls[a][b], preferred_element_type=F32)
            acc[:, at : at + width] = made if first else acc[:, at : at + width] + made
            at += width

    for a in range(3):
        local[a].wait()
    stores = []
    for m in range(3):
        local[5 + m].wait()
        stores.append(pltpu.make_async_copy(own_buf.at[m], owns[m].at[:, my_rows], here.at[5 + m]))
        stores[m].start()
    project(f, True)
    for a in range(3):
        weight(a, 0).wait_recv()
    project(flip(f, 1), False)
    for a in range(3):
        weight(a, 3).wait_recv()
        weight(a, 4).start()
        crossed[a].wait()
    project(flip(f, 2), False)
    for a in range(3):
        weight(a, 2).wait_recv()
        weight(a, 4).wait_recv()
    project(flip(f, 3), False)

    lane = lax.broadcasted_iota(jnp.int32, (BLOCK, wide), 1)
    low = lane < HEAD_SIZE
    cosine, sine = cos_ref[...], sin_ref[...]
    for m in range((QUERY_HEADS + 2 * KEY_VALUE_HEADS) // 2):
        pieces = []
        for s in range(SEQS):
            piece = acc[s * BLOCK : (s + 1) * BLOCK, m * wide : (m + 1) * wide]
            pieces.append(turn(piece, cosine, sine) if m < (QUERY_HEADS + KEY_VALUE_HEADS) // 2 else piece)
        even = jnp.where(low, pieces[0], pltpu.roll(pieces[1], HEAD_SIZE, 1)).astype(BF16)
        odd = jnp.where(low, pltpu.roll(pieces[0], HEAD_SIZE, 1), pieces[1]).astype(BF16)
        for h, value in ((2 * m, even), (2 * m + 1, odd)):
            if h < QUERY_HEADS:
                q_pack[h // REP, h % REP] = value
            else:
                h -= QUERY_HEADS
                kv_pack[h % KEY_VALUE_HEADS, h // KEY_VALUE_HEADS] = value

    q_stays = pltpu.make_async_copy(q_pack.at[head], q_ref.at[head], here.at[8])
    kv_stays = pltpu.make_async_copy(kv_pack.at[head], kv_ref.at[c], here.at[9])
    q_stays.start()
    kv_stays.start()
    to_heads = []
    for i in range(1, n_ctx):
        peer = flip(c, i)
        moves = [(kv_pack.at[lax.div(peer, parts)], kv_ref.at[c], send_kv.at[i - 1], recv_kv.at[i - 1])]
        if i % parts == 0:
            number = i // parts - 1
            moves.append(
                (q_pack.at[lax.div(peer, parts)], q_ref.at[head], send_q.at[number], recv_q.at[number])
            )
        for source, target, sent, came in moves:
            copy = pltpu.make_async_remote_copy(
                source, target, sent, came, device_id=(peer, f), device_id_type=MESH
            )
            copy.start()
            to_heads.append(copy)
    weight(3, 1).wait_recv()
    weight(3, 2).start()
    weight(3, 3).start()
    q_stays.wait()
    kv_stays.wait()
    for copy in to_heads:
        copy.wait_recv()

    count = REP * BLOCK
    halves = half_masks(BF16)
    across = lax.broadcasted_iota(jnp.int32, (count, wide), 1)

    def out_back(j):
        return pltpu.make_async_remote_copy(
            o_buf.at[j], o_back.at[head], send_o.at[j], recv_o.at[head],
            device_id=(j * parts + part, f), device_id_type=MESH,
        )

    def out_stays(j):
        return pltpu.make_async_copy(o_buf.at[j], o_back.at[head], here.at[10])

    def one_block(j, nothing):
        block = j * parts + part
        q = q_ref[j].reshape(count, wide)
        queries = [q * half for half in halves]

        def step(number, carry):
            k = kv_ref[pl.ds(2 * number, 2), 0].reshape(KEYS, wide)
            v = kv_ref[pl.ds(2 * number, 2), 1].reshape(KEYS, wide)
            codes = code_ref[number]
            after = []
            for s in range(SEQS):
                largest, total, out = carry[s]
                mask = allowed_at(block, number, seg_ref[j, s], codes[s : s + 1])
                scores = lax.dot_general(
                    queries[s], k, (((1,), (1,)), ((), ())), preferred_element_type=F32
                )
                scores = jnp.where(mask[None], scores.reshape(REP, BLOCK, KEYS) * SCALE, MASKED)
                scores = scores.reshape(count, KEYS)
                new = jnp.maximum(largest, jnp.max(scores, axis=1, keepdims=True))
                probs = jnp.exp(scores - new)
                shrink = jnp.exp(largest - new)
                total = total * shrink + jnp.sum(probs, axis=1, keepdims=True)
                out = out * shrink + jnp.dot(probs.astype(BF16), v, preferred_element_type=F32)
                after.append((new, total, out))
            return tuple(after)

        start = (
            jnp.full((count, 1), MASKED, F32),
            jnp.zeros((count, 1), F32),
            jnp.zeros((count, wide), F32),
        )
        done = lax.fori_loop(0, lax.div(block, 2) + 1, step, (start,) * SEQS)
        outs, logs = [], []
        for largest, total, out in done:
            outs.append(out / total)
            logs.append(jnp.broadcast_to(largest + jnp.log(total), (count, wide)))
        out = jnp.where(across < HEAD_SIZE, outs[0], outs[1])
        full_ref[j] = out.reshape(REP, BLOCK, wide)
        log_ref[j] = jnp.where(across < HEAD_SIZE, logs[0], logs[1]).reshape(REP, BLOCK, wide)
        o_buf[j] = out.astype(BF16).reshape(REP, BLOCK, wide)

        @pl.when(j != head)
        def _():
            out_back(j).start()

        @pl.when(j == head)
        def _():
            out_stays(j).start()

        return nothing

    lax.fori_loop(0, KEY_VALUE_HEADS, one_block, 0)
    weight(3, 3).wait_recv()
    weight(3, 4).start()

    def came_out(h, nothing):
        @pl.when(h != head)
        def _():
            pltpu.make_async_remote_copy(
                o_buf.at[h], o_back.at[h], send_o.at[h], recv_o.at[h],
                device_id=(h * parts + part, f), device_id_type=MESH,
            ).wait()

        @pl.when(h == head)
        def _():
            out_stays(h).wait()

        return nothing

    lax.fori_loop(0, KEY_VALUE_HEADS, came_out, 0)
    for kind in (0, 2, 4):
        weight(3, kind).wait_recv()
    local[3].wait()
    for copy in stores:
        copy.wait()
    for copy in experts:
        copy.wait()
    for copy in smalls + to_heads:
        copy.wait_send()
    for a in range(4):
        for kind in (0, 2, 3, 4) if a < 3 else range(5):
            weight(a, kind).wait_send()


def attention_forward(
    cid, parts, n_ctx, tok, small, w_q, w_k, w_v, w_o, nears, packs, cosine, sine, segq, codes
):
    wide = 2 * HEAD_SIZE
    anywhere = pl.BlockSpec(memory_space=pl.ANY)
    inside = pl.BlockSpec(memory_space=pltpu.VMEM)
    dma = pltpu.SemaphoreType.DMA
    heads = (KEY_VALUE_HEADS, REP, BLOCK, wide)
    keys = (n_ctx, 2, BLOCK, wide)
    others = max(n_ctx // parts - 1, 1)
    columns = w_q.shape[1] + w_k.shape[1] + w_v.shape[1]
    own = jax.ShapeDtypeStruct((OWN, D, FF), BF16)

    def full(x):
        return jax.ShapeDtypeStruct((4,) + x.shape, BF16)

    return pl.pallas_call(
        functools.partial(attention_forward_kernel, parts, n_ctx),
        name="attention_forward",
        out_shape=[
            jax.ShapeDtypeStruct(tok.shape, BF16),
            full(small), full(w_q), full(w_k), full(w_v),
            jax.ShapeDtypeStruct(heads, BF16),
            jax.ShapeDtypeStruct(keys, BF16),
            jax.ShapeDtypeStruct(heads, F32),
            jax.ShapeDtypeStruct(heads, F32),
            jax.ShapeDtypeStruct(heads, BF16),
            full(w_o), own, own, own,
        ],
        in_specs=[inside] + [anywhere] * 11 + [inside] * 4,
        out_specs=[inside] * 9 + [anywhere, inside] + [anywhere] * 3,
        scratch_shapes=[
            pltpu.VMEM((SEQS * BLOCK, columns), F32),
            pltpu.VMEM(heads, BF16),
            pltpu.VMEM((KEY_VALUE_HEADS, 2, BLOCK, wide), BF16),
            pltpu.VMEM(heads, BF16),
            pltpu.VMEM((3,) + packs[0].shape[1:], BF16),
            dma((4, 5)), dma((4, 5)), dma((3,)), dma((3,)), dma((3, 3)), dma((3, 3)),
            dma((others,)), dma((others,)), dma((n_ctx - 1,)), dma((n_ctx - 1,)),
            dma((KEY_VALUE_HEADS,)), dma((KEY_VALUE_HEADS,)), dma((14,)),
        ],
        compiler_params=pltpu.CompilerParams(
            collective_id=cid, has_side_effects=True, vmem_limit_bytes=56 << 20
        ),
        cost_estimate=lasting(130),
    )(tok, small, w_q, w_k, w_v, w_o, *nears, *packs, cosine, sine, segq, codes)


def turn_back(field, cosine, sine):
    half = HEAD_SIZE // 2
    lane = lax.broadcasted_iota(jnp.int32, field.shape, field.ndim - 1)
    up = pltpu.roll(field, 2 * HEAD_SIZE - half, field.ndim - 1)
    down = pltpu.roll(field, half, field.ndim - 1)
    turned = jnp.where(lax.rem(lane, HEAD_SIZE) < half, -up, down)
    return field * cosine - turned * sine


def attention_backward_kernel(
    parts, n_ctx, early, g_own, q_ref, kv_ref, seg_ref, code_ref, full_ref, log_ref, cos_ref, sin_ref,
    tok, gain, resid_grad, residual, grads, down_in, mix, output_part, tokens_all, q_full, k_full, v_full,
    input_grad, layer_out, gain_grad, output_sum, gate_first, gate_keep, gate_came, gate_other, up_came, down_keep, down_came,
    mix_core, mix_in, head_in, g_ref, total, kept, came, dq_ref, dkv_ref, dq_back, dkv_back, w_q, w_k, w_v, grad_qkv, grad_in,
    token_buf, field, head_acc, head_out, head_core, head_x, output_keep, output_came, output_x, output_pair,
    send_g, recv_g, send_q, recv_q, send_kv, recv_kv, send_mix, recv_mix, send_half, recv_half, here,
    send_out, recv_out, send_head, recv_head, load_t,
):
    c, f = lax.axis_index("ctx"), lax.axis_index("fsdp")
    head, part = lax.div(c, parts), lax.rem(c, parts)
    rows = REP * BLOCK
    wide = 2 * HEAD_SIZE
    barrier = pltpu.get_barrier_semaphore()
    peers = [(i, k) for i in range(n_ctx) for k in range(4) if i or k]
    for dc, df in peers:
        pl.semaphore_signal(
            barrier, inc=1, device_id=(flip(c, dc), flip(f, df)), device_id_type=MESH
        )
    pair, x_bit, core_bit = lax.rem(c, 2), lax.div(f, 2), lax.rem(f, 2)
    loads = [
        pltpu.make_async_copy(source, target, here.at[5 + i])
        for i, (source, target) in enumerate(
            (
                (q_full, w_q), (k_full, w_k), (v_full, w_v),
                (output_part.at[:, :, :, core_bit], output_keep),
            )
        )
    ]

    def bring(b):
        return pltpu.make_async_copy(
            tokens_all.at[b], token_buf.at[lax.rem(b, 2)], load_t.at[lax.rem(b, 2)]
        )

    for copy in loads[1:]:
        copy.start()
    first = pltpu.make_async_copy(g_own.at[head], g_ref.at[head], here.at[0])
    first.start()
    pl.semaphore_wait(barrier, len(peers))
    to_heads = []
    for number, i in enumerate(range(parts, n_ctx, parts)):
        to_heads.append(
            pltpu.make_async_remote_copy(
                g_own.at[lax.div(flip(c, i), parts)], g_ref.at[head],
                send_g.at[number], recv_g.at[number],
                device_id=(flip(c, i), f), device_id_type=MESH,
            )
        )
        to_heads[-1].start()
    half = grads.shape[1] // 2
    quarter = half // 2
    mine = lax.rem(lax.div(c, 2), 2)
    second = lax.rem(lax.div(c, 4), 2)

    def halving(matrix, target, number):
        return pltpu.make_async_remote_copy(
            grads.at[matrix, pl.ds((1 - mine) * half, half)], target,
            send_half.at[number], recv_half.at[number],
            device_id=(flip(c, 2), f), device_id_type=MESH,
        )

    down_halving, gate_halving = halving(2, came, 0), halving(0, gate_first, 1)
    arriving = pltpu.make_async_copy(down_in, came, here.at[10]) if early else down_halving
    arriving.start()
    up_halving = pltpu.make_async_remote_copy(
        grads.at[1, pl.ds((1 - mine) * half, half), 0], up_came, send_half.at[4], recv_half.at[4],
        device_id=(flip(c, 2), f), device_id_type=MESH,
    )
    keeping = pltpu.make_async_copy(grads.at[2, pl.ds(mine * half, half)], kept, here.at[3])
    keeping.start()
    output_stages = [
        pltpu.make_async_remote_copy(
            source, target, send_out.at[i], recv_out.at[i], device_id=device, device_id_type=MESH
        )
        for i, (source, target, device) in enumerate(
            (
                (output_part.at[:, :, :, 1 - core_bit], output_came, (c, flip(f, 1))),
                (output_keep.at[:, :, 1 - x_bit], output_x, (c, flip(f, 2))),
                (output_x.at[:, 1 - pair], output_pair, (flip(c, 1), f)),
            )
        )
    ]
    output_stages[0].start()
    to_core = [
        pltpu.make_async_remote_copy(
            mix.at[2 * k + 1], mix_core.at[k], send_mix.at[k], recv_mix.at[k],
            device_id=(c, flip(f, 1)), device_id_type=MESH,
        )
        for k in range(4)
    ]
    for copy in to_core:
        copy.start()

    def plus(mine, came):
        return (mine.astype(F32) + came.astype(F32)).astype(BF16)

    def second_halving(keep, target, number, later=None):
        def add(i, nothing):
            at, e = lax.div(i, OWN), lax.rem(i, OWN)
            kept[at, e] = plus(kept[at, e], came[at, e])
            return nothing

        lax.fori_loop(0, half * OWN, add, 0)
        source = kept.at[pl.ds((1 - second) * quarter, quarter)]
        if later is not None:
            source, target = source.at[:, 0], target.at[:, 0]
            rest = pltpu.make_async_copy(
                kept.at[pl.ds((1 - second) * quarter, quarter), 1], later, here.at[3]
            )
            rest.start()
            rest.wait()
        going = pltpu.make_async_remote_copy(
            source, target, send_half.at[number], recv_half.at[number],
            device_id=(flip(c, 4), f), device_id_type=MESH,
        )
        going.start()
        staying = pltpu.make_async_copy(kept.at[pl.ds(second * quarter, quarter)], keep, here.at[4])
        staying.start()
        return going, staying

    if early:
        keeping.wait()
        arriving.wait()
        down_second, leaving = second_halving(down_keep, down_came, 2)
    gate_halving.start()
    shares = w_q.at[:, pl.ds(0, SEQS * BLOCK)]
    for k in range(4):
        pair_in = [
            pltpu.make_async_copy(mix.at[2 * k], token_buf.at[0], load_t.at[0]),
            pltpu.make_async_copy(mix_core.at[k], token_buf.at[1], load_t.at[1]),
        ]
        pair_in[0].start()
        to_core[k].wait_recv()
        pair_in[1].start()
        for copy in pair_in:
            copy.wait()
        shares[k] = plus(token_buf[0], token_buf[1])
    own_share = pltpu.make_async_copy(shares.at[0], mix_in.at[0], here.at[5])
    own_share.start()
    returns = [
        pltpu.make_async_remote_copy(
            shares.at[k], mix_in.at[k], send_mix.at[3 + k], recv_mix.at[3 + k],
            device_id=(flip(c, k // 2), flip(f, 2 * (k % 2))), device_id_type=MESH,
        )
        for k in range(1, 4)
    ]
    for copy in returns:
        copy.start()
    for b in range(2):
        bring(b).start()
    total[...] = jnp.zeros_like(total)
    first.wait()
    for copy in to_heads:
        copy.wait_recv()
    halves = half_masks(BF16)
    lane = lax.broadcasted_iota(jnp.int32, (rows, wide), 1)

    def query_back(j):
        return pltpu.make_async_remote_copy(
            dq_ref.at[j], dq_back.at[head], send_q.at[j], recv_q.at[head],
            device_id=(j * parts + part, f), device_id_type=MESH,
        )

    def key_back(b):
        return pltpu.make_async_remote_copy(
            dkv_ref.at[b], dkv_back.at[c], send_kv.at[b], recv_kv.at[c],
            device_id=(b, f), device_id_type=MESH,
        )

    def query_stays(j):
        return pltpu.make_async_copy(dq_ref.at[j], dq_back.at[head], here.at[1])

    def key_stays(b):
        return pltpu.make_async_copy(dkv_ref.at[b], dkv_back.at[c], here.at[2])

    def one_block(j, nothing):
        block = j * parts + part
        q = q_ref[j].reshape(rows, wide)
        g = g_ref[j].reshape(rows, wide)
        queries = [q * half for half in halves]
        partial = [g * half for half in halves]
        product = g.astype(F32) * full_ref[j].reshape(rows, wide)
        logs = log_ref[j].reshape(rows, wide)
        log_total = [logs[:, :1], logs[:, HEAD_SIZE : HEAD_SIZE + 1]]
        inner = [jnp.sum(product * half, axis=1, keepdims=True) for half in half_masks(F32)]

        def step(number, carry):
            k = kv_ref[pl.ds(2 * number, 2), 0].reshape(KEYS, wide)
            v = kv_ref[pl.ds(2 * number, 2), 1].reshape(KEYS, wide)
            codes = code_ref[number]
            after = []
            dk = jnp.zeros((KEYS, wide), F32)
            dv = jnp.zeros((KEYS, wide), F32)
            for s in range(SEQS):
                mask = allowed_at(block, number, seg_ref[j, s], codes[s : s + 1])
                scores = lax.dot_general(
                    queries[s], k, (((1,), (1,)), ((), ())), preferred_element_type=F32
                )
                scores = jnp.where(mask[None], scores.reshape(REP, BLOCK, KEYS) * SCALE, MASKED)
                probs = jnp.exp(scores.reshape(rows, KEYS) - log_total[s])
                grad_probs = lax.dot_general(
                    partial[s], v, (((1,), (1,)), ((), ())), preferred_element_type=F32
                )
                grad_scores = (probs * (grad_probs - inner[s])).astype(BF16)
                dv = dv + lax.dot_general(
                    probs.astype(BF16), partial[s], (((0,), (0,)), ((), ())), preferred_element_type=F32
                )
                dk = dk + lax.dot_general(
                    grad_scores, queries[s], (((0,), (0,)), ((), ())), preferred_element_type=F32
                )
                after.append(carry[s] + jnp.dot(grad_scores, k, preferred_element_type=F32))
            total[pl.ds(2 * number, 2), 0] += dk.reshape(2, BLOCK, wide)
            total[pl.ds(2 * number, 2), 1] += dv.reshape(2, BLOCK, wide)
            return tuple(after)

        start = jnp.zeros((rows, wide), F32)
        done = lax.fori_loop(0, lax.div(block, 2) + 1, step, (start,) * SEQS)
        dq = (jnp.where(lane < HEAD_SIZE, done[0], done[1]) * SCALE).reshape(REP, BLOCK, wide)
        dq_ref[j] = turn_back(dq, cos_ref[block][None], sin_ref[block][None]).astype(BF16)

        @pl.when(j != head)
        def _():
            query_back(j).start()

        @pl.when(j == head)
        def _():
            query_stays(j).start()

        return nothing

    lax.fori_loop(0, KEY_VALUE_HEADS, one_block, 0)

    def finish(b, nothing):
        dkv_ref[b, 0] = turn_back(total[b, 0] * SCALE, cos_ref[b], sin_ref[b]).astype(BF16)
        dkv_ref[b, 1] = total[b, 1].astype(BF16)

        @pl.when(b != c)
        def _():
            key_back(b).start()

        @pl.when(b == c)
        def _():
            key_stays(b).start()

        return nothing

    lax.fori_loop(0, n_ctx, finish, 0)
    up_halving.start()
    if not early:
        keeping.wait()
        down_halving.wait_recv()
        down_second, leaving = second_halving(down_keep, down_came, 2)

    planes = output_keep.shape[0]

    loads[3].wait()
    output_stages[0].wait_recv()

    def cores(i, nothing):
        r, p, x = lax.div(i, 4), lax.rem(lax.div(i, 2), 2), lax.rem(i, 2)
        output_keep[r, p, x] = plus(output_keep[r, p, x], output_came[r, p, x])
        return nothing

    lax.fori_loop(0, planes * 4, cores, 0)
    output_stages[1].start()

    low = lax.broadcasted_iota(jnp.int32, (BLOCK, wide), 1) < HEAD_SIZE

    def side_by_side(even, odd):
        even, odd = even.astype(F32), odd.astype(F32)
        return (
            jnp.where(low, even, pltpu.roll(odd, HEAD_SIZE, 1)),
            jnp.where(low, pltpu.roll(even, HEAD_SIZE, 1), odd),
        )

    head_acc[...] = jnp.zeros_like(head_acc)

    def head_weights(b, nothing):
        bring(b).wait()
        block = token_buf[lax.rem(b, 2)]
        wide_block = block.astype(F32)
        scales = lax.rsqrt(jnp.mean(wide_block * wide_block, axis=1, keepdims=True) + EPS)
        j = lax.div(b, parts)
        have = jnp.where(lax.rem(b, parts) == part, 1.0, 0.0)
        heads = [dq_ref[j, r].astype(F32) * have for r in range(REP)] + [dkv_ref[b, 0], dkv_ref[b, 1]]
        heads.append(jnp.zeros((BLOCK, wide), F32))
        for m in range((REP + 3) // 2):
            for s, value in enumerate(side_by_side(heads[2 * m], heads[2 * m + 1])):
                at = slice(s * BLOCK, (s + 1) * BLOCK)
                field[at, m * wide : (m + 1) * wide] = (value * scales[at]).astype(BF16)
        head_acc[...] += lax.dot_general(
            block, field[...], (((0,), (0,)), ((), ())), preferred_element_type=F32
        )

        @pl.when(b + 2 < n_ctx)
        def _():
            bring(b + 2).start()

        return nothing

    lax.fori_loop(0, n_ctx, head_weights, 0)
    slab = D // (n_ctx * 4)
    for d in range(n_ctx * 4):
        head_out[d // 4, d // 2 % 2, d % 2] = head_acc[
            d * slab : (d + 1) * slab, : head_out.shape[4]
        ].astype(BF16)
    head_stages = [
        pltpu.make_async_remote_copy(
            source, target, send_head.at[i], recv_head.at[i], device_id=device, device_id_type=MESH
        )
        for i, (source, target, device) in enumerate(
            (
                (head_out.at[:, :, 1 - core_bit], head_core, (c, flip(f, 1))),
                (head_core.at[:, 1 - x_bit], head_x, (c, flip(f, 2))),
            )
        )
    ]
    head_stages[0].start()
    for copy in returns:
        copy.wait_send()
    own_share.wait()
    loads[0].start()
    down_second.wait_send()
    leaving.wait()
    gate_halving.wait_recv()
    refill = [
        pltpu.make_async_copy(grads.at[0, pl.ds(mine * half, half)], kept, here.at[3]),
        pltpu.make_async_copy(gate_first, came, here.at[10]),
    ]
    for copy in refill:
        copy.start()
    for copy in refill:
        copy.wait()
    gate_second, leaving = second_halving(gate_keep, gate_came, 3, gate_other)

    head_stages[0].wait_recv()

    def head_cores(i, nothing):
        d, x = lax.div(i, 2), lax.rem(i, 2)
        head_core[d, x] = plus(head_out[d, x, core_bit], head_core[d, x])
        return nothing

    lax.fori_loop(0, n_ctx * 2, head_cores, 0)
    head_stages[1].start()

    def came_query(h, nothing):
        @pl.when(h != head)
        def _():
            pltpu.make_async_remote_copy(
                dq_ref.at[h], dq_back.at[h], send_q.at[h], recv_q.at[h],
                device_id=(h * parts + part, f), device_id_type=MESH,
            ).wait()

        @pl.when(h == head)
        def _():
            query_stays(h).wait()

        return nothing

    def came_key(b, nothing):
        @pl.when(b != c)
        def _():
            pltpu.make_async_remote_copy(
                dkv_ref.at[b], dkv_back.at[b], send_kv.at[b], recv_kv.at[b],
                device_id=(b, f), device_id_type=MESH,
            ).wait()

        @pl.when(b == c)
        def _():
            key_stays(b).wait()

        return nothing

    lax.fori_loop(0, KEY_VALUE_HEADS, came_query, 0)
    lax.fori_loop(0, n_ctx, came_key, 0)

    def head_of(h):
        if h < QUERY_HEADS:
            return dq_back[h // REP, h % REP]
        kind, h = (h - QUERY_HEADS) // KEY_VALUE_HEADS, (h - QUERY_HEADS) % KEY_VALUE_HEADS
        value = dkv_back[h * parts, kind]
        if parts > 1:
            value = value.astype(F32)
            for p in range(1, parts):
                value = value + dkv_back[h * parts + p, kind].astype(F32)
        return value

    head_stages[1].wait_recv()

    def head_over_x(d, nothing):
        head_x[d] = plus(head_core[d, x_bit], head_x[d])
        return nothing

    lax.fori_loop(0, n_ctx, head_over_x, 0)
    head_stays = pltpu.make_async_copy(head_x.at[c], head_in.at[c], here.at[9])
    head_stays.start()
    to_all = []
    for i in range(1, n_ctx):
        to_all.append(
            pltpu.make_async_remote_copy(
                head_x.at[flip(c, i)], head_in.at[c], send_head.at[1 + i], recv_head.at[1 + i],
                device_id=(flip(c, i), f), device_id_type=MESH,
            )
        )
        to_all[-1].start()
    for m in range((QUERY_HEADS + 2 * KEY_VALUE_HEADS) // 2):
        for s, value in enumerate(side_by_side(head_of(2 * m), head_of(2 * m + 1))):
            grad_qkv[s * BLOCK : (s + 1) * BLOCK, m * wide : (m + 1) * wide] = value.astype(BF16)
    for copy in loads[:3]:
        copy.wait()
    depth = D // 4
    for b in range(4):
        made, at = 0.0, 0
        for weight in (w_q, w_k, w_v):
            width = weight.shape[2]
            made = made + lax.dot_general(
                grad_qkv[:, at : at + width], weight[b], (((1,), (1,)), ((), ())),
                preferred_element_type=F32,
            )
            at += width
        grad_in[:, b * depth : (b + 1) * depth] = made
    x = tok[...].astype(F32)
    scale = lax.rsqrt(jnp.mean(x * x, axis=1, keepdims=True) + EPS)
    gain_grad[...] = jnp.sum(grad_in[...] * x * scale, axis=0, keepdims=True)
    weighted = grad_in[...] * gain[...]
    input_grad[...] = (
        resid_grad[...]
        + scale * weighted
        - x * (scale * scale * scale) * jnp.mean(weighted * x, axis=1, keepdims=True)
    ).astype(BF16)

    staying = pltpu.make_async_copy(residual, grad_in, here.at[8])
    staying.start()
    staying.wait()

    def share(k):
        return pltpu.make_async_copy(mix_in.at[k], token_buf.at[k % 2], load_t.at[k % 2])

    share(0).start()
    for k in range(4):
        if k < 3:
            returns[k].wait_recv()
            share(k + 1).start()
        share(k).wait()
        grad_in[...] += token_buf[k % 2].astype(F32)
    layer_out[...] = grad_in[...].astype(BF16)

    output_stages[1].wait_recv()

    def over_x(i, nothing):
        r, p = lax.div(i, 2), lax.rem(i, 2)
        output_x[r, p] = plus(output_keep[r, p, x_bit], output_x[r, p])
        return nothing

    lax.fori_loop(0, planes * 2, over_x, 0)
    output_stages[2].start()
    output_stages[2].wait_recv()

    def over_pair(r, nothing):
        output_sum[r] = plus(output_x[r, pair], output_pair[r])
        return nothing

    lax.fori_loop(0, planes, over_pair, 0)
    for copy in to_heads:
        copy.wait_send()
    for copy in to_all + [gate_second, up_halving, leaving, head_stays]:
        copy.wait()
    down_second.wait_recv()
    for copy in to_core + output_stages + head_stages + [gate_halving] + ([] if early else [down_halving]):
        copy.wait_send()


def attention_backward(
    cid, parts, n_ctx, early, g_own, q, kv, segq, codes, full, logs, cosine, sine,
    tok, gain, resid_grad, residual, grads, down_in, mix, output_part, tokens_all, q_full, k_full, v_full,
):
    wide = 2 * HEAD_SIZE
    anywhere = pl.BlockSpec(memory_space=pl.ANY)
    inside = pl.BlockSpec(memory_space=pltpu.VMEM)
    dma = pltpu.SemaphoreType.DMA
    others = max(n_ctx // parts - 1, 1)
    devices, planes = n_ctx * 4, n_ctx // 2
    slab, head_width = D // devices, (REP + 2) * HEAD_SIZE
    half = (grads.shape[1] // 2,) + grads.shape[2:]
    quarter = (grads.shape[1] // 4,) + grads.shape[2:]
    columns = q_full.shape[2] + k_full.shape[2] + v_full.shape[2]
    return pl.pallas_call(
        functools.partial(attention_backward_kernel, parts, n_ctx, early),
        name="attention_backward",
        out_shape=[
            jax.ShapeDtypeStruct(tok.shape, BF16),
            jax.ShapeDtypeStruct(tok.shape, BF16),
            jax.ShapeDtypeStruct((1, D), F32),
            jax.ShapeDtypeStruct((planes, slab, D), BF16),
            jax.ShapeDtypeStruct(half, BF16),
            jax.ShapeDtypeStruct(quarter, BF16),
            jax.ShapeDtypeStruct(quarter, BF16),
            jax.ShapeDtypeStruct(quarter[:1] + quarter[2:], BF16),
            jax.ShapeDtypeStruct(half[:1] + half[2:], BF16),
            jax.ShapeDtypeStruct(quarter, BF16),
            jax.ShapeDtypeStruct(quarter, BF16),
            jax.ShapeDtypeStruct((4,) + mix.shape[1:], BF16),
            jax.ShapeDtypeStruct((4,) + mix.shape[1:], BF16),
            jax.ShapeDtypeStruct((n_ctx, slab, head_width), BF16),
        ],
        in_specs=[anywhere] + [inside] * 11 + [anywhere] * 9,
        out_specs=[inside] * 4 + [anywhere] * 10,
        scratch_shapes=[
            pltpu.VMEM(q.shape, BF16),
            pltpu.VMEM((n_ctx, 2, BLOCK, wide), F32),
            pltpu.VMEM(half, BF16),
            pltpu.VMEM(half, BF16),
            pltpu.VMEM(q.shape, BF16),
            pltpu.VMEM(kv.shape, BF16),
            pltpu.VMEM(q.shape, BF16),
            pltpu.VMEM(kv.shape, BF16),
            pltpu.VMEM(q_full.shape, BF16),
            pltpu.VMEM(k_full.shape, BF16),
            pltpu.VMEM(v_full.shape, BF16),
            pltpu.VMEM((SEQS * BLOCK, columns), BF16),
            pltpu.VMEM((SEQS * BLOCK, D), F32),
            pltpu.VMEM((2, SEQS * BLOCK, D), BF16),
            pltpu.VMEM((SEQS * BLOCK, 3 * wide), BF16),
            pltpu.VMEM((D, 3 * wide), F32),
            pltpu.VMEM((n_ctx, 2, 2, slab, head_width), BF16),
            pltpu.VMEM((n_ctx, 2, slab, head_width), BF16),
            pltpu.VMEM((n_ctx, slab, head_width), BF16),
            pltpu.VMEM((planes, 2, 2, slab, D), BF16),
            pltpu.VMEM((planes, 2, 2, slab, D), BF16),
            pltpu.VMEM((planes, 2, slab, D), BF16),
            pltpu.VMEM((planes, slab, D), BF16),
            dma((others,)), dma((others,)), dma((KEY_VALUE_HEADS,)), dma((KEY_VALUE_HEADS,)),
            dma((n_ctx,)), dma((n_ctx,)), dma((RANKS - 1,)), dma((RANKS - 1,)), dma((5,)), dma((5,)),
            dma((11,)), dma((3,)), dma((3,)), dma((n_ctx + 1,)), dma((n_ctx + 1,)), dma((2,)),
        ],
        compiler_params=pltpu.CompilerParams(
            collective_id=cid, has_side_effects=True, vmem_limit_bytes=62 << 20
        ),
        cost_estimate=lasting(125),
    )(
        g_own, q, kv, segq, codes, full, logs, cosine, sine, tok, gain, resid_grad, residual,
        grads, down_in, mix, output_part, tokens_all, q_full, k_full, v_full,
    )


def final_kernel(
    n_ctx, small, output_part, grads, gate_keep, gate_came, gate_other, up_came, down_keep, down_came,
    swapped, output_grad, small_sum,
    halves, landed, rest, rest_landed, last, last_landed, turned, output_in, small_in,
    send_half, recv_half, send_deep, recv_deep, send_out, recv_out, send_small, recv_small,
    send_swap, recv_swap, load, stay,
):
    c, f = lax.axis_index("ctx"), lax.axis_index("fsdp")
    me, plane, rank = c * 4 + f, lax.div(c, 2), lax.rem(c, 2) * 4 + f
    planes = n_ctx // 2
    half, quarter = planes // 2, planes // 4
    barrier = pltpu.get_barrier_semaphore()
    peers = [(i, k) for i in range(n_ctx) for k in range(4) if i or k]
    for dc, df in peers:
        pl.semaphore_signal(
            barrier, inc=1, device_id=(flip(c, dc), flip(f, df)), device_id_type=MESH
        )
    first, second = lax.rem(plane, 2), lax.rem(lax.div(plane, 2), 2)
    loads = [
        pltpu.make_async_copy(source, target, load.at[i])
        for i, (source, target) in enumerate(
            (
                (down_keep, rest.at[2]),
                (down_came, rest_landed.at[2]),
                (gate_keep, rest.at[0]),
                (gate_came.at[:, 0], rest_landed.at[0, :, 0]),
                (grads.at[1, pl.ds(first * half, half)], halves),
                (output_part.at[plane], output_in.at[plane]),
                (small.at[me], small_in.at[me]),
                (up_came, landed.at[:, 0]),
            )
        )
    ]
    for copy in loads:
        copy.start()
    pl.semaphore_wait(barrier, len(peers))

    def over(source, target, sent, came, bit):
        return pltpu.make_async_remote_copy(
            source, target, sent, came, device_id=(flip(c, 2 * bit), f), device_id_type=MESH
        )

    up_first = over(
        grads.at[1, pl.ds((1 - first) * half, half), 1], landed.at[:, 1],
        send_half.at[0, 1], recv_half.at[0, 1], 1,
    )
    gate_second = over(gate_other, rest_landed.at[0, :, 1], send_half.at[2, 1], recv_half.at[2, 1], 2)
    up_first.start()
    outputs = []
    for i in range(1, planes):
        outputs.append(
            pltpu.make_async_remote_copy(
                output_part.at[flip(plane, i)], output_in.at[plane], send_out.at[i - 1], recv_out.at[i - 1],
                device_id=(flip(c, 2 * i), f), device_id_type=MESH,
            )
        )
    smalls = []
    for number, (i, k) in enumerate(peers):
        peer_c, peer_f = flip(c, i), flip(f, k)
        smalls.append(
            pltpu.make_async_remote_copy(
                small.at[peer_c * 4 + peer_f], small_in.at[me], send_small.at[number], recv_small.at[number],
                device_id=(peer_c, peer_f), device_id_type=MESH,
            )
        )

    def plus(mine, came):
        return (mine.astype(F32) + came.astype(F32)).astype(BF16)

    swaps, sent = [], []

    def finish(m, e):
        count, bit, number = quarter, 4, 0
        for at in range(quarter):
            rest[m, at, e] = plus(rest[m, at, e], rest_landed[m, at, e])
        mine = rest.at[m, :, e]
        while count > 1:
            count //= 2
            chosen = lax.rem(lax.div(plane, bit), 2)
            came = last_landed.at[m, number, pl.ds(0, count), e]
            copy = over(
                mine.at[pl.ds((1 - chosen) * count, count)], came,
                send_deep.at[2 * m + number, e], recv_deep.at[2 * m + number, e], bit,
            )
            copy.start()
            copy.wait_recv()
            sent.append(copy)
            for at in range(count):
                last[m, number, at, e] = plus(mine[chosen * count + at], came[at])
            mine, bit, number = last.at[m, number, :, e], bit * 2, number + 1
        rows = turned.shape[3]
        across = mine[0].astype(F32).T
        for r in range(RANKS):
            turned[m, r, e] = across[r * rows : (r + 1) * rows].astype(BF16)
        for i in range(RANKS):
            source, target = turned.at[m, flip(rank, i), e], swapped.at[rank, m, e]
            if i:
                copy = pltpu.make_async_remote_copy(
                    source, target, send_swap.at[m * OWN + e, i], recv_swap.at[m * OWN + e, i],
                    device_id=(flip(c, i // 4), flip(f, i % 4)), device_id_type=MESH,
                )
            else:
                copy = pltpu.make_async_copy(source, target, stay.at[m * OWN + e])
            copy.start()
            swaps.append(copy)

    for copy in loads:
        copy.wait()
    up_second = []

    def second_of_up(e):
        for at in range(half):
            halves[at, e] = plus(halves[at, e], landed[at, e])
        up_second.append(
            over(
                halves.at[pl.ds((1 - second) * quarter, quarter), e], rest_landed.at[1, :, e],
                send_half.at[1, e], recv_half.at[1, e], 2,
            )
        )
        up_second[e].start()
        for at in range(quarter):
            rest[1, at, e] = halves[second * quarter + at, e]

    second_of_up(0)
    gate_second.start()
    for copy in outputs + smalls:
        copy.start()
    for e in range(OWN):
        finish(2, e)
    finish(0, 0)
    up_first.wait_recv()
    second_of_up(1)
    gate_second.wait_recv()
    finish(0, 1)
    for copy in outputs + smalls:
        copy.wait_recv()
    made = output_in[0].astype(F32)
    for i in range(1, planes):
        made = made + output_in[i].astype(F32)
    output_grad[...] = made
    small_sum[...] = jnp.sum(small_in[...], axis=0)
    for e in range(OWN):
        up_second[e].wait_recv()
        finish(1, e)
    for copy in swaps:
        copy.wait()
    for copy in smalls + outputs + sent + up_second + [up_first, gate_second]:
        copy.wait_send()


def final_sums(
    cid, n_ctx, small, output_part, grads, gate_keep, gate_came, gate_other, up_came, down_keep,
    down_came
):
    anywhere = pl.BlockSpec(memory_space=pl.ANY)
    inside = pl.BlockSpec(memory_space=pltpu.VMEM)
    dma = pltpu.SemaphoreType.DMA
    devices, planes = n_ctx * 4, n_ctx // 2
    slab, piece = D // devices, grads.shape[2:]
    half, quarter = (planes // 2,) + piece, (planes // 4,) + piece
    deep = (3, 2, max(planes // 8, 1)) + piece
    return pl.pallas_call(
        functools.partial(final_kernel, n_ctx),
        name="final_sums",
        out_shape=[
            jax.ShapeDtypeStruct((RANKS, 3, OWN, slab, FF), BF16),
            jax.ShapeDtypeStruct((slab, D), F32),
            jax.ShapeDtypeStruct(small.shape[1:], F32),
        ],
        in_specs=[anywhere] * 9,
        out_specs=[anywhere] + [inside] * 2,
        scratch_shapes=[
            pltpu.VMEM(half, BF16),
            pltpu.VMEM(half, BF16),
            pltpu.VMEM((3,) + quarter, BF16),
            pltpu.VMEM((3,) + quarter, BF16),
            pltpu.VMEM(deep if planes > 4 else (1, 1, 1, 1, 8, 128), BF16),
            pltpu.VMEM(deep if planes > 4 else (1, 1, 1, 1, 8, 128), BF16),
            pltpu.VMEM((3, RANKS, OWN, slab, FF), BF16),
            pltpu.VMEM((planes, slab, D), BF16),
            pltpu.VMEM(small.shape, F32),
            dma((3, OWN)), dma((3, OWN)), dma((6, OWN)), dma((6, OWN)),
            dma((planes - 1,)), dma((planes - 1,)), dma((devices - 1,)), dma((devices - 1,)),
            dma((3 * OWN, RANKS)), dma((3 * OWN, RANKS)), dma((8,)), dma((3 * OWN,)),
        ],
        compiler_params=pltpu.CompilerParams(
            collective_id=cid, has_side_effects=True, vmem_limit_bytes=56 << 20
        ),
        cost_estimate=lasting(80),
    )(small, output_part, grads, gate_keep, gate_came, gate_other, up_came, down_keep, down_came)


def rope_tables(positions):
    half_dim = HEAD_SIZE // 2
    frequency = ROPE_BASE ** (-jnp.arange(half_dim, dtype=F32) * 2.0 / HEAD_SIZE)
    angle = positions.astype(F32)[:, None] * frequency[None, :]
    angle = jnp.concatenate([angle, angle], axis=1)
    return (jnp.cos(angle), jnp.sin(angle))


def heads_out(field, per):
    field = field.reshape(SEQS, BLOCK, KEY_VALUE_HEADS, per, HEAD_SIZE)
    return field.transpose(2, 3, 1, 0, 4).reshape(KEY_VALUE_HEADS, per, BLOCK, SEQS * HEAD_SIZE)


def heads_in(field):
    per = field.shape[1]
    field = field.reshape(KEY_VALUE_HEADS, per, BLOCK, SEQS, HEAD_SIZE)
    return field.transpose(3, 2, 0, 1, 4).reshape(SEQS, BLOCK, KEY_VALUE_HEADS * per * HEAD_SIZE)


def on_device(
    n_ctx,
    n_fsdp,
    tokens,
    segments,
    valid,
    expert_ids,
    slot_order,
    cotangent,
    norm1_gain,
    w_query,
    key_weight,
    value_weight,
    w_output,
    norm2_gain,
    w_router,
    w_gate,
    w_up,
    w_down,
):
    parts = n_ctx // KEY_VALUE_HEADS
    replicas = n_ctx // 2
    full_len = segments.shape[1]
    c_index, f_index = lax.axis_index("ctx"), lax.axis_index("fsdp")
    pair = lax.rem(c_index, 2)
    rank = pair * n_fsdp + f_index
    part = lax.rem(c_index, parts)
    head = lax.div(c_index, parts)
    positions = c_index * BLOCK + jnp.arange(BLOCK, dtype=jnp.int32)

    span = D // n_fsdp // 2
    nears = [
        lax.ppermute(
            lax.dynamic_slice_in_dim(w, pair * span, span, 0), "fsdp", [(a, a ^ 2) for a in range(n_fsdp)]
        )
        for w in (w_query, key_weight, value_weight)
    ]
    tokens_all = lax.all_gather(tokens, "ctx", axis=0, tiled=False)
    small = jnp.concatenate(
        [
            norm1_gain[None],
            norm2_gain[None],
            w_router.T,
            jnp.zeros((SMALL - EXPERTS - 2, D // n_fsdp), BF16),
        ],
        axis=0,
    )
    packs = [
        lax.dynamic_slice_in_dim(w, pair * (EXPERTS // 2), EXPERTS // 2, 1)
        .reshape(D // n_fsdp, n_fsdp, OWN, FF)
        .transpose(1, 2, 0, 3)
        for w in (w_gate, w_up, w_down)
    ]
    inputs_f = tokens.astype(F32)
    scale_one = lax.rsqrt(jnp.mean(inputs_f * inputs_f, axis=-1, keepdims=True) + EPS)
    segq = segments.reshape(SEQS, KEY_VALUE_HEADS, parts, BLOCK)
    segq = lax.dynamic_index_in_dim(segq, part, 2, keepdims=False).transpose(1, 0, 2)[..., None]
    codes = jnp.where(valid > 0, segments, -1)
    codes = codes.reshape(SEQS, full_len // KEYS, KEYS).transpose(1, 0, 2)
    all_cosine, all_sine = rope_tables(jnp.arange(full_len, dtype=jnp.int32))
    all_cosine = jnp.tile(all_cosine, (1, 2)).reshape(n_ctx, BLOCK, 2 * HEAD_SIZE)
    all_sine = jnp.tile(all_sine, (1, 2)).reshape(n_ctx, BLOCK, 2 * HEAD_SIZE)
    (
        normed_in, small_all, full_query, full_key, full_value, q_all, kv_all, head_full, head_logs,
        attn_heads, full_output, own_gate, own_up, own_down,
    ) = attention_forward(
        0, parts, n_ctx, tokens.reshape(SEQS * BLOCK, D), small, w_query, key_weight, value_weight,
        w_output, nears, packs,
        lax.dynamic_index_in_dim(all_cosine, c_index, 0, keepdims=False),
        lax.dynamic_index_in_dim(all_sine, c_index, 0, keepdims=False),
        segq, codes,
    )
    gain_first = small_all[:, 0].reshape(D).astype(F32)
    gain_second = small_all[:, 1].reshape(D).astype(F32)
    full_router = small_all[:, 2 : 2 + EXPERTS].transpose(1, 0, 2).reshape(EXPERTS, D)
    full_output = full_output.reshape(D, D)
    attn_out = heads_in(attn_heads)
    attn_proj = jnp.einsum("sgq,dq->sgd", attn_out, full_output, preferred_element_type=F32)
    residual = inputs_f + attn_proj
    scale_two = lax.rsqrt(jnp.mean(residual * residual, axis=-1, keepdims=True) + EPS)
    normed_mid = (residual * scale_two * gain_second).astype(BF16)

    logits = jnp.einsum("sgd,ed->sge", normed_mid, full_router, preferred_element_type=F32)
    picked = jnp.any(expert_ids[..., None] == jnp.arange(EXPERTS, dtype=jnp.int32), axis=2)
    before = (slot_order[:, None, :] < slot_order[:, :, None]).astype(BF16)
    place = jnp.matmul(before, picked.astype(BF16), preferred_element_type=F32)
    is_kept = picked & (place < CAP)
    chosen = jnp.where(picked, logits, MASKED)
    raised = jnp.where(picked, jnp.exp(chosen - jnp.max(chosen, axis=-1, keepdims=True)), 0.0)
    gates = raised / jnp.sum(raised, axis=-1, keepdims=True)
    payload = jnp.concatenate(
        [
            normed_mid,
            jnp.where(is_kept, place, -1.0).astype(BF16),
            gates.astype(BF16),
            jnp.zeros((SEQS, BLOCK, 128 - 2 * EXPERTS), BF16),
        ],
        axis=2,
    )
    back, mix_part, own_grads, down_first, down_early = run_experts(
        2, replicas, payload.reshape(SEQS * BLOCK, PAY), cotangent.reshape(SEQS * BLOCK, D),
        (own_gate, own_up, own_down), tokens_all
    )

    back = back.reshape(SEQS, BLOCK, D + 128)
    grad_gates = jnp.where(is_kept, back[..., D : D + EXPERTS], 0.0)
    grad_chosen = gates * (grad_gates - jnp.sum(gates * grad_gates, axis=-1, keepdims=True))
    grad_logits = grad_chosen.astype(BF16)
    grad_mid = back[..., :D] + jnp.einsum(
        "sge,ed->sgd", grad_logits, full_router, preferred_element_type=F32
    )
    grad_router = jnp.einsum("sgd,sge->de", normed_mid, grad_logits, preferred_element_type=F32)

    grad_f = cotangent.astype(F32)
    weighted_two = gain_second * grad_mid
    grad_gain_second = jnp.sum(grad_mid * residual * scale_two, axis=(0, 1))
    cube_two = scale_two * scale_two * scale_two
    grad_resid = (
        grad_f
        + scale_two * weighted_two
        - residual * cube_two * jnp.mean(weighted_two * residual, axis=-1, keepdims=True)
    )
    grad_resid_low = grad_resid.astype(BF16)
    grad_attn = jnp.einsum("sgd,dq->sgq", grad_resid_low, full_output, preferred_element_type=F32)
    grad_attn = grad_attn.astype(BF16)
    grad_output_w = jnp.einsum("sgd,sgq->dq", grad_resid_low, attn_out, preferred_element_type=F32)
    rows = D // (n_ctx * n_fsdp)
    output_part = grad_output_w.astype(BF16).reshape(replicas, 2, 2, 2, rows, D)

    (
        input_grad, layer_out, gain_grad, output_sum, _, gate_keep, gate_came, gate_other, up_came, down_keep,
        down_came, _, _, head_grads,
    ) = attention_backward(
        6, parts, n_ctx, down_early, heads_out(grad_attn, REP), q_all, kv_all, segq, codes, head_full, head_logs,
        all_cosine, all_sine, tokens.reshape(SEQS * BLOCK, D), gain_first[None],
        grad_resid.reshape(SEQS * BLOCK, D), residual.reshape(SEQS * BLOCK, D), own_grads, down_first, mix_part, output_part,
        tokens_all.reshape(n_ctx, SEQS * BLOCK, D), full_query, full_key, full_value,
    )
    input_grad = input_grad.reshape(SEQS, BLOCK, D)
    layer_out = layer_out.reshape(SEQS, BLOCK, D)
    amount = rows * (EXPERTS + 2)
    tiles = -(-amount // 1024) * 8
    small_grads = jnp.concatenate([grad_router, gain_grad.T, grad_gain_second[:, None]], axis=1)
    small_grads = jnp.pad(
        small_grads.reshape(n_ctx * n_fsdp, amount), ((0, 0), (0, tiles * 128 - amount))
    ).reshape(n_ctx * n_fsdp, tiles, 128)
    swapped, output_grad, small_sum = final_sums(
        9, n_ctx, small_grads, output_sum, own_grads, gate_keep, gate_came, gate_other, up_came,
        down_keep, down_came,
    )
    small_sum = small_sum.reshape(tiles * 128)[:amount].reshape(rows, EXPERTS + 2)
    head_grads = head_grads.reshape(KEY_VALUE_HEADS, parts, rows, (REP + 2) * HEAD_SIZE)
    own_gain = lax.dynamic_slice_in_dim(gain_first, (c_index * n_fsdp + f_index) * rows, rows, 0)
    head_grads = jnp.sum(head_grads.astype(F32), axis=1).transpose(1, 0, 2) * own_gain[:, None, None]
    query_grad = head_grads[..., : REP * HEAD_SIZE].reshape(rows, D)
    key_grad = head_grads[..., REP * HEAD_SIZE : (REP + 1) * HEAD_SIZE].reshape(rows, -1)
    value_grad = head_grads[..., (REP + 1) * HEAD_SIZE :].reshape(rows, -1)

    def by_row(matrix):
        return swapped[:, matrix].transpose(2, 0, 1, 3).reshape(rows, EXPERTS, FF).astype(F32)

    return (
        layer_out,
        input_grad,
        small_sum[:, EXPERTS],
        query_grad,
        key_grad,
        value_grad,
        output_grad,
        small_sum[:, EXPERTS + 1],
        small_sum[:, :EXPERTS],
        by_row(0),
        by_row(1),
        by_row(2),
    )


def solution(mesh):
    placed = (
        P("fsdp", "ctx", None),
        P("fsdp", None),
        P("fsdp", None),
        P("fsdp", "ctx", None),
        P("fsdp", "ctx"),
        P("fsdp", "ctx", None),
        P("fsdp"),
        P("fsdp", None),
        P("fsdp", None),
        P("fsdp", None),
        P("fsdp", None),
        P("fsdp"),
        P("fsdp", None),
        P("fsdp", None, None),
        P("fsdp", None, None),
        P("fsdp", None, None),
    )
    return jax.shard_map(
        functools.partial(on_device, mesh.shape["ctx"], mesh.shape["fsdp"]),
        mesh=mesh,
        in_specs=placed,
        out_specs=(
            P("fsdp", "ctx", None),
            P("fsdp", "ctx", None),
            P(("ctx", "fsdp")),
            P(("ctx", "fsdp"), None),
            P(("ctx", "fsdp"), None),
            P(("ctx", "fsdp"), None),
            P(("ctx", "fsdp"), None),
            P(("ctx", "fsdp")),
            P(("ctx", "fsdp"), None),
            P(("ctx", "fsdp"), None, None),
            P(("ctx", "fsdp"), None, None),
            P(("ctx", "fsdp"), None, None),
        ),
        check_vma=False,
    )
```
